32 devices in a mesh: section: 4 (over x, core), row: 4 (over z), dp: 2 (over y).
Axes of the slice: x: 2, y: 2, z: 4, core: 2. Of those that a mesh axis runs over, the one named last changes fastest.
Arguments:
- inputs: bfloat16 [4, 2, 16, 48, 352], P(None, 'dp', 'row'), may hold values from -8 to 8
- depth_kernel: bfloat16 [4, 7, 7, 352], P('section'), may hold values from -0.875 to 0.875
- depth_bias: bfloat16 [4, 352], P('section'), may hold values from -3 to 3
- norm_gain: bfloat16 [4, 352], P('section'), may hold values from 0.099609375 to 1.8984375
- norm_bias: bfloat16 [4, 352], P('section'), may hold values from -3 to 3
- proj_in: bfloat16 [4, 352, 1408], P('section', None, 'dp'), may hold values from -0.3125 to 0.3125
- bias_in: bfloat16 [4, 1408], P('section'), may hold values from -3 to 3
- grn_gamma: bfloat16 [4, 1408], P('section'), may hold values from -3 to 3
- grn_beta: bfloat16 [4, 1408], P('section'), may hold values from -2 to 2
- proj_out: bfloat16 [4, 1408, 352], P('section', 'dp'), may hold values from -0.15625 to 0.15625
- bias_out: bfloat16 [4, 352], P('section'), may hold values from -3 to 3
Outputs:
- saved: bfloat16 [4, 4, 2, 16, 48, 352], P('section', None, 'dp', 'row')
The draws below stay inside these ranges and needn't reach their ends.
All inputs are finite; a program needn't handle non-finite values.
Results may differ from the reference program's by a relative error of at most 0.015.
Values may be sent and summed in bfloat16 or wider, within the bound.
No kernel may reach another device: no remote copies, remote signals or barrier semaphores. Data moves between devices by JAX's collectives and lax.ppermute only.
A program may use at most 64 MiB of HBM per device.

```python
import jax
import jax.numpy as jnp
from jax import lax

C = 352
FF = 1408
COLS = 48
MICRO = 4
HEIGHT = 16
IMAGES = 2
BLOCKS = 4


def draw_inputs(key, part):
    key_noise, key_rows, key_chan, key_dir, key_amp = jax.random.split(jax.random.fold_in(key, 17), 5)
    full_shape = (MICRO, IMAGES, HEIGHT, COLS, C)
    noise = jax.random.normal(key_noise, full_shape, jnp.float32)
    row_scale = jnp.exp(jax.random.uniform(key_rows, (MICRO, IMAGES, HEIGHT, 1, 1), jnp.float32, -0.7, 0.7))
    chan_scale = jnp.exp(jax.random.uniform(key_chan, (MICRO, IMAGES, 1, 1, C), jnp.float32, 0.0, 2.3)) * 0.2
    direction = jax.random.normal(key_dir, (MICRO, IMAGES, 1, 1, C), jnp.float32)
    amplitude = jax.random.uniform(key_amp, (MICRO, IMAGES, 1, 1, 1), jnp.float32, 0.75, 2.0)
    row_ramp = (jnp.arange(HEIGHT, dtype=jnp.float32) / (HEIGHT - 1)).reshape(1, 1, HEIGHT, 1, 1)
    values = noise * chan_scale * row_scale + amplitude * row_ramp * direction
    return jnp.clip(values, -8.0, 8.0).astype(jnp.bfloat16)


def block_levels(stream_key, dims, pieces, least, high):
    gain, own = 1.0, jax.random.fold_in(stream_key, 6)
    for dim, blocks in pieces:
        draws = jnp.exp(jax.random.uniform(jax.random.fold_in(own, dim), (blocks,), jnp.float32, least / len(pieces), high / len(pieces)))
        gain = gain * jnp.repeat(draws, dims[dim] // blocks).reshape([-1 if axis == dim else 1 for axis in range(len(dims))])
    return gain


def bell_draw(rng, extent, scale, limit, cuts=(), held_as=jnp.bfloat16):
    drawn = scale * jax.random.normal(rng, extent, jnp.float32)
    if cuts:
        drawn = drawn * block_levels(rng, extent, cuts, -0.22, 0.18)
    return jnp.clip(drawn, -limit, limit).astype(held_as)


def setup_inputs(seed: int = 0) -> dict:
    splits = jax.random.split(jax.random.key(seed), 12)
    return {
        "inputs": draw_inputs(jax.random.fold_in(splits[11], 71), 0),
        "depth_kernel": bell_draw(splits[1], (BLOCKS, 7, 7, C), 49 ** -0.5, 0.875, ((0, 4),)),
        "depth_bias": bell_draw(splits[2], (BLOCKS, C), 0.5, 3.0, ((0, 4),)),
        "norm_gain": jnp.clip(1.0 + 0.18 * jax.random.normal(splits[3], (BLOCKS, C), jnp.float32), 0.099609375, 1.8984375).astype(jnp.bfloat16),
        "norm_bias": bell_draw(splits[4], (BLOCKS, C), 0.5, 3.0, ((0, 4),)),
        "proj_in": bell_draw(splits[5], (BLOCKS, C, FF), C ** -0.5, 0.3125, ((0, 4), (2, 2))),
        "bias_in": bell_draw(splits[6], (BLOCKS, FF), 0.5, 3.0, ((0, 4),)),
        "grn_gamma": bell_draw(splits[7], (BLOCKS, FF), 0.5, 3.0, ((0, 4),)),
        "grn_beta": bell_draw(splits[8], (BLOCKS, FF), 0.3, 2.0, ((0, 4),)),
        "proj_out": bell_draw(splits[9], (BLOCKS, FF, C), FF ** -0.5, 0.15625, ((0, 4), (1, 2))),
        "bias_out": bell_draw(splits[10], (BLOCKS, C), 0.5, 3.0, ((0, 4),)),
    }


EPS_NORM = 1e-06
EPS_GRN = 1e-06

def depthwise(padded, kernel, bias_term):
    channels = padded.shape[-1]
    conv_out = lax.conv_general_dilated(padded.astype(jnp.float32), kernel.astype(jnp.float32)[:, :, None, :], (1, 1), 'VALID', dimension_numbers=('NHWC', 'HWIO', 'NHWC'), feature_group_count=channels, precision=lax.Precision.HIGHEST)
    return conv_out + bias_term.astype(jnp.float32)

def one_block(current, params):
    depth_kernel, depth_bias, norm_gain, norm_bias, proj_in, bias_in, grn_gamma, grn_beta, proj_out, bias_out = params
    num_items, num_rows, num_cols, channels = current.shape
    padded = jnp.pad(current, ((0, 0), (3, 3), (3, 3), (0, 0)))
    conv_out = depthwise(padded, depth_kernel, depth_bias)
    center = conv_out - lax.optimization_barrier(jnp.mean(conv_out, axis=-1, keepdims=True))
    spread = lax.optimization_barrier(jnp.mean(center * center, axis=-1, keepdims=True))
    normed = (center * lax.rsqrt(spread + EPS_NORM) * norm_gain.astype(jnp.float32) + norm_bias.astype(jnp.float32)).astype(jnp.bfloat16)
    flat_rows = normed.reshape(num_items * num_rows * num_cols, channels)
    raised = jnp.dot(flat_rows, proj_in, preferred_element_type=jnp.float32) + bias_in.astype(jnp.float32)
    active = jax.nn.gelu(raised, approximate=False).astype(jnp.bfloat16)
    grouped = active.reshape(num_items, num_rows * num_cols, -1).astype(jnp.float32)
    total_sq = lax.optimization_barrier(jnp.sum(grouped * grouped, axis=1))
    magnitude = jnp.sqrt(total_sq)
    grn_ratio = magnitude / (lax.optimization_barrier(jnp.mean(magnitude, axis=-1, keepdims=True)) + EPS_GRN)
    hidden = (grn_gamma.astype(jnp.float32) * grouped * grn_ratio[:, None, :] + grn_beta.astype(jnp.float32) + grouped).astype(jnp.bfloat16)
    update = jnp.dot(hidden.reshape(num_items * num_rows * num_cols, -1), proj_out, preferred_element_type=jnp.float32) + bias_out.astype(jnp.float32)
    return (current.astype(jnp.float32) + update.reshape(num_items, num_rows, num_cols, channels)).astype(jnp.bfloat16)

def reference(inputs, depth_kernel, depth_bias, norm_gain, norm_bias, proj_in, bias_in, grn_gamma, grn_beta, proj_out, bias_out):
    per_layer = [[] for layer_index in range(BLOCKS)]
    for micro_index in range(MICRO):
        current = inputs[micro_index]
        for layer_index in range(BLOCKS):
            params = (depth_kernel[layer_index], depth_bias[layer_index], norm_gain[layer_index], norm_bias[layer_index], proj_in[layer_index], bias_in[layer_index], grn_gamma[layer_index], grn_beta[layer_index], proj_out[layer_index], bias_out[layer_index])
            current = one_block(current, params)
            per_layer[layer_index].append(current)
    return jnp.stack([jnp.stack(layer_list) for layer_list in per_layer])
```

```python
import functools

import jax
import jax.numpy as jnp
from jax import lax
from jax.experimental import pallas as pl
from jax.experimental.pallas import tpu as pltpu
from jax.sharding import PartitionSpec as P

EPS_NORM = 1e-06
EPS_GRN = 1e-06
LANES = 128
VMEM_BYTES = 40 * 1024 * 1024
REACH = 3


def fill_padded(xp, height, width, channels, pieces):
    lanes = xp.shape[2]
    zeros = jnp.zeros((height, 8, lanes), jnp.float32)
    xp[:, 0:8, :] = zeros
    xp[:, 8 + width : 16 + width, :] = zeros
    if lanes > channels:
        xp[:, 8 : 8 + width, lanes - LANES :] = jnp.zeros((height, width, LANES), jnp.float32)
    for start, piece in pieces:
        for row in range(piece.shape[0]):
            xp[start + row, 8 : 8 + width, 0:channels] = piece[row].astype(jnp.float32)


def conv_norm(xp, taps, cvec, normed, height, width, channels):
    lanes = xp.shape[2]
    groups = lanes // LANES
    span = 2 * REACH + 1
    last = channels - (groups - 1) * LANES
    inside = lax.broadcasted_iota(jnp.int32, (8, LANES), 1) < last

    def columns(cb, carry):
        base = pl.multiple_of(cb * 8, 8)
        window = xp.at[:, pl.ds(base, 24), :]
        out = [[None] * groups for _ in range(height)]
        for g in range(groups):
            at = slice(g * LANES, (g + 1) * LANES)
            bias = jnp.broadcast_to(cvec[0:1, at], (8, LANES))
            acc = [bias] * height
            for j in range(span):
                kern = [
                    jnp.broadcast_to(taps[i * span + j : i * span + j + 1, at], (8, LANES))
                    for i in range(span)
                ]
                for r in range(height):
                    x_row = window[r, 8 - REACH + j : 16 - REACH + j, at]
                    for i in range(span):
                        h = r + REACH - i
                        if 0 <= h < height:
                            acc[h] = acc[h] + kern[i] * x_row
            for h in range(height):
                out[h][g] = acc[h]
        for h in range(height):
            v = out[h]
            total = functools.reduce(jnp.add, v)
            mean = jnp.sum(total, axis=-1, keepdims=True) * (1.0 / channels)
            c = [p - mean for p in v]
            if last < LANES:
                c[-1] = jnp.where(inside, c[-1], 0.0)
            sq = functools.reduce(jnp.add, [p * p for p in c])
            var = jnp.sum(sq, axis=-1, keepdims=True) * (1.0 / channels)
            scale = lax.rsqrt(var + EPS_NORM)
            for g in range(groups):
                at = slice(g * LANES, (g + 1) * LANES)
                normed[h, pl.ds(base, 8), at] = c[g] * scale * cvec[1:2, at] + cvec[2:3, at]
        return carry

    lax.fori_loop(0, width // 8, columns, 0)


def gelu(v):
    return 0.5 * v * (1.0 + lax.erf(v * (0.5**0.5)))


def mlp(x_ref, flat, w_in, w_out, cvec, fvec, act, ssq, out, height, width, channels):
    hidden_units = act.shape[1]
    step = 2 * LANES

    def units(start, count):
        raised = jnp.dot(
            flat[...], w_in[:, pl.ds(start, count)], preferred_element_type=jnp.float32
        )
        active = gelu(raised + fvec[0:1, pl.ds(start, count)]).astype(jnp.bfloat16)
        act[:, pl.ds(start, count)] = active
        wide = active.astype(jnp.float32)
        ssq[:, pl.ds(start, count)] = jnp.sum(
            (wide * wide).reshape(height * width // 8, 8, count), axis=0
        )

    def full(n, carry):
        units(pl.multiple_of(n * step, step), step)
        return carry

    whole = hidden_units // step
    lax.fori_loop(0, whole, full, 0)
    if hidden_units % step:
        units(whole * step, hidden_units % step)

    magnitude = jnp.sqrt(jnp.sum(ssq[...], axis=0, keepdims=True))
    mean = jnp.sum(magnitude, axis=-1, keepdims=True) * (1.0 / hidden_units)
    ratio = magnitude / (mean + EPS_GRN)
    scale = fvec[1:2, :] * ratio + 1.0
    shift = fvec[2:3, :]
    chunk = 4
    rows = chunk * width

    def lower(n, carry):
        a = act[pl.ds(pl.multiple_of(n * rows, rows), rows), :].astype(jnp.float32)
        hidden = (a * scale + shift).astype(jnp.bfloat16)
        update = jnp.dot(hidden, w_out[...], preferred_element_type=jnp.float32)
        update = update + cvec[3:4, 0:channels]
        x = x_ref[pl.ds(n * chunk, chunk)].astype(jnp.float32)
        out[pl.ds(n * chunk, chunk)] = (
            x + update.reshape(chunk, width, channels)
        ).astype(jnp.bfloat16)
        return carry

    lax.fori_loop(0, height // chunk, lower, 0)


def head_kernel(pos, *refs, height, width, channels, count):
    pieces = refs[:count]
    taps, cvec, x_out, flat_out, xp, normed = refs[count:]
    rows = height // count
    for n in range(count):
        x_out[pl.ds(pos[n] * rows, rows)] = pieces[n][...]
    fill_padded(xp, height, width, channels, [(0, x_out)])
    conv_norm(xp, taps, cvec, normed, height, width, channels)
    flat_out[...] = normed[...].reshape(flat_out.shape).astype(jnp.bfloat16)


def tail_kernel(x, flat, w_in, w_out, cvec, fvec, out, act, ssq, *, height, width, channels):
    mlp(x, flat, w_in, w_out, cvec, fvec, act, ssq, out, height, width, channels)


def block_kernel(
    x, taps, w_in, w_out, cvec, fvec, out, xp, normed, flat, act, ssq, *, height, width, channels
):
    fill_padded(xp, height, width, channels, [(0, x)])
    conv_norm(xp, taps, cvec, normed, height, width, channels)
    flat[...] = normed[...].reshape(flat.shape).astype(jnp.bfloat16)
    mlp(x, flat, w_in, w_out, cvec, fvec, act, ssq, out, height, width, channels)


def in_vmem(count):
    return [pl.BlockSpec(memory_space=pltpu.VMEM)] * count


def block_cost(cells, channels, hidden_units):
    return pl.CostEstimate(
        flops=4 * cells * channels * hidden_units,
        bytes_accessed=4 * channels * hidden_units + 4 * cells * channels,
        transcendentals=cells * hidden_units,
    )


def run_head(pos, pieces, taps, cvec, height):
    rows, width, channels = pieces[0].shape
    lanes = taps.shape[1]
    dims = dict(height=height, width=width, channels=channels)
    return pl.pallas_call(
        functools.partial(head_kernel, count=len(pieces), **dims),
        out_shape=(
            jax.ShapeDtypeStruct((height, width, channels), jnp.bfloat16),
            jax.ShapeDtypeStruct((height * width, lanes), jnp.bfloat16),
        ),
        in_specs=[pl.BlockSpec(memory_space=pltpu.SMEM)] + in_vmem(len(pieces) + 2),
        out_specs=tuple(in_vmem(2)),
        scratch_shapes=[
            pltpu.VMEM((height, width + 16, lanes), jnp.float32),
            pltpu.VMEM((height, width, lanes), jnp.float32),
        ],
        compiler_params=pltpu.CompilerParams(vmem_limit_bytes=VMEM_BYTES),
        name="conv_norm",
    )(pos, *pieces, taps, cvec)


def run_tail(x, flat, w_in, w_out, cvec, fvec):
    height, width, channels = x.shape
    hidden_units = w_in.shape[1]
    cells = height * width
    return pl.pallas_call(
        functools.partial(tail_kernel, height=height, width=width, channels=channels),
        out_shape=jax.ShapeDtypeStruct(x.shape, jnp.bfloat16),
        in_specs=in_vmem(6),
        out_specs=in_vmem(1)[0],
        scratch_shapes=[
            pltpu.VMEM((cells, hidden_units), jnp.bfloat16),
            pltpu.VMEM((8, hidden_units), jnp.float32),
        ],
        compiler_params=pltpu.CompilerParams(vmem_limit_bytes=VMEM_BYTES),
        cost_estimate=block_cost(cells, channels, hidden_units),
        name="mlp",
    )(x, flat, w_in, w_out, cvec, fvec)


def run_block(x, taps, w_in, w_out, cvec, fvec):
    height, width, channels = x.shape
    lanes = taps.shape[1]
    hidden_units = w_in.shape[1]
    cells = height * width
    return pl.pallas_call(
        functools.partial(block_kernel, height=height, width=width, channels=channels),
        out_shape=jax.ShapeDtypeStruct(x.shape, jnp.bfloat16),
        in_specs=in_vmem(6),
        out_specs=in_vmem(1)[0],
        scratch_shapes=[
            pltpu.VMEM((height, width + 16, lanes), jnp.float32),
            pltpu.VMEM((height, width, lanes), jnp.float32),
            pltpu.VMEM((cells, lanes), jnp.bfloat16),
            pltpu.VMEM((cells, hidden_units), jnp.bfloat16),
            pltpu.VMEM((8, hidden_units), jnp.float32),
        ],
        compiler_params=pltpu.CompilerParams(vmem_limit_bytes=VMEM_BYTES),
        cost_estimate=block_cost(cells, channels, hidden_units),
        name="block",
    )(x, taps, w_in, w_out, cvec, fvec)


def swap_pairs(sections, section_count, size, by):
    return [
        (s * size + p, s * size + (p ^ by)) for s in sections for p in range(size)
    ]


def image_plan(
    inputs,
    depth_kernel,
    depth_bias,
    norm_gain,
    norm_bias,
    proj_in,
    bias_in,
    grn_gamma,
    grn_beta,
    proj_out,
    bias_out,
):
    sections = lax.axis_size("section")
    rows_axis = lax.axis_size("row")
    section = lax.axis_index("section")
    me = lax.axis_index("row")
    part = lax.axis_index("dp")
    _, _, local_rows, width, channels = inputs.shape
    height = local_rows * rows_axis
    lanes = -(-channels // LANES) * LANES
    extra = lanes - channels
    half = proj_in.shape[2]

    own = lax.dynamic_index_in_dim(inputs, me, 0, keepdims=False)[0]
    pieces = [own]
    for by in (2, 3, 1):
        piece = lax.dynamic_index_in_dim(inputs, me ^ by, 0, keepdims=False)[0]
        pieces.append(
            lax.ppermute(piece, ("section", "row"), swap_pairs([0], sections, rows_axis, by))
        )
    pos = jnp.stack([me ^ by for by in (0, 2, 3, 1)]).astype(jnp.int32)

    swap = [(0, 1), (1, 0)]
    w_in = jnp.concatenate([proj_in[0], lax.ppermute(proj_in[0], "dp", swap)], axis=1)
    w_in = jnp.pad(w_in, ((0, extra), (0, 0)))
    w_out = jnp.concatenate([proj_out[0], lax.ppermute(proj_out[0], "dp", swap)], axis=0)

    def own_first(v):
        return jnp.where(part == 0, v, jnp.concatenate([v[:, half:], v[:, :half]], axis=1))

    fvec = own_first(jnp.concatenate([bias_in, grn_gamma, grn_beta], axis=0).astype(jnp.float32))
    cvec = jnp.concatenate([depth_bias, norm_gain, norm_bias, bias_out], axis=0)
    cvec = jnp.pad(cvec.astype(jnp.float32), ((0, 0), (0, extra)))
    taps = depth_kernel[0].reshape(-1, channels).astype(jnp.float32)
    taps = jnp.pad(taps, ((0, 0), (0, extra)))

    x, flat = run_head(pos, pieces, taps, cvec, height)
    produced = run_tail(x, flat, w_in, w_out, cvec, fvec)
    kept = produced
    for tick in range(1, sections):
        arriving = lax.ppermute(
            produced, "section", [(i, i + 1) for i in range(sections - 1)]
        )
        produced = run_block(arriving, taps, w_in, w_out, cvec, fvec)
        kept = jnp.where(section == tick, produced, kept)

    def rows_of(p):
        return lax.dynamic_slice_in_dim(kept, p * local_rows, local_rows, axis=0)

    saved = jnp.zeros((rows_axis, local_rows, width, channels), jnp.bfloat16)
    saved = lax.dynamic_update_index_in_dim(saved, rows_of(me), me, 0)
    for by in (2, 3, 1):
        got = lax.ppermute(rows_of(me ^ by), "row", [(p, p ^ by) for p in range(rows_axis)])
        saved = lax.dynamic_update_index_in_dim(saved, got, me ^ by, 0)
    return saved[None, :, None]


def extended(cells, sides, width):
    for axis, dim in sides:
        count = lax.axis_size(axis)
        ends = count - 1
        head = lax.slice_in_dim(cells, 0, width, axis=dim)
        tail = lax.slice_in_dim(cells, cells.shape[dim] - width, cells.shape[dim], axis=dim)
        cells = jnp.concatenate(
            [
                lax.ppermute(tail, axis, [(i, (i + 1) % count) for i in range(ends)]),
                cells,
                lax.ppermute(head, axis, [((i + 1) % count, i) for i in range(ends)]),
            ],
            axis=dim,
        )
    return cells


def depthwise(padded, kernel, bias_term):
    channels = padded.shape[-1]
    conv_out = lax.conv_general_dilated(
        padded.astype(jnp.float32),
        kernel.astype(jnp.float32)[:, :, None, :],
        (1, 1),
        "VALID",
        dimension_numbers=("NHWC", "HWIO", "NHWC"),
        feature_group_count=channels,
        precision=lax.Precision.HIGHEST,
    )
    return conv_out + bias_term.astype(jnp.float32)


def conv_block(current, params):
    (
        depth_kernel,
        depth_bias,
        norm_gain,
        norm_bias,
        proj_in,
        bias_in,
        grn_gamma,
        grn_beta,
        proj_out,
        bias_out,
    ) = params
    num_items, num_rows, num_cols, channels = current.shape
    padded = extended(current, (("row", 1),), REACH)
    padded = jnp.pad(padded, ((0, 0), (0, 0), (REACH, REACH), (0, 0)))
    conv_out = depthwise(padded, depth_kernel, depth_bias)
    center = conv_out - jnp.mean(conv_out, axis=-1, keepdims=True)
    spread = jnp.mean(center * center, axis=-1, keepdims=True)
    normed = (
        center * lax.rsqrt(spread + EPS_NORM) * norm_gain.astype(jnp.float32)
        + norm_bias.astype(jnp.float32)
    ).astype(jnp.bfloat16)
    flat_rows = normed.reshape(num_items * num_rows * num_cols, channels)
    raised = jnp.dot(flat_rows, proj_in, preferred_element_type=jnp.float32) + bias_in.astype(
        jnp.float32
    )
    active = jax.nn.gelu(raised, approximate=False).astype(jnp.bfloat16)
    grouped = active.reshape(num_items, num_rows * num_cols, -1).astype(jnp.float32)
    local_sq = jnp.sum(grouped * grouped, axis=1)
    total_sq = lax.psum(local_sq, "row")
    magnitude = jnp.sqrt(total_sq)
    grn_ratio = magnitude / (jnp.mean(magnitude, axis=-1, keepdims=True) + EPS_GRN)
    hidden = (
        grn_gamma.astype(jnp.float32) * grouped * grn_ratio[:, None, :]
        + grn_beta.astype(jnp.float32)
        + grouped
    ).astype(jnp.bfloat16)
    update = jnp.dot(
        hidden.reshape(num_items * num_rows * num_cols, -1),
        proj_out,
        preferred_element_type=jnp.float32,
    ) + bias_out.astype(jnp.float32)
    return (
        current.astype(jnp.float32) + update.reshape(num_items, num_rows, num_cols, channels)
    ).astype(jnp.bfloat16)


def rows_plan(inputs, *weights):
    (
        depth_kernel,
        depth_bias,
        norm_gain,
        norm_bias,
        proj_in,
        bias_in,
        grn_gamma,
        grn_beta,
        proj_out,
        bias_out,
    ) = weights
    proj_in = lax.all_gather(proj_in, "dp", axis=2, tiled=True)
    proj_out = lax.all_gather(proj_out, "dp", axis=1, tiled=True)
    own_params = tuple(
        w[0]
        for w in (
            depth_kernel,
            depth_bias,
            norm_gain,
            norm_bias,
            proj_in,
            bias_in,
            grn_gamma,
            grn_beta,
            proj_out,
            bias_out,
        )
    )
    sections = lax.axis_size("section")
    section_index = lax.axis_index("section")
    num_micro = inputs.shape[0]
    num_ticks = num_micro + sections - 1
    arriving = jnp.zeros_like(inputs[0])
    saved = jnp.zeros_like(inputs)
    for tick_index in range(num_ticks):
        fresh_input = inputs[min(tick_index, num_micro - 1)]
        current = jnp.where(section_index == 0, fresh_input, arriving)
        produced = conv_block(current, own_params)
        slot_index = tick_index - section_index
        is_valid = jnp.logical_and(slot_index >= 0, slot_index < num_micro)
        safe_slot = jnp.clip(slot_index, 0, num_micro - 1)
        previous = lax.dynamic_index_in_dim(saved, safe_slot, 0, keepdims=False)
        saved = lax.dynamic_update_index_in_dim(
            saved, jnp.where(is_valid, produced, previous), safe_slot, 0
        )
        if tick_index + 1 < num_ticks:
            arriving = lax.ppermute(
                produced, "section", [(i, i + 1) for i in range(sections - 1)]
            )
    return saved[None]


def on_device(inputs, *weights):
    num_micro, images, local_rows, width, _ = inputs.shape
    one_image_each = (
        images == 1
        and lax.axis_size("row") == num_micro == 4
        and lax.axis_size("dp") == 2
        and local_rows % 4 == 0
        and width % 16 == 0
    )
    plan = image_plan if one_image_each else rows_plan
    return plan(inputs, *weights)


def solution(mesh):
    return jax.shard_map(
        on_device,
        mesh=mesh,
        in_specs=(
            P(None, "dp", "row", None, None),
            P("section", None, None, None),
            P("section", None),
            P("section", None),
            P("section", None),
            P("section", None, "dp"),
            P("section", None),
            P("section", None),
            P("section", None),
            P("section", "dp", None),
            P("section", None),
        ),
        out_specs=P("section", None, "dp", "row", None, None),
        check_vma=False,
    )
```

```python
import functools

import jax
import jax.numpy as jnp
from jax import lax
from jax.experimental import pallas as pl
from jax.experimental.pallas import tpu as pltpu
from jax.sharding import PartitionSpec as P

EPS_NORM = 1e-06
EPS_GRN = 1e-06
LANES = 128
VMEM_BYTES = 40 * 1024 * 1024
REACH = 3


def fill_columns(xp, xs, x, channels):
    height, reach_cols, blocks, lanes = xs.shape
    stride = reach_cols - 2 * REACH
    width = stride * blocks
    groups = lanes // LANES
    xp[...] = jnp.zeros(xp.shape, jnp.float32)

    def rows(n, carry):
        for k in range(2):
            r = 2 * n + k
            row = x[r].astype(jnp.float32)
            for g in range(groups):
                at = slice(g * LANES, (g + 1) * LANES)
                own = row[:, g * LANES : min((g + 1) * LANES, channels)]
                xp[k * groups + g, 8 : 8 + width, 0 : own.shape[1]] = own
                for q in range(reach_cols):
                    near = pl.ds(8 - REACH + q, blocks, stride=stride)
                    xs[r, q, :, at] = xp[k * groups + g, near, :]
        return carry

    lax.fori_loop(0, height // 2, rows, 0)


def conv(xs, taps, cvec, cq):
    height, stride, blocks, lanes = cq.shape
    span = 2 * REACH + 1

    def group(g, carry):
        at = pl.ds(pl.multiple_of(g * LANES, LANES), LANES)

        def column(q, carry):
            bias = jnp.broadcast_to(cvec[0:1, at], (blocks, LANES))
            acc = [bias] * height
            for j in range(span):
                kern = [
                    jnp.broadcast_to(taps[i * span + j : i * span + j + 1, at], (blocks, LANES))
                    for i in range(span)
                ]
                for r in range(height):
                    x_row = xs[r, q + j, :, at]
                    for i in range(span):
                        h = r + REACH - i
                        if 0 <= h < height:
                            acc[h] = acc[h] + kern[i] * x_row
            for h in range(height):
                cq[h, q, :, at] = acc[h]
            return carry

        return lax.fori_loop(0, stride, column, carry)

    lax.fori_loop(0, lanes // LANES, group, 0)


def norm(cq, cvec, xp, flat, channels):
    height, stride, blocks, lanes = cq.shape
    width = stride * blocks
    groups = lanes // LANES
    inside = lax.broadcasted_iota(jnp.int32, (blocks, lanes), 1) < channels

    def rows(n, carry):
        for k in range(2):
            h = 2 * n + k
            for q in range(stride):
                v = cq[h, q]
                mean = jnp.sum(v, axis=-1, keepdims=True) * (1.0 / channels)
                c = jnp.where(inside, v - mean, 0.0)
                var = jnp.sum(c * c, axis=-1, keepdims=True) * (1.0 / channels)
                c = c * lax.rsqrt(var + EPS_NORM) * cvec[1:2, :] + cvec[2:3, :]
                for g in range(groups):
                    at = slice(g * LANES, (g + 1) * LANES)
                    xp[k * groups + g, pl.ds(q, blocks, stride=stride), :] = c[:, at]
            at_cell = pl.ds(pl.multiple_of(h * width, width), width)
            for g in range(groups):
                at = slice(g * LANES, (g + 1) * LANES)
                flat[at_cell, at] = xp[k * groups + g, 0:width, :].astype(jnp.bfloat16)
        return carry

    lax.fori_loop(0, height // 2, rows, 0)


def conv_norm(x, taps, cvec, flat, xp, xs, cq):
    channels = x.shape[2]
    fill_columns(xp, xs, x, channels)
    conv(xs, taps, cvec, cq)
    norm(cq, cvec, xp, flat, channels)


def conv_scratch(height, width, lanes):
    return [
        pltpu.VMEM((2 * lanes // LANES, width + 16, LANES), jnp.float32),
        pltpu.VMEM((height, width // 8 + 2 * REACH, 8, lanes), jnp.float32),
        pltpu.VMEM((height, width // 8, 8, lanes), jnp.float32),
    ]


def gelu(v):
    return 0.5 * v * (1.0 + lax.erf(v * (0.5**0.5)))


def mlp(x_ref, flat, w_in, w_out, cvec, fvec, act, ssq, out, height, width, channels):
    hidden_units = act.shape[1]
    step = 2 * LANES

    def units(start, count):
        raised = jnp.dot(
            flat[...], w_in[:, pl.ds(start, count)], preferred_element_type=jnp.float32
        )
        active = gelu(raised + fvec[0:1, pl.ds(start, count)]).astype(jnp.bfloat16)
        act[:, pl.ds(start, count)] = active
        wide = active.astype(jnp.float32)
        ssq[:, pl.ds(start, count)] = jnp.sum(
            (wide * wide).reshape(height * width // 8, 8, count), axis=0
        )

    def full(n, carry):
        units(pl.multiple_of(n * step, step), step)
        return carry

    whole = hidden_units // step
    lax.fori_loop(0, whole, full, 0)
    if hidden_units % step:
        units(whole * step, hidden_units % step)

    magnitude = jnp.sqrt(jnp.sum(ssq[...], axis=0, keepdims=True))
    mean = jnp.sum(magnitude, axis=-1, keepdims=True) * (1.0 / hidden_units)
    ratio = magnitude / (mean + EPS_GRN)
    scale = fvec[1:2, :] * ratio + 1.0
    shift = fvec[2:3, :]
    chunk = 4
    rows = chunk * width

    def lower(n, carry):
        a = act[pl.ds(pl.multiple_of(n * rows, rows), rows), :].astype(jnp.float32)
        hidden = (a * scale + shift).astype(jnp.bfloat16)
        update = jnp.dot(hidden, w_out[...], preferred_element_type=jnp.float32)
        update = update + cvec[3:4, 0:channels]
        x = x_ref[pl.ds(n * chunk, chunk)].astype(jnp.float32)
        out[pl.ds(n * chunk, chunk)] = (
            x + update.reshape(chunk, width, channels)
        ).astype(jnp.bfloat16)
        return carry

    lax.fori_loop(0, height // chunk, lower, 0)


def head_kernel(pos, *refs, height, count):
    pieces = refs[:count]
    taps, cvec, x_out, flat_out, xp, xs, cq = refs[count:]
    rows = height // count
    for n in range(count):
        x_out[pl.ds(pos[n] * rows, rows)] = pieces[n][...]
    conv_norm(x_out, taps, cvec, flat_out, xp, xs, cq)


def tail_kernel(x, flat, w_in, w_out, cvec, fvec, out, act, ssq, *, height, width, channels):
    mlp(x, flat, w_in, w_out, cvec, fvec, act, ssq, out, height, width, channels)


def block_kernel(
    x, taps, w_in, w_out, cvec, fvec, out, xp, xs, cq, flat, act, ssq, *, height, width, channels
):
    conv_norm(x, taps, cvec, flat, xp, xs, cq)
    mlp(x, flat, w_in, w_out, cvec, fvec, act, ssq, out, height, width, channels)


def in_vmem(count):
    return [pl.BlockSpec(memory_space=pltpu.VMEM)] * count


def block_cost(cells, channels, hidden_units):
    return pl.CostEstimate(
        flops=4 * cells * channels * hidden_units,
        bytes_accessed=4 * channels * hidden_units + 4 * cells * channels,
        transcendentals=cells * hidden_units,
    )


def run_head(pos, pieces, taps, cvec, height):
    rows, width, channels = pieces[0].shape
    lanes = taps.shape[1]
    return pl.pallas_call(
        functools.partial(head_kernel, height=height, count=len(pieces)),
        out_shape=(
            jax.ShapeDtypeStruct((height, width, channels), jnp.bfloat16),
            jax.ShapeDtypeStruct((height * width, lanes), jnp.bfloat16),
        ),
        in_specs=[pl.BlockSpec(memory_space=pltpu.SMEM)] + in_vmem(len(pieces) + 2),
        out_specs=tuple(in_vmem(2)),
        scratch_shapes=conv_scratch(height, width, lanes),
        compiler_params=pltpu.CompilerParams(vmem_limit_bytes=VMEM_BYTES),
        name="conv_norm",
    )(pos, *pieces, taps, cvec)


def run_tail(x, flat, w_in, w_out, cvec, fvec):
    height, width, channels = x.shape
    hidden_units = w_in.shape[1]
    cells = height * width
    return pl.pallas_call(
        functools.partial(tail_kernel, height=height, width=width, channels=channels),
        out_shape=jax.ShapeDtypeStruct(x.shape, jnp.bfloat16),
        in_specs=in_vmem(6),
        out_specs=in_vmem(1)[0],
        scratch_shapes=[
            pltpu.VMEM((cells, hidden_units), jnp.bfloat16),
            pltpu.VMEM((8, hidden_units), jnp.float32),
        ],
        compiler_params=pltpu.CompilerParams(vmem_limit_bytes=VMEM_BYTES),
        cost_estimate=block_cost(cells, channels, hidden_units),
        name="mlp",
    )(x, flat, w_in, w_out, cvec, fvec)


def run_block(x, taps, w_in, w_out, cvec, fvec):
    height, width, channels = x.shape
    lanes = taps.shape[1]
    hidden_units = w_in.shape[1]
    cells = height * width
    return pl.pallas_call(
        functools.partial(block_kernel, height=height, width=width, channels=channels),
        out_shape=jax.ShapeDtypeStruct(x.shape, jnp.bfloat16),
        in_specs=in_vmem(6),
        out_specs=in_vmem(1)[0],
        scratch_shapes=conv_scratch(height, width, lanes)
        + [
            pltpu.VMEM((cells, lanes), jnp.bfloat16),
            pltpu.VMEM((cells, hidden_units), jnp.bfloat16),
            pltpu.VMEM((8, hidden_units), jnp.float32),
        ],
        compiler_params=pltpu.CompilerParams(vmem_limit_bytes=VMEM_BYTES),
        cost_estimate=block_cost(cells, channels, hidden_units),
        name="block",
    )(x, taps, w_in, w_out, cvec, fvec)


def swap_pairs(sections, section_count, size, by):
    return [
        (s * size + p, s * size + (p ^ by)) for s in sections for p in range(size)
    ]


def image_plan(
    inputs,
    depth_kernel,
    depth_bias,
    norm_gain,
    norm_bias,
    proj_in,
    bias_in,
    grn_gamma,
    grn_beta,
    proj_out,
    bias_out,
):
    sections = lax.axis_size("section")
    rows_axis = lax.axis_size("row")
    section = lax.axis_index("section")
    me = lax.axis_index("row")
    part = lax.axis_index("dp")
    _, _, local_rows, width, channels = inputs.shape
    height = local_rows * rows_axis
    lanes = -(-channels // LANES) * LANES
    extra = lanes - channels
    half = proj_in.shape[2]

    own = lax.dynamic_index_in_dim(inputs, me, 0, keepdims=False)[0]
    pieces = [own]
    for by in (2, 3, 1):
        piece = lax.dynamic_index_in_dim(inputs, me ^ by, 0, keepdims=False)[0]
        pieces.append(
            lax.ppermute(piece, ("section", "row"), swap_pairs([0], sections, rows_axis, by))
        )
    pos = jnp.stack([me ^ by for by in (0, 2, 3, 1)]).astype(jnp.int32)

    swap = [(0, 1), (1, 0)]
    w_in = jnp.concatenate([proj_in[0], lax.ppermute(proj_in[0], "dp", swap)], axis=1)
    w_in = jnp.pad(w_in, ((0, extra), (0, 0)))
    w_out = jnp.concatenate([proj_out[0], lax.ppermute(proj_out[0], "dp", swap)], axis=0)

    def own_first(v):
        return jnp.where(part == 0, v, jnp.concatenate([v[:, half:], v[:, :half]], axis=1))

    fvec = own_first(jnp.concatenate([bias_in, grn_gamma, grn_beta], axis=0).astype(jnp.float32))
    cvec = jnp.concatenate([depth_bias, norm_gain, norm_bias, bias_out], axis=0)
    cvec = jnp.pad(cvec.astype(jnp.float32), ((0, 0), (0, extra)))
    taps = depth_kernel[0].reshape(-1, channels).astype(jnp.float32)
    taps = jnp.pad(taps, ((0, 0), (0, extra)))

    x, flat = run_head(pos, pieces, taps, cvec, height)
    produced = run_tail(x, flat, w_in, w_out, cvec, fvec)
    kept = produced
    for tick in range(1, sections):
        arriving = lax.ppermute(
            produced, "section", [(tick - 1, tick)]
        )
        produced = run_block(arriving, taps, w_in, w_out, cvec, fvec)
        kept = jnp.where(section == tick, produced, kept)

    def rows_of(p):
        return lax.dynamic_slice_in_dim(kept, p * local_rows, local_rows, axis=0)

    saved = jnp.zeros((rows_axis, local_rows, width, channels), jnp.bfloat16)
    saved = lax.dynamic_update_index_in_dim(saved, rows_of(me), me, 0)
    for by in (2, 3, 1):
        got = lax.ppermute(rows_of(me ^ by), "row", [(p, p ^ by) for p in range(rows_axis)])
        saved = lax.dynamic_update_index_in_dim(saved, got, me ^ by, 0)
    return saved[None, :, None]


def extended(cells, sides, width):
    for axis, dim in sides:
        count = lax.axis_size(axis)
        ends = count - 1
        head = lax.slice_in_dim(cells, 0, width, axis=dim)
        tail = lax.slice_in_dim(cells, cells.shape[dim] - width, cells.shape[dim], axis=dim)
        cells = jnp.concatenate(
            [
                lax.ppermute(tail, axis, [(i, (i + 1) % count) for i in range(ends)]),
                cells,
                lax.ppermute(head, axis, [((i + 1) % count, i) for i in range(ends)]),
            ],
            axis=dim,
        )
    return cells


def depthwise(padded, kernel, bias_term):
    channels = padded.shape[-1]
    conv_out = lax.conv_general_dilated(
        padded.astype(jnp.float32),
        kernel.astype(jnp.float32)[:, :, None, :],
        (1, 1),
        "VALID",
        dimension_numbers=("NHWC", "HWIO", "NHWC"),
        feature_group_count=channels,
        precision=lax.Precision.HIGHEST,
    )
    return conv_out + bias_term.astype(jnp.float32)


def conv_block(current, params):
    (
        depth_kernel,
        depth_bias,
        norm_gain,
        norm_bias,
        proj_in,
        bias_in,
        grn_gamma,
        grn_beta,
        proj_out,
        bias_out,
    ) = params
    num_items, num_rows, num_cols, channels = current.shape
    padded = extended(current, (("row", 1),), REACH)
    padded = jnp.pad(padded, ((0, 0), (0, 0), (REACH, REACH), (0, 0)))
    conv_out = depthwise(padded, depth_kernel, depth_bias)
    center = conv_out - jnp.mean(conv_out, axis=-1, keepdims=True)
    spread = jnp.mean(center * center, axis=-1, keepdims=True)
    normed = (
        center * lax.rsqrt(spread + EPS_NORM) * norm_gain.astype(jnp.float32)
        + norm_bias.astype(jnp.float32)
    ).astype(jnp.bfloat16)
    flat_rows = normed.reshape(num_items * num_rows * num_cols, channels)
    raised = jnp.dot(flat_rows, proj_in, preferred_element_type=jnp.float32) + bias_in.astype(
        jnp.float32
    )
    active = jax.nn.gelu(raised, approximate=False).astype(jnp.bfloat16)
    grouped = active.reshape(num_items, num_rows * num_cols, -1).astype(jnp.float32)
    local_sq = jnp.sum(grouped * grouped, axis=1)
    total_sq = lax.psum(local_sq, "row")
    magnitude = jnp.sqrt(total_sq)
    grn_ratio = magnitude / (jnp.mean(magnitude, axis=-1, keepdims=True) + EPS_GRN)
    hidden = (
        grn_gamma.astype(jnp.float32) * grouped * grn_ratio[:, None, :]
        + grn_beta.astype(jnp.float32)
        + grouped
    ).astype(jnp.bfloat16)
    update = jnp.dot(
        hidden.reshape(num_items * num_rows * num_cols, -1),
        proj_out,
        preferred_element_type=jnp.float32,
    ) + bias_out.astype(jnp.float32)
    return (
        current.astype(jnp.float32) + update.reshape(num_items, num_rows, num_cols, channels)
    ).astype(jnp.bfloat16)


def rows_plan(inputs, *weights):
    (
        depth_kernel,
        depth_bias,
        norm_gain,
        norm_bias,
        proj_in,
        bias_in,
        grn_gamma,
        grn_beta,
        proj_out,
        bias_out,
    ) = weights
    proj_in = lax.all_gather(proj_in, "dp", axis=2, tiled=True)
    proj_out = lax.all_gather(proj_out, "dp", axis=1, tiled=True)
    own_params = tuple(
        w[0]
        for w in (
            depth_kernel,
            depth_bias,
            norm_gain,
            norm_bias,
            proj_in,
            bias_in,
            grn_gamma,
            grn_beta,
            proj_out,
            bias_out,
        )
    )
    sections = lax.axis_size("section")
    section_index = lax.axis_index("section")
    num_micro = inputs.shape[0]
    num_ticks = num_micro + sections - 1
    arriving = jnp.zeros_like(inputs[0])
    saved = jnp.zeros_like(inputs)
    for tick_index in range(num_ticks):
        fresh_input = inputs[min(tick_index, num_micro - 1)]
        current = jnp.where(section_index == 0, fresh_input, arriving)
        produced = conv_block(current, own_params)
        slot_index = tick_index - section_index
        is_valid = jnp.logical_and(slot_index >= 0, slot_index < num_micro)
        safe_slot = jnp.clip(slot_index, 0, num_micro - 1)
        previous = lax.dynamic_index_in_dim(saved, safe_slot, 0, keepdims=False)
        saved = lax.dynamic_update_index_in_dim(
            saved, jnp.where(is_valid, produced, previous), safe_slot, 0
        )
        if tick_index + 1 < num_ticks:
            arriving = lax.ppermute(
                produced, "section", [(i, i + 1) for i in range(sections - 1)]
            )
    return saved[None]


def on_device(inputs, *weights):
    num_micro, images, local_rows, width, _ = inputs.shape
    one_image_each = (
        images == 1
        and lax.axis_size("row") == num_micro == 4
        and lax.axis_size("dp") == 2
        and local_rows % 4 == 0
        and width % 16 == 0
    )
    plan = image_plan if one_image_each else rows_plan
    return plan(inputs, *weights)


def solution(mesh):
    return jax.shard_map(
        on_device,
        mesh=mesh,
        in_specs=(
            P(None, "dp", "row", None, None),
            P("section", None, None, None),
            P("section", None),
            P("section", None),
            P("section", None),
            P("section", None, "dp"),
            P("section", None),
            P("section", None),
            P("section", None),
            P("section", "dp", None),
            P("section", None),
        ),
        out_specs=P("section", None, "dp", "row", None, None),
        check_vma=False,
    )
```

```python
import functools

import jax
import jax.numpy as jnp
from jax import lax
from jax.experimental import pallas as pl
from jax.experimental.pallas import tpu as pltpu
from jax.sharding import PartitionSpec as P

EPS_NORM = 1e-06
EPS_GRN = 1e-06
LANES = 128
VMEM_BYTES = 40 * 1024 * 1024
REACH = 3
CHUNK = 4


def fill_columns(xp, xs, x, channels):
    height, reach_cols, blocks, lanes = xs.shape
    stride = reach_cols - 2 * REACH
    width = stride * blocks
    groups = lanes // LANES
    xp[...] = jnp.zeros(xp.shape, jnp.float32)

    def rows(n, carry):
        for k in range(2):
            r = 2 * n + k
            row = x[r].astype(jnp.float32)
            for g in range(groups):
                at = slice(g * LANES, (g + 1) * LANES)
                own = row[:, g * LANES : min((g + 1) * LANES, channels)]
                xp[k * groups + g, 8 : 8 + width, 0 : own.shape[1]] = own
                for q in range(reach_cols):
                    near = pl.ds(8 - REACH + q, blocks, stride=stride)
                    xs[r, q, :, at] = xp[k * groups + g, near, :]
        return carry

    lax.fori_loop(0, height // 2, rows, 0)


def conv(xs, taps, cvec, cq):
    height, stride, blocks, lanes = cq.shape
    span = 2 * REACH + 1

    def group(g, carry):
        at = pl.ds(pl.multiple_of(g * LANES, LANES), LANES)

        def column(q, carry):
            bias = jnp.broadcast_to(cvec[0:1, at], (blocks, LANES))
            acc = [bias] * height
            for j in range(span):
                kern = [
                    jnp.broadcast_to(taps[i * span + j : i * span + j + 1, at], (blocks, LANES))
                    for i in range(span)
                ]
                for r in range(height):
                    x_row = xs[r, q + j, :, at]
                    for i in range(span):
                        h = r + REACH - i
                        if 0 <= h < height:
                            acc[h] = acc[h] + kern[i] * x_row
            for h in range(height):
                cq[h, q, :, at] = acc[h]
            return carry

        return lax.fori_loop(0, stride, column, carry)

    lax.fori_loop(0, lanes // LANES, group, 0)


def norm(cq, cvec, xp, flat, channels):
    height, stride, blocks, lanes = cq.shape
    width = stride * blocks
    groups = lanes // LANES
    inside = lax.broadcasted_iota(jnp.int32, (blocks, lanes), 1) < channels

    def rows(n, carry):
        for k in range(2):
            h = 2 * n + k
            for q in range(stride):
                v = cq[h, q]
                mean = jnp.sum(v, axis=-1, keepdims=True) * (1.0 / channels)
                c = jnp.where(inside, v - mean, 0.0)
                var = jnp.sum(c * c, axis=-1, keepdims=True) * (1.0 / channels)
                c = c * lax.rsqrt(var + EPS_NORM) * cvec[1:2, :] + cvec[2:3, :]
                for g in range(groups):
                    at = slice(g * LANES, (g + 1) * LANES)
                    xp[k * groups + g, pl.ds(q, blocks, stride=stride), :] = c[:, at]
            at_cell = pl.ds(pl.multiple_of(h * width, width), width)
            for g in range(groups):
                at = slice(g * LANES, (g + 1) * LANES)
                flat[at_cell, at] = xp[k * groups + g, 0:width, :].astype(jnp.bfloat16)
        return carry

    lax.fori_loop(0, height // 2, rows, 0)


def conv_norm(x, taps, cvec, flat, xp, xs, cq):
    channels = x.shape[2]
    fill_columns(xp, xs, x, channels)
    conv(xs, taps, cvec, cq)
    norm(cq, cvec, xp, flat, channels)


def conv_scratch(height, width, lanes):
    return [
        pltpu.VMEM((2 * lanes // LANES, width + 16, LANES), jnp.float32),
        pltpu.VMEM((height, width // 8 + 2 * REACH, 8, lanes), jnp.float32),
        pltpu.VMEM((height, width // 8, 8, lanes), jnp.float32),
    ]


def gelu(v):
    return 0.5 * v * (1.0 + lax.erf(v * (0.5**0.5)))


def weight_copies(weights, halves, w_out, sems):
    half = weights[2].shape[0]
    return [
        pltpu.make_async_copy(weights[0], halves.at[0], sems.at[0]),
        pltpu.make_async_copy(weights[1], halves.at[1], sems.at[1]),
        pltpu.make_async_copy(weights[2], w_out.at[pl.ds(0, half)], sems.at[2]),
        pltpu.make_async_copy(weights[3], w_out.at[pl.ds(half, half)], sems.at[3]),
    ]


def mlp(x_ref, flat, copies, halves, w_in, w_out, cvec, fvec, act, ssq, put):
    height, width, channels = x_ref.shape
    hidden_units = act.shape[1]
    half = halves.shape[2]
    step = 2 * LANES

    if w_in.shape[0] > channels:
        w_in[channels:, :] = jnp.zeros((w_in.shape[0] - channels, hidden_units), jnp.bfloat16)
    copies[0].wait()
    w_in[0:channels, 0:half] = halves[0]
    copies[1].wait()
    w_in[0:channels, half:] = halves[1]

    def units(start, count):
        raised = jnp.dot(
            flat[...], w_in[:, pl.ds(start, count)], preferred_element_type=jnp.float32
        )
        active = gelu(raised + fvec[0:1, pl.ds(start, count)]).astype(jnp.bfloat16)
        act[:, pl.ds(start, count)] = active
        wide = active.astype(jnp.float32)
        ssq[:, pl.ds(start, count)] = jnp.sum(
            (wide * wide).reshape(height * width // 8, 8, count), axis=0
        )

    def full(n, carry):
        units(pl.multiple_of(n * step, step), step)
        return carry

    whole = hidden_units // step
    lax.fori_loop(0, whole, full, 0)
    if hidden_units % step:
        units(whole * step, hidden_units % step)

    magnitude = jnp.sqrt(jnp.sum(ssq[...], axis=0, keepdims=True))
    mean = jnp.sum(magnitude, axis=-1, keepdims=True) * (1.0 / hidden_units)
    ratio = magnitude / (mean + EPS_GRN)
    scale = fvec[1:2, :] * ratio + 1.0
    shift = fvec[2:3, :]
    rows = CHUNK * width
    copies[2].wait()
    copies[3].wait()

    def lower(n, carry):
        a = act[pl.ds(pl.multiple_of(n * rows, rows), rows), :].astype(jnp.float32)
        hidden = (a * scale + shift).astype(jnp.bfloat16)
        update = jnp.dot(hidden, w_out[...], preferred_element_type=jnp.float32)
        update = update + cvec[3:4, 0:channels]
        x = x_ref[pl.ds(n * CHUNK, CHUNK)].astype(jnp.float32)
        put(n, (x + update.reshape(CHUNK, width, channels)).astype(jnp.bfloat16))
        return carry

    lax.fori_loop(0, height // CHUNK, lower, 0)


def first_conv_kernel(pos, *refs, count):
    pieces = refs[:count]
    taps, cvec, x_out, flat_out, xp, xs, cq = refs[count:]
    rows = x_out.shape[0] // count
    for n in range(count):
        x_out[pl.ds(pos[n] * rows, rows)] = pieces[n][...]
    conv_norm(x_out, taps, cvec, flat_out, xp, xs, cq)


def conv_kernel(section, x, taps, cvec, flat_out, xp, xs, cq, *, tick):
    @pl.when(section[0] == tick)
    def _():
        conv_norm(x, taps, cvec, flat_out, xp, xs, cq)


def put_rows(out, staged, sems):
    def copy(n):
        at = pl.ds(n * CHUNK, CHUNK)
        return pltpu.make_async_copy(staged.at[at], out.at[at], sems.at[n])

    def put(n, rows):
        staged[pl.ds(n * CHUNK, CHUNK)] = rows
        copy(n).start()

    def finish():
        for n in range(staged.shape[0] // CHUNK):
            copy(n).wait()

    return put, finish


def mlp_kernel(section, x, flat, cvec, fvec, wa, wb, wc, wd, prev, out, *scratch, tick):
    halves, w_in, w_out, act, ssq, staged, w_sems, o_sems = scratch

    @pl.when(section[0] == tick)
    def _():
        copies = weight_copies((wa, wb, wc, wd), halves, w_out, w_sems)
        for copy in copies:
            copy.start()
        put, finish = put_rows(out, staged, o_sems)
        mlp(x, flat, copies, halves, w_in, w_out, cvec, fvec, act, ssq, put)
        finish()


def first_mlp_kernel(x, flat, cvec, fvec, wa, wb, wc, wd, out, *scratch):
    halves, w_in, w_out, act, ssq, staged, w_sems, o_sems = scratch
    copies = weight_copies((wa, wb, wc, wd), halves, w_out, w_sems)
    for copy in copies:
        copy.start()
    put, finish = put_rows(out, staged, o_sems)
    mlp(x, flat, copies, halves, w_in, w_out, cvec, fvec, act, ssq, put)
    finish()


def block_kernel(section, x, taps, cvec, fvec, wa, wb, wc, wd, prev, out, *scratch, tick):
    xp, xs, cq, flat, halves, w_in, w_out, act, ssq, staged, w_sems, o_sems = scratch

    @pl.when(section[0] == tick)
    def _():
        copies = weight_copies((wa, wb, wc, wd), halves, w_out, w_sems)
        for copy in copies:
            copy.start()
        conv_norm(x, taps, cvec, flat, xp, xs, cq)
        put, finish = put_rows(out, staged, o_sems)
        mlp(x, flat, copies, halves, w_in, w_out, cvec, fvec, act, ssq, put)
        finish()


SMEM = pl.BlockSpec(memory_space=pltpu.SMEM)
ANY = pl.BlockSpec(memory_space=pl.ANY)
VMEM = pl.BlockSpec(memory_space=pltpu.VMEM)


def block_cost(cells, channels, hidden_units):
    return pl.CostEstimate(
        flops=4 * cells * channels * hidden_units,
        bytes_accessed=4 * channels * hidden_units + 4 * cells * channels,
        transcendentals=cells * hidden_units,
    )


def mlp_scratch(height, width, channels, lanes, half):
    return [
        pltpu.VMEM((2, channels, half), jnp.bfloat16),
        pltpu.VMEM((lanes, 2 * half), jnp.bfloat16),
        pltpu.VMEM((2 * half, channels), jnp.bfloat16),
        pltpu.VMEM((height * width, 2 * half), jnp.bfloat16),
        pltpu.VMEM((8, 2 * half), jnp.float32),
        pltpu.VMEM((height, width, channels), jnp.bfloat16),
        pltpu.SemaphoreType.DMA((4,)),
        pltpu.SemaphoreType.DMA((height // CHUNK,)),
    ]


def kernel_params():
    return pltpu.CompilerParams(vmem_limit_bytes=VMEM_BYTES)


def run_first_conv(pos, pieces, taps, cvec, height):
    _, width, channels = pieces[0].shape
    lanes = taps.shape[1]
    return pl.pallas_call(
        functools.partial(first_conv_kernel, count=len(pieces)),
        out_shape=(
            jax.ShapeDtypeStruct((height, width, channels), jnp.bfloat16),
            jax.ShapeDtypeStruct((height * width, lanes), jnp.bfloat16),
        ),
        in_specs=[SMEM] + [VMEM] * (len(pieces) + 2),
        out_specs=(VMEM, VMEM),
        scratch_shapes=conv_scratch(height, width, lanes),
        compiler_params=kernel_params(),
        name="first_conv",
    )(pos, *pieces, taps, cvec)


def run_conv(section, x, taps, cvec, tick):
    height, width, _ = x.shape
    lanes = taps.shape[1]
    return pl.pallas_call(
        functools.partial(conv_kernel, tick=tick),
        out_shape=jax.ShapeDtypeStruct((height * width, lanes), jnp.bfloat16),
        in_specs=[SMEM, VMEM, VMEM, VMEM],
        out_specs=VMEM,
        scratch_shapes=conv_scratch(height, width, lanes),
        compiler_params=kernel_params(),
        name="conv",
    )(section, x, taps, cvec)


def run_mlp(section, x, flat, cvec, fvec, weights, prev, tick):
    height, width, channels = x.shape
    half = weights[0].shape[1]
    lanes = flat.shape[1]
    first = prev is None
    return pl.pallas_call(
        first_mlp_kernel if first else functools.partial(mlp_kernel, tick=tick),
        out_shape=jax.ShapeDtypeStruct(x.shape, jnp.bfloat16),
        in_specs=([] if first else [SMEM]) + [VMEM] * 4 + [ANY] * (4 if first else 5),
        out_specs=ANY,
        scratch_shapes=mlp_scratch(height, width, channels, lanes, half),
        input_output_aliases={} if first else {9: 0},
        compiler_params=kernel_params(),
        cost_estimate=block_cost(height * width, channels, 2 * half),
        name="mlp",
    )(*([] if first else [section]), x, flat, cvec, fvec, *weights, *([] if first else [prev]))


def run_block(section, x, taps, cvec, fvec, weights, prev, tick):
    height, width, channels = x.shape
    lanes = taps.shape[1]
    half = weights[0].shape[1]
    return pl.pallas_call(
        functools.partial(block_kernel, tick=tick),
        out_shape=jax.ShapeDtypeStruct(x.shape, jnp.bfloat16),
        in_specs=[SMEM] + [VMEM] * 4 + [ANY] * 5,
        out_specs=ANY,
        scratch_shapes=conv_scratch(height, width, lanes)
        + [pltpu.VMEM((height * width, lanes), jnp.bfloat16)]
        + mlp_scratch(height, width, channels, lanes, half),
        input_output_aliases={9: 0},
        compiler_params=kernel_params(),
        cost_estimate=block_cost(height * width, channels, 2 * half),
        name="block",
    )(section, x, taps, cvec, fvec, *weights, prev)


def swap_pairs(sections, size, by):
    return [(s * size + p, s * size + (p ^ by)) for s in sections for p in range(size)]


def image_plan(
    inputs,
    depth_kernel,
    depth_bias,
    norm_gain,
    norm_bias,
    proj_in,
    bias_in,
    grn_gamma,
    grn_beta,
    proj_out,
    bias_out,
):
    sections = lax.axis_size("section")
    rows_axis = lax.axis_size("row")
    section = lax.axis_index("section")
    me = lax.axis_index("row")
    part = lax.axis_index("dp")
    _, _, local_rows, width, channels = inputs.shape
    height = local_rows * rows_axis
    lanes = -(-channels // LANES) * LANES
    extra = lanes - channels
    half = proj_in.shape[2]

    def piece(by):
        return lax.dynamic_index_in_dim(inputs, me ^ by, 0, keepdims=False)[0]

    def row_swap(x, by):
        return lax.ppermute(x, ("section", "row"), swap_pairs([0], rows_axis, by))

    def part_swap(x, which):
        return lax.ppermute(x, ("section", "dp"), swap_pairs(which, 2, 1))

    even = range(0, sections, 2)
    odd = range(1, sections, 2)
    w_in, w_out = proj_in[0], proj_out[0]
    piece_2 = row_swap(piece(2), 2)
    even_in = part_swap(w_in, even)
    piece_3 = row_swap(piece(3), 3)
    piece_1 = row_swap(piece(1), 1)
    even_out = part_swap(w_out, even)
    pieces = [piece(0), piece_2, piece_3, piece_1]
    pos = jnp.stack([me ^ by for by in (0, 2, 3, 1)]).astype(jnp.int32)

    def own_first(v):
        return jnp.where(part == 0, v, jnp.concatenate([v[:, half:], v[:, :half]], axis=1))

    fvec = own_first(jnp.concatenate([bias_in, grn_gamma, grn_beta], axis=0).astype(jnp.float32))
    cvec = jnp.concatenate([depth_bias, norm_gain, norm_bias, bias_out], axis=0)
    cvec = jnp.pad(cvec.astype(jnp.float32), ((0, 0), (0, extra)))
    taps = depth_kernel[0].reshape(-1, channels).astype(jnp.float32)
    taps = jnp.pad(taps, ((0, 0), (0, extra)))
    at = section.astype(jnp.int32).reshape(1)

    x, flat = run_first_conv(pos, pieces, taps, cvec, height)
    weights = [(w_in, even_in, w_out, even_out)]
    result = run_mlp(at, x, flat, cvec, fvec, weights[0], None, 0)
    for tick in range(1, sections):
        arriving = lax.ppermute(result, "section", [(tick - 1, tick)])
        if tick == 1:
            late_in, late_out, result = lax.optimization_barrier((w_in, w_out, result))
            weights.append(
                (w_in, part_swap(late_in, odd), w_out, part_swap(late_out, odd))
            )
            flat = run_conv(at, arriving, taps, cvec, tick)
            result = run_mlp(at, arriving, flat, cvec, fvec, weights[1], result, tick)
        else:
            result = run_block(
                at, arriving, taps, cvec, fvec, weights[tick % 2], result, tick
            )

    def rows_of(p):
        return lax.dynamic_slice_in_dim(result, p * local_rows, local_rows, axis=0)

    saved = jnp.zeros((rows_axis, local_rows, width, channels), jnp.bfloat16)
    saved = lax.dynamic_update_index_in_dim(saved, rows_of(me), me, 0)
    for by in (2, 3, 1):
        got = lax.ppermute(rows_of(me ^ by), "row", [(p, p ^ by) for p in range(rows_axis)])
        saved = lax.dynamic_update_index_in_dim(saved, got, me ^ by, 0)
    return saved[None, :, None]


def extended(cells, sides, width):
    for axis, dim in sides:
        count = lax.axis_size(axis)
        ends = count - 1
        head = lax.slice_in_dim(cells, 0, width, axis=dim)
        tail = lax.slice_in_dim(cells, cells.shape[dim] - width, cells.shape[dim], axis=dim)
        cells = jnp.concatenate(
            [
                lax.ppermute(tail, axis, [(i, (i + 1) % count) for i in range(ends)]),
                cells,
                lax.ppermute(head, axis, [((i + 1) % count, i) for i in range(ends)]),
            ],
            axis=dim,
        )
    return cells


def depthwise(padded, kernel, bias_term):
    channels = padded.shape[-1]
    conv_out = lax.conv_general_dilated(
        padded.astype(jnp.float32),
        kernel.astype(jnp.float32)[:, :, None, :],
        (1, 1),
        "VALID",
        dimension_numbers=("NHWC", "HWIO", "NHWC"),
        feature_group_count=channels,
        precision=lax.Precision.HIGHEST,
    )
    return conv_out + bias_term.astype(jnp.float32)


def conv_block(current, params):
    (
        depth_kernel,
        depth_bias,
        norm_gain,
        norm_bias,
        proj_in,
        bias_in,
        grn_gamma,
        grn_beta,
        proj_out,
        bias_out,
    ) = params
    num_items, num_rows, num_cols, channels = current.shape
    padded = extended(current, (("row", 1),), REACH)
    padded = jnp.pad(padded, ((0, 0), (0, 0), (REACH, REACH), (0, 0)))
    conv_out = depthwise(padded, depth_kernel, depth_bias)
    center = conv_out - jnp.mean(conv_out, axis=-1, keepdims=True)
    spread = jnp.mean(center * center, axis=-1, keepdims=True)
    normed = (
        center * lax.rsqrt(spread + EPS_NORM) * norm_gain.astype(jnp.float32)
        + norm_bias.astype(jnp.float32)
    ).astype(jnp.bfloat16)
    flat_rows = normed.reshape(num_items * num_rows * num_cols, channels)
    raised = jnp.dot(flat_rows, proj_in, preferred_element_type=jnp.float32) + bias_in.astype(
        jnp.float32
    )
    active = jax.nn.gelu(raised, approximate=False).astype(jnp.bfloat16)
    grouped = active.reshape(num_items, num_rows * num_cols, -1).astype(jnp.float32)
    local_sq = jnp.sum(grouped * grouped, axis=1)
    total_sq = lax.psum(local_sq, "row")
    magnitude = jnp.sqrt(total_sq)
    grn_ratio = magnitude / (jnp.mean(magnitude, axis=-1, keepdims=True) + EPS_GRN)
    hidden = (
        grn_gamma.astype(jnp.float32) * grouped * grn_ratio[:, None, :]
        + grn_beta.astype(jnp.float32)
        + grouped
    ).astype(jnp.bfloat16)
    update = jnp.dot(
        hidden.reshape(num_items * num_rows * num_cols, -1),
        proj_out,
        preferred_element_type=jnp.float32,
    ) + bias_out.astype(jnp.float32)
    return (
        current.astype(jnp.float32) + update.reshape(num_items, num_rows, num_cols, channels)
    ).astype(jnp.bfloat16)


def rows_plan(inputs, *weights):
    (
        depth_kernel,
        depth_bias,
        norm_gain,
        norm_bias,
        proj_in,
        bias_in,
        grn_gamma,
        grn_beta,
        proj_out,
        bias_out,
    ) = weights
    proj_in = lax.all_gather(proj_in, "dp", axis=2, tiled=True)
    proj_out = lax.all_gather(proj_out, "dp", axis=1, tiled=True)
    own_params = tuple(
        w[0]
        for w in (
            depth_kernel,
            depth_bias,
            norm_gain,
            norm_bias,
            proj_in,
            bias_in,
            grn_gamma,
            grn_beta,
            proj_out,
            bias_out,
        )
    )
    sections = lax.axis_size("section")
    section_index = lax.axis_index("section")
    num_micro = inputs.shape[0]
    num_ticks = num_micro + sections - 1
    arriving = jnp.zeros_like(inputs[0])
    saved = jnp.zeros_like(inputs)
    for tick_index in range(num_ticks):
        fresh_input = inputs[min(tick_index, num_micro - 1)]
        current = jnp.where(section_index == 0, fresh_input, arriving)
        produced = conv_block(current, own_params)
        slot_index = tick_index - section_index
        is_valid = jnp.logical_and(slot_index >= 0, slot_index < num_micro)
        safe_slot = jnp.clip(slot_index, 0, num_micro - 1)
        previous = lax.dynamic_index_in_dim(saved, safe_slot, 0, keepdims=False)
        saved = lax.dynamic_update_index_in_dim(
            saved, jnp.where(is_valid, produced, previous), safe_slot, 0
        )
        if tick_index + 1 < num_ticks:
            arriving = lax.ppermute(
                produced, "section", [(i, i + 1) for i in range(sections - 1)]
            )
    return saved[None]


def on_device(inputs, *weights):
    num_micro, images, local_rows, width, _ = inputs.shape
    one_image_each = (
        images == 1
        and lax.axis_size("row") == num_micro == 4
        and lax.axis_size("dp") == 2
        and local_rows % 4 == 0
        and width % 16 == 0
    )
    plan = image_plan if one_image_each else rows_plan
    return plan(inputs, *weights)


def solution(mesh):
    return jax.shard_map(
        on_device,
        mesh=mesh,
        in_specs=(
            P(None, "dp", "row", None, None),
            P("section", None, None, None),
            P("section", None),
            P("section", None),
            P("section", None),
            P("section", None, "dp"),
            P("section", None),
            P("section", None),
            P("section", None),
            P("section", "dp", None),
            P("section", None),
        ),
        out_specs=P("section", None, "dp", "row", None, None),
        check_vma=False,
    )
```

```python
import functools

import jax
import jax.numpy as jnp
from jax import lax
from jax.experimental import pallas as pl
from jax.experimental.pallas import tpu as pltpu
from jax.sharding import PartitionSpec as P

EPS_NORM = 1e-06
EPS_GRN = 1e-06
LANES = 128
VMEM_BYTES = 40 * 1024 * 1024
REACH = 3
CHUNK = 4


def fill_columns(xp, xs, x, channels):
    height, reach_cols, blocks, lanes = xs.shape
    stride = reach_cols - 2 * REACH
    width = stride * blocks
    groups = lanes // LANES
    xp[...] = jnp.zeros(xp.shape, jnp.float32)

    def rows(n, carry):
        for k in range(2):
            r = 2 * n + k
            row = x[r].astype(jnp.float32)
            for g in range(groups):
                at = slice(g * LANES, (g + 1) * LANES)
                own = row[:, g * LANES : min((g + 1) * LANES, channels)]
                xp[k * groups + g, 8 : 8 + width, 0 : own.shape[1]] = own
                for q in range(reach_cols):
                    near = pl.ds(8 - REACH + q, blocks, stride=stride)
                    xs[r, q, :, at] = xp[k * groups + g, near, :]
        return carry

    lax.fori_loop(0, height // 2, rows, 0)


def conv(xs, taps, cvec, cq):
    rows = xs.shape[0]
    height, stride, blocks, lanes = cq.shape
    span = 2 * REACH + 1
    above = (height - rows) // 2

    def group(g, carry):
        at = pl.ds(pl.multiple_of(g * LANES, LANES), LANES)

        def column(q, carry):
            bias = jnp.broadcast_to(cvec[0:1, at], (blocks, LANES))
            acc = [None if above else bias] * height
            for j in range(span):
                kern = [
                    jnp.broadcast_to(taps[i * span + j : i * span + j + 1, at], (blocks, LANES))
                    for i in range(span)
                ]
                for r in range(rows):
                    x_row = xs[r, q + j, :, at]
                    for i in range(span):
                        h = r + above + REACH - i
                        if 0 <= h < height:
                            term = kern[i] * x_row
                            acc[h] = term if acc[h] is None else acc[h] + term
            for h in range(height):
                cq[h, q, :, at] = acc[h]
            return carry

        return lax.fori_loop(0, stride, column, carry)

    lax.fori_loop(0, lanes // LANES, group, 0)


def norm(cq, cvec, xp, flat, skip=0):
    padded, stride, blocks, lanes = cq.shape
    height = padded - 2 * skip
    channels = flat.shape[1]
    width = stride * blocks
    groups = lanes // LANES
    inside = lax.broadcasted_iota(jnp.int32, (blocks, lanes), 1) < channels

    def rows(n, carry):
        for k in range(2):
            h = 2 * n + k
            for q in range(stride):
                v = cq[h + skip, q]
                mean = jnp.sum(v, axis=-1, keepdims=True) * (1.0 / channels)
                c = jnp.where(inside, v - mean, 0.0)
                var = jnp.sum(c * c, axis=-1, keepdims=True) * (1.0 / channels)
                c = c * lax.rsqrt(var + EPS_NORM) * cvec[1:2, :] + cvec[2:3, :]
                for g in range(groups):
                    at = slice(g * LANES, (g + 1) * LANES)
                    xp[k * groups + g, pl.ds(q, blocks, stride=stride), :] = c[:, at]
            at_cell = pl.ds(pl.multiple_of(h * width, width), width)
            for g in range(groups):
                at = slice(g * LANES, min((g + 1) * LANES, channels))
                flat[at_cell, at] = xp[k * groups + g, 0:width, 0 : at.stop - at.start].astype(
                    jnp.bfloat16
                )
        return carry

    lax.fori_loop(0, height // 2, rows, 0)


def conv_norm(x, taps, cvec, flat, xp, xs, cq):
    fill_columns(xp, xs, x, x.shape[2])
    conv(xs, taps, cvec, cq)
    norm(cq, cvec, xp, flat)


def conv_scratch(rows, out_rows, width, lanes):
    return [
        pltpu.VMEM((2 * lanes // LANES, width + 16, LANES), jnp.float32),
        pltpu.VMEM((rows, width // 8 + 2 * REACH, 8, lanes), jnp.float32),
        pltpu.VMEM((out_rows, width // 8, 8, lanes), jnp.float32),
    ]


def gelu(v):
    return 0.5 * v * (1.0 + lax.erf(v * (0.5**0.5)))


def mlp(x, flat, ins, outs, cvec, fvec, acts, ssq, out):
    height, width, channels = x.shape
    half = ins[0].shape[1]
    step = 2 * LANES

    def units(w_in, act, which, start, count):
        raised = jnp.dot(
            flat[...], w_in[:, pl.ds(start, count)], preferred_element_type=jnp.float32
        )
        active = gelu(raised + fvec[which, 0:1, pl.ds(start, count)]).astype(jnp.bfloat16)
        act[:, pl.ds(start, count)] = active
        wide = active.astype(jnp.float32)
        ssq[which, :, pl.ds(start, count)] = jnp.sum(
            (wide * wide).reshape(height * width // 8, 8, count), axis=0
        )

    whole = half // step
    for which in range(2):

        def full(n, carry):
            units(ins[which], acts[which], which, pl.multiple_of(n * step, step), step)
            return carry

        lax.fori_loop(0, whole, full, 0)
        if half % step:
            units(ins[which], acts[which], which, whole * step, half % step)

    magnitude = jnp.sqrt(jnp.sum(ssq[...], axis=1, keepdims=True))
    total = jnp.sum(jnp.sum(magnitude, axis=2, keepdims=True), axis=0, keepdims=True)
    ratio = magnitude / (total * (0.5 / half) + EPS_GRN)
    scale = fvec[:, 1:2, :] * ratio + 1.0
    shift = fvec[:, 2:3, :]
    rows = CHUNK * width

    def lower(n, carry):
        update = cvec[3:4, 0:channels]
        for which in range(2):
            a = acts[which][pl.ds(pl.multiple_of(n * rows, rows), rows), :].astype(jnp.float32)
            hidden = (a * scale[which] + shift[which]).astype(jnp.bfloat16)
            update = update + jnp.dot(
                hidden, outs[which][...], preferred_element_type=jnp.float32
            )
        at = pl.ds(n * CHUNK, CHUNK)
        out[at] = (
            x[at].astype(jnp.float32) + update.reshape(CHUNK, width, channels)
        ).astype(jnp.bfloat16)
        return carry

    lax.fori_loop(0, height // CHUNK, lower, 0)


def pick_kernel(pos, inputs, *refs):
    outs, sems = refs[:-1], refs[-1]
    copies = [
        pltpu.make_async_copy(inputs.at[pos[n], 0], out, sems.at[n]) for n, out in enumerate(outs)
    ]
    for copy in copies:
        copy.start()
    for copy in copies:
        copy.wait()


def piece_kernel(piece, taps, cvec, part, xp, xs):
    fill_columns(xp, xs, piece, piece.shape[2])
    conv(xs, taps, cvec, part)


def last_piece_kernel(pos, *refs, count):
    pieces, parts = refs[:count], refs[count : 2 * count - 1]
    taps, cvec, x, flat, xp, xs, own, cq = refs[2 * count - 1 :]
    rows = pieces[0].shape[0]
    height, stride, blocks, lanes = cq.shape
    cq[...] = jnp.broadcast_to(cvec[0:1, :].reshape(1, 1, 1, lanes), cq.shape)
    fill_columns(xp, xs, pieces[-1], x.shape[2])
    conv(xs, taps, cvec, own)
    for piece, part, p in zip(pieces, (*parts, own), range(count)):
        at = pos[p] * rows
        x[pl.ds(at, rows)] = piece[...]
        cq[pl.ds(at, rows + 2 * REACH)] += part[...]
    norm(cq, cvec, xp, flat, REACH)


def conv_kernel(section, x, taps, cvec, flat, xp, xs, cq, *, tick):
    @pl.when(section[0] == tick)
    def _():
        conv_norm(x, taps, cvec, flat, xp, xs, cq)


def mlp_kernel(section, *refs, tick):
    ins, outs = (refs[0], refs[1]), (refs[2], refs[3])
    x, flat, cvec, fvec, prev, out, act_a, act_b, ssq = refs[4:]

    @pl.when(jnp.logical_or(tick == 0, section[0] == tick))
    def _():
        mlp(x, flat, ins, outs, cvec, fvec, (act_a, act_b), ssq, out)

    @pl.when(jnp.logical_and(tick != 0, section[0] != tick))
    def _():
        out[...] = prev[...]


def block_kernel(section, x, taps, cvec, fvec, *refs, tick):
    ins, outs = (refs[0], refs[1]), (refs[2], refs[3])
    prev, out, xp, xs, cq, flat, act_a, act_b, ssq = refs[4:]

    @pl.when(section[0] == tick)
    def _():
        conv_norm(x, taps, cvec, flat, xp, xs, cq)
        mlp(x, flat, ins, outs, cvec, fvec, (act_a, act_b), ssq, out)

    @pl.when(section[0] != tick)
    def _():
        out[...] = prev[...]


SMEM = pl.BlockSpec(memory_space=pltpu.SMEM)
VMEM = pl.BlockSpec(memory_space=pltpu.VMEM)


def block_cost(cells, channels, hidden_units):
    return pl.CostEstimate(
        flops=4 * cells * channels * hidden_units,
        bytes_accessed=4 * channels * hidden_units + 4 * cells * channels,
        transcendentals=cells * hidden_units,
    )


def mlp_scratch(cells, half):
    return [
        pltpu.VMEM((cells, half), jnp.bfloat16),
        pltpu.VMEM((cells, half), jnp.bfloat16),
        pltpu.VMEM((2, 8, half), jnp.float32),
    ]


def kernel_params():
    return pltpu.CompilerParams(vmem_limit_bytes=VMEM_BYTES)


def run_pick(pos, inputs):
    count = pos.shape[0]
    return pl.pallas_call(
        pick_kernel,
        out_shape=(jax.ShapeDtypeStruct(inputs.shape[2:], inputs.dtype),) * count,
        in_specs=[SMEM, pl.BlockSpec(memory_space=pl.ANY)],
        out_specs=(VMEM,) * count,
        scratch_shapes=[pltpu.SemaphoreType.DMA((count,))],
        compiler_params=kernel_params(),
        name="pick_rows",
    )(pos, inputs)


def run_piece(piece, taps, cvec):
    rows, width, _ = piece.shape
    lanes = taps.shape[1]
    out_rows = rows + 2 * REACH
    return pl.pallas_call(
        piece_kernel,
        out_shape=jax.ShapeDtypeStruct((out_rows, width // 8, 8, lanes), jnp.float32),
        in_specs=[VMEM] * 3,
        out_specs=VMEM,
        scratch_shapes=conv_scratch(rows, out_rows, width, lanes)[:2],
        compiler_params=kernel_params(),
        name="conv_piece",
    )(piece, taps, cvec)


def run_last_piece(pos, pieces, parts, taps, cvec):
    rows, width, channels = pieces[0].shape
    lanes = taps.shape[1]
    height = rows * len(pieces)
    scratch = conv_scratch(rows, rows + 2 * REACH, width, lanes)
    return pl.pallas_call(
        functools.partial(last_piece_kernel, count=len(pieces)),
        out_shape=(
            jax.ShapeDtypeStruct((height, width, channels), jnp.bfloat16),
            jax.ShapeDtypeStruct((height * width, channels), jnp.bfloat16),
        ),
        in_specs=[SMEM] + [VMEM] * (len(pieces) + len(parts) + 2),
        out_specs=(VMEM, VMEM),
        scratch_shapes=scratch + [conv_scratch(1, height + 2 * REACH, width, lanes)[2]],
        compiler_params=kernel_params(),
        name="last_piece",
    )(pos, *pieces, *parts, taps, cvec)


def run_conv(section, x, taps, cvec, tick):
    height, width, channels = x.shape
    lanes = taps.shape[1]
    return pl.pallas_call(
        functools.partial(conv_kernel, tick=tick),
        out_shape=jax.ShapeDtypeStruct((height * width, channels), jnp.bfloat16),
        in_specs=[SMEM] + [VMEM] * 3,
        out_specs=VMEM,
        scratch_shapes=conv_scratch(height, height, width, lanes),
        compiler_params=kernel_params(),
        name="conv",
    )(section, x, taps, cvec)


def run_mlp(section, x, flat, cvec, fvec, weights, prev, tick):
    height, width, channels = x.shape
    half = weights[0].shape[1]
    return pl.pallas_call(
        functools.partial(mlp_kernel, tick=tick),
        out_shape=jax.ShapeDtypeStruct(x.shape, jnp.bfloat16),
        in_specs=[SMEM] + [VMEM] * 9,
        out_specs=VMEM,
        scratch_shapes=mlp_scratch(height * width, half),
        compiler_params=kernel_params(),
        cost_estimate=block_cost(height * width, channels, 2 * half),
        name="mlp",
    )(section, *weights, x, flat, cvec, fvec, prev)


def run_block(section, x, taps, cvec, fvec, weights, prev, tick):
    height, width, channels = x.shape
    lanes = taps.shape[1]
    half = weights[0].shape[1]
    return pl.pallas_call(
        functools.partial(block_kernel, tick=tick),
        out_shape=jax.ShapeDtypeStruct(x.shape, jnp.bfloat16),
        in_specs=[SMEM] + [VMEM] * 9,
        out_specs=VMEM,
        scratch_shapes=conv_scratch(height, height, width, lanes)
        + [pltpu.VMEM((height * width, channels), jnp.bfloat16)]
        + mlp_scratch(height * width, half),
        compiler_params=kernel_params(),
        cost_estimate=block_cost(height * width, channels, 2 * half),
        name="block",
    )(section, x, taps, cvec, fvec, *weights, prev)


def swap_pairs(sections, size, by):
    return [(s * size + p, s * size + (p ^ by)) for s in sections for p in range(size)]


def image_plan(
    inputs,
    depth_kernel,
    depth_bias,
    norm_gain,
    norm_bias,
    proj_in,
    bias_in,
    grn_gamma,
    grn_beta,
    proj_out,
    bias_out,
):
    sections = lax.axis_size("section")
    rows_axis = lax.axis_size("row")
    section = lax.axis_index("section")
    me = lax.axis_index("row")
    part = lax.axis_index("dp")
    _, _, local_rows, width, channels = inputs.shape
    height = local_rows * rows_axis
    lanes = -(-channels // LANES) * LANES
    extra = lanes - channels
    half = proj_in.shape[2]

    def rows_from_helper(x, by):
        pairs = [(rows_axis + (p ^ by), p) for p in range(rows_axis)]
        return lax.ppermute(x, ("section", "row"), pairs)

    def part_swap(x, which):
        return lax.ppermute(x, ("section", "dp"), swap_pairs(which, 2, 1))

    even = range(0, sections, 2)
    odd = range(1, sections, 2)
    w_in, w_out = proj_in[0], proj_out[0]
    order = (0, 2, 3, 1)
    pos = jnp.stack([me ^ by for by in order]).astype(jnp.int32)
    pieces = run_pick(pos, inputs)
    pieces = [pieces[0]] + [rows_from_helper(p, by) for p, by in zip(pieces[1:], order[1:])]
    even_in = part_swap(w_in, even)
    even_out = part_swap(w_out, even)

    fvec = jnp.concatenate([bias_in, grn_gamma, grn_beta], axis=0).astype(jnp.float32)
    fvec = fvec.reshape(3, 2, half).transpose(1, 0, 2)
    fvec = jnp.where(part == 0, fvec, fvec[::-1])
    cvec = jnp.concatenate([depth_bias, norm_gain, norm_bias, bias_out], axis=0)
    cvec = jnp.pad(cvec.astype(jnp.float32), ((0, 0), (0, extra)))
    taps = depth_kernel[0].reshape(-1, channels).astype(jnp.float32)
    taps = jnp.pad(taps, ((0, 0), (0, extra)))
    at = section.astype(jnp.int32).reshape(1)

    parts = [run_piece(p, taps, cvec) for p in pieces[:-1]]
    x, flat = run_last_piece(pos, pieces, parts, taps, cvec)
    weights = [(w_in, even_in, w_out, even_out)]
    result = run_mlp(at, x, flat, cvec, fvec, weights[0], x, 0)
    for tick in range(1, sections):
        arriving = lax.ppermute(result, "section", [(tick - 1, tick)])
        if tick == 1:
            late_in, late_out, result = lax.optimization_barrier((w_in, w_out, result))
            weights.append(
                (w_in, part_swap(late_in, odd), w_out, part_swap(late_out, odd))
            )
            flat = run_conv(at, arriving, taps, cvec, tick)
            result = run_mlp(at, arriving, flat, cvec, fvec, weights[1], result, tick)
        else:
            result = run_block(
                at, arriving, taps, cvec, fvec, weights[tick % 2], result, tick
            )

    def rows_of(p):
        return lax.dynamic_slice_in_dim(result, p * local_rows, local_rows, axis=0)

    saved = jnp.zeros((rows_axis, local_rows, width, channels), jnp.bfloat16)
    saved = lax.dynamic_update_index_in_dim(saved, rows_of(me), me, 0)
    for by in (2, 3, 1):
        got = lax.ppermute(rows_of(me ^ by), "row", [(p, p ^ by) for p in range(rows_axis)])
        saved = lax.dynamic_update_index_in_dim(saved, got, me ^ by, 0)
    return saved[None, :, None]


def extended(cells, sides, width):
    for axis, dim in sides:
        count = lax.axis_size(axis)
        ends = count - 1
        head = lax.slice_in_dim(cells, 0, width, axis=dim)
        tail = lax.slice_in_dim(cells, cells.shape[dim] - width, cells.shape[dim], axis=dim)
        cells = jnp.concatenate(
            [
                lax.ppermute(tail, axis, [(i, (i + 1) % count) for i in range(ends)]),
                cells,
                lax.ppermute(head, axis, [((i + 1) % count, i) for i in range(ends)]),
            ],
            axis=dim,
        )
    return cells


def depthwise(padded, kernel, bias_term):
    channels = padded.shape[-1]
    conv_out = lax.conv_general_dilated(
        padded.astype(jnp.float32),
        kernel.astype(jnp.float32)[:, :, None, :],
        (1, 1),
        "VALID",
        dimension_numbers=("NHWC", "HWIO", "NHWC"),
        feature_group_count=channels,
        precision=lax.Precision.HIGHEST,
    )
    return conv_out + bias_term.astype(jnp.float32)


def conv_block(current, params):
    (
        depth_kernel,
        depth_bias,
        norm_gain,
        norm_bias,
        proj_in,
        bias_in,
        grn_gamma,
        grn_beta,
        proj_out,
        bias_out,
    ) = params
    num_items, num_rows, num_cols, channels = current.shape
    padded = extended(current, (("row", 1),), REACH)
    padded = jnp.pad(padded, ((0, 0), (0, 0), (REACH, REACH), (0, 0)))
    conv_out = depthwise(padded, depth_kernel, depth_bias)
    center = conv_out - jnp.mean(conv_out, axis=-1, keepdims=True)
    spread = jnp.mean(center * center, axis=-1, keepdims=True)
    normed = (
        center * lax.rsqrt(spread + EPS_NORM) * norm_gain.astype(jnp.float32)
        + norm_bias.astype(jnp.float32)
    ).astype(jnp.bfloat16)
    flat_rows = normed.reshape(num_items * num_rows * num_cols, channels)
    raised = jnp.dot(flat_rows, proj_in, preferred_element_type=jnp.float32) + bias_in.astype(
        jnp.float32
    )
    active = jax.nn.gelu(raised, approximate=False).astype(jnp.bfloat16)
    grouped = active.reshape(num_items, num_rows * num_cols, -1).astype(jnp.float32)
    local_sq = jnp.sum(grouped * grouped, axis=1)
    total_sq = lax.psum(local_sq, "row")
    magnitude = jnp.sqrt(total_sq)
    grn_ratio = magnitude / (jnp.mean(magnitude, axis=-1, keepdims=True) + EPS_GRN)
    hidden = (
        grn_gamma.astype(jnp.float32) * grouped * grn_ratio[:, None, :]
        + grn_beta.astype(jnp.float32)
        + grouped
    ).astype(jnp.bfloat16)
    update = jnp.dot(
        hidden.reshape(num_items * num_rows * num_cols, -1),
        proj_out,
        preferred_element_type=jnp.float32,
    ) + bias_out.astype(jnp.float32)
    return (
        current.astype(jnp.float32) + update.reshape(num_items, num_rows, num_cols, channels)
    ).astype(jnp.bfloat16)


def rows_plan(inputs, *weights):
    (
        depth_kernel,
        depth_bias,
        norm_gain,
        norm_bias,
        proj_in,
        bias_in,
        grn_gamma,
        grn_beta,
        proj_out,
        bias_out,
    ) = weights
    proj_in = lax.all_gather(proj_in, "dp", axis=2, tiled=True)
    proj_out = lax.all_gather(proj_out, "dp", axis=1, tiled=True)
    own_params = tuple(
        w[0]
        for w in (
            depth_kernel,
            depth_bias,
            norm_gain,
            norm_bias,
            proj_in,
            bias_in,
            grn_gamma,
            grn_beta,
            proj_out,
            bias_out,
        )
    )
    sections = lax.axis_size("section")
    section_index = lax.axis_index("section")
    num_micro = inputs.shape[0]
    num_ticks = num_micro + sections - 1
    arriving = jnp.zeros_like(inputs[0])
    saved = jnp.zeros_like(inputs)
    for tick_index in range(num_ticks):
        fresh_input = inputs[min(tick_index, num_micro - 1)]
        current = jnp.where(section_index == 0, fresh_input, arriving)
        produced = conv_block(current, own_params)
        slot_index = tick_index - section_index
        is_valid = jnp.logical_and(slot_index >= 0, slot_index < num_micro)
        safe_slot = jnp.clip(slot_index, 0, num_micro - 1)
        previous = lax.dynamic_index_in_dim(saved, safe_slot, 0, keepdims=False)
        saved = lax.dynamic_update_index_in_dim(
            saved, jnp.where(is_valid, produced, previous), safe_slot, 0
        )
        if tick_index + 1 < num_ticks:
            arriving = lax.ppermute(
                produced, "section", [(i, i + 1) for i in range(sections - 1)]
            )
    return saved[None]


def on_device(inputs, *weights):
    num_micro, images, local_rows, width, _ = inputs.shape
    one_image_each = (
        images == 1
        and lax.axis_size("row") == num_micro == 4
        and lax.axis_size("dp") == 2
        and lax.axis_size("section") > 1
        and local_rows % 4 == 0
        and width % 16 == 0
    )
    plan = image_plan if one_image_each else rows_plan
    return plan(inputs, *weights)


def solution(mesh):
    return jax.shard_map(
        on_device,
        mesh=mesh,
        in_specs=(
            P(None, "dp", "row", None, None),
            P("section", None, None, None),
            P("section", None),
            P("section", None),
            P("section", None),
            P("section", None, "dp"),
            P("section", None),
            P("section", None),
            P("section", None),
            P("section", "dp", None),
            P("section", None),
        ),
        out_specs=P("section", None, "dp", "row", None, None),
        check_vma=False,
    )
```

```python
import functools

import jax
import jax.numpy as jnp
from jax import lax
from jax.experimental import pallas as pl
from jax.experimental.pallas import tpu as pltpu
from jax.sharding import PartitionSpec as P

EPS_NORM = 1e-06
EPS_GRN = 1e-06
LANES = 128
VMEM_BYTES = 20 * 1024 * 1024
PREPARE_VMEM_BYTES = 60 * 1024 * 1024
REACH = 3
CHUNK = 4
NORM_ROWS = 4


def fill_columns(xp, xs, x, channels):
    height, reach_cols, blocks, lanes = xs.shape
    stride = reach_cols - 2 * REACH
    width = stride * blocks
    groups = lanes // LANES
    xp[...] = jnp.zeros(xp.shape, jnp.float32)

    def rows(n, carry):
        for k in range(2):
            r = 2 * n + k
            row = x[r].astype(jnp.float32)
            for g in range(groups):
                at = slice(g * LANES, (g + 1) * LANES)
                own = row[:, g * LANES : min((g + 1) * LANES, channels)]
                xp[k * groups + g, 8 : 8 + width, 0 : own.shape[1]] = own
                for q in range(reach_cols):
                    near = pl.ds(8 - REACH + q, blocks, stride=stride)
                    xs[r, q, :, at] = xp[k * groups + g, near, :]
        return carry

    lax.fori_loop(0, height // 2, rows, 0)


def conv(xs, taps, cvec, cq):
    rows = xs.shape[0]
    height, stride, blocks, lanes = cq.shape
    span = 2 * REACH + 1
    above = (height - rows) // 2

    def group(g, carry):
        at = pl.ds(pl.multiple_of(g * LANES, LANES), LANES)

        def column(q, carry):
            bias = jnp.broadcast_to(cvec[0:1, at], (blocks, LANES))
            acc = [None if above else bias] * height
            for j in range(span):
                kern = [
                    jnp.broadcast_to(taps[i * span + j : i * span + j + 1, at], (blocks, LANES))
                    for i in range(span)
                ]
                for r in range(rows):
                    x_row = xs[r, q + j, :, at]
                    for i in range(span):
                        h = r + above + REACH - i
                        if 0 <= h < height:
                            term = kern[i] * x_row
                            acc[h] = term if acc[h] is None else acc[h] + term
            for h in range(height):
                cq[h, q, :, at] = acc[h]
            return carry

        return lax.fori_loop(0, stride, column, carry)

    lax.fori_loop(0, lanes // LANES, group, 0)


def norm(cq, cvec, xp, flat, skip=0):
    padded, stride, blocks, lanes = cq.shape
    height = padded - 2 * skip
    channels = flat.shape[1]
    width = stride * blocks
    groups = lanes // LANES
    inside = lax.broadcasted_iota(jnp.int32, (blocks, lanes), 1) < channels

    def rows(n, carry):
        for k in range(NORM_ROWS):
            h = NORM_ROWS * n + k
            for q in range(stride):
                v = cq[h + skip, q]
                mean = jnp.sum(v, axis=-1, keepdims=True) * (1.0 / channels)
                c = jnp.where(inside, v - mean, 0.0)
                var = jnp.sum(c * c, axis=-1, keepdims=True) * (1.0 / channels)
                c = c * lax.rsqrt(var + EPS_NORM) * cvec[1:2, :] + cvec[2:3, :]
                for g in range(groups):
                    at = slice(g * LANES, (g + 1) * LANES)
                    xp[k * groups + g, pl.ds(q, blocks, stride=stride), :] = c[:, at]
            at_cell = pl.ds(pl.multiple_of(h * width, width), width)
            for g in range(groups):
                at = slice(g * LANES, min((g + 1) * LANES, channels))
                flat[at_cell, at] = xp[k * groups + g, 0:width, 0 : at.stop - at.start].astype(
                    jnp.bfloat16
                )
        return carry

    lax.fori_loop(0, height // NORM_ROWS, rows, 0)


def conv_norm(x, taps, cvec, flat, xp, xs, cq):
    fill_columns(xp, xs, x, x.shape[2])
    conv(xs, taps, cvec, cq)
    norm(cq, cvec, xp, flat)


def conv_scratch(rows, out_rows, width, lanes):
    return [
        pltpu.VMEM((NORM_ROWS * lanes // LANES, width + 16, LANES), jnp.float32),
        pltpu.VMEM((rows, width // 8 + 2 * REACH, 8, lanes), jnp.float32),
        pltpu.VMEM((out_rows, width // 8, 8, lanes), jnp.float32),
    ]


def gelu(v):
    return 0.5 * v * (1.0 + lax.erf(v * (0.5**0.5)))


def mlp(x, flat, ins, outs, cvec, fvec, acts, ssq, out):
    height, width, channels = x.shape
    half = ins[0].shape[1]
    step = 2 * LANES

    def units(w_in, act, which, start, count):
        raised = jnp.dot(
            flat[...], w_in[:, pl.ds(start, count)], preferred_element_type=jnp.float32
        )
        active = gelu(raised + fvec[which, 0:1, pl.ds(start, count)]).astype(jnp.bfloat16)
        act[:, pl.ds(start, count)] = active
        wide = active.astype(jnp.float32)
        ssq[which, :, pl.ds(start, count)] = jnp.sum(
            (wide * wide).reshape(height * width // 8, 8, count), axis=0
        )

    whole = half // step
    for which in range(2):

        def full(n, carry):
            units(ins[which], acts[which], which, pl.multiple_of(n * step, step), step)
            return carry

        lax.fori_loop(0, whole, full, 0)
        if half % step:
            units(ins[which], acts[which], which, whole * step, half % step)

    magnitude = jnp.sqrt(jnp.sum(ssq[...], axis=1, keepdims=True))
    total = jnp.sum(jnp.sum(magnitude, axis=2, keepdims=True), axis=0, keepdims=True)
    ratio = magnitude / (total * (0.5 / half) + EPS_GRN)
    scale = fvec[:, 1:2, :] * ratio + 1.0
    shift = fvec[:, 2:3, :]
    rows = CHUNK * width

    def lower(n, carry):
        update = cvec[3:4, 0:channels]
        for which in range(2):
            a = acts[which][pl.ds(pl.multiple_of(n * rows, rows), rows), :].astype(jnp.float32)
            hidden = (a * scale[which] + shift[which]).astype(jnp.bfloat16)
            update = update + jnp.dot(
                hidden, outs[which][...], preferred_element_type=jnp.float32
            )
        at = pl.ds(n * CHUNK, CHUNK)
        out[at] = (
            x[at].astype(jnp.float32) + update.reshape(CHUNK, width, channels)
        ).astype(jnp.bfloat16)
        return carry

    lax.fori_loop(0, height // CHUNK, lower, 0)


def prepare_kernel(index, inputs, kernel, *refs):
    vectors, refs = refs[:7], refs[7:]
    count = len(refs) - 12
    pieces, (taps, cvec, fvec) = refs[:count], refs[count : count + 3]
    held, staged, sems = refs[count + 3], refs[count + 4 : -1], refs[-1]
    moves = [(kernel, held), *zip(vectors, staged)]
    moves += [(inputs.at[index[n], 0], piece) for n, piece in enumerate(pieces)]
    copies = [pltpu.make_async_copy(a, b, sems.at[n]) for n, (a, b) in enumerate(moves)]
    for copy in copies:
        copy.start()
    taps[...] = jnp.zeros(taps.shape, jnp.float32)
    cvec[...] = jnp.zeros(cvec.shape, jnp.float32)
    for copy in copies:
        copy.wait()
    channels = kernel.shape[3]
    span = kernel.shape[1]
    half = fvec.shape[2]
    for i in range(span):
        taps[i * span : (i + 1) * span, 0:channels] = held[0, i].astype(jnp.float32)
    for n in range(4):
        cvec[n : n + 1, 0:channels] = staged[n][...].astype(jnp.float32)
    first = index[count] == 0
    for n in range(3):
        v = staged[4 + n][...].astype(jnp.float32)
        low, high = v[:, 0:half], v[:, half:]
        fvec[0, n : n + 1, :] = jnp.where(first, low, high)
        fvec[1, n : n + 1, :] = jnp.where(first, high, low)


def piece_kernel(piece, taps, cvec, part, xp, xs):
    fill_columns(xp, xs, piece, piece.shape[2])
    conv(xs, taps, cvec, part)


def last_piece_kernel(index, *refs, count):
    pieces, parts = refs[:count], refs[count : 2 * count - 1]
    taps, cvec, x, flat, xp, xs, own, cq = refs[2 * count - 1 :]
    rows = pieces[0].shape[0]
    height, stride, blocks, lanes = cq.shape
    cq[...] = jnp.broadcast_to(cvec[0:1, :].reshape(1, 1, 1, lanes), cq.shape)
    fill_columns(xp, xs, pieces[-1], x.shape[2])
    conv(xs, taps, cvec, own)
    for piece, part, p in zip(pieces, (*parts, own), range(count)):
        at = index[p] * rows
        x[pl.ds(at, rows)] = piece[...]
        cq[pl.ds(at, rows + 2 * REACH)] += part[...]
    norm(cq, cvec, xp, flat, REACH)


def conv_kernel(section, x, taps, cvec, flat, xp, xs, cq, *, tick):
    @pl.when(section[0] == tick)
    def _():
        conv_norm(x, taps, cvec, flat, xp, xs, cq)


def mlp_kernel(section, *refs, tick):
    ins, outs = (refs[0], refs[1]), (refs[2], refs[3])
    x, flat, cvec, fvec, prev, out, act_a, act_b, ssq = refs[4:]

    @pl.when(section[0] == tick)
    def _():
        mlp(x, flat, ins, outs, cvec, fvec, (act_a, act_b), ssq, out)

    @pl.when(section[0] != tick)
    def _():
        out[...] = prev[...]


def block_kernel(section, x, taps, cvec, fvec, *refs, tick):
    ins, outs = (refs[0], refs[1]), (refs[2], refs[3])
    prev, out, xp, xs, cq, flat, act_a, act_b, ssq = refs[4:]

    @pl.when(section[0] == tick)
    def _():
        conv_norm(x, taps, cvec, flat, xp, xs, cq)
        mlp(x, flat, ins, outs, cvec, fvec, (act_a, act_b), ssq, out)

    @pl.when(section[0] != tick)
    def _():
        out[...] = prev[...]


SMEM = pl.BlockSpec(memory_space=pltpu.SMEM)
VMEM = pl.BlockSpec(memory_space=pltpu.VMEM)
HBM = pl.BlockSpec(memory_space=pltpu.HBM)


def block_cost(cells, channels, hidden_units):
    return pl.CostEstimate(
        flops=4 * cells * channels * hidden_units,
        bytes_accessed=4 * channels * hidden_units + 4 * cells * channels,
        transcendentals=cells * hidden_units,
    )


def mlp_scratch(cells, half):
    return [
        pltpu.VMEM((cells, half), jnp.bfloat16),
        pltpu.VMEM((cells, half), jnp.bfloat16),
        pltpu.VMEM((2, 8, half), jnp.float32),
    ]


def kernel_params():
    return pltpu.CompilerParams(vmem_limit_bytes=VMEM_BYTES)


def run_prepare(index, inputs, kernel, vectors, lanes):
    count = index.shape[0] - 1
    half = vectors[-1].shape[1] // 2
    held = (kernel, *vectors)
    return pl.pallas_call(
        prepare_kernel,
        out_shape=(jax.ShapeDtypeStruct(inputs.shape[2:], inputs.dtype),) * count
        + (
            jax.ShapeDtypeStruct((kernel.shape[1] * kernel.shape[2], lanes), jnp.float32),
            jax.ShapeDtypeStruct((4, lanes), jnp.float32),
            jax.ShapeDtypeStruct((2, 3, half), jnp.float32),
        ),
        in_specs=[SMEM] + [HBM] * (len(held) + 1),
        out_specs=(VMEM,) * (count + 3),
        scratch_shapes=[pltpu.VMEM(v.shape, v.dtype) for v in held]
        + [pltpu.SemaphoreType.DMA((len(held) + count,))],
        compiler_params=pltpu.CompilerParams(vmem_limit_bytes=PREPARE_VMEM_BYTES),
        name="prepare",
    )(index, inputs, *held)


def run_piece(piece, taps, cvec):
    rows, width, _ = piece.shape
    lanes = taps.shape[1]
    out_rows = rows + 2 * REACH
    return pl.pallas_call(
        piece_kernel,
        out_shape=jax.ShapeDtypeStruct((out_rows, width // 8, 8, lanes), jnp.float32),
        in_specs=[VMEM] * 3,
        out_specs=VMEM,
        scratch_shapes=conv_scratch(rows, out_rows, width, lanes)[:2],
        compiler_params=kernel_params(),
        name="conv_piece",
    )(piece, taps, cvec)


def run_last_piece(index, pieces, parts, taps, cvec):
    rows, width, channels = pieces[0].shape
    lanes = taps.shape[1]
    height = rows * len(pieces)
    scratch = conv_scratch(rows, rows + 2 * REACH, width, lanes)
    return pl.pallas_call(
        functools.partial(last_piece_kernel, count=len(pieces)),
        out_shape=(
            jax.ShapeDtypeStruct((height, width, channels), jnp.bfloat16),
            jax.ShapeDtypeStruct((height * width, channels), jnp.bfloat16),
        ),
        in_specs=[SMEM] + [VMEM] * (len(pieces) + len(parts) + 2),
        out_specs=(VMEM, VMEM),
        scratch_shapes=scratch + [conv_scratch(1, height + 2 * REACH, width, lanes)[2]],
        compiler_params=kernel_params(),
        name="last_piece",
    )(index, *pieces, *parts, taps, cvec)


def run_conv(section, x, taps, cvec, tick):
    height, width, channels = x.shape
    lanes = taps.shape[1]
    return pl.pallas_call(
        functools.partial(conv_kernel, tick=tick),
        out_shape=jax.ShapeDtypeStruct((height * width, channels), jnp.bfloat16),
        in_specs=[SMEM] + [VMEM] * 3,
        out_specs=VMEM,
        scratch_shapes=conv_scratch(height, height, width, lanes),
        compiler_params=kernel_params(),
        name="conv",
    )(section, x, taps, cvec)


def run_mlp(section, x, flat, cvec, fvec, weights, prev, tick):
    height, width, channels = x.shape
    half = weights[0].shape[1]
    return pl.pallas_call(
        functools.partial(mlp_kernel, tick=tick),
        out_shape=jax.ShapeDtypeStruct(x.shape, jnp.bfloat16),
        in_specs=[SMEM] + [VMEM] * 9,
        out_specs=VMEM,
        scratch_shapes=mlp_scratch(height * width, half),
        compiler_params=kernel_params(),
        cost_estimate=block_cost(height * width, channels, 2 * half),
        name="mlp",
    )(section, *weights, x, flat, cvec, fvec, prev)


def run_block(section, x, taps, cvec, fvec, weights, prev, tick):
    height, width, channels = x.shape
    lanes = taps.shape[1]
    half = weights[0].shape[1]
    return pl.pallas_call(
        functools.partial(block_kernel, tick=tick),
        out_shape=jax.ShapeDtypeStruct(x.shape, jnp.bfloat16),
        in_specs=[SMEM] + [VMEM] * 9,
        out_specs=VMEM,
        scratch_shapes=conv_scratch(height, height, width, lanes)
        + [pltpu.VMEM((height * width, channels), jnp.bfloat16)]
        + mlp_scratch(height * width, half),
        compiler_params=kernel_params(),
        cost_estimate=block_cost(height * width, channels, 2 * half),
        name="block",
    )(section, x, taps, cvec, fvec, *weights, prev)


def swap_pairs(sections, size, by):
    return [(s * size + p, s * size + (p ^ by)) for s in sections for p in range(size)]


def image_plan(
    inputs,
    depth_kernel,
    depth_bias,
    norm_gain,
    norm_bias,
    proj_in,
    bias_in,
    grn_gamma,
    grn_beta,
    proj_out,
    bias_out,
):
    sections = lax.axis_size("section")
    rows_axis = lax.axis_size("row")
    section = lax.axis_index("section")
    me = lax.axis_index("row")
    part = lax.axis_index("dp")
    _, _, local_rows, width, channels = inputs.shape
    height = local_rows * rows_axis
    lanes = -(-channels // LANES) * LANES

    def rows_from_helper(x, by):
        pairs = [(rows_axis + (p ^ by), p) for p in range(rows_axis)]
        return lax.ppermute(x, ("section", "row"), pairs)

    def part_swap(x, which):
        return lax.ppermute(x, ("section", "dp"), swap_pairs(which, 2, 1))

    even = range(0, sections, 2)
    odd = range(1, sections, 2)
    w_in, w_out = proj_in[0], proj_out[0]
    order = (0, 2, 3, 1)
    vectors = (depth_bias, norm_gain, norm_bias, bias_out, bias_in, grn_gamma, grn_beta)
    index = jnp.stack([me ^ by for by in order] + [part]).astype(jnp.int32)
    *pieces, taps, cvec, fvec = run_prepare(index, inputs, depth_kernel, vectors, lanes)
    pieces = [pieces[0]] + [rows_from_helper(p, by) for p, by in zip(pieces[1:], order[1:])]
    even_in = part_swap(w_in, even)
    even_out = part_swap(w_out, even)

    at = section.astype(jnp.int32).reshape(1)

    parts = [run_piece(p, taps, cvec) for p in pieces[:-1]]
    x, flat = run_last_piece(index, pieces, parts, taps, cvec)
    weights = [(w_in, even_in, w_out, even_out)]
    result = run_mlp(at, x, flat, cvec, fvec, weights[0], x, 0)
    for tick in range(1, sections):
        arriving = lax.ppermute(result, "section", [(tick - 1, tick)])
        if tick == 1:
            late_in, late_out, result = lax.optimization_barrier((w_in, w_out, result))
            weights.append(
                (w_in, part_swap(late_in, odd), w_out, part_swap(late_out, odd))
            )
            flat = run_conv(at, arriving, taps, cvec, tick)
            result = run_mlp(at, arriving, flat, cvec, fvec, weights[1], result, tick)
        else:
            result = run_block(
                at, arriving, taps, cvec, fvec, weights[tick % 2], result, tick
            )

    def rows_of(p):
        return lax.dynamic_slice_in_dim(result, p * local_rows, local_rows, axis=0)

    saved = jnp.zeros((rows_axis, local_rows, width, channels), jnp.bfloat16)
    saved = lax.dynamic_update_index_in_dim(saved, rows_of(me), me, 0)
    for by in (2, 3, 1):
        got = lax.ppermute(rows_of(me ^ by), "row", [(p, p ^ by) for p in range(rows_axis)])
        saved = lax.dynamic_update_index_in_dim(saved, got, me ^ by, 0)
    return saved[None, :, None]


def extended(cells, sides, width):
    for axis, dim in sides:
        count = lax.axis_size(axis)
        ends = count - 1
        head = lax.slice_in_dim(cells, 0, width, axis=dim)
        tail = lax.slice_in_dim(cells, cells.shape[dim] - width, cells.shape[dim], axis=dim)
        cells = jnp.concatenate(
            [
                lax.ppermute(tail, axis, [(i, (i + 1) % count) for i in range(ends)]),
                cells,
                lax.ppermute(head, axis, [((i + 1) % count, i) for i in range(ends)]),
            ],
            axis=dim,
        )
    return cells


def depthwise(padded, kernel, bias_term):
    channels = padded.shape[-1]
    conv_out = lax.conv_general_dilated(
        padded.astype(jnp.float32),
        kernel.astype(jnp.float32)[:, :, None, :],
        (1, 1),
        "VALID",
        dimension_numbers=("NHWC", "HWIO", "NHWC"),
        feature_group_count=channels,
        precision=lax.Precision.HIGHEST,
    )
    return conv_out + bias_term.astype(jnp.float32)


def conv_block(current, params):
    (
        depth_kernel,
        depth_bias,
        norm_gain,
        norm_bias,
        proj_in,
        bias_in,
        grn_gamma,
        grn_beta,
        proj_out,
        bias_out,
    ) = params
    num_items, num_rows, num_cols, channels = current.shape
    padded = extended(current, (("row", 1),), REACH)
    padded = jnp.pad(padded, ((0, 0), (0, 0), (REACH, REACH), (0, 0)))
    conv_out = depthwise(padded, depth_kernel, depth_bias)
    center = conv_out - jnp.mean(conv_out, axis=-1, keepdims=True)
    spread = jnp.mean(center * center, axis=-1, keepdims=True)
    normed = (
        center * lax.rsqrt(spread + EPS_NORM) * norm_gain.astype(jnp.float32)
        + norm_bias.astype(jnp.float32)
    ).astype(jnp.bfloat16)
    flat_rows = normed.reshape(num_items * num_rows * num_cols, channels)
    raised = jnp.dot(flat_rows, proj_in, preferred_element_type=jnp.float32) + bias_in.astype(
        jnp.float32
    )
    active = jax.nn.gelu(raised, approximate=False).astype(jnp.bfloat16)
    grouped = active.reshape(num_items, num_rows * num_cols, -1).astype(jnp.float32)
    local_sq = jnp.sum(grouped * grouped, axis=1)
    total_sq = lax.psum(local_sq, "row")
    magnitude = jnp.sqrt(total_sq)
    grn_ratio = magnitude / (jnp.mean(magnitude, axis=-1, keepdims=True) + EPS_GRN)
    hidden = (
        grn_gamma.astype(jnp.float32) * grouped * grn_ratio[:, None, :]
        + grn_beta.astype(jnp.float32)
        + grouped
    ).astype(jnp.bfloat16)
    update = jnp.dot(
        hidden.reshape(num_items * num_rows * num_cols, -1),
        proj_out,
        preferred_element_type=jnp.float32,
    ) + bias_out.astype(jnp.float32)
    return (
        current.astype(jnp.float32) + update.reshape(num_items, num_rows, num_cols, channels)
    ).astype(jnp.bfloat16)


def rows_plan(inputs, *weights):
    (
        depth_kernel,
        depth_bias,
        norm_gain,
        norm_bias,
        proj_in,
        bias_in,
        grn_gamma,
        grn_beta,
        proj_out,
        bias_out,
    ) = weights
    proj_in = lax.all_gather(proj_in, "dp", axis=2, tiled=True)
    proj_out = lax.all_gather(proj_out, "dp", axis=1, tiled=True)
    own_params = tuple(
        w[0]
        for w in (
            depth_kernel,
            depth_bias,
            norm_gain,
            norm_bias,
            proj_in,
            bias_in,
            grn_gamma,
            grn_beta,
            proj_out,
            bias_out,
        )
    )
    sections = lax.axis_size("section")
    section_index = lax.axis_index("section")
    num_micro = inputs.shape[0]
    num_ticks = num_micro + sections - 1
    arriving = jnp.zeros_like(inputs[0])
    saved = jnp.zeros_like(inputs)
    for tick_index in range(num_ticks):
        fresh_input = inputs[min(tick_index, num_micro - 1)]
        current = jnp.where(section_index == 0, fresh_input, arriving)
        produced = conv_block(current, own_params)
        slot_index = tick_index - section_index
        is_valid = jnp.logical_and(slot_index >= 0, slot_index < num_micro)
        safe_slot = jnp.clip(slot_index, 0, num_micro - 1)
        previous = lax.dynamic_index_in_dim(saved, safe_slot, 0, keepdims=False)
        saved = lax.dynamic_update_index_in_dim(
            saved, jnp.where(is_valid, produced, previous), safe_slot, 0
        )
        if tick_index + 1 < num_ticks:
            arriving = lax.ppermute(
                produced, "section", [(i, i + 1) for i in range(sections - 1)]
            )
    return saved[None]


def on_device(inputs, *weights):
    num_micro, images, local_rows, width, _ = inputs.shape
    one_image_each = (
        images == 1
        and lax.axis_size("row") == num_micro == 4
        and lax.axis_size("dp") == 2
        and lax.axis_size("section") > 1
        and local_rows % 4 == 0
        and width % 16 == 0
    )
    plan = image_plan if one_image_each else rows_plan
    return plan(inputs, *weights)


def solution(mesh):
    return jax.shard_map(
        on_device,
        mesh=mesh,
        in_specs=(
            P(None, "dp", "row", None, None),
            P("section", None, None, None),
            P("section", None),
            P("section", None),
            P("section", None),
            P("section", None, "dp"),
            P("section", None),
            P("section", None),
            P("section", None),
            P("section", "dp", None),
            P("section", None),
        ),
        out_specs=P("section", None, "dp", "row", None, None),
        check_vma=False,
    )
```

```python
import functools

import jax
import jax.numpy as jnp
from jax import lax
from jax.experimental import pallas as pl
from jax.experimental.pallas import tpu as pltpu
from jax.sharding import PartitionSpec as P

EPS_NORM = 1e-06
EPS_GRN = 1e-06
LANES = 128
VMEM_BYTES = 20 * 1024 * 1024
REACH = 3
CHUNK = 4
NORM_ROWS = 4


def fill_columns(xp, xs, x, channels):
    height, reach_cols, blocks, lanes = xs.shape
    stride = reach_cols - 2 * REACH
    width = stride * blocks
    groups = lanes // LANES
    xp[...] = jnp.zeros(xp.shape, jnp.float32)

    def rows(n, carry):
        for k in range(2):
            r = 2 * n + k
            row = x[r].astype(jnp.float32)
            for g in range(groups):
                at = slice(g * LANES, (g + 1) * LANES)
                own = row[:, g * LANES : min((g + 1) * LANES, channels)]
                xp[k * groups + g, 8 : 8 + width, 0 : own.shape[1]] = own
                for q in range(reach_cols):
                    near = pl.ds(8 - REACH + q, blocks, stride=stride)
                    xs[r, q, :, at] = xp[k * groups + g, near, :]
        return carry

    lax.fori_loop(0, height // 2, rows, 0)


def conv(xs, taps, cvec, cq):
    rows = xs.shape[0]
    height, stride, blocks, lanes = cq.shape
    span = 2 * REACH + 1
    above = (height - rows) // 2

    def group(g, carry):
        at = pl.ds(pl.multiple_of(g * LANES, LANES), LANES)

        def column(q, carry):
            bias = jnp.broadcast_to(cvec[0:1, at], (blocks, LANES))
            acc = [None if above else bias] * height
            for j in range(span):
                kern = [
                    jnp.broadcast_to(taps[i * span + j : i * span + j + 1, at], (blocks, LANES))
                    for i in range(span)
                ]
                for r in range(rows):
                    x_row = xs[r, q + j, :, at]
                    for i in range(span):
                        h = r + above + REACH - i
                        if 0 <= h < height:
                            term = kern[i] * x_row
                            acc[h] = term if acc[h] is None else acc[h] + term
            for h in range(height):
                cq[h, q, :, at] = acc[h]
            return carry

        return lax.fori_loop(0, stride, column, carry)

    lax.fori_loop(0, lanes // LANES, group, 0)


def norm(cq, cvec, xp, flat, skip=0):
    padded, stride, blocks, lanes = cq.shape
    height = padded - 2 * skip
    channels = flat.shape[1]
    width = stride * blocks
    groups = lanes // LANES
    inside = lax.broadcasted_iota(jnp.int32, (blocks, lanes), 1) < channels

    def rows(n, carry):
        for k in range(NORM_ROWS):
            h = NORM_ROWS * n + k
            for q in range(stride):
                v = cq[h + skip, q]
                mean = jnp.sum(v, axis=-1, keepdims=True) * (1.0 / channels)
                c = jnp.where(inside, v - mean, 0.0)
                var = jnp.sum(c * c, axis=-1, keepdims=True) * (1.0 / channels)
                c = c * lax.rsqrt(var + EPS_NORM) * cvec[1:2, :] + cvec[2:3, :]
                for g in range(groups):
                    at = slice(g * LANES, (g + 1) * LANES)
                    xp[k * groups + g, pl.ds(q, blocks, stride=stride), :] = c[:, at]
            at_cell = pl.ds(pl.multiple_of(h * width, width), width)
            for g in range(groups):
                at = slice(g * LANES, min((g + 1) * LANES, channels))
                flat[at_cell, at] = xp[k * groups + g, 0:width, 0 : at.stop - at.start].astype(
                    jnp.bfloat16
                )
        return carry

    lax.fori_loop(0, height // NORM_ROWS, rows, 0)


def conv_norm(x, taps, cvec, flat, xp, xs, cq):
    fill_columns(xp, xs, x, x.shape[2])
    conv(xs, taps, cvec, cq)
    norm(cq, cvec, xp, flat)


def conv_scratch(rows, out_rows, width, lanes):
    return [
        pltpu.VMEM((NORM_ROWS * lanes // LANES, width + 16, LANES), jnp.float32),
        pltpu.VMEM((rows, width // 8 + 2 * REACH, 8, lanes), jnp.float32),
        pltpu.VMEM((out_rows, width // 8, 8, lanes), jnp.float32),
    ]


def gelu(v):
    return 0.5 * v * (1.0 + lax.erf(v * (0.5**0.5)))


def up(flat, w_in, bias, act, ssq):
    cells = flat.shape[0]
    half = w_in.shape[1]
    step = 2 * LANES

    def units(start, count):
        raised = jnp.dot(
            flat[...], w_in[:, pl.ds(start, count)], preferred_element_type=jnp.float32
        )
        active = gelu(raised + bias[0:1, pl.ds(start, count)]).astype(jnp.bfloat16)
        act[:, pl.ds(start, count)] = active
        wide = active.astype(jnp.float32)
        ssq[:, pl.ds(start, count)] = jnp.sum((wide * wide).reshape(cells // 8, 8, count), axis=0)

    def full(n, carry):
        units(pl.multiple_of(n * step, step), step)
        return carry

    whole = half // step
    lax.fori_loop(0, whole, full, 0)
    if half % step:
        units(whole * step, half % step)


def norm_scale(ssqs, fvec, scale):
    half = fvec.shape[2]
    magnitude = [jnp.sqrt(jnp.sum(ssq[...], axis=0, keepdims=True)) for ssq in ssqs]
    mean = jnp.sum(magnitude[0] + magnitude[1], axis=1, keepdims=True) * (0.5 / half)
    for which in range(2):
        ratio = magnitude[which] / (mean + EPS_GRN)
        scale[which] = fvec[which, 1:2, :] * ratio + 1.0


def down(x_rows, first_row, acts, outs, scale, fvec, cvec):
    _, width, channels = x_rows.shape
    cells = CHUNK * width
    at = pl.ds(pl.multiple_of(first_row * width, cells), cells)
    update = cvec[3:4, 0:channels]
    for which in range(2):
        a = acts[which][at, :].astype(jnp.float32)
        hidden = (a * scale[which] + fvec[which, 2:3, :]).astype(jnp.bfloat16)
        update = update + jnp.dot(hidden, outs[which][...], preferred_element_type=jnp.float32)
    return (x_rows.astype(jnp.float32) + update.reshape(CHUNK, width, channels)).astype(
        jnp.bfloat16
    )


def down_all(x, acts, outs, scale, fvec, cvec, out):
    def rows(n, carry):
        at = pl.ds(n * CHUNK, CHUNK)
        out[at] = down(x[at], n * CHUNK, acts, outs, scale, fvec, cvec)
        return carry

    lax.fori_loop(0, x.shape[0] // CHUNK, rows, 0)


def prepare_kernel(part, kernel, *refs):
    vectors, (taps, cvec, fvec), (held, *staged), sems = refs[:7], refs[7:10], refs[10:-1], refs[-1]
    moves = [(kernel, held), *zip(vectors, staged)]
    copies = [pltpu.make_async_copy(a, b, sems.at[n]) for n, (a, b) in enumerate(moves)]
    for copy in copies:
        copy.start()
    taps[...] = jnp.zeros(taps.shape, jnp.float32)
    cvec[...] = jnp.zeros(cvec.shape, jnp.float32)
    for copy in copies:
        copy.wait()
    channels = kernel.shape[3]
    span = kernel.shape[1]
    half = fvec.shape[2]
    for i in range(span):
        taps[i * span : (i + 1) * span, 0:channels] = held[0, i].astype(jnp.float32)
    for n in range(4):
        cvec[n : n + 1, 0:channels] = staged[n][...].astype(jnp.float32)
    first = part[0] == 0
    for n in range(3):
        v = staged[4 + n][...].astype(jnp.float32)
        low, high = v[:, 0:half], v[:, half:]
        fvec[0, n : n + 1, :] = jnp.where(first, low, high)
        fvec[1, n : n + 1, :] = jnp.where(first, high, low)


def piece_kernel(section, piece, taps, cvec, part, xp, xs, *, tick):
    @pl.when(jnp.logical_or(tick == 0, section[0] == tick))
    def _():
        fill_columns(xp, xs, piece, piece.shape[2])
        conv(xs, taps, cvec, part)


def last_piece_kernel(section, index, *refs, count, tick):
    pieces, parts = refs[:count], refs[count : 2 * count - 1]
    taps, cvec, x, flat, xp, xs, own, cq = refs[2 * count - 1 :]
    rows = pieces[0].shape[0]

    @pl.when(jnp.logical_or(tick == 0, section[0] == tick))
    def _():
        cq[...] = jnp.broadcast_to(cvec[0:1, :].reshape(1, 1, 1, cq.shape[3]), cq.shape)
        fill_columns(xp, xs, pieces[-1], x.shape[2])
        conv(xs, taps, cvec, own)
        for n, (piece, part) in enumerate(zip(pieces, (*parts, own))):
            at = index[n] * rows
            x[pl.ds(at, rows)] = piece[...]
            cq[pl.ds(at, rows + 2 * REACH)] += part[...]
        norm(cq, cvec, xp, flat, REACH)


def conv_kernel(section, x, taps, cvec, flat, xp, xs, cq, *, tick):
    @pl.when(section[0] == tick)
    def _():
        conv_norm(x, taps, cvec, flat, xp, xs, cq)


def up_first_kernel(section, flat, w_in, fvec, act, ssq, *, tick):
    @pl.when(section[0] == tick)
    def _():
        up(flat, w_in, fvec.at[0], act, ssq)


def up_second_kernel(section, flat, w_in, fvec, other, act, scale, ssq, *, tick):
    @pl.when(section[0] == tick)
    def _():
        up(flat, w_in, fvec.at[1], act, ssq)
        norm_scale((other, ssq), fvec, scale)


def first_down_kernel(section, x, act_a, act_b, out_a, out_b, scale, fvec, cvec, out):
    @pl.when(section[0] == 0)
    def _():
        down_all(x, (act_a, act_b), (out_a, out_b), scale, fvec, cvec, out)


def down_piece_kernel(
    section, index, x, act_a, act_b, out_a, out_b, scale, fvec, cvec, prev, out, *, tick, n
):
    first_row = index[n] * CHUNK
    at = pl.ds(first_row, CHUNK)

    @pl.when(section[0] == tick)
    def _():
        out[...] = down(x[at], first_row, (act_a, act_b), (out_a, out_b), scale, fvec, cvec)

    @pl.when(section[0] != tick)
    def _():
        out[...] = prev[at]


def mlp_kernel(section, x, flat, in_a, in_b, out_a, out_b, fvec, cvec, *refs, tick):
    *pieces, prev, out, act_a, act_b, ssq_a, ssq_b, scale = refs

    @pl.when(section[0] == tick)
    def _():
        up(flat, in_a, fvec.at[0], act_a, ssq_a)
        up(flat, in_b, fvec.at[1], act_b, ssq_b)
        norm_scale((ssq_a, ssq_b), fvec, scale)
        down_all(x, (act_a, act_b), (out_a, out_b), scale, fvec, cvec, out)

    @pl.when(section[0] == tick - 1)
    def _():
        for n, piece in enumerate(pieces):
            out[n * CHUNK : (n + 1) * CHUNK] = piece[...]

    @pl.when(section[0] < tick - 1)
    def _():
        out[...] = prev[...]


def conv_up_kernel(section, x, taps, cvec, in_a, in_b, fvec, *refs, tick):
    act_a, act_b, scale, xp, xs, cq, flat, ssq_a, ssq_b = refs

    @pl.when(section[0] == tick)
    def _():
        conv_norm(x, taps, cvec, flat, xp, xs, cq)
        up(flat, in_a, fvec.at[0], act_a, ssq_a)
        up(flat, in_b, fvec.at[1], act_b, ssq_b)
        norm_scale((ssq_a, ssq_b), fvec, scale)


def place_kernel(index, *refs):
    *pieces, saved, sems = refs
    copies = [
        pltpu.make_async_copy(piece, saved.at[0, index[n], 0], sems.at[n])
        for n, piece in enumerate(pieces)
    ]
    for copy in copies:
        copy.start()
    for copy in copies:
        copy.wait()


SMEM = pl.BlockSpec(memory_space=pltpu.SMEM)
VMEM = pl.BlockSpec(memory_space=pltpu.VMEM)
HBM = pl.BlockSpec(memory_space=pltpu.HBM)


def call(kernel, name, args, out, specs=None, out_specs=None, scratch=(), flops=0, **static):
    if specs is None:
        specs = [SMEM if a.dtype == jnp.int32 else VMEM for a in args]
    if out_specs is None:
        out_specs = jax.tree.map(lambda _: VMEM, out)
    moved = sum(a.size * a.dtype.itemsize for a in args)
    return pl.pallas_call(
        functools.partial(kernel, **static),
        out_shape=out,
        in_specs=specs,
        out_specs=out_specs,
        scratch_shapes=list(scratch),
        compiler_params=pltpu.CompilerParams(vmem_limit_bytes=VMEM_BYTES),
        cost_estimate=pl.CostEstimate(flops=flops, bytes_accessed=moved, transcendentals=0),
        name=name,
    )(*args)


def shape(*dims, dtype=jnp.float32):
    return jax.ShapeDtypeStruct(dims, dtype)


def ssq_scratch(half):
    return pltpu.VMEM((8, half), jnp.float32)


def image_plan(
    inputs,
    depth_kernel,
    depth_bias,
    norm_gain,
    norm_bias,
    proj_in,
    bias_in,
    grn_gamma,
    grn_beta,
    proj_out,
    bias_out,
):
    sections = lax.axis_size("section")
    count = lax.axis_size("row")
    me = lax.axis_index("row").astype(jnp.int32)
    section = lax.axis_index("section").astype(jnp.int32).reshape(1)
    part = lax.axis_index("dp").astype(jnp.int32).reshape(1)
    _, _, rows, width, channels = inputs.shape
    height = rows * count
    cells = height * width
    lanes = -(-channels // LANES) * LANES
    half = proj_in.shape[2]
    span = depth_kernel.shape[1]
    order = (0, 2, 3, 1)
    index = jnp.stack([me ^ by for by in order])
    in_order = jnp.arange(count, dtype=jnp.int32)
    bf16 = jnp.bfloat16
    whole = shape(height, width, channels, dtype=bf16)
    flat_shape = shape(cells, channels, dtype=bf16)
    piece_shape = shape(rows, width, channels, dtype=bf16)
    act_shape = shape(cells, half, dtype=bf16)
    scale_shape = shape(2, 1, half)
    matmul = 2 * cells * channels * half

    pieces = []
    for by in order:
        piece = lax.dynamic_index_in_dim(inputs, me ^ by, 0, keepdims=False)[0]
        if by:
            pairs = [(count + (p ^ by), p) for p in range(count)]
            piece = lax.ppermute(piece, ("section", "row"), pairs)
        pieces.append(piece)

    def other_half(x, which):
        pairs = [(2 * s + p, 2 * s + 1 - p) for s in which for p in range(2)]
        return lax.ppermute(x, ("section", "dp"), pairs)

    w_in, w_out = proj_in[0], proj_out[0]
    even = range(0, sections, 2)
    odd = range(1, sections, 2)
    other_in = other_half(w_in, even)
    other_out = other_half(w_out, even)

    held = (
        depth_kernel, depth_bias, norm_gain, norm_bias, bias_out, bias_in, grn_gamma, grn_beta
    )
    taps, cvec, fvec = call(
        prepare_kernel,
        "prepare",
        (part, *held),
        (shape(span * span, lanes), shape(4, lanes), shape(2, 3, half)),
        specs=[SMEM] + [HBM] * len(held),
        scratch=[pltpu.VMEM(v.shape, v.dtype) for v in held]
        + [pltpu.SemaphoreType.DMA((len(held),))],
    )

    def conv_pieces(pieces, at, tick):
        out_rows = rows + 2 * REACH
        scratch = conv_scratch(rows, out_rows, width, lanes)
        parts = []
        for piece in pieces[:-1]:
            if parts:
                piece, parts[-1] = lax.optimization_barrier((piece, parts[-1]))
            part = call(
                piece_kernel,
                "conv_piece",
                (section, piece, taps, cvec),
                shape(out_rows, width // 8, 8, lanes),
                scratch=scratch[:2],
                tick=tick,
            )
            parts.append(part)
        return call(
            last_piece_kernel,
            "last_piece",
            (section, at, *pieces, *parts, taps, cvec),
            (whole, flat_shape),
            scratch=scratch + [conv_scratch(1, height + 2 * REACH, width, lanes)[2]],
            count=count,
            tick=tick,
        )

    def up_halves(flat, other_in, tick):
        act_a, ssq = call(
            up_first_kernel,
            "up_own",
            (section, flat, w_in, fvec),
            (act_shape, shape(8, half)),
            flops=matmul,
            tick=tick,
        )
        act_b, scale = call(
            up_second_kernel,
            "up_other",
            (section, flat, other_in, fvec, ssq),
            (act_shape, scale_shape),
            scratch=[ssq_scratch(half)],
            flops=matmul,
            tick=tick,
        )
        return act_a, act_b, scale

    def down_piece(x, acts, other_out, prev, at, tick, n):
        act_a, act_b, scale = acts
        return call(
            down_piece_kernel,
            "down_piece",
            (section, at, x, act_a, act_b, w_out, other_out, scale, fvec, cvec, prev),
            piece_shape,
            flops=2 * matmul // count,
            tick=tick,
            n=n,
        )

    def pass_on(x, tick):
        return lax.ppermute(x, "section", [(tick - 1, tick)])

    x, flat = conv_pieces(pieces, index, 0)
    act_a, act_b, scale = up_halves(flat, other_in, 0)
    result = call(
        first_down_kernel,
        "down",
        (section, x, act_a, act_b, w_out, other_out, scale, fvec, cvec),
        whole,
        flops=2 * matmul,
    )
    x = pass_on(result, 1)
    late_in, late_out, result = lax.optimization_barrier((w_in, w_out, result))
    odd_in = other_half(late_in, odd)
    odd_out = other_half(late_out, odd)
    flat = call(
        conv_kernel,
        "conv",
        (section, x, taps, cvec),
        flat_shape,
        scratch=conv_scratch(height, height, width, lanes),
        tick=1,
    )
    acts = up_halves(flat, odd_in, 1)
    kept = [down_piece(x, acts, odd_out, result, in_order, 1, n) for n in range(count)]
    x, flat = conv_pieces([pass_on(piece, 2) for piece in kept], in_order, 2)
    result = call(
        mlp_kernel,
        "mlp",
        (section, x, flat, w_in, other_in, w_out, other_out, fvec, cvec, *kept, result),
        whole,
        scratch=[pltpu.VMEM((cells, half), bf16)] * 2
        + [ssq_scratch(half)] * 2
        + [pltpu.VMEM((2, 1, half), jnp.float32)],
        flops=4 * matmul,
        tick=2,
    )
    x = pass_on(result, 3)
    acts = call(
        conv_up_kernel,
        "conv_up",
        (section, x, taps, cvec, w_in, odd_in, fvec),
        (act_shape, act_shape, scale_shape),
        scratch=conv_scratch(height, height, width, lanes)
        + [pltpu.VMEM((cells, channels), bf16)]
        + [ssq_scratch(half)] * 2,
        flops=2 * matmul,
        tick=3,
    )
    done = []
    for n in (1, 2, 3, 0):
        piece = down_piece(x, acts, odd_out, result, index, 3, n)
        if n:
            piece = lax.ppermute(piece, "row", [(p, p ^ order[n]) for p in range(count)])
        done.append(piece)
    return call(
        place_kernel,
        "place",
        (index, done[3], *done[:3]),
        shape(1, count, 1, rows, width, channels, dtype=bf16),
        out_specs=HBM,
        scratch=[pltpu.SemaphoreType.DMA((count,))],
    )


def extended(cells, sides, width):
    for axis, dim in sides:
        count = lax.axis_size(axis)
        ends = count - 1
        head = lax.slice_in_dim(cells, 0, width, axis=dim)
        tail = lax.slice_in_dim(cells, cells.shape[dim] - width, cells.shape[dim], axis=dim)
        cells = jnp.concatenate(
            [
                lax.ppermute(tail, axis, [(i, (i + 1) % count) for i in range(ends)]),
                cells,
                lax.ppermute(head, axis, [((i + 1) % count, i) for i in range(ends)]),
            ],
            axis=dim,
        )
    return cells


def depthwise(padded, kernel, bias_term):
    channels = padded.shape[-1]
    conv_out = lax.conv_general_dilated(
        padded.astype(jnp.float32),
        kernel.astype(jnp.float32)[:, :, None, :],
        (1, 1),
        "VALID",
        dimension_numbers=("NHWC", "HWIO", "NHWC"),
        feature_group_count=channels,
        precision=lax.Precision.HIGHEST,
    )
    return conv_out + bias_term.astype(jnp.float32)


def conv_block(current, params):
    (
        depth_kernel,
        depth_bias,
        norm_gain,
        norm_bias,
        proj_in,
        bias_in,
        grn_gamma,
        grn_beta,
        proj_out,
        bias_out,
    ) = params
    num_items, num_rows, num_cols, channels = current.shape
    padded = extended(current, (("row", 1),), REACH)
    padded = jnp.pad(padded, ((0, 0), (0, 0), (REACH, REACH), (0, 0)))
    conv_out = depthwise(padded, depth_kernel, depth_bias)
    center = conv_out - jnp.mean(conv_out, axis=-1, keepdims=True)
    spread = jnp.mean(center * center, axis=-1, keepdims=True)
    normed = (
        center * lax.rsqrt(spread + EPS_NORM) * norm_gain.astype(jnp.float32)
        + norm_bias.astype(jnp.float32)
    ).astype(jnp.bfloat16)
    flat_rows = normed.reshape(num_items * num_rows * num_cols, channels)
    raised = jnp.dot(flat_rows, proj_in, preferred_element_type=jnp.float32) + bias_in.astype(
        jnp.float32
    )
    active = jax.nn.gelu(raised, approximate=False).astype(jnp.bfloat16)
    grouped = active.reshape(num_items, num_rows * num_cols, -1).astype(jnp.float32)
    local_sq = jnp.sum(grouped * grouped, axis=1)
    total_sq = lax.psum(local_sq, "row")
    magnitude = jnp.sqrt(total_sq)
    grn_ratio = magnitude / (jnp.mean(magnitude, axis=-1, keepdims=True) + EPS_GRN)
    hidden = (
        grn_gamma.astype(jnp.float32) * grouped * grn_ratio[:, None, :]
        + grn_beta.astype(jnp.float32)
        + grouped
    ).astype(jnp.bfloat16)
    update = jnp.dot(
        hidden.reshape(num_items * num_rows * num_cols, -1),
        proj_out,
        preferred_element_type=jnp.float32,
    ) + bias_out.astype(jnp.float32)
    return (
        current.astype(jnp.float32) + update.reshape(num_items, num_rows, num_cols, channels)
    ).astype(jnp.bfloat16)


def rows_plan(inputs, *weights):
    (
        depth_kernel,
        depth_bias,
        norm_gain,
        norm_bias,
        proj_in,
        bias_in,
        grn_gamma,
        grn_beta,
        proj_out,
        bias_out,
    ) = weights
    proj_in = lax.all_gather(proj_in, "dp", axis=2, tiled=True)
    proj_out = lax.all_gather(proj_out, "dp", axis=1, tiled=True)
    own_params = tuple(
        w[0]
        for w in (
            depth_kernel,
            depth_bias,
            norm_gain,
            norm_bias,
            proj_in,
            bias_in,
            grn_gamma,
            grn_beta,
            proj_out,
            bias_out,
        )
    )
    sections = lax.axis_size("section")
    section_index = lax.axis_index("section")
    num_micro = inputs.shape[0]
    num_ticks = num_micro + sections - 1
    arriving = jnp.zeros_like(inputs[0])
    saved = jnp.zeros_like(inputs)
    for tick_index in range(num_ticks):
        fresh_input = inputs[min(tick_index, num_micro - 1)]
        current = jnp.where(section_index == 0, fresh_input, arriving)
        produced = conv_block(current, own_params)
        slot_index = tick_index - section_index
        is_valid = jnp.logical_and(slot_index >= 0, slot_index < num_micro)
        safe_slot = jnp.clip(slot_index, 0, num_micro - 1)
        previous = lax.dynamic_index_in_dim(saved, safe_slot, 0, keepdims=False)
        saved = lax.dynamic_update_index_in_dim(
            saved, jnp.where(is_valid, produced, previous), safe_slot, 0
        )
        if tick_index + 1 < num_ticks:
            arriving = lax.ppermute(
                produced, "section", [(i, i + 1) for i in range(sections - 1)]
            )
    return saved[None]


def on_device(inputs, *weights):
    num_micro, images, local_rows, width, _ = inputs.shape
    one_image_each = (
        images == 1
        and lax.axis_size("row") == num_micro == 4
        and lax.axis_size("dp") == 2
        and lax.axis_size("section") == 4
        and local_rows % 4 == 0
        and width % 16 == 0
    )
    plan = image_plan if one_image_each else rows_plan
    return plan(inputs, *weights)


def solution(mesh):
    return jax.shard_map(
        on_device,
        mesh=mesh,
        in_specs=(
            P(None, "dp", "row", None, None),
            P("section", None, None, None),
            P("section", None),
            P("section", None),
            P("section", None),
            P("section", None, "dp"),
            P("section", None),
            P("section", None),
            P("section", None),
            P("section", "dp", None),
            P("section", None),
        ),
        out_specs=P("section", None, "dp", "row", None, None),
        check_vma=False,
    )
```

```python
import functools

import jax
import jax.numpy as jnp
from jax import lax
from jax.experimental import pallas as pl
from jax.experimental.pallas import tpu as pltpu
from jax.sharding import PartitionSpec as P

EPS_NORM = 1e-06
EPS_GRN = 1e-06
LANES = 128
VMEM_BYTES = 20 * 1024 * 1024
REACH = 3
CHUNK = 4
NORM_ROWS = 4
IN_ORDER = (0, 1, 2, 3)
VECTORS = 56


def fill_columns(xp, xs, x, channels):
    height, reach_cols, blocks, lanes = xs.shape
    stride = reach_cols - 2 * REACH
    width = stride * blocks
    groups = lanes // LANES
    xp[...] = jnp.zeros(xp.shape, jnp.float32)

    def rows(n, carry):
        for k in range(2):
            r = 2 * n + k
            row = x[r].astype(jnp.float32)
            for g in range(groups):
                at = slice(g * LANES, (g + 1) * LANES)
                own = row[:, g * LANES : min((g + 1) * LANES, channels)]
                xp[k * groups + g, 8 : 8 + width, 0 : own.shape[1]] = own
                for q in range(reach_cols):
                    near = pl.ds(8 - REACH + q, blocks, stride=stride)
                    xs[r, q, :, at] = xp[k * groups + g, near, :]
        return carry

    lax.fori_loop(0, height // 2, rows, 0)


def conv(xs, cpar, cq):
    rows = xs.shape[0]
    height, stride, blocks, lanes = cq.shape
    span = 2 * REACH + 1
    above = (height - rows) // 2

    def group(g, carry):
        at = pl.ds(pl.multiple_of(g * LANES, LANES), LANES)

        def column(q, carry):
            bias = jnp.broadcast_to(cpar[VECTORS : VECTORS + 1, at], (blocks, LANES))
            acc = [None if above else bias] * height
            for j in range(span):
                kern = [
                    jnp.broadcast_to(cpar[i * span + j : i * span + j + 1, at], (blocks, LANES))
                    for i in range(span)
                ]
                for r in range(rows):
                    x_row = xs[r, q + j, :, at]
                    for i in range(span):
                        h = r + above + REACH - i
                        if 0 <= h < height:
                            term = kern[i] * x_row
                            acc[h] = term if acc[h] is None else acc[h] + term
            for h in range(height):
                cq[h, q, :, at] = acc[h]
            return carry

        return lax.fori_loop(0, stride, column, carry)

    lax.fori_loop(0, lanes // LANES, group, 0)


def norm(cq, cpar, xp, flat, skip=0):
    padded, stride, blocks, lanes = cq.shape
    height = padded - 2 * skip
    gain = cpar[VECTORS + 1 : VECTORS + 2, :]
    shift = cpar[VECTORS + 2 : VECTORS + 3, :]
    channels = flat.shape[2]
    width = stride * blocks
    groups = lanes // LANES
    inside = lax.broadcasted_iota(jnp.int32, (blocks, lanes), 1) < channels

    def rows(n, carry):
        for k in range(NORM_ROWS):
            h = NORM_ROWS * n + k
            for q in range(stride):
                v = cq[h + skip, q]
                mean = jnp.sum(v, axis=-1, keepdims=True) * (1.0 / channels)
                c = jnp.where(inside, v - mean, 0.0)
                var = jnp.sum(c * c, axis=-1, keepdims=True) * (1.0 / channels)
                c = c * lax.rsqrt(var + EPS_NORM) * gain + shift
                for g in range(groups):
                    at = slice(g * LANES, (g + 1) * LANES)
                    xp[k * groups + g, pl.ds(q, blocks, stride=stride), :] = c[:, at]
            for g in range(groups):
                at = slice(g * LANES, min((g + 1) * LANES, channels))
                flat[h, :, at] = xp[k * groups + g, 0:width, 0 : at.stop - at.start].astype(
                    jnp.bfloat16
                )
        return carry

    lax.fori_loop(0, height // NORM_ROWS, rows, 0)


def conv_norm(x, cpar, flat, xp, xs, cq):
    fill_columns(xp, xs, x, x.shape[2])
    conv(xs, cpar, cq)
    norm(cq, cpar, xp, flat)


def conv_scratch(rows, out_rows, width, lanes):
    return [
        pltpu.VMEM((NORM_ROWS * lanes // LANES, width + 16, LANES), jnp.float32),
        pltpu.VMEM((rows, width // 8 + 2 * REACH, 8, lanes), jnp.float32),
        pltpu.VMEM((out_rows, width // 8, 8, lanes), jnp.float32),
    ]


def gelu(v):
    return 0.5 * v * (1.0 + lax.erf(v * (0.5**0.5)))


def up(flat, w_in, bias, act, ssq):
    height, width, channels = flat.shape
    cells = height * width
    half = w_in.shape[1]
    step = 2 * LANES

    def units(start, count):
        raised = jnp.dot(
            flat[...].reshape(cells, channels),
            w_in[:, pl.ds(start, count)],
            preferred_element_type=jnp.float32,
        )
        active = gelu(raised + bias[0:1, pl.ds(start, count)]).astype(jnp.bfloat16)
        act[:, pl.ds(start, count)] = active
        wide = active.astype(jnp.float32)
        ssq[:, pl.ds(start, count)] = jnp.sum((wide * wide).reshape(cells // 8, 8, count), axis=0)

    def full(n, carry):
        units(pl.multiple_of(n * step, step), step)
        return carry

    whole = half // step
    lax.fori_loop(0, whole, full, 0)
    if half % step:
        units(whole * step, half % step)


def norm_scale(ssqs, fvec, scale):
    half = fvec.shape[2]
    magnitude = [jnp.sqrt(jnp.sum(ssq[...], axis=0, keepdims=True)) for ssq in ssqs]
    mean = jnp.sum(magnitude[0] + magnitude[1], axis=1, keepdims=True) * (0.5 / half)
    for which in range(2):
        ratio = magnitude[which] / (mean + EPS_GRN)
        scale[which] = fvec[which, 1:2, :] * ratio + 1.0


def down(x_rows, first_row, acts, outs, scale, fvec, cpar):
    _, width, channels = x_rows.shape
    cells = CHUNK * width
    at = pl.ds(pl.multiple_of(first_row * width, cells), cells)
    update = cpar[VECTORS + 3 : VECTORS + 4, 0:channels]
    for which in range(2):
        a = acts[which][at, :].astype(jnp.float32)
        hidden = (a * scale[which] + fvec[which, 2:3, :]).astype(jnp.bfloat16)
        update = update + jnp.dot(hidden, outs[which][...], preferred_element_type=jnp.float32)
    return (x_rows.astype(jnp.float32) + update.reshape(CHUNK, width, channels)).astype(
        jnp.bfloat16
    )


def down_all(x, acts, outs, scale, fvec, cvec, out):
    def rows(n, carry):
        at = pl.ds(n * CHUNK, CHUNK)
        out[at] = down(x[at], n * CHUNK, acts, outs, scale, fvec, cvec)
        return carry

    lax.fori_loop(0, x.shape[0] // CHUNK, rows, 0)


def prepare_kernel(part, kernel, *refs):
    vectors, (cpar, fvec), (held, *staged), sems = refs[:7], refs[7:9], refs[9:-1], refs[-1]
    moves = [(kernel, held), *zip(vectors, staged)]
    copies = [pltpu.make_async_copy(a, b, sems.at[n]) for n, (a, b) in enumerate(moves)]
    for copy in copies:
        copy.start()
    cpar[...] = jnp.zeros(cpar.shape, jnp.float32)
    for copy in copies:
        copy.wait()
    channels = kernel.shape[3]
    span = kernel.shape[1]
    half = fvec.shape[2]
    for i in range(span):
        cpar[i * span : (i + 1) * span, 0:channels] = held[0, i].astype(jnp.float32)
    for n in range(4):
        cpar[VECTORS + n : VECTORS + n + 1, 0:channels] = staged[n][...].astype(jnp.float32)
    first = part[0] == 0
    for n in range(3):
        v = staged[4 + n][...].astype(jnp.float32)
        low, high = v[:, 0:half], v[:, half:]
        fvec[0, n : n + 1, :] = jnp.where(first, low, high)
        fvec[1, n : n + 1, :] = jnp.where(first, high, low)


def block_of(me, order, n):
    return n if order is None else me[0] ^ order[n]


def piece_kernel(section, piece, cpar, part, xp, xs, *, on):
    @pl.when(section[0] == on)
    def _():
        fill_columns(xp, xs, piece, piece.shape[2])
        conv(xs, cpar, part)


def last_piece_kernel(section, me, *refs, order, on):
    count = len(order or IN_ORDER)
    pieces, parts = refs[:count], refs[count : 2 * count - 1]
    cpar, x, flat, xp, xs, own, cq = refs[2 * count - 1 :]
    rows = pieces[0].shape[0]

    @pl.when(section[0] == on)
    def _():
        bias = cpar[VECTORS : VECTORS + 1, :].reshape(1, 1, 1, cq.shape[3])
        cq[...] = jnp.broadcast_to(bias, cq.shape)
        fill_columns(xp, xs, pieces[-1], x.shape[2])
        conv(xs, cpar, own)
        for n, (piece, part) in enumerate(zip(pieces, (*parts, own))):
            at = block_of(me, order, n) * rows
            x[pl.ds(at, rows)] = piece[...]
            cq[pl.ds(at, rows + 2 * REACH)] += part[...]
        norm(cq, cpar, xp, flat, REACH)


def conv_kernel(section, x, cpar, flat, xp, xs, cq, *, tick):
    @pl.when(section[0] == tick)
    def _():
        conv_norm(x, cpar, flat, xp, xs, cq)


def up_first_kernel(section, flat, w_in, fvec, act, ssq, *, tick):
    @pl.when(section[0] == tick)
    def _():
        up(flat, w_in, fvec.at[0], act, ssq)


def up_second_kernel(section, flat, w_in, fvec, other, act, scale, ssq, *, tick):
    @pl.when(section[0] == tick)
    def _():
        up(flat, w_in, fvec.at[1], act, ssq)
        norm_scale((other, ssq), fvec, scale)


def first_down_kernel(section, x, act_a, act_b, out_a, out_b, scale, fvec, cpar, out):
    @pl.when(section[0] == 0)
    def _():
        down_all(x, (act_a, act_b), (out_a, out_b), scale, fvec, cpar, out)


def down_piece_kernel(
    section, me, x, act_a, act_b, out_a, out_b, scale, fvec, cpar, prev, out, *, order, tick, n
):
    first_row = block_of(me, order, n) * CHUNK
    at = pl.ds(first_row, CHUNK)

    @pl.when(section[0] == tick)
    def _():
        out[...] = down(x[at], first_row, (act_a, act_b), (out_a, out_b), scale, fvec, cpar)

    @pl.when(section[0] != tick)
    def _():
        out[...] = prev[at]


def mlp_kernel(section, x, flat, in_a, in_b, out_a, out_b, fvec, cpar, *refs, tick):
    *pieces, prev, out, act_a, act_b, ssq_a, ssq_b, scale = refs

    @pl.when(section[0] == tick)
    def _():
        up(flat, in_a, fvec.at[0], act_a, ssq_a)
        up(flat, in_b, fvec.at[1], act_b, ssq_b)
        norm_scale((ssq_a, ssq_b), fvec, scale)
        down_all(x, (act_a, act_b), (out_a, out_b), scale, fvec, cpar, out)

    @pl.when(section[0] == tick - 1)
    def _():
        for n, piece in enumerate(pieces):
            out[n * CHUNK : (n + 1) * CHUNK] = piece[...]

    @pl.when(section[0] < tick - 1)
    def _():
        out[...] = prev[...]


def conv_up_kernel(section, x, cpar, in_a, in_b, fvec, *refs, tick):
    act_a, act_b, scale, xp, xs, cq, flat, ssq_a, ssq_b = refs

    @pl.when(section[0] == tick)
    def _():
        conv_norm(x, cpar, flat, xp, xs, cq)
        up(flat, in_a, fvec.at[0], act_a, ssq_a)
        up(flat, in_b, fvec.at[1], act_b, ssq_b)
        norm_scale((ssq_a, ssq_b), fvec, scale)


def place_kernel(me, *refs, order):
    *pieces, saved, sems = refs
    copies = [
        pltpu.make_async_copy(piece, saved.at[0, block_of(me, order, n), 0], sems.at[n])
        for n, piece in enumerate(pieces)
    ]
    for copy in copies:
        copy.start()
    for copy in copies:
        copy.wait()


SMEM = pl.BlockSpec(memory_space=pltpu.SMEM)
VMEM = pl.BlockSpec(memory_space=pltpu.VMEM)
HBM = pl.BlockSpec(memory_space=pltpu.HBM)


def call(kernel, name, args, out, specs=None, out_specs=None, scratch=(), flops=0, **static):
    if specs is None:
        specs = [SMEM if a.dtype == jnp.int32 else VMEM for a in args]
    if out_specs is None:
        out_specs = jax.tree.map(lambda _: VMEM, out)
    moved = sum(a.size * a.dtype.itemsize for a in args)
    return pl.pallas_call(
        functools.partial(kernel, **static),
        out_shape=out,
        in_specs=specs,
        out_specs=out_specs,
        scratch_shapes=list(scratch),
        compiler_params=pltpu.CompilerParams(vmem_limit_bytes=VMEM_BYTES),
        cost_estimate=pl.CostEstimate(flops=flops, bytes_accessed=moved, transcendentals=0),
        name=name,
    )(*args)


def shape(*dims, dtype=jnp.float32):
    return jax.ShapeDtypeStruct(dims, dtype)


def ssq_scratch(half):
    return pltpu.VMEM((8, half), jnp.float32)


def image_plan(
    inputs,
    depth_kernel,
    depth_bias,
    norm_gain,
    norm_bias,
    proj_in,
    bias_in,
    grn_gamma,
    grn_beta,
    proj_out,
    bias_out,
):
    sections = lax.axis_size("section")
    count = lax.axis_size("row")
    me = lax.axis_index("row").astype(jnp.int32)
    section = lax.axis_index("section").astype(jnp.int32).reshape(1)
    me_ref = me.reshape(1)
    part = lax.axis_index("dp").astype(jnp.int32).reshape(1)
    _, _, rows, width, channels = inputs.shape
    height = rows * count
    cells = height * width
    lanes = -(-channels // LANES) * LANES
    half = proj_in.shape[2]
    span = depth_kernel.shape[1]
    order = (0, 2, 3, 1)
    bf16 = jnp.bfloat16
    whole = shape(height, width, channels, dtype=bf16)
    piece_shape = shape(rows, width, channels, dtype=bf16)
    act_shape = shape(cells, half, dtype=bf16)
    scale_shape = shape(2, 1, half)
    matmul = 2 * cells * channels * half

    helper, source = 1, sections - 1
    pieces = []
    for by in order:
        piece = lax.dynamic_index_in_dim(inputs, me ^ by, 0, keepdims=False)[0]
        if by:
            pairs = [(source * count + (p ^ by), helper * count + p) for p in range(count)]
            piece = lax.ppermute(piece, ("section", "row"), pairs)
        pieces.append(piece)

    def other_half(x, which):
        pairs = [(2 * s + p, 2 * s + 1 - p) for s in which for p in range(2)]
        return lax.ppermute(x, ("section", "dp"), pairs)

    w_in, w_out = proj_in[0], proj_out[0]
    even = range(0, sections, 2)
    odd = range(1, sections, 2)
    other_in = other_half(w_in, even)
    other_out = other_half(w_out, even)

    held = (
        depth_kernel, depth_bias, norm_gain, norm_bias, bias_out, bias_in, grn_gamma, grn_beta
    )
    cpar, fvec = call(
        prepare_kernel,
        "prepare",
        (part, *held),
        (shape(VECTORS + 8, lanes), shape(2, 3, half)),
        specs=[SMEM] + [HBM] * len(held),
        scratch=[pltpu.VMEM(v.shape, v.dtype) for v in held]
        + [pltpu.SemaphoreType.DMA((len(held),))],
    )

    def send(x, start, end):
        return lax.ppermute(x, "section", [(start, end)])

    def conv_pieces(pieces, cpar, order, on):
        out_rows = rows + 2 * REACH
        scratch = conv_scratch(rows, out_rows, width, lanes)
        parts = []
        for piece in pieces[:-1]:
            if parts:
                piece, parts[-1] = lax.optimization_barrier((piece, parts[-1]))
            part = call(
                piece_kernel,
                "conv_piece",
                (section, piece, cpar),
                shape(out_rows, width // 8, 8, lanes),
                scratch=scratch[:2],
                on=on,
            )
            parts.append(part)
        return call(
            last_piece_kernel,
            "last_piece",
            (section, me_ref, *pieces, *parts, cpar),
            (whole, whole),
            scratch=scratch + [conv_scratch(1, height + 2 * REACH, width, lanes)[2]],
            order=order,
            on=on,
        )

    def up_own(flat, tick):
        return call(
            up_first_kernel,
            "up_own",
            (section, flat, w_in, fvec),
            (act_shape, shape(8, half)),
            flops=matmul,
            tick=tick,
        )

    def up_other(flat, other_in, ssq, tick):
        return call(
            up_second_kernel,
            "up_other",
            (section, flat, other_in, fvec, ssq),
            (act_shape, scale_shape),
            scratch=[ssq_scratch(half)],
            flops=matmul,
            tick=tick,
        )

    def down_piece(x, acts, other_out, prev, order, tick, n):
        act_a, act_b, scale = acts
        return call(
            down_piece_kernel,
            "down_piece",
            (section, me_ref, x, act_a, act_b, w_out, other_out, scale, fvec, cpar, prev),
            piece_shape,
            flops=2 * matmul // count,
            order=order,
            tick=tick,
            n=n,
        )

    x, flat = conv_pieces(pieces, send(cpar, 0, helper), order, helper)
    flat, other_in = lax.optimization_barrier((flat, other_in))
    flat = send(flat, helper, 0)
    act_a, ssq = up_own(flat, 0)
    x, other_out, act_a = lax.optimization_barrier((x, other_out, act_a))
    x = send(x, helper, 0)
    act_b, scale = up_other(flat, other_in, ssq, 0)
    result = call(
        first_down_kernel,
        "down",
        (section, x, act_a, act_b, w_out, other_out, scale, fvec, cpar),
        whole,
        flops=2 * matmul,
    )
    x = send(result, 0, 1)
    late_in, late_out, result = lax.optimization_barrier((w_in, w_out, result))
    odd_in = other_half(late_in, odd)
    odd_out = other_half(late_out, odd)
    flat = call(
        conv_kernel,
        "conv",
        (section, x, cpar),
        whole,
        scratch=conv_scratch(height, height, width, lanes),
        tick=1,
    )
    act_a, ssq = up_own(flat, 1)
    acts = (act_a, *up_other(flat, odd_in, ssq, 1))
    kept = [down_piece(x, acts, odd_out, result, None, 1, n) for n in range(count)]
    x, flat = conv_pieces([send(piece, 1, 2) for piece in kept], cpar, None, 2)
    result = call(
        mlp_kernel,
        "mlp",
        (section, x, flat, w_in, other_in, w_out, other_out, fvec, cpar, *kept, result),
        whole,
        scratch=[pltpu.VMEM((cells, half), bf16)] * 2
        + [ssq_scratch(half)] * 2
        + [pltpu.VMEM((2, 1, half), jnp.float32)],
        flops=4 * matmul,
        tick=2,
    )
    x = send(result, 2, 3)
    acts = call(
        conv_up_kernel,
        "conv_up",
        (section, x, cpar, w_in, odd_in, fvec),
        (act_shape, act_shape, scale_shape),
        scratch=conv_scratch(height, height, width, lanes)
        + [pltpu.VMEM((height, width, channels), bf16)]
        + [ssq_scratch(half)] * 2,
        flops=2 * matmul,
        tick=3,
    )
    done = []
    for n in (1, 2, 3, 0):
        piece = down_piece(x, acts, odd_out, result, order, 3, n)
        if n:
            piece = lax.ppermute(piece, "row", [(p, p ^ order[n]) for p in range(count)])
        done.append(piece)
    return call(
        place_kernel,
        "place",
        (me_ref, done[3], *done[:3]),
        shape(1, count, 1, rows, width, channels, dtype=bf16),
        out_specs=HBM,
        scratch=[pltpu.SemaphoreType.DMA((count,))],
        order=order,
    )


def extended(cells, sides, width):
    for axis, dim in sides:
        count = lax.axis_size(axis)
        ends = count - 1
        head = lax.slice_in_dim(cells, 0, width, axis=dim)
        tail = lax.slice_in_dim(cells, cells.shape[dim] - width, cells.shape[dim], axis=dim)
        cells = jnp.concatenate(
            [
                lax.ppermute(tail, axis, [(i, (i + 1) % count) for i in range(ends)]),
                cells,
                lax.ppermute(head, axis, [((i + 1) % count, i) for i in range(ends)]),
            ],
            axis=dim,
        )
    return cells


def depthwise(padded, kernel, bias_term):
    channels = padded.shape[-1]
    conv_out = lax.conv_general_dilated(
        padded.astype(jnp.float32),
        kernel.astype(jnp.float32)[:, :, None, :],
        (1, 1),
        "VALID",
        dimension_numbers=("NHWC", "HWIO", "NHWC"),
        feature_group_count=channels,
        precision=lax.Precision.HIGHEST,
    )
    return conv_out + bias_term.astype(jnp.float32)


def conv_block(current, params):
    (
        depth_kernel,
        depth_bias,
        norm_gain,
        norm_bias,
        proj_in,
        bias_in,
        grn_gamma,
        grn_beta,
        proj_out,
        bias_out,
    ) = params
    num_items, num_rows, num_cols, channels = current.shape
    padded = extended(current, (("row", 1),), REACH)
    padded = jnp.pad(padded, ((0, 0), (0, 0), (REACH, REACH), (0, 0)))
    conv_out = depthwise(padded, depth_kernel, depth_bias)
    center = conv_out - jnp.mean(conv_out, axis=-1, keepdims=True)
    spread = jnp.mean(center * center, axis=-1, keepdims=True)
    normed = (
        center * lax.rsqrt(spread + EPS_NORM) * norm_gain.astype(jnp.float32)
        + norm_bias.astype(jnp.float32)
    ).astype(jnp.bfloat16)
    flat_rows = normed.reshape(num_items * num_rows * num_cols, channels)
    raised = jnp.dot(flat_rows, proj_in, preferred_element_type=jnp.float32) + bias_in.astype(
        jnp.float32
    )
    active = jax.nn.gelu(raised, approximate=False).astype(jnp.bfloat16)
    grouped = active.reshape(num_items, num_rows * num_cols, -1).astype(jnp.float32)
    local_sq = jnp.sum(grouped * grouped, axis=1)
    total_sq = lax.psum(local_sq, "row")
    magnitude = jnp.sqrt(total_sq)
    grn_ratio = magnitude / (jnp.mean(magnitude, axis=-1, keepdims=True) + EPS_GRN)
    hidden = (
        grn_gamma.astype(jnp.float32) * grouped * grn_ratio[:, None, :]
        + grn_beta.astype(jnp.float32)
        + grouped
    ).astype(jnp.bfloat16)
    update = jnp.dot(
        hidden.reshape(num_items * num_rows * num_cols, -1),
        proj_out,
        preferred_element_type=jnp.float32,
    ) + bias_out.astype(jnp.float32)
    return (
        current.astype(jnp.float32) + update.reshape(num_items, num_rows, num_cols, channels)
    ).astype(jnp.bfloat16)


def rows_plan(inputs, *weights):
    (
        depth_kernel,
        depth_bias,
        norm_gain,
        norm_bias,
        proj_in,
        bias_in,
        grn_gamma,
        grn_beta,
        proj_out,
        bias_out,
    ) = weights
    proj_in = lax.all_gather(proj_in, "dp", axis=2, tiled=True)
    proj_out = lax.all_gather(proj_out, "dp", axis=1, tiled=True)
    own_params = tuple(
        w[0]
        for w in (
            depth_kernel,
            depth_bias,
            norm_gain,
            norm_bias,
            proj_in,
            bias_in,
            grn_gamma,
            grn_beta,
            proj_out,
            bias_out,
        )
    )
    sections = lax.axis_size("section")
    section_index = lax.axis_index("section")
    num_micro = inputs.shape[0]
    num_ticks = num_micro + sections - 1
    arriving = jnp.zeros_like(inputs[0])
    saved = jnp.zeros_like(inputs)
    for tick_index in range(num_ticks):
        fresh_input = inputs[min(tick_index, num_micro - 1)]
        current = jnp.where(section_index == 0, fresh_input, arriving)
        produced = conv_block(current, own_params)
        slot_index = tick_index - section_index
        is_valid = jnp.logical_and(slot_index >= 0, slot_index < num_micro)
        safe_slot = jnp.clip(slot_index, 0, num_micro - 1)
        previous = lax.dynamic_index_in_dim(saved, safe_slot, 0, keepdims=False)
        saved = lax.dynamic_update_index_in_dim(
            saved, jnp.where(is_valid, produced, previous), safe_slot, 0
        )
        if tick_index + 1 < num_ticks:
            arriving = lax.ppermute(
                produced, "section", [(i, i + 1) for i in range(sections - 1)]
            )
    return saved[None]


def on_device(inputs, *weights):
    num_micro, images, local_rows, width, _ = inputs.shape
    one_image_each = (
        images == 1
        and lax.axis_size("row") == num_micro == 4
        and lax.axis_size("dp") == 2
        and lax.axis_size("section") == 4
        and local_rows % 4 == 0
        and width % 16 == 0
    )
    plan = image_plan if one_image_each else rows_plan
    return plan(inputs, *weights)


def solution(mesh):
    return jax.shard_map(
        on_device,
        mesh=mesh,
        in_specs=(
            P(None, "dp", "row", None, None),
            P("section", None, None, None),
            P("section", None),
            P("section", None),
            P("section", None),
            P("section", None, "dp"),
            P("section", None),
            P("section", None),
            P("section", None),
            P("section", "dp", None),
            P("section", None),
        ),
        out_specs=P("section", None, "dp", "row", None, None),
        check_vma=False,
    )
```

```python
import functools

import jax
import jax.numpy as jnp
from jax import lax
from jax.experimental import pallas as pl
from jax.experimental.pallas import tpu as pltpu
from jax.sharding import PartitionSpec as P

EPS_NORM = 1e-06
EPS_GRN = 1e-06
LANES = 128
VMEM_BYTES = 20 * 1024 * 1024
REACH = 3
CHUNK = 4
NORM_ROWS = 4
IN_ORDER = (0, 1, 2, 3)
VECTORS = 56


def fill_columns(xp, xs, x, channels):
    height, reach_cols, blocks, lanes = xs.shape
    stride = reach_cols - 2 * REACH
    width = stride * blocks
    groups = lanes // LANES
    xp[...] = jnp.zeros(xp.shape, jnp.float32)

    def rows(n, carry):
        for k in range(2):
            r = 2 * n + k
            row = x[r].astype(jnp.float32)
            for g in range(groups):
                at = slice(g * LANES, (g + 1) * LANES)
                own = row[:, g * LANES : min((g + 1) * LANES, channels)]
                xp[k * groups + g, 8 : 8 + width, 0 : own.shape[1]] = own
                for q in range(reach_cols):
                    near = pl.ds(8 - REACH + q, blocks, stride=stride)
                    xs[r, q, :, at] = xp[k * groups + g, near, :]
        return carry

    lax.fori_loop(0, height // 2, rows, 0)


def conv(xs, cpar, cq):
    rows = xs.shape[0]
    height, stride, blocks, lanes = cq.shape
    span = 2 * REACH + 1
    above = (height - rows) // 2

    def group(g, carry):
        at = pl.ds(pl.multiple_of(g * LANES, LANES), LANES)

        def column(q, carry):
            bias = jnp.broadcast_to(cpar[VECTORS : VECTORS + 1, at], (blocks, LANES))
            acc = [None if above else bias] * height
            for j in range(span):
                kern = [
                    jnp.broadcast_to(cpar[i * span + j : i * span + j + 1, at], (blocks, LANES))
                    for i in range(span)
                ]
                for r in range(rows):
                    x_row = xs[r, q + j, :, at]
                    for i in range(span):
                        h = r + above + REACH - i
                        if 0 <= h < height:
                            term = kern[i] * x_row
                            acc[h] = term if acc[h] is None else acc[h] + term
            for h in range(height):
                cq[h, q, :, at] = acc[h]
            return carry

        return lax.fori_loop(0, stride, column, carry)

    lax.fori_loop(0, lanes // LANES, group, 0)


def norm(cq, cpar, xp, flat, skip=0):
    padded, stride, blocks, lanes = cq.shape
    height = padded - 2 * skip
    gain = cpar[VECTORS + 1 : VECTORS + 2, :]
    shift = cpar[VECTORS + 2 : VECTORS + 3, :]
    channels = flat.shape[2]
    width = stride * blocks
    groups = lanes // LANES
    inside = lax.broadcasted_iota(jnp.int32, (blocks, lanes), 1) < channels

    def rows(n, carry):
        for k in range(NORM_ROWS):
            h = NORM_ROWS * n + k
            for q in range(stride):
                v = cq[h + skip, q]
                mean = jnp.sum(v, axis=-1, keepdims=True) * (1.0 / channels)
                c = jnp.where(inside, v - mean, 0.0)
                var = jnp.sum(c * c, axis=-1, keepdims=True) * (1.0 / channels)
                c = c * lax.rsqrt(var + EPS_NORM) * gain + shift
                for g in range(groups):
                    at = slice(g * LANES, (g + 1) * LANES)
                    xp[k * groups + g, pl.ds(q, blocks, stride=stride), :] = c[:, at]
            for g in range(groups):
                at = slice(g * LANES, min((g + 1) * LANES, channels))
                flat[h, :, at] = xp[k * groups + g, 0:width, 0 : at.stop - at.start].astype(
                    jnp.bfloat16
                )
        return carry

    lax.fori_loop(0, height // NORM_ROWS, rows, 0)


def conv_norm(x, cpar, flat, xp, xs, cq):
    fill_columns(xp, xs, x, x.shape[2])
    conv(xs, cpar, cq)
    norm(cq, cpar, xp, flat)


def conv_scratch(rows, out_rows, width, lanes):
    return [
        pltpu.VMEM((NORM_ROWS * lanes // LANES, width + 16, LANES), jnp.float32),
        pltpu.VMEM((rows, width // 8 + 2 * REACH, 8, lanes), jnp.float32),
        pltpu.VMEM((out_rows, width // 8, 8, lanes), jnp.float32),
    ]


def gelu(v):
    return 0.5 * v * (1.0 + lax.erf(v * (0.5**0.5)))


def up(flat, w_in, bias, act, ssq):
    height, width, channels = flat.shape
    cells = height * width
    half = w_in.shape[1]
    step = 2 * LANES

    def units(start, count):
        raised = jnp.dot(
            flat[...].reshape(cells, channels),
            w_in[:, pl.ds(start, count)],
            preferred_element_type=jnp.float32,
        )
        active = gelu(raised + bias[0:1, pl.ds(start, count)]).astype(jnp.bfloat16)
        act[:, pl.ds(start, count)] = active
        wide = active.astype(jnp.float32)
        ssq[:, pl.ds(start, count)] = jnp.sum((wide * wide).reshape(cells // 8, 8, count), axis=0)

    def full(n, carry):
        units(pl.multiple_of(n * step, step), step)
        return carry

    whole = half // step
    lax.fori_loop(0, whole, full, 0)
    if half % step:
        units(whole * step, half % step)


def norm_scale(ssqs, fvec, scale):
    half = fvec.shape[2]
    magnitude = [jnp.sqrt(jnp.sum(ssq[...], axis=0, keepdims=True)) for ssq in ssqs]
    mean = jnp.sum(magnitude[0] + magnitude[1], axis=1, keepdims=True) * (0.5 / half)
    for which in range(2):
        ratio = magnitude[which] / (mean + EPS_GRN)
        scale[which] = fvec[which, 1:2, :] * ratio + 1.0


def down(x_rows, first_row, acts, outs, scale, fvec, cpar):
    _, width, channels = x_rows.shape
    cells = CHUNK * width
    at = pl.ds(pl.multiple_of(first_row * width, cells), cells)
    update = cpar[VECTORS + 3 : VECTORS + 4, 0:channels]
    for which in range(2):
        a = acts[which][at, :].astype(jnp.float32)
        hidden = (a * scale[which] + fvec[which, 2:3, :]).astype(jnp.bfloat16)
        update = update + jnp.dot(hidden, outs[which][...], preferred_element_type=jnp.float32)
    return (x_rows.astype(jnp.float32) + update.reshape(CHUNK, width, channels)).astype(
        jnp.bfloat16
    )


def down_all(x, acts, outs, scale, fvec, cvec, out):
    def rows(n, carry):
        at = pl.ds(n * CHUNK, CHUNK)
        out[at] = down(x[at], n * CHUNK, acts, outs, scale, fvec, cvec)
        return carry

    lax.fori_loop(0, x.shape[0] // CHUNK, rows, 0)


def prepare_kernel(part, kernel, *refs):
    vectors, (cpar, fvec), (held, *staged), sems = refs[:7], refs[7:9], refs[9:-1], refs[-1]
    moves = [(kernel, held), *zip(vectors, staged)]
    copies = [pltpu.make_async_copy(a, b, sems.at[n]) for n, (a, b) in enumerate(moves)]
    for copy in copies:
        copy.start()
    cpar[...] = jnp.zeros(cpar.shape, jnp.float32)
    for copy in copies:
        copy.wait()
    channels = kernel.shape[3]
    span = kernel.shape[1]
    half = fvec.shape[2]
    for i in range(span):
        cpar[i * span : (i + 1) * span, 0:channels] = held[0, i].astype(jnp.float32)
    for n in range(4):
        cpar[VECTORS + n : VECTORS + n + 1, 0:channels] = staged[n][...].astype(jnp.float32)
    first = part[0] == 0
    for n in range(3):
        v = staged[4 + n][...].astype(jnp.float32)
        low, high = v[:, 0:half], v[:, half:]
        fvec[0, n : n + 1, :] = jnp.where(first, low, high)
        fvec[1, n : n + 1, :] = jnp.where(first, high, low)


def block_of(me, order, n):
    return n if order is None else me[0] ^ order[n]


def piece_kernel(section, piece, cpar, part, xp, xs, *, on):
    @pl.when(section[0] == on)
    def _():
        fill_columns(xp, xs, piece, piece.shape[2])
        conv(xs, cpar, part)


def last_piece_kernel(section, me, *refs, order, on):
    count = len(order or IN_ORDER)
    pieces, parts = refs[:count], refs[count : 2 * count - 1]
    cpar, x, flat, xp, xs, own, cq = refs[2 * count - 1 :]
    rows = pieces[0].shape[0]

    @pl.when(section[0] == on)
    def _():
        bias = cpar[VECTORS : VECTORS + 1, :].reshape(1, 1, 1, cq.shape[3])
        cq[...] = jnp.broadcast_to(bias, cq.shape)
        fill_columns(xp, xs, pieces[-1], x.shape[2])
        conv(xs, cpar, own)
        for n, (piece, part) in enumerate(zip(pieces, (*parts, own))):
            at = block_of(me, order, n) * rows
            x[pl.ds(at, rows)] = piece[...]
            cq[pl.ds(at, rows + 2 * REACH)] += part[...]
        norm(cq, cpar, xp, flat, REACH)


def conv_kernel(section, x, cpar, flat, xp, xs, cq, *, tick):
    @pl.when(section[0] == tick)
    def _():
        conv_norm(x, cpar, flat, xp, xs, cq)


def up_first_kernel(section, flat, w_in, fvec, act, ssq, *, tick):
    @pl.when(section[0] == tick)
    def _():
        up(flat, w_in, fvec.at[0], act, ssq)


def up_second_kernel(section, flat, w_in, fvec, other, act, scale, ssq, *, tick):
    @pl.when(section[0] == tick)
    def _():
        up(flat, w_in, fvec.at[1], act, ssq)
        norm_scale((other, ssq), fvec, scale)


def first_down_kernel(section, x, act_a, act_b, out_a, out_b, scale, fvec, cpar, out):
    @pl.when(section[0] == 0)
    def _():
        down_all(x, (act_a, act_b), (out_a, out_b), scale, fvec, cpar, out)


def down_piece_kernel(
    section, me, x, act_a, act_b, out_a, out_b, scale, fvec, cpar, prev, out, *, order, tick, n
):
    first_row = block_of(me, order, n) * CHUNK
    at = pl.ds(first_row, CHUNK)

    @pl.when(section[0] == tick)
    def _():
        out[...] = down(x[at], first_row, (act_a, act_b), (out_a, out_b), scale, fvec, cpar)

    @pl.when(section[0] != tick)
    def _():
        out[...] = prev[at]


def mlp_kernel(section, x, flat, in_a, in_b, out_a, out_b, fvec, cpar, *refs, tick):
    *pieces, prev, out, act_a, act_b, ssq_a, ssq_b, scale = refs

    @pl.when(section[0] == tick)
    def _():
        up(flat, in_a, fvec.at[0], act_a, ssq_a)
        up(flat, in_b, fvec.at[1], act_b, ssq_b)
        norm_scale((ssq_a, ssq_b), fvec, scale)
        down_all(x, (act_a, act_b), (out_a, out_b), scale, fvec, cpar, out)

    @pl.when(section[0] == tick - 1)
    def _():
        for n, piece in enumerate(pieces):
            out[n * CHUNK : (n + 1) * CHUNK] = piece[...]

    @pl.when(section[0] < tick - 1)
    def _():
        out[...] = prev[...]


def conv_up_kernel(section, x, cpar, in_a, in_b, fvec, *refs, tick):
    act_a, act_b, scale, xp, xs, cq, flat, ssq_a, ssq_b = refs

    @pl.when(section[0] == tick)
    def _():
        conv_norm(x, cpar, flat, xp, xs, cq)
        up(flat, in_a, fvec.at[0], act_a, ssq_a)
        up(flat, in_b, fvec.at[1], act_b, ssq_b)
        norm_scale((ssq_a, ssq_b), fvec, scale)


def place_kernel(me, *refs, order):
    *pieces, saved, sems = refs
    copies = [
        pltpu.make_async_copy(piece, saved.at[0, block_of(me, order, n), 0], sems.at[n])
        for n, piece in enumerate(pieces)
    ]
    for copy in copies:
        copy.start()
    for copy in copies:
        copy.wait()


SMEM = pl.BlockSpec(memory_space=pltpu.SMEM)
VMEM = pl.BlockSpec(memory_space=pltpu.VMEM)
HBM = pl.BlockSpec(memory_space=pltpu.HBM)


def call(kernel, name, args, out, specs=None, out_specs=None, scratch=(), flops=0, **static):
    if specs is None:
        specs = [SMEM if a.dtype == jnp.int32 else VMEM for a in args]
    if out_specs is None:
        out_specs = jax.tree.map(lambda _: VMEM, out)
    moved = sum(a.size * a.dtype.itemsize for a in args)
    return pl.pallas_call(
        functools.partial(kernel, **static),
        out_shape=out,
        in_specs=specs,
        out_specs=out_specs,
        scratch_shapes=list(scratch),
        compiler_params=pltpu.CompilerParams(vmem_limit_bytes=VMEM_BYTES),
        cost_estimate=pl.CostEstimate(flops=flops, bytes_accessed=moved, transcendentals=0),
        name=name,
    )(*args)


def shape(*dims, dtype=jnp.float32):
    return jax.ShapeDtypeStruct(dims, dtype)


def ssq_scratch(half):
    return pltpu.VMEM((8, half), jnp.float32)


def image_plan(
    inputs,
    depth_kernel,
    depth_bias,
    norm_gain,
    norm_bias,
    proj_in,
    bias_in,
    grn_gamma,
    grn_beta,
    proj_out,
    bias_out,
):
    sections = lax.axis_size("section")
    count = lax.axis_size("row")
    me = lax.axis_index("row").astype(jnp.int32)
    section = lax.axis_index("section").astype(jnp.int32).reshape(1)
    me_ref = me.reshape(1)
    part = lax.axis_index("dp").astype(jnp.int32).reshape(1)
    _, _, rows, width, channels = inputs.shape
    height = rows * count
    cells = height * width
    lanes = -(-channels // LANES) * LANES
    half = proj_in.shape[2]
    span = depth_kernel.shape[1]
    order = (0, 2, 3, 1)
    bf16 = jnp.bfloat16
    whole = shape(height, width, channels, dtype=bf16)
    piece_shape = shape(rows, width, channels, dtype=bf16)
    act_shape = shape(cells, half, dtype=bf16)
    scale_shape = shape(2, 1, half)
    matmul = 2 * cells * channels * half

    helper, source = 1, sections - 1
    pieces = []
    for by in order:
        piece = lax.dynamic_index_in_dim(inputs, me ^ by, 0, keepdims=False)[0]
        if by:
            pairs = [(source * count + (p ^ by), helper * count + p) for p in range(count)]
            piece = lax.ppermute(piece, ("section", "row"), pairs)
        pieces.append(piece)

    def other_half(x, which):
        pairs = [(2 * s + p, 2 * s + 1 - p) for s in which for p in range(2)]
        return lax.ppermute(x, ("section", "dp"), pairs)

    w_in, w_out = proj_in[0], proj_out[0]
    even = range(0, sections, 2)
    odd = range(1, sections, 2)
    other_in = other_half(w_in, even)
    other_out = other_half(w_out, even)

    held = (
        depth_kernel, depth_bias, norm_gain, norm_bias, bias_out, bias_in, grn_gamma, grn_beta
    )
    cpar, fvec = call(
        prepare_kernel,
        "prepare",
        (part, *held),
        (shape(VECTORS + 8, lanes), shape(2, 3, half)),
        specs=[SMEM] + [HBM] * len(held),
        scratch=[pltpu.VMEM(v.shape, v.dtype) for v in held]
        + [pltpu.SemaphoreType.DMA((len(held),))],
    )

    def send(x, start, end):
        return lax.ppermute(x, "section", [(start, end)])

    def conv_pieces(pieces, cpar, order, on):
        out_rows = rows + 2 * REACH
        scratch = conv_scratch(rows, out_rows, width, lanes)
        parts = []
        for piece in pieces[:-1]:
            if parts:
                piece, parts[-1] = lax.optimization_barrier((piece, parts[-1]))
            part = call(
                piece_kernel,
                "conv_piece",
                (section, piece, cpar),
                shape(out_rows, width // 8, 8, lanes),
                scratch=scratch[:2],
                on=on,
            )
            parts.append(part)
        return call(
            last_piece_kernel,
            "last_piece",
            (section, me_ref, *pieces, *parts, cpar),
            (whole, whole),
            scratch=scratch + [conv_scratch(1, height + 2 * REACH, width, lanes)[2]],
            order=order,
            on=on,
        )

    def up_own(flat, tick):
        return call(
            up_first_kernel,
            "up_own",
            (section, flat, w_in, fvec),
            (act_shape, shape(8, half)),
            flops=matmul,
            tick=tick,
        )

    def up_other(flat, other_in, ssq, tick):
        return call(
            up_second_kernel,
            "up_other",
            (section, flat, other_in, fvec, ssq),
            (act_shape, scale_shape),
            scratch=[ssq_scratch(half)],
            flops=matmul,
            tick=tick,
        )

    def down_piece(x, acts, other_out, prev, order, tick, n):
        act_a, act_b, scale = acts
        return call(
            down_piece_kernel,
            "down_piece",
            (section, me_ref, x, act_a, act_b, w_out, other_out, scale, fvec, cpar, prev),
            piece_shape,
            flops=2 * matmul // count,
            order=order,
            tick=tick,
            n=n,
        )

    x, flat = conv_pieces(pieces, send(cpar, 0, helper), order, helper)
    flat, other_in = lax.optimization_barrier((flat, other_in))
    flat = send(flat, helper, 0)
    x, other_out = lax.optimization_barrier((x, other_out))
    x = send(x, helper, 0)
    act_a, ssq = up_own(flat, 0)
    act_b, scale = up_other(flat, other_in, ssq, 0)
    result = call(
        first_down_kernel,
        "down",
        (section, x, act_a, act_b, w_out, other_out, scale, fvec, cpar),
        whole,
        flops=2 * matmul,
    )
    x = send(result, 0, 1)
    late_in, late_out, result = lax.optimization_barrier((w_in, w_out, result))
    odd_in = other_half(late_in, odd)
    odd_out = other_half(late_out, odd)
    flat = call(
        conv_kernel,
        "conv",
        (section, x, cpar),
        whole,
        scratch=conv_scratch(height, height, width, lanes),
        tick=1,
    )
    act_a, ssq = up_own(flat, 1)
    acts = (act_a, *up_other(flat, odd_in, ssq, 1))
    kept = [down_piece(x, acts, odd_out, result, None, 1, n) for n in range(count)]
    x, flat = conv_pieces([send(piece, 1, 2) for piece in kept], cpar, None, 2)
    result = call(
        mlp_kernel,
        "mlp",
        (section, x, flat, w_in, other_in, w_out, other_out, fvec, cpar, *kept, result),
        whole,
        scratch=[pltpu.VMEM((cells, half), bf16)] * 2
        + [ssq_scratch(half)] * 2
        + [pltpu.VMEM((2, 1, half), jnp.float32)],
        flops=4 * matmul,
        tick=2,
    )
    x = send(result, 2, 3)
    acts = call(
        conv_up_kernel,
        "conv_up",
        (section, x, cpar, w_in, odd_in, fvec),
        (act_shape, act_shape, scale_shape),
        scratch=conv_scratch(height, height, width, lanes)
        + [pltpu.VMEM((height, width, channels), bf16)]
        + [ssq_scratch(half)] * 2,
        flops=2 * matmul,
        tick=3,
    )
    done = []
    for n in (1, 2, 3, 0):
        piece = down_piece(x, acts, odd_out, result, order, 3, n)
        if n:
            piece = lax.ppermute(piece, "row", [(p, p ^ order[n]) for p in range(count)])
        done.append(piece)
    return call(
        place_kernel,
        "place",
        (me_ref, done[3], *done[:3]),
        shape(1, count, 1, rows, width, channels, dtype=bf16),
        out_specs=HBM,
        scratch=[pltpu.SemaphoreType.DMA((count,))],
        order=order,
    )


def extended(cells, sides, width):
    for axis, dim in sides:
        count = lax.axis_size(axis)
        ends = count - 1
        head = lax.slice_in_dim(cells, 0, width, axis=dim)
        tail = lax.slice_in_dim(cells, cells.shape[dim] - width, cells.shape[dim], axis=dim)
        cells = jnp.concatenate(
            [
                lax.ppermute(tail, axis, [(i, (i + 1) % count) for i in range(ends)]),
                cells,
                lax.ppermute(head, axis, [((i + 1) % count, i) for i in range(ends)]),
            ],
            axis=dim,
        )
    return cells


def depthwise(padded, kernel, bias_term):
    channels = padded.shape[-1]
    conv_out = lax.conv_general_dilated(
        padded.astype(jnp.float32),
        kernel.astype(jnp.float32)[:, :, None, :],
        (1, 1),
        "VALID",
        dimension_numbers=("NHWC", "HWIO", "NHWC"),
        feature_group_count=channels,
        precision=lax.Precision.HIGHEST,
    )
    return conv_out + bias_term.astype(jnp.float32)


def conv_block(current, params):
    (
        depth_kernel,
        depth_bias,
        norm_gain,
        norm_bias,
        proj_in,
        bias_in,
        grn_gamma,
        grn_beta,
        proj_out,
        bias_out,
    ) = params
    num_items, num_rows, num_cols, channels = current.shape
    padded = extended(current, (("row", 1),), REACH)
    padded = jnp.pad(padded, ((0, 0), (0, 0), (REACH, REACH), (0, 0)))
    conv_out = depthwise(padded, depth_kernel, depth_bias)
    center = conv_out - jnp.mean(conv_out, axis=-1, keepdims=True)
    spread = jnp.mean(center * center, axis=-1, keepdims=True)
    normed = (
        center * lax.rsqrt(spread + EPS_NORM) * norm_gain.astype(jnp.float32)
        + norm_bias.astype(jnp.float32)
    ).astype(jnp.bfloat16)
    flat_rows = normed.reshape(num_items * num_rows * num_cols, channels)
    raised = jnp.dot(flat_rows, proj_in, preferred_element_type=jnp.float32) + bias_in.astype(
        jnp.float32
    )
    active = jax.nn.gelu(raised, approximate=False).astype(jnp.bfloat16)
    grouped = active.reshape(num_items, num_rows * num_cols, -1).astype(jnp.float32)
    local_sq = jnp.sum(grouped * grouped, axis=1)
    total_sq = lax.psum(local_sq, "row")
    magnitude = jnp.sqrt(total_sq)
    grn_ratio = magnitude / (jnp.mean(magnitude, axis=-1, keepdims=True) + EPS_GRN)
    hidden = (
        grn_gamma.astype(jnp.float32) * grouped * grn_ratio[:, None, :]
        + grn_beta.astype(jnp.float32)
        + grouped
    ).astype(jnp.bfloat16)
    update = jnp.dot(
        hidden.reshape(num_items * num_rows * num_cols, -1),
        proj_out,
        preferred_element_type=jnp.float32,
    ) + bias_out.astype(jnp.float32)
    return (
        current.astype(jnp.float32) + update.reshape(num_items, num_rows, num_cols, channels)
    ).astype(jnp.bfloat16)


def rows_plan(inputs, *weights):
    (
        depth_kernel,
        depth_bias,
        norm_gain,
        norm_bias,
        proj_in,
        bias_in,
        grn_gamma,
        grn_beta,
        proj_out,
        bias_out,
    ) = weights
    proj_in = lax.all_gather(proj_in, "dp", axis=2, tiled=True)
    proj_out = lax.all_gather(proj_out, "dp", axis=1, tiled=True)
    own_params = tuple(
        w[0]
        for w in (
            depth_kernel,
            depth_bias,
            norm_gain,
            norm_bias,
            proj_in,
            bias_in,
            grn_gamma,
            grn_beta,
            proj_out,
            bias_out,
        )
    )
    sections = lax.axis_size("section")
    section_index = lax.axis_index("section")
    num_micro = inputs.shape[0]
    num_ticks = num_micro + sections - 1
    arriving = jnp.zeros_like(inputs[0])
    saved = jnp.zeros_like(inputs)
    for tick_index in range(num_ticks):
        fresh_input = inputs[min(tick_index, num_micro - 1)]
        current = jnp.where(section_index == 0, fresh_input, arriving)
        produced = conv_block(current, own_params)
        slot_index = tick_index - section_index
        is_valid = jnp.logical_and(slot_index >= 0, slot_index < num_micro)
        safe_slot = jnp.clip(slot_index, 0, num_micro - 1)
        previous = lax.dynamic_index_in_dim(saved, safe_slot, 0, keepdims=False)
        saved = lax.dynamic_update_index_in_dim(
            saved, jnp.where(is_valid, produced, previous), safe_slot, 0
        )
        if tick_index + 1 < num_ticks:
            arriving = lax.ppermute(
                produced, "section", [(i, i + 1) for i in range(sections - 1)]
            )
    return saved[None]


def on_device(inputs, *weights):
    num_micro, images, local_rows, width, _ = inputs.shape
    one_image_each = (
        images == 1
        and lax.axis_size("row") == num_micro == 4
        and lax.axis_size("dp") == 2
        and lax.axis_size("section") == 4
        and local_rows % 4 == 0
        and width % 16 == 0
    )
    plan = image_plan if one_image_each else rows_plan
    return plan(inputs, *weights)


def solution(mesh):
    return jax.shard_map(
        on_device,
        mesh=mesh,
        in_specs=(
            P(None, "dp", "row", None, None),
            P("section", None, None, None),
            P("section", None),
            P("section", None),
            P("section", None),
            P("section", None, "dp"),
            P("section", None),
            P("section", None),
            P("section", None),
            P("section", "dp", None),
            P("section", None),
        ),
        out_specs=P("section", None, "dp", "row", None, None),
        check_vma=False,
    )
```

```python
import functools

import jax
import jax.numpy as jnp
from jax import lax
from jax.experimental import pallas as pl
from jax.experimental.pallas import tpu as pltpu
from jax.sharding import PartitionSpec as P

EPS_NORM = 1e-06
EPS_GRN = 1e-06
LANES = 128
VMEM_BYTES = 20 * 1024 * 1024
REACH = 3
CHUNK = 4
NORM_ROWS = 4
IN_ORDER = (0, 1, 2, 3)
VECTORS = 56


def fill_columns(xp, xs, x, channels):
    height, reach_cols, blocks, lanes = xs.shape
    stride = reach_cols - 2 * REACH
    width = stride * blocks
    groups = lanes // LANES
    xp[...] = jnp.zeros(xp.shape, jnp.float32)

    def rows(n, carry):
        for k in range(2):
            r = 2 * n + k
            row = x[r].astype(jnp.float32)
            for g in range(groups):
                at = slice(g * LANES, (g + 1) * LANES)
                own = row[:, g * LANES : min((g + 1) * LANES, channels)]
                xp[k * groups + g, 8 : 8 + width, 0 : own.shape[1]] = own
                for q in range(reach_cols):
                    near = pl.ds(8 - REACH + q, blocks, stride=stride)
                    xs[r, q, :, at] = xp[k * groups + g, near, :]
        return carry

    lax.fori_loop(0, height // 2, rows, 0)


def conv(xs, cpar, cq):
    rows = xs.shape[0]
    height, stride, blocks, lanes = cq.shape
    span = 2 * REACH + 1
    above = (height - rows) // 2

    def group(g, carry):
        at = pl.ds(pl.multiple_of(g * LANES, LANES), LANES)

        def column(q, carry):
            bias = jnp.broadcast_to(cpar[VECTORS : VECTORS + 1, at], (blocks, LANES))
            acc = [None if above else bias] * height
            for j in range(span):
                kern = [
                    jnp.broadcast_to(cpar[i * span + j : i * span + j + 1, at], (blocks, LANES))
                    for i in range(span)
                ]
                for r in range(rows):
                    x_row = xs[r, q + j, :, at]
                    for i in range(span):
                        h = r + above + REACH - i
                        if 0 <= h < height:
                            term = kern[i] * x_row
                            acc[h] = term if acc[h] is None else acc[h] + term
            for h in range(height):
                cq[h, q, :, at] = acc[h]
            return carry

        return lax.fori_loop(0, stride, column, carry)

    lax.fori_loop(0, lanes // LANES, group, 0)


def norm(cq, cpar, xp, flat, skip=0):
    padded, stride, blocks, lanes = cq.shape
    height = padded - 2 * skip
    gain = cpar[VECTORS + 1 : VECTORS + 2, :]
    shift = cpar[VECTORS + 2 : VECTORS + 3, :]
    channels = flat.shape[2]
    width = stride * blocks
    groups = lanes // LANES
    inside = lax.broadcasted_iota(jnp.int32, (blocks, lanes), 1) < channels

    def rows(n, carry):
        for k in range(NORM_ROWS):
            h = NORM_ROWS * n + k
            for q in range(stride):
                v = cq[h + skip, q]
                mean = jnp.sum(v, axis=-1, keepdims=True) * (1.0 / channels)
                c = jnp.where(inside, v - mean, 0.0)
                var = jnp.sum(c * c, axis=-1, keepdims=True) * (1.0 / channels)
                c = c * lax.rsqrt(var + EPS_NORM) * gain + shift
                for g in range(groups):
                    at = slice(g * LANES, (g + 1) * LANES)
                    xp[k * groups + g, pl.ds(q, blocks, stride=stride), :] = c[:, at]
            for g in range(groups):
                at = slice(g * LANES, min((g + 1) * LANES, channels))
                flat[h, :, at] = xp[k * groups + g, 0:width, 0 : at.stop - at.start].astype(
                    jnp.bfloat16
                )
        return carry

    lax.fori_loop(0, height // NORM_ROWS, rows, 0)


def conv_norm(x, cpar, flat, xp, xs, cq):
    fill_columns(xp, xs, x, x.shape[2])
    conv(xs, cpar, cq)
    norm(cq, cpar, xp, flat)


def conv_scratch(rows, out_rows, width, lanes):
    return [
        pltpu.VMEM((NORM_ROWS * lanes // LANES, width + 16, LANES), jnp.float32),
        pltpu.VMEM((rows, width // 8 + 2 * REACH, 8, lanes), jnp.float32),
        pltpu.VMEM((out_rows, width // 8, 8, lanes), jnp.float32),
    ]


def gelu(v):
    return 0.5 * v * (1.0 + lax.erf(v * (0.5**0.5)))


def up(flat, w_in, bias, act, ssq):
    height, width, channels = flat.shape
    cells = height * width
    half = w_in.shape[1]
    step = 2 * LANES

    def units(start, count):
        raised = jnp.dot(
            flat[...].reshape(cells, channels),
            w_in[:, pl.ds(start, count)],
            preferred_element_type=jnp.float32,
        )
        active = gelu(raised + bias[0:1, pl.ds(start, count)]).astype(jnp.bfloat16)
        act[:, pl.ds(start, count)] = active
        wide = active.astype(jnp.float32)
        ssq[:, pl.ds(start, count)] = jnp.sum((wide * wide).reshape(cells // 8, 8, count), axis=0)

    def full(n, carry):
        units(pl.multiple_of(n * step, step), step)
        return carry

    whole = half // step
    lax.fori_loop(0, whole, full, 0)
    if half % step:
        units(whole * step, half % step)


def norm_scale(ssqs, fvec, scale):
    half = fvec.shape[2]
    magnitude = [jnp.sqrt(jnp.sum(ssq[...], axis=0, keepdims=True)) for ssq in ssqs]
    mean = jnp.sum(magnitude[0] + magnitude[1], axis=1, keepdims=True) * (0.5 / half)
    for which in range(2):
        ratio = magnitude[which] / (mean + EPS_GRN)
        scale[which] = fvec[which, 1:2, :] * ratio + 1.0


def down(x_rows, first_row, acts, outs, scale, fvec, cpar):
    _, width, channels = x_rows.shape
    cells = CHUNK * width
    at = pl.ds(pl.multiple_of(first_row * width, cells), cells)
    update = cpar[VECTORS + 3 : VECTORS + 4, 0:channels]
    for which in range(2):
        a = acts[which][at, :].astype(jnp.float32)
        hidden = (a * scale[which] + fvec[which, 2:3, :]).astype(jnp.bfloat16)
        update = update + jnp.dot(hidden, outs[which][...], preferred_element_type=jnp.float32)
    return (x_rows.astype(jnp.float32) + update.reshape(CHUNK, width, channels)).astype(
        jnp.bfloat16
    )


def down_all(x, acts, outs, scale, fvec, cvec, out):
    def rows(n, carry):
        at = pl.ds(n * CHUNK, CHUNK)
        out[at] = down(x[at], n * CHUNK, acts, outs, scale, fvec, cvec)
        return carry

    lax.fori_loop(0, x.shape[0] // CHUNK, rows, 0)


def prepare_kernel(part, kernel, *refs):
    vectors, (cpar, fvec), (held, *staged), sems = refs[:7], refs[7:9], refs[9:-1], refs[-1]
    moves = [(kernel, held), *zip(vectors, staged)]
    copies = [pltpu.make_async_copy(a, b, sems.at[n]) for n, (a, b) in enumerate(moves)]
    for copy in copies:
        copy.start()
    cpar[...] = jnp.zeros(cpar.shape, jnp.float32)
    for copy in copies:
        copy.wait()
    channels = kernel.shape[3]
    span = kernel.shape[1]
    half = fvec.shape[2]
    for i in range(span):
        cpar[i * span : (i + 1) * span, 0:channels] = held[0, i].astype(jnp.float32)
    for n in range(4):
        cpar[VECTORS + n : VECTORS + n + 1, 0:channels] = staged[n][...].astype(jnp.float32)
    first = part[0] == 0
    for n in range(3):
        v = staged[4 + n][...].astype(jnp.float32)
        low, high = v[:, 0:half], v[:, half:]
        fvec[0, n : n + 1, :] = jnp.where(first, low, high)
        fvec[1, n : n + 1, :] = jnp.where(first, high, low)


def block_of(me, order, n):
    return n if order is None else me[0] ^ order[n]


def piece_kernel(section, piece, cpar, part, xp, xs, *, on):
    @pl.when(section[0] == on)
    def _():
        fill_columns(xp, xs, piece, piece.shape[2])
        conv(xs, cpar, part)


def last_piece_kernel(section, me, *refs, order, on):
    count = len(order or IN_ORDER)
    pieces, parts = refs[:count], refs[count : 2 * count - 1]
    cpar, x, flat, xp, xs, own, cq = refs[2 * count - 1 :]
    rows = pieces[0].shape[0]

    @pl.when(section[0] == on)
    def _():
        bias = cpar[VECTORS : VECTORS + 1, :].reshape(1, 1, 1, cq.shape[3])
        cq[...] = jnp.broadcast_to(bias, cq.shape)
        fill_columns(xp, xs, pieces[-1], x.shape[2])
        conv(xs, cpar, own)
        for n, (piece, part) in enumerate(zip(pieces, (*parts, own))):
            at = block_of(me, order, n) * rows
            x[pl.ds(at, rows)] = piece[...]
            cq[pl.ds(at, rows + 2 * REACH)] += part[...]
        norm(cq, cpar, xp, flat, REACH)


def conv_kernel(section, x, cpar, flat, xp, xs, cq, *, tick):
    @pl.when(section[0] == tick)
    def _():
        conv_norm(x, cpar, flat, xp, xs, cq)


def up_first_kernel(section, flat, w_in, fvec, act, ssq, *, tick):
    @pl.when(section[0] == tick)
    def _():
        up(flat, w_in, fvec.at[0], act, ssq)


def up_second_kernel(section, flat, w_in, fvec, other, act, scale, ssq, *, tick):
    @pl.when(section[0] == tick)
    def _():
        up(flat, w_in, fvec.at[1], act, ssq)
        norm_scale((other, ssq), fvec, scale)


def first_down_kernel(section, x, act_a, act_b, out_a, out_b, scale, fvec, cpar, out):
    @pl.when(section[0] == 0)
    def _():
        down_all(x, (act_a, act_b), (out_a, out_b), scale, fvec, cpar, out)


def down_piece_kernel(
    section, me, x, act_a, act_b, out_a, out_b, scale, fvec, cpar, prev, out, *, order, tick, n
):
    first_row = block_of(me, order, n) * CHUNK
    at = pl.ds(first_row, CHUNK)

    @pl.when(section[0] == tick)
    def _():
        out[...] = down(x[at], first_row, (act_a, act_b), (out_a, out_b), scale, fvec, cpar)

    @pl.when(section[0] != tick)
    def _():
        out[...] = prev[at]


def mlp_kernel(section, x, flat, in_a, in_b, out_a, out_b, fvec, cpar, *refs, tick):
    *pieces, prev, out, act_a, act_b, ssq_a, ssq_b, scale = refs

    @pl.when(section[0] == tick)
    def _():
        up(flat, in_a, fvec.at[0], act_a, ssq_a)
        up(flat, in_b, fvec.at[1], act_b, ssq_b)
        norm_scale((ssq_a, ssq_b), fvec, scale)
        down_all(x, (act_a, act_b), (out_a, out_b), scale, fvec, cpar, out)

    @pl.when(section[0] == tick - 1)
    def _():
        for n, piece in enumerate(pieces):
            out[n * CHUNK : (n + 1) * CHUNK] = piece[...]

    @pl.when(section[0] < tick - 1)
    def _():
        out[...] = prev[...]


def conv_up_kernel(section, x, cpar, in_a, in_b, fvec, *refs, tick):
    act_a, act_b, scale, xp, xs, cq, flat, ssq_a, ssq_b = refs

    @pl.when(section[0] == tick)
    def _():
        conv_norm(x, cpar, flat, xp, xs, cq)
        up(flat, in_a, fvec.at[0], act_a, ssq_a)
        up(flat, in_b, fvec.at[1], act_b, ssq_b)
        norm_scale((ssq_a, ssq_b), fvec, scale)


def place_kernel(me, *refs, order):
    *pieces, saved, sems = refs
    copies = [
        pltpu.make_async_copy(piece, saved.at[0, block_of(me, order, n), 0], sems.at[n])
        for n, piece in enumerate(pieces)
    ]
    for copy in copies:
        copy.start()
    for copy in copies:
        copy.wait()


SMEM = pl.BlockSpec(memory_space=pltpu.SMEM)
VMEM = pl.BlockSpec(memory_space=pltpu.VMEM)
HBM = pl.BlockSpec(memory_space=pltpu.HBM)


def call(kernel, name, args, out, specs=None, out_specs=None, scratch=(), flops=0, **static):
    if specs is None:
        specs = [SMEM if a.dtype == jnp.int32 else VMEM for a in args]
    if out_specs is None:
        out_specs = jax.tree.map(lambda _: VMEM, out)
    moved = sum(a.size * a.dtype.itemsize for a in args)
    return pl.pallas_call(
        functools.partial(kernel, **static),
        out_shape=out,
        in_specs=specs,
        out_specs=out_specs,
        scratch_shapes=list(scratch),
        compiler_params=pltpu.CompilerParams(vmem_limit_bytes=VMEM_BYTES),
        cost_estimate=pl.CostEstimate(flops=flops, bytes_accessed=moved, transcendentals=0),
        name=name,
    )(*args)


def shape(*dims, dtype=jnp.float32):
    return jax.ShapeDtypeStruct(dims, dtype)


def ssq_scratch(half):
    return pltpu.VMEM((8, half), jnp.float32)


def image_plan(
    inputs,
    depth_kernel,
    depth_bias,
    norm_gain,
    norm_bias,
    proj_in,
    bias_in,
    grn_gamma,
    grn_beta,
    proj_out,
    bias_out,
):
    sections = lax.axis_size("section")
    count = lax.axis_size("row")
    me = lax.axis_index("row").astype(jnp.int32)
    section = lax.axis_index("section").astype(jnp.int32).reshape(1)
    me_ref = me.reshape(1)
    part = lax.axis_index("dp").astype(jnp.int32).reshape(1)
    _, _, rows, width, channels = inputs.shape
    height = rows * count
    cells = height * width
    lanes = -(-channels // LANES) * LANES
    half = proj_in.shape[2]
    span = depth_kernel.shape[1]
    order = (0, 2, 3, 1)
    bf16 = jnp.bfloat16
    whole = shape(height, width, channels, dtype=bf16)
    piece_shape = shape(rows, width, channels, dtype=bf16)
    act_shape = shape(cells, half, dtype=bf16)
    scale_shape = shape(2, 1, half)
    matmul = 2 * cells * channels * half

    helper, source = 1, sections - 1
    pieces = []
    for by in order:
        piece = lax.dynamic_index_in_dim(inputs, me ^ by, 0, keepdims=False)[0]
        if by:
            pairs = [(source * count + (p ^ by), helper * count + p) for p in range(count)]
            piece = lax.ppermute(piece, ("section", "row"), pairs)
        pieces.append(piece)

    def other_half(x, which):
        pairs = [(2 * s + p, 2 * s + 1 - p) for s in which for p in range(2)]
        return lax.ppermute(x, ("section", "dp"), pairs)

    w_in, w_out = proj_in[0], proj_out[0]
    even = range(0, sections, 2)
    odd = range(1, sections, 2)
    other_in = other_half(w_in, even)
    other_out = other_half(w_out, even)

    held = (
        depth_kernel, depth_bias, norm_gain, norm_bias, bias_out, bias_in, grn_gamma, grn_beta
    )
    cpar, fvec = call(
        prepare_kernel,
        "prepare",
        (part, *held),
        (shape(VECTORS + 8, lanes), shape(2, 3, half)),
        specs=[SMEM] + [HBM] * len(held),
        scratch=[pltpu.VMEM(v.shape, v.dtype) for v in held]
        + [pltpu.SemaphoreType.DMA((len(held),))],
    )

    def send(x, start, end):
        return lax.ppermute(x, "section", [(start, end)])

    def conv_pieces(pieces, cpar, order, on):
        out_rows = rows + 2 * REACH
        scratch = conv_scratch(rows, out_rows, width, lanes)
        parts = []
        for piece in pieces[:-1]:
            if parts:
                piece, parts[-1] = lax.optimization_barrier((piece, parts[-1]))
            part = call(
                piece_kernel,
                "conv_piece",
                (section, piece, cpar),
                shape(out_rows, width // 8, 8, lanes),
                scratch=scratch[:2],
                on=on,
            )
            parts.append(part)
        return call(
            last_piece_kernel,
            "last_piece",
            (section, me_ref, *pieces, *parts, cpar),
            (whole, whole),
            scratch=scratch + [conv_scratch(1, height + 2 * REACH, width, lanes)[2]],
            order=order,
            on=on,
        )

    def up_own(flat, tick):
        return call(
            up_first_kernel,
            "up_own",
            (section, flat, w_in, fvec),
            (act_shape, shape(8, half)),
            flops=matmul,
            tick=tick,
        )

    def up_other(flat, other_in, ssq, tick):
        return call(
            up_second_kernel,
            "up_other",
            (section, flat, other_in, fvec, ssq),
            (act_shape, scale_shape),
            scratch=[ssq_scratch(half)],
            flops=matmul,
            tick=tick,
        )

    def down_piece(x, acts, other_out, prev, order, tick, n):
        act_a, act_b, scale = acts
        return call(
            down_piece_kernel,
            "down_piece",
            (section, me_ref, x, act_a, act_b, w_out, other_out, scale, fvec, cpar, prev),
            piece_shape,
            flops=2 * matmul // count,
            order=order,
            tick=tick,
            n=n,
        )

    x, flat = conv_pieces(pieces, send(cpar, 0, helper), order, helper)
    flat, x = send(flat, helper, 0), send(x, helper, 0)
    act_a, ssq = up_own(flat, 0)
    act_b, scale = up_other(flat, other_in, ssq, 0)
    result = call(
        first_down_kernel,
        "down",
        (section, x, act_a, act_b, w_out, other_out, scale, fvec, cpar),
        whole,
        flops=2 * matmul,
    )
    x = send(result, 0, 1)
    late_in, late_out, result = lax.optimization_barrier((w_in, w_out, result))
    odd_in = other_half(late_in, odd)
    odd_out = other_half(late_out, odd)
    flat = call(
        conv_kernel,
        "conv",
        (section, x, cpar),
        whole,
        scratch=conv_scratch(height, height, width, lanes),
        tick=1,
    )
    act_a, ssq = up_own(flat, 1)
    acts = (act_a, *up_other(flat, odd_in, ssq, 1))
    kept = [down_piece(x, acts, odd_out, result, None, 1, n) for n in range(count)]
    x, flat = conv_pieces([send(piece, 1, 2) for piece in kept], cpar, None, 2)
    result = call(
        mlp_kernel,
        "mlp",
        (section, x, flat, w_in, other_in, w_out, other_out, fvec, cpar, *kept, result),
        whole,
        scratch=[pltpu.VMEM((cells, half), bf16)] * 2
        + [ssq_scratch(half)] * 2
        + [pltpu.VMEM((2, 1, half), jnp.float32)],
        flops=4 * matmul,
        tick=2,
    )
    x = send(result, 2, 3)
    acts = call(
        conv_up_kernel,
        "conv_up",
        (section, x, cpar, w_in, odd_in, fvec),
        (act_shape, act_shape, scale_shape),
        scratch=conv_scratch(height, height, width, lanes)
        + [pltpu.VMEM((height, width, channels), bf16)]
        + [ssq_scratch(half)] * 2,
        flops=2 * matmul,
        tick=3,
    )
    done = []
    for n in (1, 2, 3, 0):
        piece = down_piece(x, acts, odd_out, result, order, 3, n)
        if n:
            piece = lax.ppermute(piece, "row", [(p, p ^ order[n]) for p in range(count)])
        done.append(piece)
    return call(
        place_kernel,
        "place",
        (me_ref, done[3], *done[:3]),
        shape(1, count, 1, rows, width, channels, dtype=bf16),
        out_specs=HBM,
        scratch=[pltpu.SemaphoreType.DMA((count,))],
        order=order,
    )


def extended(cells, sides, width):
    for axis, dim in sides:
        count = lax.axis_size(axis)
        ends = count - 1
        head = lax.slice_in_dim(cells, 0, width, axis=dim)
        tail = lax.slice_in_dim(cells, cells.shape[dim] - width, cells.shape[dim], axis=dim)
        cells = jnp.concatenate(
            [
                lax.ppermute(tail, axis, [(i, (i + 1) % count) for i in range(ends)]),
                cells,
                lax.ppermute(head, axis, [((i + 1) % count, i) for i in range(ends)]),
            ],
            axis=dim,
        )
    return cells


def depthwise(padded, kernel, bias_term):
    channels = padded.shape[-1]
    conv_out = lax.conv_general_dilated(
        padded.astype(jnp.float32),
        kernel.astype(jnp.float32)[:, :, None, :],
        (1, 1),
        "VALID",
        dimension_numbers=("NHWC", "HWIO", "NHWC"),
        feature_group_count=channels,
        precision=lax.Precision.HIGHEST,
    )
    return conv_out + bias_term.astype(jnp.float32)


def conv_block(current, params):
    (
        depth_kernel,
        depth_bias,
        norm_gain,
        norm_bias,
        proj_in,
        bias_in,
        grn_gamma,
        grn_beta,
        proj_out,
        bias_out,
    ) = params
    num_items, num_rows, num_cols, channels = current.shape
    padded = extended(current, (("row", 1),), REACH)
    padded = jnp.pad(padded, ((0, 0), (0, 0), (REACH, REACH), (0, 0)))
    conv_out = depthwise(padded, depth_kernel, depth_bias)
    center = conv_out - jnp.mean(conv_out, axis=-1, keepdims=True)
    spread = jnp.mean(center * center, axis=-1, keepdims=True)
    normed = (
        center * lax.rsqrt(spread + EPS_NORM) * norm_gain.astype(jnp.float32)
        + norm_bias.astype(jnp.float32)
    ).astype(jnp.bfloat16)
    flat_rows = normed.reshape(num_items * num_rows * num_cols, channels)
    raised = jnp.dot(flat_rows, proj_in, preferred_element_type=jnp.float32) + bias_in.astype(
        jnp.float32
    )
    active = jax.nn.gelu(raised, approximate=False).astype(jnp.bfloat16)
    grouped = active.reshape(num_items, num_rows * num_cols, -1).astype(jnp.float32)
    local_sq = jnp.sum(grouped * grouped, axis=1)
    total_sq = lax.psum(local_sq, "row")
    magnitude = jnp.sqrt(total_sq)
    grn_ratio = magnitude / (jnp.mean(magnitude, axis=-1, keepdims=True) + EPS_GRN)
    hidden = (
        grn_gamma.astype(jnp.float32) * grouped * grn_ratio[:, None, :]
        + grn_beta.astype(jnp.float32)
        + grouped
    ).astype(jnp.bfloat16)
    update = jnp.dot(
        hidden.reshape(num_items * num_rows * num_cols, -1),
        proj_out,
        preferred_element_type=jnp.float32,
    ) + bias_out.astype(jnp.float32)
    return (
        current.astype(jnp.float32) + update.reshape(num_items, num_rows, num_cols, channels)
    ).astype(jnp.bfloat16)


def rows_plan(inputs, *weights):
    (
        depth_kernel,
        depth_bias,
        norm_gain,
        norm_bias,
        proj_in,
        bias_in,
        grn_gamma,
        grn_beta,
        proj_out,
        bias_out,
    ) = weights
    proj_in = lax.all_gather(proj_in, "dp", axis=2, tiled=True)
    proj_out = lax.all_gather(proj_out, "dp", axis=1, tiled=True)
    own_params = tuple(
        w[0]
        for w in (
            depth_kernel,
            depth_bias,
            norm_gain,
            norm_bias,
            proj_in,
            bias_in,
            grn_gamma,
            grn_beta,
            proj_out,
            bias_out,
        )
    )
    sections = lax.axis_size("section")
    section_index = lax.axis_index("section")
    num_micro = inputs.shape[0]
    num_ticks = num_micro + sections - 1
    arriving = jnp.zeros_like(inputs[0])
    saved = jnp.zeros_like(inputs)
    for tick_index in range(num_ticks):
        fresh_input = inputs[min(tick_index, num_micro - 1)]
        current = jnp.where(section_index == 0, fresh_input, arriving)
        produced = conv_block(current, own_params)
        slot_index = tick_index - section_index
        is_valid = jnp.logical_and(slot_index >= 0, slot_index < num_micro)
        safe_slot = jnp.clip(slot_index, 0, num_micro - 1)
        previous = lax.dynamic_index_in_dim(saved, safe_slot, 0, keepdims=False)
        saved = lax.dynamic_update_index_in_dim(
            saved, jnp.where(is_valid, produced, previous), safe_slot, 0
        )
        if tick_index + 1 < num_ticks:
            arriving = lax.ppermute(
                produced, "section", [(i, i + 1) for i in range(sections - 1)]
            )
    return saved[None]


def on_device(inputs, *weights):
    num_micro, images, local_rows, width, _ = inputs.shape
    one_image_each = (
        images == 1
        and lax.axis_size("row") == num_micro == 4
        and lax.axis_size("dp") == 2
        and lax.axis_size("section") == 4
        and local_rows % 4 == 0
        and width % 16 == 0
    )
    plan = image_plan if one_image_each else rows_plan
    return plan(inputs, *weights)


def solution(mesh):
    return jax.shard_map(
        on_device,
        mesh=mesh,
        in_specs=(
            P(None, "dp", "row", None, None),
            P("section", None, None, None),
            P("section", None),
            P("section", None),
            P("section", None),
            P("section", None, "dp"),
            P("section", None),
            P("section", None),
            P("section", None),
            P("section", "dp", None),
            P("section", None),
        ),
        out_specs=P("section", None, "dp", "row", None, None),
        check_vma=False,
    )
```

```python
import functools

import jax
import jax.numpy as jnp
from jax import lax
from jax.experimental import pallas as pl
from jax.experimental.pallas import tpu as pltpu
from jax.sharding import PartitionSpec as P

EPS_NORM = 1e-06
EPS_GRN = 1e-06
LANES = 128
VMEM_BYTES = 20 * 1024 * 1024
PREPARE_VMEM_BYTES = 60 * 1024 * 1024
REACH = 3
CHUNK = 4
NORM_ROWS = 4
IN_ORDER = (0, 1, 2, 3)
VECTORS = 56


def fill_columns(xp, xs, x, channels):
    height, reach_cols, blocks, lanes = xs.shape
    stride = reach_cols - 2 * REACH
    width = stride * blocks
    groups = lanes // LANES
    xp[...] = jnp.zeros(xp.shape, jnp.float32)

    def rows(n, carry):
        for k in range(2):
            r = 2 * n + k
            row = x[r].astype(jnp.float32)
            for g in range(groups):
                at = slice(g * LANES, (g + 1) * LANES)
                own = row[:, g * LANES : min((g + 1) * LANES, channels)]
                xp[k * groups + g, 8 : 8 + width, 0 : own.shape[1]] = own
                for q in range(reach_cols):
                    near = pl.ds(8 - REACH + q, blocks, stride=stride)
                    xs[r, q, :, at] = xp[k * groups + g, near, :]
        return carry

    lax.fori_loop(0, height // 2, rows, 0)


def conv(xs, cpar, cq):
    rows = xs.shape[0]
    height, stride, blocks, lanes = cq.shape
    span = 2 * REACH + 1
    above = (height - rows) // 2

    def group(g, carry):
        at = pl.ds(pl.multiple_of(g * LANES, LANES), LANES)

        def column(q, carry):
            bias = jnp.broadcast_to(cpar[VECTORS : VECTORS + 1, at], (blocks, LANES))
            acc = [None if above else bias] * height
            for j in range(span):
                kern = [
                    jnp.broadcast_to(cpar[i * span + j : i * span + j + 1, at], (blocks, LANES))
                    for i in range(span)
                ]
                for r in range(rows):
                    x_row = xs[r, q + j, :, at]
                    for i in range(span):
                        h = r + above + REACH - i
                        if 0 <= h < height:
                            term = kern[i] * x_row
                            acc[h] = term if acc[h] is None else acc[h] + term
            for h in range(height):
                cq[h, q, :, at] = acc[h]
            return carry

        return lax.fori_loop(0, stride, column, carry)

    lax.fori_loop(0, lanes // LANES, group, 0)


def norm(cq, cpar, xp, flat, skip=0):
    padded, stride, blocks, lanes = cq.shape
    height = padded - 2 * skip
    gain = cpar[VECTORS + 1 : VECTORS + 2, :]
    shift = cpar[VECTORS + 2 : VECTORS + 3, :]
    channels = flat.shape[2]
    width = stride * blocks
    groups = lanes // LANES
    inside = lax.broadcasted_iota(jnp.int32, (blocks, lanes), 1) < channels

    def rows(n, carry):
        for k in range(NORM_ROWS):
            h = NORM_ROWS * n + k
            for q in range(stride):
                v = cq[h + skip, q]
                mean = jnp.sum(v, axis=-1, keepdims=True) * (1.0 / channels)
                c = jnp.where(inside, v - mean, 0.0)
                var = jnp.sum(c * c, axis=-1, keepdims=True) * (1.0 / channels)
                c = c * lax.rsqrt(var + EPS_NORM) * gain + shift
                for g in range(groups):
                    at = slice(g * LANES, (g + 1) * LANES)
                    xp[k * groups + g, pl.ds(q, blocks, stride=stride), :] = c[:, at]
            for g in range(groups):
                at = slice(g * LANES, min((g + 1) * LANES, channels))
                flat[h, :, at] = xp[k * groups + g, 0:width, 0 : at.stop - at.start].astype(
                    jnp.bfloat16
                )
        return carry

    lax.fori_loop(0, height // NORM_ROWS, rows, 0)


def conv_norm(x, cpar, flat, xp, xs, cq):
    fill_columns(xp, xs, x, x.shape[2])
    conv(xs, cpar, cq)
    norm(cq, cpar, xp, flat)


def conv_scratch(rows, out_rows, width, lanes):
    return [
        pltpu.VMEM((NORM_ROWS * lanes // LANES, width + 16, LANES), jnp.float32),
        pltpu.VMEM((rows, width // 8 + 2 * REACH, 8, lanes), jnp.float32),
        pltpu.VMEM((out_rows, width // 8, 8, lanes), jnp.float32),
    ]


def gelu(v):
    return 0.5 * v * (1.0 + lax.erf(v * (0.5**0.5)))


def up(flat, w_in, bias, act, ssq):
    height, width, channels = flat.shape
    cells = height * width
    half = w_in.shape[1]
    step = 2 * LANES

    def units(start, count):
        raised = jnp.dot(
            flat[...].reshape(cells, channels),
            w_in[:, pl.ds(start, count)],
            preferred_element_type=jnp.float32,
        )
        active = gelu(raised + bias[0:1, pl.ds(start, count)]).astype(jnp.bfloat16)
        act[:, pl.ds(start, count)] = active
        wide = active.astype(jnp.float32)
        ssq[:, pl.ds(start, count)] = jnp.sum((wide * wide).reshape(cells // 8, 8, count), axis=0)

    def full(n, carry):
        units(pl.multiple_of(n * step, step), step)
        return carry

    whole = half // step
    lax.fori_loop(0, whole, full, 0)
    if half % step:
        units(whole * step, half % step)


def norm_scale(ssqs, fvec, scale):
    half = fvec.shape[2]
    magnitude = [jnp.sqrt(jnp.sum(ssq[...], axis=0, keepdims=True)) for ssq in ssqs]
    mean = jnp.sum(magnitude[0] + magnitude[1], axis=1, keepdims=True) * (0.5 / half)
    for which in range(2):
        ratio = magnitude[which] / (mean + EPS_GRN)
        scale[which] = fvec[which, 1:2, :] * ratio + 1.0


def down(x_rows, first_row, acts, outs, scale, fvec, cpar):
    _, width, channels = x_rows.shape
    cells = CHUNK * width
    at = pl.ds(pl.multiple_of(first_row * width, cells), cells)
    update = cpar[VECTORS + 3 : VECTORS + 4, 0:channels]
    for which in range(2):
        a = acts[which][at, :].astype(jnp.float32)
        hidden = (a * scale[which] + fvec[which, 2:3, :]).astype(jnp.bfloat16)
        update = update + jnp.dot(hidden, outs[which][...], preferred_element_type=jnp.float32)
    return (x_rows.astype(jnp.float32) + update.reshape(CHUNK, width, channels)).astype(
        jnp.bfloat16
    )


def down_all(x, acts, outs, scale, fvec, cvec, out):
    def rows(n, carry):
        at = pl.ds(n * CHUNK, CHUNK)
        out[at] = down(x[at], n * CHUNK, acts, outs, scale, fvec, cvec)
        return carry

    lax.fori_loop(0, x.shape[0] // CHUNK, rows, 0)


def prepare_kernel(part, kernel, *refs):
    vectors, (cpar, fvec), (held, *staged), sems = refs[:7], refs[7:9], refs[9:-1], refs[-1]
    moves = [(kernel, held), *zip(vectors, staged)]
    copies = [pltpu.make_async_copy(a, b, sems.at[n]) for n, (a, b) in enumerate(moves)]
    for copy in copies:
        copy.start()
    cpar[...] = jnp.zeros(cpar.shape, jnp.float32)
    for copy in copies:
        copy.wait()
    channels = kernel.shape[3]
    span = kernel.shape[1]
    half = fvec.shape[2]
    for i in range(span):
        cpar[i * span : (i + 1) * span, 0:channels] = held[0, i].astype(jnp.float32)
    for n in range(4):
        cpar[VECTORS + n : VECTORS + n + 1, 0:channels] = staged[n][...].astype(jnp.float32)
    first = part[0] == 0
    for n in range(3):
        v = staged[4 + n][...].astype(jnp.float32)
        low, high = v[:, 0:half], v[:, half:]
        fvec[0, n : n + 1, :] = jnp.where(first, low, high)
        fvec[1, n : n + 1, :] = jnp.where(first, high, low)


def block_of(me, order, n):
    return n if order is None else me[0] ^ order[n]


def piece_kernel(section, piece, cpar, part, xp, xs, *, on):
    @pl.when(section[0] == on)
    def _():
        fill_columns(xp, xs, piece, piece.shape[2])
        conv(xs, cpar, part)


def last_piece_kernel(section, me, *refs, order, on):
    count = len(order or IN_ORDER)
    pieces, parts = refs[:count], refs[count : 2 * count - 1]
    cpar, x, flat, xp, xs, own, cq = refs[2 * count - 1 :]
    rows = pieces[0].shape[0]

    @pl.when(section[0] == on)
    def _():
        bias = cpar[VECTORS : VECTORS + 1, :].reshape(1, 1, 1, cq.shape[3])
        cq[...] = jnp.broadcast_to(bias, cq.shape)
        fill_columns(xp, xs, pieces[-1], x.shape[2])
        conv(xs, cpar, own)
        for n, (piece, part) in enumerate(zip(pieces, (*parts, own))):
            at = block_of(me, order, n) * rows
            x[pl.ds(at, rows)] = piece[...]
            cq[pl.ds(at, rows + 2 * REACH)] += part[...]
        norm(cq, cpar, xp, flat, REACH)


def conv_kernel(section, x, cpar, flat, xp, xs, cq, *, tick):
    @pl.when(section[0] == tick)
    def _():
        conv_norm(x, cpar, flat, xp, xs, cq)


def up_first_kernel(section, flat, w_in, fvec, act, ssq, *, tick):
    @pl.when(section[0] == tick)
    def _():
        up(flat, w_in, fvec.at[0], act, ssq)


def up_second_kernel(section, flat, w_in, fvec, other, act, scale, ssq, *, tick):
    @pl.when(section[0] == tick)
    def _():
        up(flat, w_in, fvec.at[1], act, ssq)
        norm_scale((other, ssq), fvec, scale)


def first_down_kernel(section, x, act_a, act_b, out_a, out_b, scale, fvec, cpar, out):
    @pl.when(section[0] == 0)
    def _():
        down_all(x, (act_a, act_b), (out_a, out_b), scale, fvec, cpar, out)


def down_piece_kernel(
    section, me, x, act_a, act_b, out_a, out_b, scale, fvec, cpar, prev, out, *, order, tick, n
):
    first_row = block_of(me, order, n) * CHUNK
    at = pl.ds(first_row, CHUNK)

    @pl.when(section[0] == tick)
    def _():
        out[...] = down(x[at], first_row, (act_a, act_b), (out_a, out_b), scale, fvec, cpar)

    @pl.when(section[0] != tick)
    def _():
        out[...] = prev[at]


def mlp_kernel(section, x, flat, in_a, in_b, out_a, out_b, fvec, cpar, *refs, tick):
    *pieces, prev, out, act_a, act_b, ssq_a, ssq_b, scale = refs

    @pl.when(section[0] == tick)
    def _():
        up(flat, in_a, fvec.at[0], act_a, ssq_a)
        up(flat, in_b, fvec.at[1], act_b, ssq_b)
        norm_scale((ssq_a, ssq_b), fvec, scale)
        down_all(x, (act_a, act_b), (out_a, out_b), scale, fvec, cpar, out)

    @pl.when(section[0] == tick - 1)
    def _():
        for n, piece in enumerate(pieces):
            out[n * CHUNK : (n + 1) * CHUNK] = piece[...]

    @pl.when(section[0] < tick - 1)
    def _():
        out[...] = prev[...]


def conv_up_kernel(section, x, cpar, in_a, in_b, fvec, *refs, tick):
    act_a, act_b, scale, xp, xs, cq, flat, ssq_a, ssq_b = refs

    @pl.when(section[0] == tick)
    def _():
        conv_norm(x, cpar, flat, xp, xs, cq)
        up(flat, in_a, fvec.at[0], act_a, ssq_a)
        up(flat, in_b, fvec.at[1], act_b, ssq_b)
        norm_scale((ssq_a, ssq_b), fvec, scale)


def place_kernel(me, *refs, order):
    *pieces, saved, sems = refs
    copies = [
        pltpu.make_async_copy(piece, saved.at[0, block_of(me, order, n), 0], sems.at[n])
        for n, piece in enumerate(pieces)
    ]
    for copy in copies:
        copy.start()
    for copy in copies:
        copy.wait()


SMEM = pl.BlockSpec(memory_space=pltpu.SMEM)
VMEM = pl.BlockSpec(memory_space=pltpu.VMEM)
HBM = pl.BlockSpec(memory_space=pltpu.HBM)


def call(
    kernel, name, args, out, specs=None, out_specs=None, scratch=(), flops=0, vmem=VMEM_BYTES, **static
):
    if specs is None:
        specs = [SMEM if a.dtype == jnp.int32 else VMEM for a in args]
    if out_specs is None:
        out_specs = jax.tree.map(lambda _: VMEM, out)
    moved = sum(a.size * a.dtype.itemsize for a in args)
    return pl.pallas_call(
        functools.partial(kernel, **static),
        out_shape=out,
        in_specs=specs,
        out_specs=out_specs,
        scratch_shapes=list(scratch),
        compiler_params=pltpu.CompilerParams(vmem_limit_bytes=vmem),
        cost_estimate=pl.CostEstimate(flops=flops, bytes_accessed=moved, transcendentals=0),
        name=name,
    )(*args)


def shape(*dims, dtype=jnp.float32):
    return jax.ShapeDtypeStruct(dims, dtype)


def ssq_scratch(half):
    return pltpu.VMEM((8, half), jnp.float32)


def image_plan(
    inputs,
    depth_kernel,
    depth_bias,
    norm_gain,
    norm_bias,
    proj_in,
    bias_in,
    grn_gamma,
    grn_beta,
    proj_out,
    bias_out,
):
    sections = lax.axis_size("section")
    count = lax.axis_size("row")
    me = lax.axis_index("row").astype(jnp.int32)
    section = lax.axis_index("section").astype(jnp.int32).reshape(1)
    me_ref = me.reshape(1)
    part = lax.axis_index("dp").astype(jnp.int32).reshape(1)
    _, _, rows, width, channels = inputs.shape
    height = rows * count
    cells = height * width
    lanes = -(-channels // LANES) * LANES
    half = proj_in.shape[2]
    span = depth_kernel.shape[1]
    order = (0, 2, 3, 1)
    bf16 = jnp.bfloat16
    whole = shape(height, width, channels, dtype=bf16)
    piece_shape = shape(rows, width, channels, dtype=bf16)
    act_shape = shape(cells, half, dtype=bf16)
    scale_shape = shape(2, 1, half)
    matmul = 2 * cells * channels * half

    helper, source = 1, sections - 1
    pieces = []
    for by in order:
        piece = lax.dynamic_index_in_dim(inputs, me ^ by, 0, keepdims=False)[0]
        if by:
            pairs = [(source * count + (p ^ by), helper * count + p) for p in range(count)]
            piece = lax.ppermute(piece, ("section", "row"), pairs)
        pieces.append(piece)

    def other_half(x, which):
        pairs = [(2 * s + p, 2 * s + 1 - p) for s in which for p in range(2)]
        return lax.ppermute(x, ("section", "dp"), pairs)

    w_in, w_out = proj_in[0], proj_out[0]
    even = range(0, sections, 2)
    odd = range(1, sections, 2)

    held = (
        depth_kernel, depth_bias, norm_gain, norm_bias, bias_out, bias_in, grn_gamma, grn_beta
    )
    cpar, fvec = call(
        prepare_kernel,
        "prepare",
        (part, *held),
        (shape(VECTORS + 8, lanes), shape(2, 3, half)),
        specs=[SMEM] + [HBM] * len(held),
        scratch=[pltpu.VMEM(v.shape, v.dtype) for v in held]
        + [pltpu.SemaphoreType.DMA((len(held),))],
        vmem=PREPARE_VMEM_BYTES,
    )

    def send(x, start, end):
        return lax.ppermute(x, "section", [(start, end)])

    lent_cpar = send(cpar, 0, helper)
    early_in, early_out, lent_cpar = lax.optimization_barrier((w_in, w_out, lent_cpar))
    other_in = other_half(early_in, even)
    other_out = other_half(early_out, even)

    def conv_pieces(pieces, cpar, order, on):
        out_rows = rows + 2 * REACH
        scratch = conv_scratch(rows, out_rows, width, lanes)
        parts = []
        for piece in pieces[:-1]:
            if parts:
                piece, parts[-1] = lax.optimization_barrier((piece, parts[-1]))
            part = call(
                piece_kernel,
                "conv_piece",
                (section, piece, cpar),
                shape(out_rows, width // 8, 8, lanes),
                scratch=scratch[:2],
                on=on,
            )
            parts.append(part)
        return call(
            last_piece_kernel,
            "last_piece",
            (section, me_ref, *pieces, *parts, cpar),
            (whole, whole),
            scratch=scratch + [conv_scratch(1, height + 2 * REACH, width, lanes)[2]],
            order=order,
            on=on,
        )

    def up_own(flat, tick):
        return call(
            up_first_kernel,
            "up_own",
            (section, flat, w_in, fvec),
            (act_shape, shape(8, half)),
            flops=matmul,
            tick=tick,
        )

    def up_other(flat, other_in, ssq, tick):
        return call(
            up_second_kernel,
            "up_other",
            (section, flat, other_in, fvec, ssq),
            (act_shape, scale_shape),
            scratch=[ssq_scratch(half)],
            flops=matmul,
            tick=tick,
        )

    def down_piece(x, acts, other_out, prev, order, tick, n):
        act_a, act_b, scale = acts
        return call(
            down_piece_kernel,
            "down_piece",
            (section, me_ref, x, act_a, act_b, w_out, other_out, scale, fvec, cpar, prev),
            piece_shape,
            flops=2 * matmul // count,
            order=order,
            tick=tick,
            n=n,
        )

    x, flat = conv_pieces(pieces, lent_cpar, order, helper)
    flat = send(flat, helper, 0)
    x, other_in, other_out = lax.optimization_barrier((x, other_in, other_out))
    x = send(x, helper, 0)
    act_a, ssq = up_own(flat, 0)
    act_b, scale = up_other(flat, other_in, ssq, 0)
    result = call(
        first_down_kernel,
        "down",
        (section, x, act_a, act_b, w_out, other_out, scale, fvec, cpar),
        whole,
        flops=2 * matmul,
    )
    x = send(result, 0, 1)
    late_in, late_out, result = lax.optimization_barrier((w_in, w_out, result))
    odd_in = other_half(late_in, odd)
    odd_out = other_half(late_out, odd)
    flat = call(
        conv_kernel,
        "conv",
        (section, x, cpar),
        whole,
        scratch=conv_scratch(height, height, width, lanes),
        tick=1,
    )
    act_a, ssq = up_own(flat, 1)
    acts = (act_a, *up_other(flat, odd_in, ssq, 1))
    kept = [down_piece(x, acts, odd_out, result, None, 1, n) for n in range(count)]
    x, flat = conv_pieces([send(piece, 1, 2) for piece in kept], cpar, None, 2)
    result = call(
        mlp_kernel,
        "mlp",
        (section, x, flat, w_in, other_in, w_out, other_out, fvec, cpar, *kept, result),
        whole,
        scratch=[pltpu.VMEM((cells, half), bf16)] * 2
        + [ssq_scratch(half)] * 2
        + [pltpu.VMEM((2, 1, half), jnp.float32)],
        flops=4 * matmul,
        tick=2,
    )
    x = send(result, 2, 3)
    acts = call(
        conv_up_kernel,
        "conv_up",
        (section, x, cpar, w_in, odd_in, fvec),
        (act_shape, act_shape, scale_shape),
        scratch=conv_scratch(height, height, width, lanes)
        + [pltpu.VMEM((height, width, channels), bf16)]
        + [ssq_scratch(half)] * 2,
        flops=2 * matmul,
        tick=3,
    )
    done = []
    for n in (1, 2, 3, 0):
        piece = down_piece(x, acts, odd_out, result, order, 3, n)
        if n:
            piece = lax.ppermute(piece, "row", [(p, p ^ order[n]) for p in range(count)])
        done.append(piece)
    return call(
        place_kernel,
        "place",
        (me_ref, done[3], *done[:3]),
        shape(1, count, 1, rows, width, channels, dtype=bf16),
        out_specs=HBM,
        scratch=[pltpu.SemaphoreType.DMA((count,))],
        order=order,
    )


def extended(cells, sides, width):
    for axis, dim in sides:
        count = lax.axis_size(axis)
        ends = count - 1
        head = lax.slice_in_dim(cells, 0, width, axis=dim)
        tail = lax.slice_in_dim(cells, cells.shape[dim] - width, cells.shape[dim], axis=dim)
        cells = jnp.concatenate(
            [
                lax.ppermute(tail, axis, [(i, (i + 1) % count) for i in range(ends)]),
                cells,
                lax.ppermute(head, axis, [((i + 1) % count, i) for i in range(ends)]),
            ],
            axis=dim,
        )
    return cells


def depthwise(padded, kernel, bias_term):
    channels = padded.shape[-1]
    conv_out = lax.conv_general_dilated(
        padded.astype(jnp.float32),
        kernel.astype(jnp.float32)[:, :, None, :],
        (1, 1),
        "VALID",
        dimension_numbers=("NHWC", "HWIO", "NHWC"),
        feature_group_count=channels,
        precision=lax.Precision.HIGHEST,
    )
    return conv_out + bias_term.astype(jnp.float32)


def conv_block(current, params):
    (
        depth_kernel,
        depth_bias,
        norm_gain,
        norm_bias,
        proj_in,
        bias_in,
        grn_gamma,
        grn_beta,
        proj_out,
        bias_out,
    ) = params
    num_items, num_rows, num_cols, channels = current.shape
    padded = extended(current, (("row", 1),), REACH)
    padded = jnp.pad(padded, ((0, 0), (0, 0), (REACH, REACH), (0, 0)))
    conv_out = depthwise(padded, depth_kernel, depth_bias)
    center = conv_out - jnp.mean(conv_out, axis=-1, keepdims=True)
    spread = jnp.mean(center * center, axis=-1, keepdims=True)
    normed = (
        center * lax.rsqrt(spread + EPS_NORM) * norm_gain.astype(jnp.float32)
        + norm_bias.astype(jnp.float32)
    ).astype(jnp.bfloat16)
    flat_rows = normed.reshape(num_items * num_rows * num_cols, channels)
    raised = jnp.dot(flat_rows, proj_in, preferred_element_type=jnp.float32) + bias_in.astype(
        jnp.float32
    )
    active = jax.nn.gelu(raised, approximate=False).astype(jnp.bfloat16)
    grouped = active.reshape(num_items, num_rows * num_cols, -1).astype(jnp.float32)
    local_sq = jnp.sum(grouped * grouped, axis=1)
    total_sq = lax.psum(local_sq, "row")
    magnitude = jnp.sqrt(total_sq)
    grn_ratio = magnitude / (jnp.mean(magnitude, axis=-1, keepdims=True) + EPS_GRN)
    hidden = (
        grn_gamma.astype(jnp.float32) * grouped * grn_ratio[:, None, :]
        + grn_beta.astype(jnp.float32)
        + grouped
    ).astype(jnp.bfloat16)
    update = jnp.dot(
        hidden.reshape(num_items * num_rows * num_cols, -1),
        proj_out,
        preferred_element_type=jnp.float32,
    ) + bias_out.astype(jnp.float32)
    return (
        current.astype(jnp.float32) + update.reshape(num_items, num_rows, num_cols, channels)
    ).astype(jnp.bfloat16)


def rows_plan(inputs, *weights):
    (
        depth_kernel,
        depth_bias,
        norm_gain,
        norm_bias,
        proj_in,
        bias_in,
        grn_gamma,
        grn_beta,
        proj_out,
        bias_out,
    ) = weights
    proj_in = lax.all_gather(proj_in, "dp", axis=2, tiled=True)
    proj_out = lax.all_gather(proj_out, "dp", axis=1, tiled=True)
    own_params = tuple(
        w[0]
        for w in (
            depth_kernel,
            depth_bias,
            norm_gain,
            norm_bias,
            proj_in,
            bias_in,
            grn_gamma,
            grn_beta,
            proj_out,
            bias_out,
        )
    )
    sections = lax.axis_size("section")
    section_index = lax.axis_index("section")
    num_micro = inputs.shape[0]
    num_ticks = num_micro + sections - 1
    arriving = jnp.zeros_like(inputs[0])
    saved = jnp.zeros_like(inputs)
    for tick_index in range(num_ticks):
        fresh_input = inputs[min(tick_index, num_micro - 1)]
        current = jnp.where(section_index == 0, fresh_input, arriving)
        produced = conv_block(current, own_params)
        slot_index = tick_index - section_index
        is_valid = jnp.logical_and(slot_index >= 0, slot_index < num_micro)
        safe_slot = jnp.clip(slot_index, 0, num_micro - 1)
        previous = lax.dynamic_index_in_dim(saved, safe_slot, 0, keepdims=False)
        saved = lax.dynamic_update_index_in_dim(
            saved, jnp.where(is_valid, produced, previous), safe_slot, 0
        )
        if tick_index + 1 < num_ticks:
            arriving = lax.ppermute(
                produced, "section", [(i, i + 1) for i in range(sections - 1)]
            )
    return saved[None]


def on_device(inputs, *weights):
    num_micro, images, local_rows, width, _ = inputs.shape
    one_image_each = (
        images == 1
        and lax.axis_size("row") == num_micro == 4
        and lax.axis_size("dp") == 2
        and lax.axis_size("section") == 4
        and local_rows % 4 == 0
        and width % 16 == 0
    )
    plan = image_plan if one_image_each else rows_plan
    return plan(inputs, *weights)


def solution(mesh):
    return jax.shard_map(
        on_device,
        mesh=mesh,
        in_specs=(
            P(None, "dp", "row", None, None),
            P("section", None, None, None),
            P("section", None),
            P("section", None),
            P("section", None),
            P("section", None, "dp"),
            P("section", None),
            P("section", None),
            P("section", None),
            P("section", "dp", None),
            P("section", None),
        ),
        out_specs=P("section", None, "dp", "row", None, None),
        check_vma=False,
    )
```

```python
import functools

import jax
import jax.numpy as jnp
from jax import lax
from jax.experimental import pallas as pl
from jax.experimental.pallas import tpu as pltpu
from jax.sharding import PartitionSpec as P

EPS_NORM = 1e-06
EPS_GRN = 1e-06
LANES = 128
VMEM_BYTES = 20 * 1024 * 1024
REACH = 3
CHUNK = 4
NORM_ROWS = 4
IN_ORDER = (0, 1, 2, 3)
VECTORS = 56


def fill_columns(xp, xs, x, channels):
    height, reach_cols, blocks, lanes = xs.shape
    stride = reach_cols - 2 * REACH
    width = stride * blocks
    groups = lanes // LANES
    xp[...] = jnp.zeros(xp.shape, jnp.float32)

    def rows(n, carry):
        for k in range(2):
            r = 2 * n + k
            row = x[r].astype(jnp.float32)
            for g in range(groups):
                at = slice(g * LANES, (g + 1) * LANES)
                own = row[:, g * LANES : min((g + 1) * LANES, channels)]
                xp[k * groups + g, 8 : 8 + width, 0 : own.shape[1]] = own
                for q in range(reach_cols):
                    near = pl.ds(8 - REACH + q, blocks, stride=stride)
                    xs[r, q, :, at] = xp[k * groups + g, near, :]
        return carry

    lax.fori_loop(0, height // 2, rows, 0)


def conv(xs, cpar, cq):
    rows = xs.shape[0]
    height, stride, blocks, lanes = cq.shape
    span = 2 * REACH + 1
    above = (height - rows) // 2

    def group(g, carry):
        at = pl.ds(pl.multiple_of(g * LANES, LANES), LANES)

        def column(q, carry):
            bias = jnp.broadcast_to(cpar[VECTORS : VECTORS + 1, at], (blocks, LANES))
            acc = [None if above else bias] * height
            for j in range(span):
                kern = [
                    jnp.broadcast_to(cpar[i * span + j : i * span + j + 1, at], (blocks, LANES))
                    for i in range(span)
                ]
                for r in range(rows):
                    x_row = xs[r, q + j, :, at]
                    for i in range(span):
                        h = r + above + REACH - i
                        if 0 <= h < height:
                            term = kern[i] * x_row
                            acc[h] = term if acc[h] is None else acc[h] + term
            for h in range(height):
                cq[h, q, :, at] = acc[h]
            return carry

        return lax.fori_loop(0, stride, column, carry)

    lax.fori_loop(0, lanes // LANES, group, 0)


def norm(cq, cpar, xp, flat, skip=0):
    padded, stride, blocks, lanes = cq.shape
    height = padded - 2 * skip
    gain = cpar[VECTORS + 1 : VECTORS + 2, :]
    shift = cpar[VECTORS + 2 : VECTORS + 3, :]
    channels = flat.shape[2]
    width = stride * blocks
    groups = lanes // LANES
    inside = lax.broadcasted_iota(jnp.int32, (blocks, lanes), 1) < channels

    def rows(n, carry):
        for k in range(NORM_ROWS):
            h = NORM_ROWS * n + k
            for q in range(stride):
                v = cq[h + skip, q]
                mean = jnp.sum(v, axis=-1, keepdims=True) * (1.0 / channels)
                c = jnp.where(inside, v - mean, 0.0)
                var = jnp.sum(c * c, axis=-1, keepdims=True) * (1.0 / channels)
                c = c * lax.rsqrt(var + EPS_NORM) * gain + shift
                for g in range(groups):
                    at = slice(g * LANES, (g + 1) * LANES)
                    xp[k * groups + g, pl.ds(q, blocks, stride=stride), :] = c[:, at]
            for g in range(groups):
                at = slice(g * LANES, min((g + 1) * LANES, channels))
                flat[h, :, at] = xp[k * groups + g, 0:width, 0 : at.stop - at.start].astype(
                    jnp.bfloat16
                )
        return carry

    lax.fori_loop(0, height // NORM_ROWS, rows, 0)


def conv_norm(x, cpar, flat, xp, xs, cq):
    fill_columns(xp, xs, x, x.shape[2])
    conv(xs, cpar, cq)
    norm(cq, cpar, xp, flat)


def conv_scratch(rows, out_rows, width, lanes):
    return [
        pltpu.VMEM((NORM_ROWS * lanes // LANES, width + 16, LANES), jnp.float32),
        pltpu.VMEM((rows, width // 8 + 2 * REACH, 8, lanes), jnp.float32),
        pltpu.VMEM((out_rows, width // 8, 8, lanes), jnp.float32),
    ]


def gelu(v):
    return 0.5 * v * (1.0 + lax.erf(v * (0.5**0.5)))


def up(flat, w_in, bias, act, ssq):
    height, width, channels = flat.shape
    cells = height * width
    half = w_in.shape[1]
    step = 2 * LANES

    def units(start, count):
        raised = jnp.dot(
            flat[...].reshape(cells, channels),
            w_in[:, pl.ds(start, count)],
            preferred_element_type=jnp.float32,
        )
        active = gelu(raised + bias[0:1, pl.ds(start, count)]).astype(jnp.bfloat16)
        act[:, pl.ds(start, count)] = active
        wide = active.astype(jnp.float32)
        ssq[:, pl.ds(start, count)] = jnp.sum((wide * wide).reshape(cells // 8, 8, count), axis=0)

    def full(n, carry):
        units(pl.multiple_of(n * step, step), step)
        return carry

    whole = half // step
    lax.fori_loop(0, whole, full, 0)
    if half % step:
        units(whole * step, half % step)


def norm_scale(ssqs, fvec, scale):
    half = fvec.shape[2]
    magnitude = [jnp.sqrt(jnp.sum(ssq[...], axis=0, keepdims=True)) for ssq in ssqs]
    mean = jnp.sum(magnitude[0] + magnitude[1], axis=1, keepdims=True) * (0.5 / half)
    for which in range(2):
        ratio = magnitude[which] / (mean + EPS_GRN)
        scale[which] = fvec[which, 1:2, :] * ratio + 1.0


def down(x_rows, first_row, acts, outs, scale, fvec, cpar):
    _, width, channels = x_rows.shape
    cells = CHUNK * width
    at = pl.ds(pl.multiple_of(first_row * width, cells), cells)
    update = cpar[VECTORS + 3 : VECTORS + 4, 0:channels]
    for which in range(2):
        a = acts[which][at, :].astype(jnp.float32)
        hidden = (a * scale[which] + fvec[which, 2:3, :]).astype(jnp.bfloat16)
        update = update + jnp.dot(hidden, outs[which][...], preferred_element_type=jnp.float32)
    return (x_rows.astype(jnp.float32) + update.reshape(CHUNK, width, channels)).astype(
        jnp.bfloat16
    )


def down_all(x, acts, outs, scale, fvec, cvec, out):
    def rows(n, carry):
        at = pl.ds(n * CHUNK, CHUNK)
        out[at] = down(x[at], n * CHUNK, acts, outs, scale, fvec, cvec)
        return carry

    lax.fori_loop(0, x.shape[0] // CHUNK, rows, 0)


def prepare_kernel(part, kernel, *refs):
    vectors, (cpar, fvec), (held, *staged), sems = refs[:7], refs[7:9], refs[9:-1], refs[-1]
    moves = [(kernel, held), *zip(vectors, staged)]
    copies = [pltpu.make_async_copy(a, b, sems.at[n]) for n, (a, b) in enumerate(moves)]
    for copy in copies:
        copy.start()
    cpar[...] = jnp.zeros(cpar.shape, jnp.float32)
    for copy in copies:
        copy.wait()
    channels = kernel.shape[3]
    span = kernel.shape[1]
    half = fvec.shape[2]
    for i in range(span):
        cpar[i * span : (i + 1) * span, 0:channels] = held[0, i].astype(jnp.float32)
    for n in range(4):
        cpar[VECTORS + n : VECTORS + n + 1, 0:channels] = staged[n][...].astype(jnp.float32)
    first = part[0] == 0
    for n in range(3):
        v = staged[4 + n][...].astype(jnp.float32)
        low, high = v[:, 0:half], v[:, half:]
        fvec[0, n : n + 1, :] = jnp.where(first, low, high)
        fvec[1, n : n + 1, :] = jnp.where(first, high, low)


def block_of(me, order, n):
    return n if order is None else me[0] ^ order[n]


def piece_kernel(section, piece, cpar, part, xp, xs, *, on):
    @pl.when(section[0] == on)
    def _():
        fill_columns(xp, xs, piece, piece.shape[2])
        conv(xs, cpar, part)


def last_piece_kernel(section, me, *refs, order, on):
    count = len(order or IN_ORDER)
    pieces, parts = refs[:count], refs[count : 2 * count - 1]
    cpar, x, flat, xp, xs, own, cq = refs[2 * count - 1 :]
    rows = pieces[0].shape[0]

    @pl.when(section[0] == on)
    def _():
        bias = cpar[VECTORS : VECTORS + 1, :].reshape(1, 1, 1, cq.shape[3])
        cq[...] = jnp.broadcast_to(bias, cq.shape)
        fill_columns(xp, xs, pieces[-1], x.shape[2])
        conv(xs, cpar, own)
        for n, (piece, part) in enumerate(zip(pieces, (*parts, own))):
            at = block_of(me, order, n) * rows
            x[pl.ds(at, rows)] = piece[...]
            cq[pl.ds(at, rows + 2 * REACH)] += part[...]
        norm(cq, cpar, xp, flat, REACH)


def conv_kernel(section, x, cpar, flat, xp, xs, cq, *, tick):
    @pl.when(section[0] == tick)
    def _():
        conv_norm(x, cpar, flat, xp, xs, cq)


def up_first_kernel(section, flat, w_in, fvec, act, ssq, *, tick):
    @pl.when(section[0] == tick)
    def _():
        up(flat, w_in, fvec.at[0], act, ssq)


def up_second_kernel(section, flat, w_in, fvec, other, act, scale, ssq, *, tick):
    @pl.when(section[0] == tick)
    def _():
        up(flat, w_in, fvec.at[1], act, ssq)
        norm_scale((other, ssq), fvec, scale)


def first_down_kernel(section, x, act_a, act_b, out_a, out_b, scale, fvec, cpar, out):
    @pl.when(section[0] == 0)
    def _():
        down_all(x, (act_a, act_b), (out_a, out_b), scale, fvec, cpar, out)


def down_piece_kernel(
    section, me, x, act_a, act_b, out_a, out_b, scale, fvec, cpar, prev, out, *, order, tick, n
):
    first_row = block_of(me, order, n) * CHUNK
    at = pl.ds(first_row, CHUNK)

    @pl.when(section[0] == tick)
    def _():
        out[...] = down(x[at], first_row, (act_a, act_b), (out_a, out_b), scale, fvec, cpar)

    @pl.when(section[0] != tick)
    def _():
        out[...] = prev[at]


def mlp_kernel(section, x, flat, in_a, in_b, out_a, out_b, fvec, cpar, *refs, tick):
    *pieces, prev, out, act_a, act_b, ssq_a, ssq_b, scale = refs

    @pl.when(section[0] == tick)
    def _():
        up(flat, in_a, fvec.at[0], act_a, ssq_a)
        up(flat, in_b, fvec.at[1], act_b, ssq_b)
        norm_scale((ssq_a, ssq_b), fvec, scale)
        down_all(x, (act_a, act_b), (out_a, out_b), scale, fvec, cpar, out)

    @pl.when(section[0] == tick - 1)
    def _():
        for n, piece in enumerate(pieces):
            out[n * CHUNK : (n + 1) * CHUNK] = piece[...]

    @pl.when(section[0] < tick - 1)
    def _():
        out[...] = prev[...]


def conv_up_kernel(section, x, cpar, in_a, in_b, fvec, *refs, tick):
    act_a, act_b, scale, xp, xs, cq, flat, ssq_a, ssq_b = refs

    @pl.when(section[0] == tick)
    def _():
        conv_norm(x, cpar, flat, xp, xs, cq)
        up(flat, in_a, fvec.at[0], act_a, ssq_a)
        up(flat, in_b, fvec.at[1], act_b, ssq_b)
        norm_scale((ssq_a, ssq_b), fvec, scale)


def place_kernel(me, *refs, order):
    *pieces, saved, sems = refs
    copies = [
        pltpu.make_async_copy(piece, saved.at[0, block_of(me, order, n), 0], sems.at[n])
        for n, piece in enumerate(pieces)
    ]
    for copy in copies:
        copy.start()
    for copy in copies:
        copy.wait()


SMEM = pl.BlockSpec(memory_space=pltpu.SMEM)
VMEM = pl.BlockSpec(memory_space=pltpu.VMEM)
HBM = pl.BlockSpec(memory_space=pltpu.HBM)


def call(kernel, name, args, out, specs=None, out_specs=None, scratch=(), flops=0, **static):
    if specs is None:
        specs = [SMEM if a.dtype == jnp.int32 else VMEM for a in args]
    if out_specs is None:
        out_specs = jax.tree.map(lambda _: VMEM, out)
    moved = sum(a.size * a.dtype.itemsize for a in args)
    return pl.pallas_call(
        functools.partial(kernel, **static),
        out_shape=out,
        in_specs=specs,
        out_specs=out_specs,
        scratch_shapes=list(scratch),
        compiler_params=pltpu.CompilerParams(vmem_limit_bytes=VMEM_BYTES),
        cost_estimate=pl.CostEstimate(flops=flops, bytes_accessed=moved, transcendentals=0),
        name=name,
    )(*args)


def shape(*dims, dtype=jnp.float32):
    return jax.ShapeDtypeStruct(dims, dtype)


def ssq_scratch(half):
    return pltpu.VMEM((8, half), jnp.float32)


def image_plan(
    inputs,
    depth_kernel,
    depth_bias,
    norm_gain,
    norm_bias,
    proj_in,
    bias_in,
    grn_gamma,
    grn_beta,
    proj_out,
    bias_out,
):
    sections = lax.axis_size("section")
    count = lax.axis_size("row")
    me = lax.axis_index("row").astype(jnp.int32)
    section = lax.axis_index("section").astype(jnp.int32).reshape(1)
    me_ref = me.reshape(1)
    part = lax.axis_index("dp").astype(jnp.int32).reshape(1)
    _, _, rows, width, channels = inputs.shape
    height = rows * count
    cells = height * width
    lanes = -(-channels // LANES) * LANES
    half = proj_in.shape[2]
    span = depth_kernel.shape[1]
    order = (0, 2, 3, 1)
    bf16 = jnp.bfloat16
    whole = shape(height, width, channels, dtype=bf16)
    piece_shape = shape(rows, width, channels, dtype=bf16)
    act_shape = shape(cells, half, dtype=bf16)
    scale_shape = shape(2, 1, half)
    matmul = 2 * cells * channels * half

    helper, source = 1, sections - 1
    pieces = []
    for by in order:
        piece = lax.dynamic_index_in_dim(inputs, me ^ by, 0, keepdims=False)[0]
        if by:
            pairs = [(source * count + (p ^ by), helper * count + p) for p in range(count)]
            piece = lax.ppermute(piece, ("section", "row"), pairs)
        pieces.append(piece)

    def other_half(x, which):
        pairs = [(2 * s + p, 2 * s + 1 - p) for s in which for p in range(2)]
        return lax.ppermute(x, ("section", "dp"), pairs)

    w_in, w_out = proj_in[0], proj_out[0]
    even = range(0, sections, 2)
    odd = range(1, sections, 2)
    other_in = other_half(w_in, even)
    other_out = other_half(w_out, even)

    held = (
        depth_kernel, depth_bias, norm_gain, norm_bias, bias_out, bias_in, grn_gamma, grn_beta
    )
    cpar, fvec = call(
        prepare_kernel,
        "prepare",
        (part, *held),
        (shape(VECTORS + 8, lanes), shape(2, 3, half)),
        specs=[SMEM] + [HBM] * len(held),
        scratch=[pltpu.VMEM(v.shape, v.dtype) for v in held]
        + [pltpu.SemaphoreType.DMA((len(held),))],
    )

    def send(x, start, end):
        return lax.ppermute(x, "section", [(start, end)])

    def conv_pieces(pieces, cpar, order, on):
        out_rows = rows + 2 * REACH
        scratch = conv_scratch(rows, out_rows, width, lanes)
        parts = []
        for piece in pieces[:-1]:
            if parts:
                piece, parts[-1] = lax.optimization_barrier((piece, parts[-1]))
            part = call(
                piece_kernel,
                "conv_piece",
                (section, piece, cpar),
                shape(out_rows, width // 8, 8, lanes),
                scratch=scratch[:2],
                on=on,
            )
            parts.append(part)
        return call(
            last_piece_kernel,
            "last_piece",
            (section, me_ref, *pieces, *parts, cpar),
            (whole, whole),
            scratch=scratch + [conv_scratch(1, height + 2 * REACH, width, lanes)[2]],
            order=order,
            on=on,
        )

    def up_own(flat, tick):
        return call(
            up_first_kernel,
            "up_own",
            (section, flat, w_in, fvec),
            (act_shape, shape(8, half)),
            flops=matmul,
            tick=tick,
        )

    def up_other(flat, other_in, ssq, tick):
        return call(
            up_second_kernel,
            "up_other",
            (section, flat, other_in, fvec, ssq),
            (act_shape, scale_shape),
            scratch=[ssq_scratch(half)],
            flops=matmul,
            tick=tick,
        )

    def down_piece(x, acts, other_out, prev, order, tick, n):
        act_a, act_b, scale = acts
        return call(
            down_piece_kernel,
            "down_piece",
            (section, me_ref, x, act_a, act_b, w_out, other_out, scale, fvec, cpar, prev),
            piece_shape,
            flops=2 * matmul // count,
            order=order,
            tick=tick,
            n=n,
        )

    x, flat = conv_pieces(pieces, send(cpar, 0, helper), order, helper)
    flat, other_in = lax.optimization_barrier((flat, other_in))
    flat, x = send(flat, helper, 0), send(x, helper, 0)
    act_a, ssq = up_own(flat, 0)
    act_b, scale = up_other(flat, other_in, ssq, 0)
    result = call(
        first_down_kernel,
        "down",
        (section, x, act_a, act_b, w_out, other_out, scale, fvec, cpar),
        whole,
        flops=2 * matmul,
    )
    x = send(result, 0, 1)
    late_in, late_out, result = lax.optimization_barrier((w_in, w_out, result))
    odd_in = other_half(late_in, odd)
    odd_out = other_half(late_out, odd)
    flat = call(
        conv_kernel,
        "conv",
        (section, x, cpar),
        whole,
        scratch=conv_scratch(height, height, width, lanes),
        tick=1,
    )
    act_a, ssq = up_own(flat, 1)
    acts = (act_a, *up_other(flat, odd_in, ssq, 1))
    kept = [down_piece(x, acts, odd_out, result, None, 1, n) for n in range(count)]
    x, flat = conv_pieces([send(piece, 1, 2) for piece in kept], cpar, None, 2)
    result = call(
        mlp_kernel,
        "mlp",
        (section, x, flat, w_in, other_in, w_out, other_out, fvec, cpar, *kept, result),
        whole,
        scratch=[pltpu.VMEM((cells, half), bf16)] * 2
        + [ssq_scratch(half)] * 2
        + [pltpu.VMEM((2, 1, half), jnp.float32)],
        flops=4 * matmul,
        tick=2,
    )
    x = send(result, 2, 3)
    acts = call(
        conv_up_kernel,
        "conv_up",
        (section, x, cpar, w_in, odd_in, fvec),
        (act_shape, act_shape, scale_shape),
        scratch=conv_scratch(height, height, width, lanes)
        + [pltpu.VMEM((height, width, channels), bf16)]
        + [ssq_scratch(half)] * 2,
        flops=2 * matmul,
        tick=3,
    )
    done = []
    for n in (1, 2, 3, 0):
        piece = down_piece(x, acts, odd_out, result, order, 3, n)
        if n:
            piece = lax.ppermute(piece, "row", [(p, p ^ order[n]) for p in range(count)])
        done.append(piece)
    return call(
        place_kernel,
        "place",
        (me_ref, done[3], *done[:3]),
        shape(1, count, 1, rows, width, channels, dtype=bf16),
        out_specs=HBM,
        scratch=[pltpu.SemaphoreType.DMA((count,))],
        order=order,
    )


def extended(cells, sides, width):
    for axis, dim in sides:
        count = lax.axis_size(axis)
        ends = count - 1
        head = lax.slice_in_dim(cells, 0, width, axis=dim)
        tail = lax.slice_in_dim(cells, cells.shape[dim] - width, cells.shape[dim], axis=dim)
        cells = jnp.concatenate(
            [
                lax.ppermute(tail, axis, [(i, (i + 1) % count) for i in range(ends)]),
                cells,
                lax.ppermute(head, axis, [((i + 1) % count, i) for i in range(ends)]),
            ],
            axis=dim,
        )
    return cells


def depthwise(padded, kernel, bias_term):
    channels = padded.shape[-1]
    conv_out = lax.conv_general_dilated(
        padded.astype(jnp.float32),
        kernel.astype(jnp.float32)[:, :, None, :],
        (1, 1),
        "VALID",
        dimension_numbers=("NHWC", "HWIO", "NHWC"),
        feature_group_count=channels,
        precision=lax.Precision.HIGHEST,
    )
    return conv_out + bias_term.astype(jnp.float32)


def conv_block(current, params):
    (
        depth_kernel,
        depth_bias,
        norm_gain,
        norm_bias,
        proj_in,
        bias_in,
        grn_gamma,
        grn_beta,
        proj_out,
        bias_out,
    ) = params
    num_items, num_rows, num_cols, channels = current.shape
    padded = extended(current, (("row", 1),), REACH)
    padded = jnp.pad(padded, ((0, 0), (0, 0), (REACH, REACH), (0, 0)))
    conv_out = depthwise(padded, depth_kernel, depth_bias)
    center = conv_out - jnp.mean(conv_out, axis=-1, keepdims=True)
    spread = jnp.mean(center * center, axis=-1, keepdims=True)
    normed = (
        center * lax.rsqrt(spread + EPS_NORM) * norm_gain.astype(jnp.float32)
        + norm_bias.astype(jnp.float32)
    ).astype(jnp.bfloat16)
    flat_rows = normed.reshape(num_items * num_rows * num_cols, channels)
    raised = jnp.dot(flat_rows, proj_in, preferred_element_type=jnp.float32) + bias_in.astype(
        jnp.float32
    )
    active = jax.nn.gelu(raised, approximate=False).astype(jnp.bfloat16)
    grouped = active.reshape(num_items, num_rows * num_cols, -1).astype(jnp.float32)
    local_sq = jnp.sum(grouped * grouped, axis=1)
    total_sq = lax.psum(local_sq, "row")
    magnitude = jnp.sqrt(total_sq)
    grn_ratio = magnitude / (jnp.mean(magnitude, axis=-1, keepdims=True) + EPS_GRN)
    hidden = (
        grn_gamma.astype(jnp.float32) * grouped * grn_ratio[:, None, :]
        + grn_beta.astype(jnp.float32)
        + grouped
    ).astype(jnp.bfloat16)
    update = jnp.dot(
        hidden.reshape(num_items * num_rows * num_cols, -1),
        proj_out,
        preferred_element_type=jnp.float32,
    ) + bias_out.astype(jnp.float32)
    return (
        current.astype(jnp.float32) + update.reshape(num_items, num_rows, num_cols, channels)
    ).astype(jnp.bfloat16)


def rows_plan(inputs, *weights):
    (
        depth_kernel,
        depth_bias,
        norm_gain,
        norm_bias,
        proj_in,
        bias_in,
        grn_gamma,
        grn_beta,
        proj_out,
        bias_out,
    ) = weights
    proj_in = lax.all_gather(proj_in, "dp", axis=2, tiled=True)
    proj_out = lax.all_gather(proj_out, "dp", axis=1, tiled=True)
    own_params = tuple(
        w[0]
        for w in (
            depth_kernel,
            depth_bias,
            norm_gain,
            norm_bias,
            proj_in,
            bias_in,
            grn_gamma,
            grn_beta,
            proj_out,
            bias_out,
        )
    )
    sections = lax.axis_size("section")
    section_index = lax.axis_index("section")
    num_micro = inputs.shape[0]
    num_ticks = num_micro + sections - 1
    arriving = jnp.zeros_like(inputs[0])
    saved = jnp.zeros_like(inputs)
    for tick_index in range(num_ticks):
        fresh_input = inputs[min(tick_index, num_micro - 1)]
        current = jnp.where(section_index == 0, fresh_input, arriving)
        produced = conv_block(current, own_params)
        slot_index = tick_index - section_index
        is_valid = jnp.logical_and(slot_index >= 0, slot_index < num_micro)
        safe_slot = jnp.clip(slot_index, 0, num_micro - 1)
        previous = lax.dynamic_index_in_dim(saved, safe_slot, 0, keepdims=False)
        saved = lax.dynamic_update_index_in_dim(
            saved, jnp.where(is_valid, produced, previous), safe_slot, 0
        )
        if tick_index + 1 < num_ticks:
            arriving = lax.ppermute(
                produced, "section", [(i, i + 1) for i in range(sections - 1)]
            )
    return saved[None]


def on_device(inputs, *weights):
    num_micro, images, local_rows, width, _ = inputs.shape
    one_image_each = (
        images == 1
        and lax.axis_size("row") == num_micro == 4
        and lax.axis_size("dp") == 2
        and lax.axis_size("section") == 4
        and local_rows % 4 == 0
        and width % 16 == 0
    )
    plan = image_plan if one_image_each else rows_plan
    return plan(inputs, *weights)


def solution(mesh):
    return jax.shard_map(
        on_device,
        mesh=mesh,
        in_specs=(
            P(None, "dp", "row", None, None),
            P("section", None, None, None),
            P("section", None),
            P("section", None),
            P("section", None),
            P("section", None, "dp"),
            P("section", None),
            P("section", None),
            P("section", None),
            P("section", "dp", None),
            P("section", None),
        ),
        out_specs=P("section", None, "dp", "row", None, None),
        check_vma=False,
    )
```

```python
import functools

import jax
import jax.numpy as jnp
from jax import lax
from jax.experimental import pallas as pl
from jax.experimental.pallas import tpu as pltpu
from jax.sharding import PartitionSpec as P

EPS_NORM = 1e-06
EPS_GRN = 1e-06
LANES = 128
VMEM_BYTES = 20 * 1024 * 1024
REACH = 3
CHUNK = 4
NORM_ROWS = 4
IN_ORDER = (0, 1, 2, 3)
VECTORS = 56


def fill_columns(xp, xs, x, channels):
    height, reach_cols, blocks, lanes = xs.shape
    stride = reach_cols - 2 * REACH
    width = stride * blocks
    groups = lanes // LANES
    xp[...] = jnp.zeros(xp.shape, jnp.float32)

    def rows(n, carry):
        for k in range(2):
            r = 2 * n + k
            row = x[r].astype(jnp.float32)
            for g in range(groups):
                at = slice(g * LANES, (g + 1) * LANES)
                own = row[:, g * LANES : min((g + 1) * LANES, channels)]
                xp[k * groups + g, 8 : 8 + width, 0 : own.shape[1]] = own
                for q in range(reach_cols):
                    near = pl.ds(8 - REACH + q, blocks, stride=stride)
                    xs[r, q, :, at] = xp[k * groups + g, near, :]
        return carry

    lax.fori_loop(0, height // 2, rows, 0)


def conv(xs, cpar, cq):
    rows = xs.shape[0]
    height, stride, blocks, lanes = cq.shape
    span = 2 * REACH + 1
    above = (height - rows) // 2

    def group(g, carry):
        at = pl.ds(pl.multiple_of(g * LANES, LANES), LANES)

        def column(q, carry):
            bias = jnp.broadcast_to(cpar[VECTORS : VECTORS + 1, at], (blocks, LANES))
            acc = [None if above else bias] * height
            for j in range(span):
                kern = [
                    jnp.broadcast_to(cpar[i * span + j : i * span + j + 1, at], (blocks, LANES))
                    for i in range(span)
                ]
                for r in range(rows):
                    x_row = xs[r, q + j, :, at]
                    for i in range(span):
                        h = r + above + REACH - i
                        if 0 <= h < height:
                            term = kern[i] * x_row
                            acc[h] = term if acc[h] is None else acc[h] + term
            for h in range(height):
                cq[h, q, :, at] = acc[h]
            return carry

        return lax.fori_loop(0, stride, column, carry)

    lax.fori_loop(0, lanes // LANES, group, 0)


def norm(cq, cpar, xp, flat, skip=0):
    padded, stride, blocks, lanes = cq.shape
    height = padded - 2 * skip
    gain = cpar[VECTORS + 1 : VECTORS + 2, :]
    shift = cpar[VECTORS + 2 : VECTORS + 3, :]
    channels = flat.shape[2]
    width = stride * blocks
    groups = lanes // LANES
    inside = lax.broadcasted_iota(jnp.int32, (blocks, lanes), 1) < channels

    def rows(n, carry):
        for k in range(NORM_ROWS):
            h = NORM_ROWS * n + k
            for q in range(stride):
                v = cq[h + skip, q]
                mean = jnp.sum(v, axis=-1, keepdims=True) * (1.0 / channels)
                c = jnp.where(inside, v - mean, 0.0)
                var = jnp.sum(c * c, axis=-1, keepdims=True) * (1.0 / channels)
                c = c * lax.rsqrt(var + EPS_NORM) * gain + shift
                for g in range(groups):
                    at = slice(g * LANES, (g + 1) * LANES)
                    xp[k * groups + g, pl.ds(q, blocks, stride=stride), :] = c[:, at]
            for g in range(groups):
                at = slice(g * LANES, min((g + 1) * LANES, channels))
                flat[h, :, at] = xp[k * groups + g, 0:width, 0 : at.stop - at.start].astype(
                    jnp.bfloat16
                )
        return carry

    lax.fori_loop(0, height // NORM_ROWS, rows, 0)


def conv_norm(x, cpar, flat, xp, xs, cq):
    fill_columns(xp, xs, x, x.shape[2])
    conv(xs, cpar, cq)
    norm(cq, cpar, xp, flat)


def conv_scratch(rows, out_rows, width, lanes):
    return [
        pltpu.VMEM((NORM_ROWS * lanes // LANES, width + 16, LANES), jnp.float32),
        pltpu.VMEM((rows, width // 8 + 2 * REACH, 8, lanes), jnp.float32),
        pltpu.VMEM((out_rows, width // 8, 8, lanes), jnp.float32),
    ]


def gelu(v):
    return 0.5 * v * (1.0 + lax.erf(v * (0.5**0.5)))


def up(flat, w_in, bias, act, ssq):
    height, width, channels = flat.shape
    cells = height * width
    half = w_in.shape[1]
    step = 2 * LANES

    def units(start, count):
        raised = jnp.dot(
            flat[...].reshape(cells, channels),
            w_in[:, pl.ds(start, count)],
            preferred_element_type=jnp.float32,
        )
        active = gelu(raised + bias[0:1, pl.ds(start, count)]).astype(jnp.bfloat16)
        act[:, pl.ds(start, count)] = active
        wide = active.astype(jnp.float32)
        ssq[:, pl.ds(start, count)] = jnp.sum((wide * wide).reshape(cells // 8, 8, count), axis=0)

    def full(n, carry):
        units(pl.multiple_of(n * step, step), step)
        return carry

    whole = half // step
    lax.fori_loop(0, whole, full, 0)
    if half % step:
        units(whole * step, half % step)


def norm_scale(ssqs, fvec, scale):
    half = fvec.shape[2]
    magnitude = [jnp.sqrt(jnp.sum(ssq[...], axis=0, keepdims=True)) for ssq in ssqs]
    mean = jnp.sum(magnitude[0] + magnitude[1], axis=1, keepdims=True) * (0.5 / half)
    for which in range(2):
        ratio = magnitude[which] / (mean + EPS_GRN)
        scale[which] = fvec[which, 1:2, :] * ratio + 1.0


def down(x_rows, first_row, acts, outs, scale, fvec, cpar):
    _, width, channels = x_rows.shape
    cells = CHUNK * width
    at = pl.ds(pl.multiple_of(first_row * width, cells), cells)
    update = cpar[VECTORS + 3 : VECTORS + 4, :].astype(jnp.float32)
    for which in range(2):
        a = acts[which][at, :].astype(jnp.float32)
        hidden = (a * scale[which] + fvec[which, 2:3, :]).astype(jnp.bfloat16)
        update = update + jnp.dot(hidden, outs[which][...], preferred_element_type=jnp.float32)
    return (x_rows.astype(jnp.float32) + update.reshape(CHUNK, width, channels)).astype(
        jnp.bfloat16
    )


def down_all(x, acts, outs, scale, fvec, cvec, out):
    def rows(n, carry):
        at = pl.ds(n * CHUNK, CHUNK)
        out[at] = down(x[at], n * CHUNK, acts, outs, scale, fvec, cvec)
        return carry

    lax.fori_loop(0, x.shape[0] // CHUNK, rows, 0)


def prepare_kernel(part, bias_in, gamma, beta, fvec):
    half = fvec.shape[2]
    first = part[0] == 0
    for n, ref in enumerate((bias_in, gamma, beta)):
        v = ref[...].astype(jnp.float32)
        low, high = v[:, 0:half], v[:, half:]
        fvec[0, n : n + 1, :] = jnp.where(first, low, high)
        fvec[1, n : n + 1, :] = jnp.where(first, high, low)


def widen(raw, cpar):
    cpar[...] = jnp.zeros(cpar.shape, jnp.float32)
    cpar[:, 0 : raw.shape[1]] = raw[...].astype(jnp.float32)


def block_of(me, order, n):
    return n if order is None else me[0] ^ order[n]


def piece_kernel(section, piece, raw, part, xp, xs, cpar, *, on):
    @pl.when(section[0] == on)
    def _():
        widen(raw, cpar)
        fill_columns(xp, xs, piece, piece.shape[2])
        conv(xs, cpar, part)


def last_piece_kernel(section, me, *refs, order, on):
    count = len(order or IN_ORDER)
    pieces, parts = refs[:count], refs[count : 2 * count - 1]
    raw, x, flat, xp, xs, own, cq, cpar = refs[2 * count - 1 :]
    rows = pieces[0].shape[0]

    @pl.when(section[0] == on)
    def _():
        widen(raw, cpar)
        bias = cpar[VECTORS : VECTORS + 1, :].reshape(1, 1, 1, cq.shape[3])
        cq[...] = jnp.broadcast_to(bias, cq.shape)
        fill_columns(xp, xs, pieces[-1], x.shape[2])
        conv(xs, cpar, own)
        for n, (piece, part) in enumerate(zip(pieces, (*parts, own))):
            at = block_of(me, order, n) * rows
            x[pl.ds(at, rows)] = piece[...]
            cq[pl.ds(at, rows + 2 * REACH)] += part[...]
        norm(cq, cpar, xp, flat, REACH)


def conv_kernel(section, x, raw, flat, xp, xs, cq, cpar, *, tick):
    @pl.when(section[0] == tick)
    def _():
        widen(raw, cpar)
        conv_norm(x, cpar, flat, xp, xs, cq)


def up_first_kernel(section, flat, w_in, fvec, act, ssq, *, tick):
    @pl.when(section[0] == tick)
    def _():
        up(flat, w_in, fvec.at[0], act, ssq)


def up_second_kernel(section, flat, w_in, fvec, other, act, scale, ssq, *, tick):
    @pl.when(section[0] == tick)
    def _():
        up(flat, w_in, fvec.at[1], act, ssq)
        norm_scale((other, ssq), fvec, scale)


def first_down_kernel(section, x, act_a, act_b, out_a, out_b, scale, fvec, cpar, out):
    @pl.when(section[0] == 0)
    def _():
        down_all(x, (act_a, act_b), (out_a, out_b), scale, fvec, cpar, out)


def down_piece_kernel(
    section, me, x, act_a, act_b, out_a, out_b, scale, fvec, cpar, prev, out, *, order, tick, n
):
    first_row = block_of(me, order, n) * CHUNK
    at = pl.ds(first_row, CHUNK)

    @pl.when(section[0] == tick)
    def _():
        out[...] = down(x[at], first_row, (act_a, act_b), (out_a, out_b), scale, fvec, cpar)

    @pl.when(section[0] != tick)
    def _():
        out[...] = prev[at]


def mlp_kernel(section, x, flat, in_a, in_b, out_a, out_b, fvec, cpar, *refs, tick):
    *pieces, prev, out, act_a, act_b, ssq_a, ssq_b, scale = refs

    @pl.when(section[0] == tick)
    def _():
        up(flat, in_a, fvec.at[0], act_a, ssq_a)
        up(flat, in_b, fvec.at[1], act_b, ssq_b)
        norm_scale((ssq_a, ssq_b), fvec, scale)
        down_all(x, (act_a, act_b), (out_a, out_b), scale, fvec, cpar, out)

    @pl.when(section[0] == tick - 1)
    def _():
        for n, piece in enumerate(pieces):
            out[n * CHUNK : (n + 1) * CHUNK] = piece[...]

    @pl.when(section[0] < tick - 1)
    def _():
        out[...] = prev[...]


def conv_up_kernel(section, x, raw, in_a, in_b, fvec, *refs, tick):
    act_a, act_b, scale, xp, xs, cq, cpar, flat, ssq_a, ssq_b = refs

    @pl.when(section[0] == tick)
    def _():
        widen(raw, cpar)
        conv_norm(x, cpar, flat, xp, xs, cq)
        up(flat, in_a, fvec.at[0], act_a, ssq_a)
        up(flat, in_b, fvec.at[1], act_b, ssq_b)
        norm_scale((ssq_a, ssq_b), fvec, scale)


def place_kernel(me, *refs, order):
    *pieces, saved, sems = refs
    copies = [
        pltpu.make_async_copy(piece, saved.at[0, block_of(me, order, n), 0], sems.at[n])
        for n, piece in enumerate(pieces)
    ]
    for copy in copies:
        copy.start()
    for copy in copies:
        copy.wait()


SMEM = pl.BlockSpec(memory_space=pltpu.SMEM)
VMEM = pl.BlockSpec(memory_space=pltpu.VMEM)
HBM = pl.BlockSpec(memory_space=pltpu.HBM)


def call(kernel, name, args, out, specs=None, out_specs=None, scratch=(), flops=0, **static):
    if specs is None:
        specs = [SMEM if a.dtype == jnp.int32 else VMEM for a in args]
    if out_specs is None:
        out_specs = jax.tree.map(lambda _: VMEM, out)
    moved = sum(a.size * a.dtype.itemsize for a in args)
    return pl.pallas_call(
        functools.partial(kernel, **static),
        out_shape=out,
        in_specs=specs,
        out_specs=out_specs,
        scratch_shapes=list(scratch),
        compiler_params=pltpu.CompilerParams(vmem_limit_bytes=VMEM_BYTES),
        cost_estimate=pl.CostEstimate(flops=flops, bytes_accessed=moved, transcendentals=0),
        name=name,
    )(*args)


def shape(*dims, dtype=jnp.float32):
    return jax.ShapeDtypeStruct(dims, dtype)


def ssq_scratch(half):
    return pltpu.VMEM((8, half), jnp.float32)


def image_plan(
    inputs,
    depth_kernel,
    depth_bias,
    norm_gain,
    norm_bias,
    proj_in,
    bias_in,
    grn_gamma,
    grn_beta,
    proj_out,
    bias_out,
):
    sections = lax.axis_size("section")
    count = lax.axis_size("row")
    me = lax.axis_index("row").astype(jnp.int32)
    section = lax.axis_index("section").astype(jnp.int32).reshape(1)
    me_ref = me.reshape(1)
    part = lax.axis_index("dp").astype(jnp.int32).reshape(1)
    _, _, rows, width, channels = inputs.shape
    height = rows * count
    cells = height * width
    lanes = -(-channels // LANES) * LANES
    half = proj_in.shape[2]
    span = depth_kernel.shape[1]
    order = (0, 2, 3, 1)
    bf16 = jnp.bfloat16
    whole = shape(height, width, channels, dtype=bf16)
    piece_shape = shape(rows, width, channels, dtype=bf16)
    act_shape = shape(cells, half, dtype=bf16)
    scale_shape = shape(2, 1, half)
    matmul = 2 * cells * channels * half

    helper, source = 1, sections - 1
    pieces = []
    for by in order:
        piece = lax.dynamic_index_in_dim(inputs, me ^ by, 0, keepdims=False)[0]
        if by:
            pairs = [(source * count + (p ^ by), helper * count + p) for p in range(count)]
            piece = lax.ppermute(piece, ("section", "row"), pairs)
        pieces.append(piece)

    def other_half(x, which):
        pairs = [(2 * s + p, 2 * s + 1 - p) for s in which for p in range(2)]
        return lax.ppermute(x, ("section", "dp"), pairs)

    w_in, w_out = proj_in[0], proj_out[0]
    even = range(0, sections, 2)
    odd = range(1, sections, 2)
    other_in = other_half(w_in, even)
    other_out = other_half(w_out, even)

    fvec = call(
        prepare_kernel, "prepare", (part, bias_in, grn_gamma, grn_beta), shape(2, 3, half)
    )
    taps = depth_kernel.reshape(span * span, channels)
    gap = jnp.zeros((VECTORS - span * span, channels), bf16)
    cpar = jnp.concatenate(
        [taps, gap, depth_bias, norm_gain, norm_bias, bias_out, jnp.zeros((4, channels), bf16)]
    )
    wide_cpar = pltpu.VMEM((VECTORS + 8, lanes), jnp.float32)

    def send(x, start, end):
        return lax.ppermute(x, "section", [(start, end)])

    def conv_pieces(pieces, cpar, order, on):
        out_rows = rows + 2 * REACH
        scratch = conv_scratch(rows, out_rows, width, lanes)
        parts = []
        for piece in pieces[:-1]:
            if parts:
                piece, parts[-1] = lax.optimization_barrier((piece, parts[-1]))
            part = call(
                piece_kernel,
                "conv_piece",
                (section, piece, cpar),
                shape(out_rows, width // 8, 8, lanes),
                scratch=scratch[:2] + [wide_cpar],
                on=on,
            )
            parts.append(part)
        return call(
            last_piece_kernel,
            "last_piece",
            (section, me_ref, *pieces, *parts, cpar),
            (whole, whole),
            scratch=scratch + [conv_scratch(1, height + 2 * REACH, width, lanes)[2], wide_cpar],
            order=order,
            on=on,
        )

    def up_own(flat, tick):
        return call(
            up_first_kernel,
            "up_own",
            (section, flat, w_in, fvec),
            (act_shape, shape(8, half)),
            flops=matmul,
            tick=tick,
        )

    def up_other(flat, other_in, ssq, tick):
        return call(
            up_second_kernel,
            "up_other",
            (section, flat, other_in, fvec, ssq),
            (act_shape, scale_shape),
            scratch=[ssq_scratch(half)],
            flops=matmul,
            tick=tick,
        )

    def down_piece(x, acts, other_out, prev, order, tick, n):
        act_a, act_b, scale = acts
        return call(
            down_piece_kernel,
            "down_piece",
            (section, me_ref, x, act_a, act_b, w_out, other_out, scale, fvec, cpar, prev),
            piece_shape,
            flops=2 * matmul // count,
            order=order,
            tick=tick,
            n=n,
        )

    x, flat = conv_pieces(pieces, send(cpar, 0, helper), order, helper)
    flat, other_in = lax.optimization_barrier((flat, other_in))
    flat = send(flat, helper, 0)
    x, other_out = lax.optimization_barrier((x, other_out))
    x = send(x, helper, 0)
    act_a, ssq = up_own(flat, 0)
    act_b, scale = up_other(flat, other_in, ssq, 0)
    result = call(
        first_down_kernel,
        "down",
        (section, x, act_a, act_b, w_out, other_out, scale, fvec, cpar),
        whole,
        flops=2 * matmul,
    )
    x = send(result, 0, 1)
    late_in, late_out, result = lax.optimization_barrier((w_in, w_out, result))
    odd_in = other_half(late_in, odd)
    odd_out = other_half(late_out, odd)
    flat = call(
        conv_kernel,
        "conv",
        (section, x, cpar),
        whole,
        scratch=conv_scratch(height, height, width, lanes) + [wide_cpar],
        tick=1,
    )
    act_a, ssq = up_own(flat, 1)
    acts = (act_a, *up_other(flat, odd_in, ssq, 1))
    kept = [down_piece(x, acts, odd_out, result, None, 1, n) for n in range(count)]
    x, flat = conv_pieces([send(piece, 1, 2) for piece in kept], cpar, None, 2)
    result = call(
        mlp_kernel,
        "mlp",
        (section, x, flat, w_in, other_in, w_out, other_out, fvec, cpar, *kept, result),
        whole,
        scratch=[pltpu.VMEM((cells, half), bf16)] * 2
        + [ssq_scratch(half)] * 2
        + [pltpu.VMEM((2, 1, half), jnp.float32)],
        flops=4 * matmul,
        tick=2,
    )
    x = send(result, 2, 3)
    acts = call(
        conv_up_kernel,
        "conv_up",
        (section, x, cpar, w_in, odd_in, fvec),
        (act_shape, act_shape, scale_shape),
        scratch=conv_scratch(height, height, width, lanes)
        + [wide_cpar]
        + [pltpu.VMEM((height, width, channels), bf16)]
        + [ssq_scratch(half)] * 2,
        flops=2 * matmul,
        tick=3,
    )
    done = []
    for n in (1, 2, 3, 0):
        piece = down_piece(x, acts, odd_out, result, order, 3, n)
        if n:
            piece = lax.ppermute(piece, "row", [(p, p ^ order[n]) for p in range(count)])
        done.append(piece)
    return call(
        place_kernel,
        "place",
        (me_ref, done[3], *done[:3]),
        shape(1, count, 1, rows, width, channels, dtype=bf16),
        out_specs=HBM,
        scratch=[pltpu.SemaphoreType.DMA((count,))],
        order=order,
    )


def extended(cells, sides, width):
    for axis, dim in sides:
        count = lax.axis_size(axis)
        ends = count - 1
        head = lax.slice_in_dim(cells, 0, width, axis=dim)
        tail = lax.slice_in_dim(cells, cells.shape[dim] - width, cells.shape[dim], axis=dim)
        cells = jnp.concatenate(
            [
                lax.ppermute(tail, axis, [(i, (i + 1) % count) for i in range(ends)]),
                cells,
                lax.ppermute(head, axis, [((i + 1) % count, i) for i in range(ends)]),
            ],
            axis=dim,
        )
    return cells


def depthwise(padded, kernel, bias_term):
    channels = padded.shape[-1]
    conv_out = lax.conv_general_dilated(
        padded.astype(jnp.float32),
        kernel.astype(jnp.float32)[:, :, None, :],
        (1, 1),
        "VALID",
        dimension_numbers=("NHWC", "HWIO", "NHWC"),
        feature_group_count=channels,
        precision=lax.Precision.HIGHEST,
    )
    return conv_out + bias_term.astype(jnp.float32)


def conv_block(current, params):
    (
        depth_kernel,
        depth_bias,
        norm_gain,
        norm_bias,
        proj_in,
        bias_in,
        grn_gamma,
        grn_beta,
        proj_out,
        bias_out,
    ) = params
    num_items, num_rows, num_cols, channels = current.shape
    padded = extended(current, (("row", 1),), REACH)
    padded = jnp.pad(padded, ((0, 0), (0, 0), (REACH, REACH), (0, 0)))
    conv_out = depthwise(padded, depth_kernel, depth_bias)
    center = conv_out - jnp.mean(conv_out, axis=-1, keepdims=True)
    spread = jnp.mean(center * center, axis=-1, keepdims=True)
    normed = (
        center * lax.rsqrt(spread + EPS_NORM) * norm_gain.astype(jnp.float32)
        + norm_bias.astype(jnp.float32)
    ).astype(jnp.bfloat16)
    flat_rows = normed.reshape(num_items * num_rows * num_cols, channels)
    raised = jnp.dot(flat_rows, proj_in, preferred_element_type=jnp.float32) + bias_in.astype(
        jnp.float32
    )
    active = jax.nn.gelu(raised, approximate=False).astype(jnp.bfloat16)
    grouped = active.reshape(num_items, num_rows * num_cols, -1).astype(jnp.float32)
    local_sq = jnp.sum(grouped * grouped, axis=1)
    total_sq = lax.psum(local_sq, "row")
    magnitude = jnp.sqrt(total_sq)
    grn_ratio = magnitude / (jnp.mean(magnitude, axis=-1, keepdims=True) + EPS_GRN)
    hidden = (
        grn_gamma.astype(jnp.float32) * grouped * grn_ratio[:, None, :]
        + grn_beta.astype(jnp.float32)
        + grouped
    ).astype(jnp.bfloat16)
    update = jnp.dot(
        hidden.reshape(num_items * num_rows * num_cols, -1),
        proj_out,
        preferred_element_type=jnp.float32,
    ) + bias_out.astype(jnp.float32)
    return (
        current.astype(jnp.float32) + update.reshape(num_items, num_rows, num_cols, channels)
    ).astype(jnp.bfloat16)


def rows_plan(inputs, *weights):
    (
        depth_kernel,
        depth_bias,
        norm_gain,
        norm_bias,
        proj_in,
        bias_in,
        grn_gamma,
        grn_beta,
        proj_out,
        bias_out,
    ) = weights
    proj_in = lax.all_gather(proj_in, "dp", axis=2, tiled=True)
    proj_out = lax.all_gather(proj_out, "dp", axis=1, tiled=True)
    own_params = tuple(
        w[0]
        for w in (
            depth_kernel,
            depth_bias,
            norm_gain,
            norm_bias,
            proj_in,
            bias_in,
            grn_gamma,
            grn_beta,
            proj_out,
            bias_out,
        )
    )
    sections = lax.axis_size("section")
    section_index = lax.axis_index("section")
    num_micro = inputs.shape[0]
    num_ticks = num_micro + sections - 1
    arriving = jnp.zeros_like(inputs[0])
    saved = jnp.zeros_like(inputs)
    for tick_index in range(num_ticks):
        fresh_input = inputs[min(tick_index, num_micro - 1)]
        current = jnp.where(section_index == 0, fresh_input, arriving)
        produced = conv_block(current, own_params)
        slot_index = tick_index - section_index
        is_valid = jnp.logical_and(slot_index >= 0, slot_index < num_micro)
        safe_slot = jnp.clip(slot_index, 0, num_micro - 1)
        previous = lax.dynamic_index_in_dim(saved, safe_slot, 0, keepdims=False)
        saved = lax.dynamic_update_index_in_dim(
            saved, jnp.where(is_valid, produced, previous), safe_slot, 0
        )
        if tick_index + 1 < num_ticks:
            arriving = lax.ppermute(
                produced, "section", [(i, i + 1) for i in range(sections - 1)]
            )
    return saved[None]


def on_device(inputs, *weights):
    num_micro, images, local_rows, width, _ = inputs.shape
    one_image_each = (
        images == 1
        and lax.axis_size("row") == num_micro == 4
        and lax.axis_size("dp") == 2
        and lax.axis_size("section") == 4
        and local_rows % 4 == 0
        and width % 16 == 0
    )
    plan = image_plan if one_image_each else rows_plan
    return plan(inputs, *weights)


def solution(mesh):
    return jax.shard_map(
        on_device,
        mesh=mesh,
        in_specs=(
            P(None, "dp", "row", None, None),
            P("section", None, None, None),
            P("section", None),
            P("section", None),
            P("section", None),
            P("section", None, "dp"),
            P("section", None),
            P("section", None),
            P("section", None),
            P("section", "dp", None),
            P("section", None),
        ),
        out_specs=P("section", None, "dp", "row", None, None),
        check_vma=False,
    )
```

```python
import functools

import jax
import jax.numpy as jnp
from jax import lax
from jax.experimental import pallas as pl
from jax.experimental.pallas import tpu as pltpu
from jax.sharding import PartitionSpec as P

EPS_NORM = 1e-06
EPS_GRN = 1e-06
LANES = 128
VMEM_BYTES = 20 * 1024 * 1024
REACH = 3
CHUNK = 4
NORM_ROWS = 4
IN_ORDER = (0, 1, 2, 3)
VECTORS = 56


def fill_columns(xp, xs, x, channels, first=0):
    height, reach_cols, blocks, lanes = xs.shape
    stride = reach_cols - 2 * REACH
    width = stride * blocks
    groups = lanes // LANES
    xp[...] = jnp.zeros(xp.shape, jnp.float32)

    def rows(n, carry):
        for k in range(2):
            r = 2 * n + k
            row = x[first + r].astype(jnp.float32)
            for g in range(groups):
                at = slice(g * LANES, (g + 1) * LANES)
                own = row[:, g * LANES : min((g + 1) * LANES, channels)]
                xp[k * groups + g, 8 : 8 + width, 0 : own.shape[1]] = own
                for q in range(reach_cols):
                    near = pl.ds(8 - REACH + q, blocks, stride=stride)
                    xs[r, q, :, at] = xp[k * groups + g, near, :]
        return carry

    lax.fori_loop(0, height // 2, rows, 0)


def conv(xs, cpar, cq, above=0):
    rows = xs.shape[0]
    height, stride, blocks, lanes = cq.shape
    span = 2 * REACH + 1

    def group(g, carry):
        at = pl.ds(pl.multiple_of(g * LANES, LANES), LANES)

        def column(q, carry):
            bias = jnp.broadcast_to(cpar[VECTORS : VECTORS + 1, at], (blocks, LANES))
            acc = [None if above > 0 else bias] * height
            for j in range(span):
                kern = [
                    jnp.broadcast_to(cpar[i * span + j : i * span + j + 1, at], (blocks, LANES))
                    for i in range(span)
                ]
                for r in range(rows):
                    taken = [i for i in range(span) if 0 <= r + above + REACH - i < height]
                    if not taken:
                        continue
                    x_row = xs[r, q + j, :, at]
                    for i in taken:
                        h = r + above + REACH - i
                        term = kern[i] * x_row
                        acc[h] = term if acc[h] is None else acc[h] + term
            for h in range(height):
                cq[h, q, :, at] = acc[h]
            return carry

        return lax.fori_loop(0, stride, column, carry)

    lax.fori_loop(0, lanes // LANES, group, 0)


def norm(cq, cpar, xp, flat, skip=0):
    padded, stride, blocks, lanes = cq.shape
    height = padded - 2 * skip
    gain = cpar[VECTORS + 1 : VECTORS + 2, :]
    shift = cpar[VECTORS + 2 : VECTORS + 3, :]
    channels = flat.shape[2]
    width = stride * blocks
    groups = lanes // LANES
    inside = lax.broadcasted_iota(jnp.int32, (blocks, lanes), 1) < channels

    def rows(n, carry):
        for k in range(NORM_ROWS):
            h = NORM_ROWS * n + k
            for q in range(stride):
                v = cq[h + skip, q]
                mean = jnp.sum(v, axis=-1, keepdims=True) * (1.0 / channels)
                c = jnp.where(inside, v - mean, 0.0)
                var = jnp.sum(c * c, axis=-1, keepdims=True) * (1.0 / channels)
                c = c * lax.rsqrt(var + EPS_NORM) * gain + shift
                for g in range(groups):
                    at = slice(g * LANES, (g + 1) * LANES)
                    xp[k * groups + g, pl.ds(q, blocks, stride=stride), :] = c[:, at]
            for g in range(groups):
                at = slice(g * LANES, min((g + 1) * LANES, channels))
                flat[h, :, at] = xp[k * groups + g, 0:width, 0 : at.stop - at.start].astype(
                    jnp.bfloat16
                )
        return carry

    lax.fori_loop(0, height // NORM_ROWS, rows, 0)


def conv_norm(x, cpar, flat, xp, xs, cq):
    fill_columns(xp, xs, x, x.shape[2])
    conv(xs, cpar, cq)
    norm(cq, cpar, xp, flat)


def conv_norm_half(x, cpar, flat, xp, xs, cq, lower):
    height = x.shape[0]
    first = height - xs.shape[0] if lower else 0
    fill_columns(xp, xs, x, x.shape[2], first)
    conv(xs, cpar, cq, first - height // 2 if lower else 0)
    norm(cq, cpar, xp, flat)


def conv_scratch(rows, out_rows, width, lanes):
    return [
        pltpu.VMEM((NORM_ROWS * lanes // LANES, width + 16, LANES), jnp.float32),
        pltpu.VMEM((rows, width // 8 + 2 * REACH, 8, lanes), jnp.float32),
        pltpu.VMEM((out_rows, width // 8, 8, lanes), jnp.float32),
    ]


def gelu(v):
    return 0.5 * v * (1.0 + lax.erf(v * (0.5**0.5)))


def up(flat, w_in, bias, act, ssq):
    height, width, channels = flat.shape
    cells = height * width
    half = w_in.shape[1]
    step = 2 * LANES

    def units(start, count):
        raised = jnp.dot(
            flat[...].reshape(cells, channels),
            w_in[:, pl.ds(start, count)],
            preferred_element_type=jnp.float32,
        )
        active = gelu(raised + bias[0:1, pl.ds(start, count)]).astype(jnp.bfloat16)
        act[:, pl.ds(start, count)] = active
        wide = active.astype(jnp.float32)
        ssq[:, pl.ds(start, count)] = jnp.sum((wide * wide).reshape(cells // 8, 8, count), axis=0)

    def full(n, carry):
        units(pl.multiple_of(n * step, step), step)
        return carry

    whole = half // step
    lax.fori_loop(0, whole, full, 0)
    if half % step:
        units(whole * step, half % step)


def norm_scale(ssqs, fvec, scale):
    half = fvec.shape[2]
    magnitude = [jnp.sqrt(jnp.sum(ssq[...], axis=0, keepdims=True)) for ssq in ssqs]
    mean = jnp.sum(magnitude[0] + magnitude[1], axis=1, keepdims=True) * (0.5 / half)
    for which in range(2):
        ratio = magnitude[which] / (mean + EPS_GRN)
        scale[which] = fvec[which, 1:2, :] * ratio + 1.0


def down(x_rows, first_row, acts, outs, scale, fvec, cpar):
    _, width, channels = x_rows.shape
    cells = CHUNK * width
    at = pl.ds(pl.multiple_of(first_row * width, 16), cells)
    update = cpar[VECTORS + 3 : VECTORS + 4, 0:channels]
    for which in range(2):
        a = acts[which][at, :].astype(jnp.float32)
        hidden = (a * scale[which] + fvec[which, 2:3, :]).astype(jnp.bfloat16)
        update = update + jnp.dot(hidden, outs[which][...], preferred_element_type=jnp.float32)
    return (x_rows.astype(jnp.float32) + update.reshape(CHUNK, width, channels)).astype(
        jnp.bfloat16
    )


def down_all(x, acts, outs, scale, fvec, cvec, out):
    def rows(n, carry):
        at = pl.ds(n * CHUNK, CHUNK)
        out[at] = down(x[at], n * CHUNK, acts, outs, scale, fvec, cvec)
        return carry

    lax.fori_loop(0, x.shape[0] // CHUNK, rows, 0)


def prepare_kernel(part, kernel, *refs):
    vectors, (cpar, fvec), (held, *staged), sems = refs[:7], refs[7:9], refs[9:-1], refs[-1]
    moves = [(kernel, held), *zip(vectors, staged)]
    copies = [pltpu.make_async_copy(a, b, sems.at[n]) for n, (a, b) in enumerate(moves)]
    for copy in copies:
        copy.start()
    cpar[...] = jnp.zeros(cpar.shape, jnp.float32)
    for copy in copies:
        copy.wait()
    channels = kernel.shape[3]
    span = kernel.shape[1]
    half = fvec.shape[2]
    for i in range(span):
        cpar[i * span : (i + 1) * span, 0:channels] = held[0, i].astype(jnp.float32)
    for n in range(4):
        cpar[VECTORS + n : VECTORS + n + 1, 0:channels] = staged[n][...].astype(jnp.float32)
    first = part[0] == 0
    for n in range(3):
        v = staged[4 + n][...].astype(jnp.float32)
        low, high = v[:, 0:half], v[:, half:]
        fvec[0, n : n + 1, :] = jnp.where(first, low, high)
        fvec[1, n : n + 1, :] = jnp.where(first, high, low)


def block_of(me, order, n):
    return n if order is None else me[0] ^ order[n]


def piece_kernel(section, piece, cpar, part, xp, xs, *, on):
    @pl.when(section[0] == on)
    def _():
        fill_columns(xp, xs, piece, piece.shape[2])
        conv(xs, cpar, part, REACH)


def last_piece_kernel(section, me, *refs, order, on):
    count = len(order or IN_ORDER)
    pieces, parts = refs[:count], refs[count : 2 * count - 1]
    cpar, x, flat, xp, xs, own, cq = refs[2 * count - 1 :]
    rows = pieces[0].shape[0]

    @pl.when(section[0] == on)
    def _():
        bias = cpar[VECTORS : VECTORS + 1, :].reshape(1, 1, 1, cq.shape[3])
        cq[...] = jnp.broadcast_to(bias, cq.shape)
        fill_columns(xp, xs, pieces[-1], x.shape[2])
        conv(xs, cpar, own, REACH)
        for n, (piece, part) in enumerate(zip(pieces, (*parts, own))):
            at = block_of(me, order, n) * rows
            x[pl.ds(at, rows)] = piece[...]
            cq[pl.ds(at, rows + 2 * REACH)] += part[...]
        norm(cq, cpar, xp, flat, REACH)


def conv_kernel(section, x, cpar, flat, xp, xs, cq, *, tick):
    @pl.when(section[0] == tick)
    def _():
        conv_norm(x, cpar, flat, xp, xs, cq)


def up_first_kernel(section, flat, w_in, fvec, act, ssq, *, tick):
    @pl.when(section[0] == tick)
    def _():
        up(flat, w_in, fvec.at[0], act, ssq)


def up_second_kernel(section, flat, w_in, fvec, other, act, scale, ssq, *, tick):
    @pl.when(section[0] == tick)
    def _():
        up(flat, w_in, fvec.at[1], act, ssq)
        norm_scale((other, ssq), fvec, scale)


def first_down_kernel(section, x, act_a, act_b, out_a, out_b, scale, fvec, cpar, out):
    @pl.when(section[0] == 0)
    def _():
        down_all(x, (act_a, act_b), (out_a, out_b), scale, fvec, cpar, out)


def down_piece_kernel(
    section, me, x, out_a, out_b, scale, fvec, cpar, prev, *refs, order, tick, n
):
    *acts, out = refs
    block = block_of(me, order, n)
    at = pl.ds(block * CHUNK, CHUNK)
    parts = len(acts) // 2
    blocks = prev.shape[0] // CHUNK // parts

    for part in range(parts):

        @pl.when(jnp.logical_and(section[0] == tick, block // blocks == part))
        def _():
            first_row = (block - part * blocks) * CHUNK
            pair = acts[2 * part : 2 * part + 2]
            out[...] = down(x[at], first_row, pair, (out_a, out_b), scale, fvec, cpar)

    @pl.when(section[0] != tick)
    def _():
        out[...] = prev[at]


def mlp_kernel(section, x, flat, in_a, in_b, out_a, out_b, fvec, cpar, *refs, tick):
    *pieces, prev, out, act_a, act_b, ssq_a, ssq_b, scale = refs

    @pl.when(section[0] == tick)
    def _():
        up(flat, in_a, fvec.at[0], act_a, ssq_a)
        up(flat, in_b, fvec.at[1], act_b, ssq_b)
        norm_scale((ssq_a, ssq_b), fvec, scale)
        down_all(x, (act_a, act_b), (out_a, out_b), scale, fvec, cpar, out)

    @pl.when(section[0] == tick - 1)
    def _():
        for n, piece in enumerate(pieces):
            out[n * CHUNK : (n + 1) * CHUNK] = piece[...]

    @pl.when(section[0] < tick - 1)
    def _():
        out[...] = prev[...]


def conv_lower_kernel(section, x, cpar, flat, xp, xs, cq, *, on):
    @pl.when(section[0] == on)
    def _():
        conv_norm_half(x, cpar, flat, xp, xs, cq, True)


def conv_up_upper_kernel(section, x, cpar, in_a, in_b, fvec, *refs, tick):
    act_a, act_b, ssq_a, ssq_b, xp, xs, cq, flat = refs

    @pl.when(section[0] == tick)
    def _():
        conv_norm_half(x, cpar, flat, xp, xs, cq, False)
        up(flat, in_a, fvec.at[0], act_a, ssq_a)
        up(flat, in_b, fvec.at[1], act_b, ssq_b)


def up_lower_kernel(section, flat, in_a, in_b, fvec, upper_a, upper_b, *refs, tick):
    act_a, act_b, scale, ssq_a, ssq_b = refs

    @pl.when(section[0] == tick)
    def _():
        up(flat, in_a, fvec.at[0], act_a, ssq_a)
        up(flat, in_b, fvec.at[1], act_b, ssq_b)
        ssq_a[...] += upper_a[...]
        ssq_b[...] += upper_b[...]
        norm_scale((ssq_a, ssq_b), fvec, scale)


def place_kernel(me, *refs, order):
    *pieces, saved, sems = refs
    copies = [
        pltpu.make_async_copy(piece, saved.at[0, block_of(me, order, n), 0], sems.at[n])
        for n, piece in enumerate(pieces)
    ]
    for copy in copies:
        copy.start()
    for copy in copies:
        copy.wait()


SMEM = pl.BlockSpec(memory_space=pltpu.SMEM)
VMEM = pl.BlockSpec(memory_space=pltpu.VMEM)
HBM = pl.BlockSpec(memory_space=pltpu.HBM)


def call(kernel, name, args, out, specs=None, out_specs=None, scratch=(), flops=0, **static):
    if specs is None:
        specs = [SMEM if a.dtype == jnp.int32 else VMEM for a in args]
    if out_specs is None:
        out_specs = jax.tree.map(lambda _: VMEM, out)
    moved = sum(a.size * a.dtype.itemsize for a in args)
    return pl.pallas_call(
        functools.partial(kernel, **static),
        out_shape=out,
        in_specs=specs,
        out_specs=out_specs,
        scratch_shapes=list(scratch),
        compiler_params=pltpu.CompilerParams(vmem_limit_bytes=VMEM_BYTES),
        cost_estimate=pl.CostEstimate(flops=flops, bytes_accessed=moved, transcendentals=0),
        name=name,
    )(*args)


def shape(*dims, dtype=jnp.float32):
    return jax.ShapeDtypeStruct(dims, dtype)


def ssq_scratch(half):
    return pltpu.VMEM((8, half), jnp.float32)


def image_plan(
    inputs,
    depth_kernel,
    depth_bias,
    norm_gain,
    norm_bias,
    proj_in,
    bias_in,
    grn_gamma,
    grn_beta,
    proj_out,
    bias_out,
):
    sections = lax.axis_size("section")
    count = lax.axis_size("row")
    me = lax.axis_index("row").astype(jnp.int32)
    section = lax.axis_index("section").astype(jnp.int32).reshape(1)
    me_ref = me.reshape(1)
    part = lax.axis_index("dp").astype(jnp.int32).reshape(1)
    _, _, rows, width, channels = inputs.shape
    height = rows * count
    cells = height * width
    lanes = -(-channels // LANES) * LANES
    half = proj_in.shape[2]
    span = depth_kernel.shape[1]
    order = (0, 2, 3, 1)
    bf16 = jnp.bfloat16
    whole = shape(height, width, channels, dtype=bf16)
    piece_shape = shape(rows, width, channels, dtype=bf16)
    act_shape = shape(cells, half, dtype=bf16)
    scale_shape = shape(2, 1, half)
    matmul = 2 * cells * channels * half

    helper = 1
    sources = {1: sections - 1, 2: sections - 1, 3: helper}
    pieces = []
    for by in order:
        piece = lax.dynamic_index_in_dim(inputs, me ^ by, 0, keepdims=False)[0]
        if by:
            pairs = [(sources[by] * count + (p ^ by), helper * count + p) for p in range(count)]
            piece = lax.ppermute(piece, ("section", "row"), pairs)
        pieces.append(piece)

    def other_half(x, which):
        pairs = [(2 * s + p, 2 * s + 1 - p) for s in which for p in range(2)]
        return lax.ppermute(x, ("section", "dp"), pairs)

    w_in, w_out = proj_in[0], proj_out[0]
    even = range(0, sections, 2)
    odd = range(1, sections, 2)
    other_in = other_half(w_in, even)
    other_out = other_half(w_out, even)

    held = (
        depth_kernel, depth_bias, norm_gain, norm_bias, bias_out, bias_in, grn_gamma, grn_beta
    )
    cpar, fvec = call(
        prepare_kernel,
        "prepare",
        (part, *held),
        (shape(VECTORS + 8, lanes), shape(2, 3, half)),
        specs=[SMEM] + [HBM] * len(held),
        scratch=[pltpu.VMEM(v.shape, v.dtype) for v in held]
        + [pltpu.SemaphoreType.DMA((len(held),))],
    )

    def send(x, start, end):
        return lax.ppermute(x, "section", [(start, end)])

    def conv_pieces(pieces, cpar, order, on):
        out_rows = rows + 2 * REACH
        scratch = conv_scratch(rows, out_rows, width, lanes)
        parts = []
        for piece in pieces[:-1]:
            if parts:
                piece, parts[-1] = lax.optimization_barrier((piece, parts[-1]))
            part = call(
                piece_kernel,
                "conv_piece",
                (section, piece, cpar),
                shape(out_rows, width // 8, 8, lanes),
                scratch=scratch[:2],
                on=on,
            )
            parts.append(part)
        return call(
            last_piece_kernel,
            "last_piece",
            (section, me_ref, *pieces, *parts, cpar),
            (whole, whole),
            scratch=scratch + [conv_scratch(1, height + 2 * REACH, width, lanes)[2]],
            order=order,
            on=on,
        )

    def up_own(flat, tick):
        return call(
            up_first_kernel,
            "up_own",
            (section, flat, w_in, fvec),
            (act_shape, shape(8, half)),
            flops=matmul,
            tick=tick,
        )

    def up_other(flat, other_in, ssq, tick):
        return call(
            up_second_kernel,
            "up_other",
            (section, flat, other_in, fvec, ssq),
            (act_shape, scale_shape),
            scratch=[ssq_scratch(half)],
            flops=matmul,
            tick=tick,
        )

    def down_piece(x, acts, scale, other_out, prev, order, tick, n):
        return call(
            down_piece_kernel,
            "down_piece",
            (section, me_ref, x, w_out, other_out, scale, fvec, cpar, prev, *acts),
            piece_shape,
            flops=2 * matmul // count,
            order=order,
            tick=tick,
            n=n,
        )

    lent_cpar = lax.ppermute(cpar, "section", [(0, helper), (3, 2)])
    x, flat = conv_pieces(pieces, lent_cpar, order, helper)
    flat, other_in = lax.optimization_barrier((flat, other_in))
    flat, x = send(flat, helper, 0), send(x, helper, 0)
    act_a, ssq = up_own(flat, 0)
    act_b, scale = up_other(flat, other_in, ssq, 0)
    result = call(
        first_down_kernel,
        "down",
        (section, x, act_a, act_b, w_out, other_out, scale, fvec, cpar),
        whole,
        flops=2 * matmul,
    )
    x = send(result, 0, 1)
    late_in, late_out, result = lax.optimization_barrier((w_in, w_out, result))
    odd_in = other_half(late_in, odd)
    odd_out = other_half(late_out, odd)
    flat = call(
        conv_kernel,
        "conv",
        (section, x, cpar),
        whole,
        scratch=conv_scratch(height, height, width, lanes),
        tick=1,
    )
    act_a, ssq = up_own(flat, 1)
    act_b, scale = up_other(flat, odd_in, ssq, 1)
    kept = [down_piece(x, (act_a, act_b), scale, odd_out, result, None, 1, n) for n in range(count)]
    x, flat = conv_pieces([send(piece, 1, 2) for piece in kept], cpar, None, 2)
    result = call(
        mlp_kernel,
        "mlp",
        (section, x, flat, w_in, other_in, w_out, other_out, fvec, cpar, *kept, result),
        whole,
        scratch=[pltpu.VMEM((cells, half), bf16)] * 2
        + [ssq_scratch(half)] * 2
        + [pltpu.VMEM((2, 1, half), jnp.float32)],
        flops=4 * matmul,
        tick=2,
    )
    x = send(result, 2, 3)
    half_map = shape(height // 2, width, channels, dtype=bf16)
    half_act = shape(cells // 2, half, dtype=bf16)
    half_scratch = conv_scratch(height // 2 + 4, height // 2, width, lanes)
    lower = call(
        conv_lower_kernel,
        "conv_lower",
        (section, result, lent_cpar),
        half_map,
        scratch=half_scratch,
        on=2,
    )
    lower = send(lower, 2, 3)
    upper_a, upper_b, ssq_a, ssq_b = call(
        conv_up_upper_kernel,
        "conv_up_upper",
        (section, x, cpar, w_in, odd_in, fvec),
        (half_act, half_act, shape(8, half), shape(8, half)),
        scratch=half_scratch + [pltpu.VMEM((height // 2, width, channels), bf16)],
        flops=matmul,
        tick=3,
    )
    lower_a, lower_b, scale = call(
        up_lower_kernel,
        "up_lower",
        (section, lower, w_in, odd_in, fvec, ssq_a, ssq_b),
        (half_act, half_act, scale_shape),
        scratch=[ssq_scratch(half)] * 2,
        flops=matmul,
        tick=3,
    )
    acts = (upper_a, upper_b, lower_a, lower_b)
    done = []
    for n in (1, 2, 3, 0):
        piece = down_piece(x, acts, scale, odd_out, result, order, 3, n)
        if n:
            piece = lax.ppermute(piece, "row", [(p, p ^ order[n]) for p in range(count)])
        done.append(piece)
    return call(
        place_kernel,
        "place",
        (me_ref, done[3], *done[:3]),
        shape(1, count, 1, rows, width, channels, dtype=bf16),
        out_specs=HBM,
        scratch=[pltpu.SemaphoreType.DMA((count,))],
        order=order,
    )


def extended(cells, sides, width):
    for axis, dim in sides:
        count = lax.axis_size(axis)
        ends = count - 1
        head = lax.slice_in_dim(cells, 0, width, axis=dim)
        tail = lax.slice_in_dim(cells, cells.shape[dim] - width, cells.shape[dim], axis=dim)
        cells = jnp.concatenate(
            [
                lax.ppermute(tail, axis, [(i, (i + 1) % count) for i in range(ends)]),
                cells,
                lax.ppermute(head, axis, [((i + 1) % count, i) for i in range(ends)]),
            ],
            axis=dim,
        )
    return cells


def depthwise(padded, kernel, bias_term):
    channels = padded.shape[-1]
    conv_out = lax.conv_general_dilated(
        padded.astype(jnp.float32),
        kernel.astype(jnp.float32)[:, :, None, :],
        (1, 1),
        "VALID",
        dimension_numbers=("NHWC", "HWIO", "NHWC"),
        feature_group_count=channels,
        precision=lax.Precision.HIGHEST,
    )
    return conv_out + bias_term.astype(jnp.float32)


def conv_block(current, params):
    (
        depth_kernel,
        depth_bias,
        norm_gain,
        norm_bias,
        proj_in,
        bias_in,
        grn_gamma,
        grn_beta,
        proj_out,
        bias_out,
    ) = params
    num_items, num_rows, num_cols, channels = current.shape
    padded = extended(current, (("row", 1),), REACH)
    padded = jnp.pad(padded, ((0, 0), (0, 0), (REACH, REACH), (0, 0)))
    conv_out = depthwise(padded, depth_kernel, depth_bias)
    center = conv_out - jnp.mean(conv_out, axis=-1, keepdims=True)
    spread = jnp.mean(center * center, axis=-1, keepdims=True)
    normed = (
        center * lax.rsqrt(spread + EPS_NORM) * norm_gain.astype(jnp.float32)
        + norm_bias.astype(jnp.float32)
    ).astype(jnp.bfloat16)
    flat_rows = normed.reshape(num_items * num_rows * num_cols, channels)
    raised = jnp.dot(flat_rows, proj_in, preferred_element_type=jnp.float32) + bias_in.astype(
        jnp.float32
    )
    active = jax.nn.gelu(raised, approximate=False).astype(jnp.bfloat16)
    grouped = active.reshape(num_items, num_rows * num_cols, -1).astype(jnp.float32)
    local_sq = jnp.sum(grouped * grouped, axis=1)
    total_sq = lax.psum(local_sq, "row")
    magnitude = jnp.sqrt(total_sq)
    grn_ratio = magnitude / (jnp.mean(magnitude, axis=-1, keepdims=True) + EPS_GRN)
    hidden = (
        grn_gamma.astype(jnp.float32) * grouped * grn_ratio[:, None, :]
        + grn_beta.astype(jnp.float32)
        + grouped
    ).astype(jnp.bfloat16)
    update = jnp.dot(
        hidden.reshape(num_items * num_rows * num_cols, -1),
        proj_out,
        preferred_element_type=jnp.float32,
    ) + bias_out.astype(jnp.float32)
    return (
        current.astype(jnp.float32) + update.reshape(num_items, num_rows, num_cols, channels)
    ).astype(jnp.bfloat16)


def rows_plan(inputs, *weights):
    (
        depth_kernel,
        depth_bias,
        norm_gain,
        norm_bias,
        proj_in,
        bias_in,
        grn_gamma,
        grn_beta,
        proj_out,
        bias_out,
    ) = weights
    proj_in = lax.all_gather(proj_in, "dp", axis=2, tiled=True)
    proj_out = lax.all_gather(proj_out, "dp", axis=1, tiled=True)
    own_params = tuple(
        w[0]
        for w in (
            depth_kernel,
            depth_bias,
            norm_gain,
            norm_bias,
            proj_in,
            bias_in,
            grn_gamma,
            grn_beta,
            proj_out,
            bias_out,
        )
    )
    sections = lax.axis_size("section")
    section_index = lax.axis_index("section")
    num_micro = inputs.shape[0]
    num_ticks = num_micro + sections - 1
    arriving = jnp.zeros_like(inputs[0])
    saved = jnp.zeros_like(inputs)
    for tick_index in range(num_ticks):
        fresh_input = inputs[min(tick_index, num_micro - 1)]
        current = jnp.where(section_index == 0, fresh_input, arriving)
        produced = conv_block(current, own_params)
        slot_index = tick_index - section_index
        is_valid = jnp.logical_and(slot_index >= 0, slot_index < num_micro)
        safe_slot = jnp.clip(slot_index, 0, num_micro - 1)
        previous = lax.dynamic_index_in_dim(saved, safe_slot, 0, keepdims=False)
        saved = lax.dynamic_update_index_in_dim(
            saved, jnp.where(is_valid, produced, previous), safe_slot, 0
        )
        if tick_index + 1 < num_ticks:
            arriving = lax.ppermute(
                produced, "section", [(i, i + 1) for i in range(sections - 1)]
            )
    return saved[None]


def on_device(inputs, *weights):
    num_micro, images, local_rows, width, _ = inputs.shape
    one_image_each = (
        images == 1
        and lax.axis_size("row") == num_micro == 4
        and lax.axis_size("dp") == 2
        and lax.axis_size("section") == 4
        and local_rows % 4 == 0
        and width % 16 == 0
    )
    plan = image_plan if one_image_each else rows_plan
    return plan(inputs, *weights)


def solution(mesh):
    return jax.shard_map(
        on_device,
        mesh=mesh,
        in_specs=(
            P(None, "dp", "row", None, None),
            P("section", None, None, None),
            P("section", None),
            P("section", None),
            P("section", None),
            P("section", None, "dp"),
            P("section", None),
            P("section", None),
            P("section", None),
            P("section", "dp", None),
            P("section", None),
        ),
        out_specs=P("section", None, "dp", "row", None, None),
        check_vma=False,
    )
```

```python
import functools

import jax
import jax.numpy as jnp
from jax import lax
from jax.experimental import pallas as pl
from jax.experimental.pallas import tpu as pltpu
from jax.sharding import PartitionSpec as P

EPS_NORM = 1e-06
EPS_GRN = 1e-06
LANES = 128
VMEM_BYTES = 20 * 1024 * 1024
REACH = 3
CHUNK = 4
NORM_ROWS = 4
IN_ORDER = (0, 1, 2, 3)
VECTORS = 56


def fill_columns(xp, xs, x, channels):
    height, reach_cols, blocks, lanes = xs.shape
    stride = reach_cols - 2 * REACH
    width = stride * blocks
    groups = lanes // LANES
    xp[...] = jnp.zeros(xp.shape, jnp.float32)

    def rows(n, carry):
        for k in range(2):
            r = 2 * n + k
            row = x[r].astype(jnp.float32)
            for g in range(groups):
                at = slice(g * LANES, (g + 1) * LANES)
                own = row[:, g * LANES : min((g + 1) * LANES, channels)]
                xp[k * groups + g, 8 : 8 + width, 0 : own.shape[1]] = own
                for q in range(reach_cols):
                    near = pl.ds(8 - REACH + q, blocks, stride=stride)
                    xs[r, q, :, at] = xp[k * groups + g, near, :]
        return carry

    lax.fori_loop(0, height // 2, rows, 0)


def conv(xs, cpar, cq):
    rows = xs.shape[0]
    height, stride, blocks, lanes = cq.shape
    span = 2 * REACH + 1
    above = (height - rows) // 2

    def group(g, carry):
        at = pl.ds(pl.multiple_of(g * LANES, LANES), LANES)

        def column(q, carry):
            bias = jnp.broadcast_to(cpar[VECTORS : VECTORS + 1, at], (blocks, LANES))
            acc = [None if above else bias] * height
            for j in range(span):
                kern = [
                    jnp.broadcast_to(cpar[i * span + j : i * span + j + 1, at], (blocks, LANES))
                    for i in range(span)
                ]
                for r in range(rows):
                    x_row = xs[r, q + j, :, at]
                    for i in range(span):
                        h = r + above + REACH - i
                        if 0 <= h < height:
                            term = kern[i] * x_row
                            acc[h] = term if acc[h] is None else acc[h] + term
            for h in range(height):
                cq[h, q, :, at] = acc[h]
            return carry

        return lax.fori_loop(0, stride, column, carry)

    lax.fori_loop(0, lanes // LANES, group, 0)


def norm(cq, cpar, xp, flat, skip=0):
    padded, stride, blocks, lanes = cq.shape
    height = padded - 2 * skip
    gain = cpar[VECTORS + 1 : VECTORS + 2, :]
    shift = cpar[VECTORS + 2 : VECTORS + 3, :]
    channels = flat.shape[2]
    width = stride * blocks
    groups = lanes // LANES
    inside = lax.broadcasted_iota(jnp.int32, (blocks, lanes), 1) < channels

    def rows(n, carry):
        for k in range(NORM_ROWS):
            h = NORM_ROWS * n + k
            for q in range(stride):
                v = cq[h + skip, q]
                mean = jnp.sum(v, axis=-1, keepdims=True) * (1.0 / channels)
                c = jnp.where(inside, v - mean, 0.0)
                var = jnp.sum(c * c, axis=-1, keepdims=True) * (1.0 / channels)
                c = c * lax.rsqrt(var + EPS_NORM) * gain + shift
                for g in range(groups):
                    at = slice(g * LANES, (g + 1) * LANES)
                    xp[k * groups + g, pl.ds(q, blocks, stride=stride), :] = c[:, at]
            for g in range(groups):
                at = slice(g * LANES, min((g + 1) * LANES, channels))
                flat[h, :, at] = xp[k * groups + g, 0:width, 0 : at.stop - at.start].astype(
                    jnp.bfloat16
                )
        return carry

    lax.fori_loop(0, height // NORM_ROWS, rows, 0)


def conv_norm(x, cpar, flat, xp, xs, cq):
    fill_columns(xp, xs, x, x.shape[2])
    conv(xs, cpar, cq)
    norm(cq, cpar, xp, flat)


def conv_scratch(rows, out_rows, width, lanes):
    return [
        pltpu.VMEM((NORM_ROWS * lanes // LANES, width + 16, LANES), jnp.float32),
        pltpu.VMEM((rows, width // 8 + 2 * REACH, 8, lanes), jnp.float32),
        pltpu.VMEM((out_rows, width // 8, 8, lanes), jnp.float32),
    ]


def gelu(v):
    return 0.5 * v * (1.0 + lax.erf(v * (0.5**0.5)))


def up(flat, w_in, bias, act, ssq):
    height, width, channels = flat.shape
    cells = height * width
    half = w_in.shape[1]
    step = 2 * LANES

    def units(start, count):
        raised = jnp.dot(
            flat[...].reshape(cells, channels),
            w_in[:, pl.ds(start, count)],
            preferred_element_type=jnp.float32,
        )
        active = gelu(raised + bias[0:1, pl.ds(start, count)]).astype(jnp.bfloat16)
        act[:, pl.ds(start, count)] = active
        wide = active.astype(jnp.float32)
        ssq[:, pl.ds(start, count)] = jnp.sum((wide * wide).reshape(cells // 8, 8, count), axis=0)

    def full(n, carry):
        units(pl.multiple_of(n * step, step), step)
        return carry

    whole = half // step
    lax.fori_loop(0, whole, full, 0)
    if half % step:
        units(whole * step, half % step)


def norm_scale(ssqs, fvec, scale):
    half = fvec.shape[2]
    magnitude = [jnp.sqrt(jnp.sum(ssq[...], axis=0, keepdims=True)) for ssq in ssqs]
    mean = jnp.sum(magnitude[0] + magnitude[1], axis=1, keepdims=True) * (0.5 / half)
    for which in range(2):
        ratio = magnitude[which] / (mean + EPS_GRN)
        scale[which] = fvec[which, 1:2, :] * ratio + 1.0


def down(x_rows, first_row, acts, outs, scale, fvec, cpar):
    _, width, channels = x_rows.shape
    cells = CHUNK * width
    at = pl.ds(pl.multiple_of(first_row * width, cells), cells)
    update = cpar[VECTORS + 3 : VECTORS + 4, 0:channels]
    for which in range(2):
        a = acts[which][at, :].astype(jnp.float32)
        hidden = (a * scale[which] + fvec[which, 2:3, :]).astype(jnp.bfloat16)
        update = update + jnp.dot(hidden, outs[which][...], preferred_element_type=jnp.float32)
    return (x_rows.astype(jnp.float32) + update.reshape(CHUNK, width, channels)).astype(
        jnp.bfloat16
    )


def down_all(x, acts, outs, scale, fvec, cvec, out):
    def rows(n, carry):
        at = pl.ds(n * CHUNK, CHUNK)
        out[at] = down(x[at], n * CHUNK, acts, outs, scale, fvec, cvec)
        return carry

    lax.fori_loop(0, x.shape[0] // CHUNK, rows, 0)


def prepare_kernel(part, kernel, *refs):
    vectors, (cpar, fvec), (held, *staged), sems = refs[:7], refs[7:9], refs[9:-1], refs[-1]
    moves = [(kernel, held), *zip(vectors, staged)]
    copies = [pltpu.make_async_copy(a, b, sems.at[n]) for n, (a, b) in enumerate(moves)]
    for copy in copies:
        copy.start()
    cpar[...] = jnp.zeros(cpar.shape, jnp.float32)
    for copy in copies:
        copy.wait()
    channels = kernel.shape[3]
    span = kernel.shape[1]
    half = fvec.shape[2]
    for i in range(span):
        cpar[i * span : (i + 1) * span, 0:channels] = held[0, i].astype(jnp.float32)
    for n in range(4):
        cpar[VECTORS + n : VECTORS + n + 1, 0:channels] = staged[n][...].astype(jnp.float32)
    first = part[0] == 0
    for n in range(3):
        v = staged[4 + n][...].astype(jnp.float32)
        low, high = v[:, 0:half], v[:, half:]
        fvec[0, n : n + 1, :] = jnp.where(first, low, high)
        fvec[1, n : n + 1, :] = jnp.where(first, high, low)


def block_of(me, order, n):
    return n if order is None else me[0] ^ order[n]


def piece_kernel(section, piece, cpar, part, xp, xs, *, on):
    @pl.when(section[0] == on)
    def _():
        fill_columns(xp, xs, piece, piece.shape[2])
        conv(xs, cpar, part)


def last_piece_kernel(section, me, *refs, order, on):
    count = len(order or IN_ORDER)
    pieces, parts = refs[:count], refs[count : 2 * count - 1]
    cpar, both, xp, xs, own, cq = refs[2 * count - 1 :]
    x, flat = both.at[0], both.at[1]
    rows = pieces[0].shape[0]

    @pl.when(section[0] == on)
    def _():
        bias = cpar[VECTORS : VECTORS + 1, :].reshape(1, 1, 1, cq.shape[3])
        cq[...] = jnp.broadcast_to(bias, cq.shape)
        fill_columns(xp, xs, pieces[-1], x.shape[2])
        conv(xs, cpar, own)
        for n, (piece, part) in enumerate(zip(pieces, (*parts, own))):
            at = block_of(me, order, n) * rows
            x[pl.ds(at, rows)] = piece[...]
            cq[pl.ds(at, rows + 2 * REACH)] += part[...]
        norm(cq, cpar, xp, flat, REACH)


def conv_kernel(section, x, cpar, flat, xp, xs, cq, *, tick):
    @pl.when(section[0] == tick)
    def _():
        conv_norm(x, cpar, flat, xp, xs, cq)


def normed_part(ref):
    return ref if len(ref.shape) == 3 else ref.at[1]


def up_first_kernel(section, flat, w_in, fvec, act, ssq, *, tick):
    @pl.when(section[0] == tick)
    def _():
        up(normed_part(flat), w_in, fvec.at[0], act, ssq)


def up_second_kernel(section, flat, w_in, fvec, other, act, scale, ssq, *, tick):
    @pl.when(section[0] == tick)
    def _():
        up(normed_part(flat), w_in, fvec.at[1], act, ssq)
        norm_scale((other, ssq), fvec, scale)


def first_down_kernel(section, both, act_a, act_b, out_a, out_b, scale, fvec, cpar, out):
    @pl.when(section[0] == 0)
    def _():
        down_all(both.at[0], (act_a, act_b), (out_a, out_b), scale, fvec, cpar, out)


def down_piece_kernel(
    section, me, x, act_a, act_b, out_a, out_b, scale, fvec, cpar, prev, out, *, order, tick, n
):
    first_row = block_of(me, order, n) * CHUNK
    at = pl.ds(first_row, CHUNK)

    @pl.when(section[0] == tick)
    def _():
        out[...] = down(x[at], first_row, (act_a, act_b), (out_a, out_b), scale, fvec, cpar)

    @pl.when(section[0] != tick)
    def _():
        out[...] = prev[at]


def mlp_kernel(section, both, in_a, in_b, out_a, out_b, fvec, cpar, *refs, tick):
    *pieces, prev, out, act_a, act_b, ssq_a, ssq_b, scale = refs
    x, flat = both.at[0], both.at[1]

    @pl.when(section[0] == tick)
    def _():
        up(flat, in_a, fvec.at[0], act_a, ssq_a)
        up(flat, in_b, fvec.at[1], act_b, ssq_b)
        norm_scale((ssq_a, ssq_b), fvec, scale)
        down_all(x, (act_a, act_b), (out_a, out_b), scale, fvec, cpar, out)

    @pl.when(section[0] == tick - 1)
    def _():
        for n, piece in enumerate(pieces):
            out[n * CHUNK : (n + 1) * CHUNK] = piece[...]

    @pl.when(section[0] < tick - 1)
    def _():
        out[...] = prev[...]


def conv_up_kernel(section, x, cpar, in_a, in_b, fvec, *refs, tick):
    act_a, act_b, scale, xp, xs, cq, flat, ssq_a, ssq_b = refs

    @pl.when(section[0] == tick)
    def _():
        conv_norm(x, cpar, flat, xp, xs, cq)
        up(flat, in_a, fvec.at[0], act_a, ssq_a)
        up(flat, in_b, fvec.at[1], act_b, ssq_b)
        norm_scale((ssq_a, ssq_b), fvec, scale)


def place_kernel(me, *refs, order):
    *pieces, saved, sems = refs
    copies = [
        pltpu.make_async_copy(piece, saved.at[0, block_of(me, order, n), 0], sems.at[n])
        for n, piece in enumerate(pieces)
    ]
    for copy in copies:
        copy.start()
    for copy in copies:
        copy.wait()


SMEM = pl.BlockSpec(memory_space=pltpu.SMEM)
VMEM = pl.BlockSpec(memory_space=pltpu.VMEM)
HBM = pl.BlockSpec(memory_space=pltpu.HBM)


def call(kernel, name, args, out, specs=None, out_specs=None, scratch=(), flops=0, **static):
    if specs is None:
        specs = [SMEM if a.dtype == jnp.int32 else VMEM for a in args]
    if out_specs is None:
        out_specs = jax.tree.map(lambda _: VMEM, out)
    moved = sum(a.size * a.dtype.itemsize for a in args)
    return pl.pallas_call(
        functools.partial(kernel, **static),
        out_shape=out,
        in_specs=specs,
        out_specs=out_specs,
        scratch_shapes=list(scratch),
        compiler_params=pltpu.CompilerParams(vmem_limit_bytes=VMEM_BYTES),
        cost_estimate=pl.CostEstimate(flops=flops, bytes_accessed=moved, transcendentals=0),
        name=name,
    )(*args)


def shape(*dims, dtype=jnp.float32):
    return jax.ShapeDtypeStruct(dims, dtype)


def ssq_scratch(half):
    return pltpu.VMEM((8, half), jnp.float32)


def image_plan(
    inputs,
    depth_kernel,
    depth_bias,
    norm_gain,
    norm_bias,
    proj_in,
    bias_in,
    grn_gamma,
    grn_beta,
    proj_out,
    bias_out,
):
    sections = lax.axis_size("section")
    count = lax.axis_size("row")
    me = lax.axis_index("row").astype(jnp.int32)
    section = lax.axis_index("section").astype(jnp.int32).reshape(1)
    me_ref = me.reshape(1)
    part = lax.axis_index("dp").astype(jnp.int32).reshape(1)
    _, _, rows, width, channels = inputs.shape
    height = rows * count
    cells = height * width
    lanes = -(-channels // LANES) * LANES
    half = proj_in.shape[2]
    span = depth_kernel.shape[1]
    order = (0, 2, 3, 1)
    bf16 = jnp.bfloat16
    whole = shape(height, width, channels, dtype=bf16)
    piece_shape = shape(rows, width, channels, dtype=bf16)
    act_shape = shape(cells, half, dtype=bf16)
    scale_shape = shape(2, 1, half)
    matmul = 2 * cells * channels * half

    helper, source = 1, sections - 1
    pieces = []
    for by in order:
        piece = lax.dynamic_index_in_dim(inputs, me ^ by, 0, keepdims=False)[0]
        if by:
            pairs = [(source * count + (p ^ by), helper * count + p) for p in range(count)]
            piece = lax.ppermute(piece, ("section", "row"), pairs)
        pieces.append(piece)

    def other_half(x, which):
        pairs = [(2 * s + p, 2 * s + 1 - p) for s in which for p in range(2)]
        return lax.ppermute(x, ("section", "dp"), pairs)

    w_in, w_out = proj_in[0], proj_out[0]
    even = range(0, sections, 2)
    odd = range(1, sections, 2)
    other_in = other_half(w_in, even)
    other_out = other_half(w_out, even)

    held = (
        depth_kernel, depth_bias, norm_gain, norm_bias, bias_out, bias_in, grn_gamma, grn_beta
    )
    cpar, fvec = call(
        prepare_kernel,
        "prepare",
        (part, *held),
        (shape(VECTORS + 8, lanes), shape(2, 3, half)),
        specs=[SMEM] + [HBM] * len(held),
        scratch=[pltpu.VMEM(v.shape, v.dtype) for v in held]
        + [pltpu.SemaphoreType.DMA((len(held),))],
    )

    def send(x, start, end):
        return lax.ppermute(x, "section", [(start, end)])

    def conv_pieces(pieces, cpar, order, on):
        out_rows = rows + 2 * REACH
        scratch = conv_scratch(rows, out_rows, width, lanes)
        parts = []
        for piece in pieces[:-1]:
            if parts:
                piece, parts[-1] = lax.optimization_barrier((piece, parts[-1]))
            part = call(
                piece_kernel,
                "conv_piece",
                (section, piece, cpar),
                shape(out_rows, width // 8, 8, lanes),
                scratch=scratch[:2],
                on=on,
            )
            parts.append(part)
        return call(
            last_piece_kernel,
            "last_piece",
            (section, me_ref, *pieces, *parts, cpar),
            shape(2, height, width, channels, dtype=bf16),
            scratch=scratch + [conv_scratch(1, height + 2 * REACH, width, lanes)[2]],
            order=order,
            on=on,
        )

    def up_own(flat, tick):
        return call(
            up_first_kernel,
            "up_own",
            (section, flat, w_in, fvec),
            (act_shape, shape(8, half)),
            flops=matmul,
            tick=tick,
        )

    def up_other(flat, other_in, ssq, tick):
        return call(
            up_second_kernel,
            "up_other",
            (section, flat, other_in, fvec, ssq),
            (act_shape, scale_shape),
            scratch=[ssq_scratch(half)],
            flops=matmul,
            tick=tick,
        )

    def down_piece(x, acts, other_out, prev, order, tick, n):
        act_a, act_b, scale = acts
        return call(
            down_piece_kernel,
            "down_piece",
            (section, me_ref, x, act_a, act_b, w_out, other_out, scale, fvec, cpar, prev),
            piece_shape,
            flops=2 * matmul // count,
            order=order,
            tick=tick,
            n=n,
        )

    both = conv_pieces(pieces, send(cpar, 0, helper), order, helper)
    both, other_in = lax.optimization_barrier((both, other_in))
    both = send(both, helper, 0)
    act_a, ssq = up_own(both, 0)
    act_b, scale = up_other(both, other_in, ssq, 0)
    result = call(
        first_down_kernel,
        "down",
        (section, both, act_a, act_b, w_out, other_out, scale, fvec, cpar),
        whole,
        flops=2 * matmul,
    )
    x = send(result, 0, 1)
    late_in, late_out, result = lax.optimization_barrier((w_in, w_out, result))
    odd_in = other_half(late_in, odd)
    odd_out = other_half(late_out, odd)
    flat = call(
        conv_kernel,
        "conv",
        (section, x, cpar),
        whole,
        scratch=conv_scratch(height, height, width, lanes),
        tick=1,
    )
    act_a, ssq = up_own(flat, 1)
    acts = (act_a, *up_other(flat, odd_in, ssq, 1))
    kept = [down_piece(x, acts, odd_out, result, None, 1, n) for n in range(count)]
    both = conv_pieces([send(piece, 1, 2) for piece in kept], cpar, None, 2)
    result = call(
        mlp_kernel,
        "mlp",
        (section, both, w_in, other_in, w_out, other_out, fvec, cpar, *kept, result),
        whole,
        scratch=[pltpu.VMEM((cells, half), bf16)] * 2
        + [ssq_scratch(half)] * 2
        + [pltpu.VMEM((2, 1, half), jnp.float32)],
        flops=4 * matmul,
        tick=2,
    )
    x = send(result, 2, 3)
    acts = call(
        conv_up_kernel,
        "conv_up",
        (section, x, cpar, w_in, odd_in, fvec),
        (act_shape, act_shape, scale_shape),
        scratch=conv_scratch(height, height, width, lanes)
        + [pltpu.VMEM((height, width, channels), bf16)]
        + [ssq_scratch(half)] * 2,
        flops=2 * matmul,
        tick=3,
    )
    done = []
    for n in (1, 2, 3, 0):
        piece = down_piece(x, acts, odd_out, result, order, 3, n)
        if n:
            piece = lax.ppermute(piece, "row", [(p, p ^ order[n]) for p in range(count)])
        done.append(piece)
    return call(
        place_kernel,
        "place",
        (me_ref, done[3], *done[:3]),
        shape(1, count, 1, rows, width, channels, dtype=bf16),
        out_specs=HBM,
        scratch=[pltpu.SemaphoreType.DMA((count,))],
        order=order,
    )


def extended(cells, sides, width):
    for axis, dim in sides:
        count = lax.axis_size(axis)
        ends = count - 1
        head = lax.slice_in_dim(cells, 0, width, axis=dim)
        tail = lax.slice_in_dim(cells, cells.shape[dim] - width, cells.shape[dim], axis=dim)
        cells = jnp.concatenate(
            [
                lax.ppermute(tail, axis, [(i, (i + 1) % count) for i in range(ends)]),
                cells,
                lax.ppermute(head, axis, [((i + 1) % count, i) for i in range(ends)]),
            ],
            axis=dim,
        )
    return cells


def depthwise(padded, kernel, bias_term):
    channels = padded.shape[-1]
    conv_out = lax.conv_general_dilated(
        padded.astype(jnp.float32),
        kernel.astype(jnp.float32)[:, :, None, :],
        (1, 1),
        "VALID",
        dimension_numbers=("NHWC", "HWIO", "NHWC"),
        feature_group_count=channels,
        precision=lax.Precision.HIGHEST,
    )
    return conv_out + bias_term.astype(jnp.float32)


def conv_block(current, params):
    (
        depth_kernel,
        depth_bias,
        norm_gain,
        norm_bias,
        proj_in,
        bias_in,
        grn_gamma,
        grn_beta,
        proj_out,
        bias_out,
    ) = params
    num_items, num_rows, num_cols, channels = current.shape
    padded = extended(current, (("row", 1),), REACH)
    padded = jnp.pad(padded, ((0, 0), (0, 0), (REACH, REACH), (0, 0)))
    conv_out = depthwise(padded, depth_kernel, depth_bias)
    center = conv_out - jnp.mean(conv_out, axis=-1, keepdims=True)
    spread = jnp.mean(center * center, axis=-1, keepdims=True)
    normed = (
        center * lax.rsqrt(spread + EPS_NORM) * norm_gain.astype(jnp.float32)
        + norm_bias.astype(jnp.float32)
    ).astype(jnp.bfloat16)
    flat_rows = normed.reshape(num_items * num_rows * num_cols, channels)
    raised = jnp.dot(flat_rows, proj_in, preferred_element_type=jnp.float32) + bias_in.astype(
        jnp.float32
    )
    active = jax.nn.gelu(raised, approximate=False).astype(jnp.bfloat16)
    grouped = active.reshape(num_items, num_rows * num_cols, -1).astype(jnp.float32)
    local_sq = jnp.sum(grouped * grouped, axis=1)
    total_sq = lax.psum(local_sq, "row")
    magnitude = jnp.sqrt(total_sq)
    grn_ratio = magnitude / (jnp.mean(magnitude, axis=-1, keepdims=True) + EPS_GRN)
    hidden = (
        grn_gamma.astype(jnp.float32) * grouped * grn_ratio[:, None, :]
        + grn_beta.astype(jnp.float32)
        + grouped
    ).astype(jnp.bfloat16)
    update = jnp.dot(
        hidden.reshape(num_items * num_rows * num_cols, -1),
        proj_out,
        preferred_element_type=jnp.float32,
    ) + bias_out.astype(jnp.float32)
    return (
        current.astype(jnp.float32) + update.reshape(num_items, num_rows, num_cols, channels)
    ).astype(jnp.bfloat16)


def rows_plan(inputs, *weights):
    (
        depth_kernel,
        depth_bias,
        norm_gain,
        norm_bias,
        proj_in,
        bias_in,
        grn_gamma,
        grn_beta,
        proj_out,
        bias_out,
    ) = weights
    proj_in = lax.all_gather(proj_in, "dp", axis=2, tiled=True)
    proj_out = lax.all_gather(proj_out, "dp", axis=1, tiled=True)
    own_params = tuple(
        w[0]
        for w in (
            depth_kernel,
            depth_bias,
            norm_gain,
            norm_bias,
            proj_in,
            bias_in,
            grn_gamma,
            grn_beta,
            proj_out,
            bias_out,
        )
    )
    sections = lax.axis_size("section")
    section_index = lax.axis_index("section")
    num_micro = inputs.shape[0]
    num_ticks = num_micro + sections - 1
    arriving = jnp.zeros_like(inputs[0])
    saved = jnp.zeros_like(inputs)
    for tick_index in range(num_ticks):
        fresh_input = inputs[min(tick_index, num_micro - 1)]
        current = jnp.where(section_index == 0, fresh_input, arriving)
        produced = conv_block(current, own_params)
        slot_index = tick_index - section_index
        is_valid = jnp.logical_and(slot_index >= 0, slot_index < num_micro)
        safe_slot = jnp.clip(slot_index, 0, num_micro - 1)
        previous = lax.dynamic_index_in_dim(saved, safe_slot, 0, keepdims=False)
        saved = lax.dynamic_update_index_in_dim(
            saved, jnp.where(is_valid, produced, previous), safe_slot, 0
        )
        if tick_index + 1 < num_ticks:
            arriving = lax.ppermute(
                produced, "section", [(i, i + 1) for i in range(sections - 1)]
            )
    return saved[None]


def on_device(inputs, *weights):
    num_micro, images, local_rows, width, _ = inputs.shape
    one_image_each = (
        images == 1
        and lax.axis_size("row") == num_micro == 4
        and lax.axis_size("dp") == 2
        and lax.axis_size("section") == 4
        and local_rows % 4 == 0
        and width % 16 == 0
    )
    plan = image_plan if one_image_each else rows_plan
    return plan(inputs, *weights)


def solution(mesh):
    return jax.shard_map(
        on_device,
        mesh=mesh,
        in_specs=(
            P(None, "dp", "row", None, None),
            P("section", None, None, None),
            P("section", None),
            P("section", None),
            P("section", None),
            P("section", None, "dp"),
            P("section", None),
            P("section", None),
            P("section", None),
            P("section", "dp", None),
            P("section", None),
        ),
        out_specs=P("section", None, "dp", "row", None, None),
        check_vma=False,
    )
```

```python
import functools

import jax
import jax.numpy as jnp
from jax import lax
from jax.experimental import pallas as pl
from jax.experimental.pallas import tpu as pltpu
from jax.sharding import PartitionSpec as P

EPS_NORM = 1e-06
EPS_GRN = 1e-06
LANES = 128
VMEM_BYTES = 20 * 1024 * 1024
REACH = 3
CHUNK = 4
SUBLANES = 16
CONV_ROWS = 10
NORM_ROWS = 4
IN_ORDER = (0, 1, 2, 3)
VECTORS = 56


def fill_columns(xp, xs, x, channels):
    height, reach_cols, blocks, lanes = xs.shape
    stride = reach_cols - 2 * REACH
    width = stride * blocks
    groups = lanes // LANES
    xp[...] = jnp.zeros(xp.shape, jnp.float32)

    def rows(n, carry):
        for k in range(2):
            r = 2 * n + k
            row = x[r].astype(jnp.float32)
            for g in range(groups):
                at = slice(g * LANES, (g + 1) * LANES)
                own = row[:, g * LANES : min((g + 1) * LANES, channels)]
                xp[k * groups + g, 8 : 8 + width, 0 : own.shape[1]] = own
                for q in range(reach_cols):
                    near = pl.ds(8 - REACH + q, blocks, stride=stride)
                    xs[r, q, :, at] = xp[k * groups + g, near, :].astype(jnp.bfloat16)
        return carry

    lax.fori_loop(0, height // 2, rows, 0)


def conv(xs, cpar, kernels, cq):
    rows = xs.shape[0]
    height, stride, blocks, lanes = cq.shape
    span = 2 * REACH + 1
    above = (height - rows) // 2
    for tap in range(span * span):
        kernels[tap] = jnp.broadcast_to(cpar[tap : tap + 1, :], (blocks, lanes)).astype(jnp.bfloat16)
    parts = -(-height // CONV_ROWS)
    size = height // parts

    def group(g, carry):
        at = pl.ds(pl.multiple_of(g * LANES, LANES), LANES)

        def column(q, carry):
            for first in range(0, height, size):
                if above:
                    acc = [jnp.zeros((blocks, LANES), jnp.float32)] * size
                else:
                    bias = cpar[VECTORS : VECTORS + 1, at]
                    acc = [jnp.broadcast_to(bias, (blocks, LANES))] * size
                for j in range(span):
                    kern = [kernels[i * span + j, :, at] for i in range(span)]
                    part = [None] * size
                    for r in range(rows):
                        low = r + above + REACH - first
                        taken = [i for i in range(span) if 0 <= low - i < size]
                        if not taken:
                            continue
                        x_row = xs[r, q + j, :, at]
                        for i in taken:
                            h = low - i
                            term = kern[i] * x_row
                            part[h] = term if part[h] is None else part[h] + term
                    acc = [a + p.astype(jnp.float32) for a, p in zip(acc, part)]
                for h in range(size):
                    cq[first + h, q, :, at] = acc[h]
            return carry

        return lax.fori_loop(0, stride, column, carry)

    lax.fori_loop(0, lanes // LANES, group, 0)


def norm(cq, cpar, xp, flat, skip=0):
    padded, stride, blocks, lanes = cq.shape
    height = padded - 2 * skip
    gain = cpar[VECTORS + 1 : VECTORS + 2, :]
    shift = cpar[VECTORS + 2 : VECTORS + 3, :]
    channels = flat.shape[2]
    width = stride * blocks
    groups = lanes // LANES
    inside = lax.broadcasted_iota(jnp.int32, (blocks, lanes), 1) < channels

    def rows(n, carry):
        for k in range(NORM_ROWS):
            h = NORM_ROWS * n + k
            for q in range(stride):
                v = cq[h + skip, q]
                mean = jnp.sum(v, axis=-1, keepdims=True) * (1.0 / channels)
                c = jnp.where(inside, v - mean, 0.0)
                var = jnp.sum(c * c, axis=-1, keepdims=True) * (1.0 / channels)
                c = c * lax.rsqrt(var + EPS_NORM) * gain + shift
                for g in range(groups):
                    at = slice(g * LANES, (g + 1) * LANES)
                    xp[k * groups + g, pl.ds(q, blocks, stride=stride), :] = c[:, at]
            for g in range(groups):
                at = slice(g * LANES, min((g + 1) * LANES, channels))
                flat[h, :, at] = xp[k * groups + g, 0:width, 0 : at.stop - at.start].astype(
                    jnp.bfloat16
                )
        return carry

    lax.fori_loop(0, height // NORM_ROWS, rows, 0)


def conv_norm(x, cpar, flat, xp, xs, kernels, cq):
    fill_columns(xp, xs, x, x.shape[2])
    conv(xs, cpar, kernels, cq)
    norm(cq, cpar, xp, flat)


def conv_scratch(rows, out_rows, width, lanes):
    return [
        pltpu.VMEM((NORM_ROWS * lanes // LANES, width + 16, LANES), jnp.float32),
        pltpu.VMEM((rows, width // SUBLANES + 2 * REACH, SUBLANES, lanes), jnp.bfloat16),
        pltpu.VMEM(((2 * REACH + 1) ** 2, SUBLANES, lanes), jnp.bfloat16),
        pltpu.VMEM((out_rows, width // SUBLANES, SUBLANES, lanes), jnp.float32),
    ]


def gelu(v):
    return 0.5 * v * (1.0 + lax.erf(v * (0.5**0.5)))


def up(flat, w_in, bias, act, ssq):
    height, width, channels = flat.shape
    cells = height * width
    half = w_in.shape[1]
    step = 2 * LANES

    def units(start, count):
        raised = jnp.dot(
            flat[...].reshape(cells, channels),
            w_in[:, pl.ds(start, count)],
            preferred_element_type=jnp.float32,
        )
        active = gelu(raised + bias[0:1, pl.ds(start, count)]).astype(jnp.bfloat16)
        act[:, pl.ds(start, count)] = active
        wide = active.astype(jnp.float32)
        ssq[:, pl.ds(start, count)] = jnp.sum((wide * wide).reshape(cells // 8, 8, count), axis=0)

    def full(n, carry):
        units(pl.multiple_of(n * step, step), step)
        return carry

    whole = half // step
    lax.fori_loop(0, whole, full, 0)
    if half % step:
        units(whole * step, half % step)


def norm_scale(ssqs, fvec, scale):
    half = fvec.shape[2]
    magnitude = [jnp.sqrt(jnp.sum(ssq[...], axis=0, keepdims=True)) for ssq in ssqs]
    mean = jnp.sum(magnitude[0] + magnitude[1], axis=1, keepdims=True) * (0.5 / half)
    for which in range(2):
        ratio = magnitude[which] / (mean + EPS_GRN)
        scale[which] = fvec[which, 1:2, :] * ratio + 1.0


def down(x_rows, first_row, acts, outs, scale, fvec, cpar):
    _, width, channels = x_rows.shape
    cells = CHUNK * width
    at = pl.ds(pl.multiple_of(first_row * width, cells), cells)
    update = cpar[VECTORS + 3 : VECTORS + 4, 0:channels]
    for which in range(2):
        a = acts[which][at, :].astype(jnp.float32)
        hidden = (a * scale[which] + fvec[which, 2:3, :]).astype(jnp.bfloat16)
        update = update + jnp.dot(hidden, outs[which][...], preferred_element_type=jnp.float32)
    return (x_rows.astype(jnp.float32) + update.reshape(CHUNK, width, channels)).astype(
        jnp.bfloat16
    )


def down_all(x, acts, outs, scale, fvec, cvec, out):
    def rows(n, carry):
        at = pl.ds(n * CHUNK, CHUNK)
        out[at] = down(x[at], n * CHUNK, acts, outs, scale, fvec, cvec)
        return carry

    lax.fori_loop(0, x.shape[0] // CHUNK, rows, 0)


def prepare_kernel(part, kernel, *refs):
    vectors, (cpar, fvec), (held, *staged), sems = refs[:7], refs[7:9], refs[9:-1], refs[-1]
    moves = [(kernel, held), *zip(vectors, staged)]
    copies = [pltpu.make_async_copy(a, b, sems.at[n]) for n, (a, b) in enumerate(moves)]
    for copy in copies:
        copy.start()
    cpar[...] = jnp.zeros(cpar.shape, jnp.float32)
    for copy in copies:
        copy.wait()
    channels = kernel.shape[3]
    span = kernel.shape[1]
    half = fvec.shape[2]
    for i in range(span):
        cpar[i * span : (i + 1) * span, 0:channels] = held[0, i].astype(jnp.float32)
    for n in range(4):
        cpar[VECTORS + n : VECTORS + n + 1, 0:channels] = staged[n][...].astype(jnp.float32)
    first = part[0] == 0
    for n in range(3):
        v = staged[4 + n][...].astype(jnp.float32)
        low, high = v[:, 0:half], v[:, half:]
        fvec[0, n : n + 1, :] = jnp.where(first, low, high)
        fvec[1, n : n + 1, :] = jnp.where(first, high, low)


def block_of(me, order, n):
    return n if order is None else me[0] ^ order[n]


def piece_kernel(section, piece, cpar, part, xp, xs, kernels, *, on):
    @pl.when(section[0] == on)
    def _():
        fill_columns(xp, xs, piece, piece.shape[2])
        conv(xs, cpar, kernels, part)


def last_piece_kernel(section, me, *refs, order, on):
    count = len(order or IN_ORDER)
    pieces, parts = refs[:count], refs[count : 2 * count - 1]
    cpar, both, xp, xs, kernels, own, cq = refs[2 * count - 1 :]
    x, flat = both.at[0], both.at[1]
    rows = pieces[0].shape[0]

    @pl.when(section[0] == on)
    def _():
        bias = cpar[VECTORS : VECTORS + 1, :].reshape(1, 1, 1, cq.shape[3])
        cq[...] = jnp.broadcast_to(bias, cq.shape)
        fill_columns(xp, xs, pieces[-1], x.shape[2])
        conv(xs, cpar, kernels, own)
        for n, (piece, part) in enumerate(zip(pieces, (*parts, own))):
            at = block_of(me, order, n) * rows
            x[pl.ds(at, rows)] = piece[...]
            cq[pl.ds(at, rows + 2 * REACH)] += part[...]
        norm(cq, cpar, xp, flat, REACH)


def conv_kernel(section, x, cpar, flat, xp, xs, kernels, cq, *, tick):
    @pl.when(section[0] == tick)
    def _():
        conv_norm(x, cpar, flat, xp, xs, kernels, cq)


def normed_part(ref):
    return ref if len(ref.shape) == 3 else ref.at[1]


def up_first_kernel(section, flat, w_in, fvec, act, ssq, *, tick):
    @pl.when(section[0] == tick)
    def _():
        up(normed_part(flat), w_in, fvec.at[0], act, ssq)


def up_second_kernel(section, flat, w_in, fvec, other, act, scale, ssq, *, tick):
    @pl.when(section[0] == tick)
    def _():
        up(normed_part(flat), w_in, fvec.at[1], act, ssq)
        norm_scale((other, ssq), fvec, scale)


def first_down_kernel(section, both, act_a, act_b, out_a, out_b, scale, fvec, cpar, out):
    @pl.when(section[0] == 0)
    def _():
        down_all(both.at[0], (act_a, act_b), (out_a, out_b), scale, fvec, cpar, out)


def down_piece_kernel(
    section, me, x, act_a, act_b, out_a, out_b, scale, fvec, cpar, prev, out, *, order, tick, n
):
    first_row = block_of(me, order, n) * CHUNK
    at = pl.ds(first_row, CHUNK)

    @pl.when(section[0] == tick)
    def _():
        out[...] = down(x[at], first_row, (act_a, act_b), (out_a, out_b), scale, fvec, cpar)

    @pl.when(section[0] != tick)
    def _():
        out[...] = prev[at]


def mlp_kernel(section, both, in_a, in_b, out_a, out_b, fvec, cpar, *refs, tick):
    *pieces, prev, out, act_a, act_b, ssq_a, ssq_b, scale = refs
    x, flat = both.at[0], both.at[1]

    @pl.when(section[0] == tick)
    def _():
        up(flat, in_a, fvec.at[0], act_a, ssq_a)
        up(flat, in_b, fvec.at[1], act_b, ssq_b)
        norm_scale((ssq_a, ssq_b), fvec, scale)
        down_all(x, (act_a, act_b), (out_a, out_b), scale, fvec, cpar, out)

    @pl.when(section[0] == tick - 1)
    def _():
        for n, piece in enumerate(pieces):
            out[n * CHUNK : (n + 1) * CHUNK] = piece[...]

    @pl.when(section[0] < tick - 1)
    def _():
        out[...] = prev[...]


def conv_up_kernel(section, x, cpar, in_a, in_b, fvec, *refs, tick):
    act_a, act_b, scale, xp, xs, kernels, cq, flat, ssq_a, ssq_b = refs

    @pl.when(section[0] == tick)
    def _():
        conv_norm(x, cpar, flat, xp, xs, kernels, cq)
        up(flat, in_a, fvec.at[0], act_a, ssq_a)
        up(flat, in_b, fvec.at[1], act_b, ssq_b)
        norm_scale((ssq_a, ssq_b), fvec, scale)


def place_kernel(me, *refs, order):
    *pieces, saved, sems = refs
    copies = [
        pltpu.make_async_copy(piece, saved.at[0, block_of(me, order, n), 0], sems.at[n])
        for n, piece in enumerate(pieces)
    ]
    for copy in copies:
        copy.start()
    for copy in copies:
        copy.wait()


SMEM = pl.BlockSpec(memory_space=pltpu.SMEM)
VMEM = pl.BlockSpec(memory_space=pltpu.VMEM)
HBM = pl.BlockSpec(memory_space=pltpu.HBM)


def call(kernel, name, args, out, specs=None, out_specs=None, scratch=(), flops=0, **static):
    if specs is None:
        specs = [SMEM if a.dtype == jnp.int32 else VMEM for a in args]
    if out_specs is None:
        out_specs = jax.tree.map(lambda _: VMEM, out)
    moved = sum(a.size * a.dtype.itemsize for a in args)
    return pl.pallas_call(
        functools.partial(kernel, **static),
        out_shape=out,
        in_specs=specs,
        out_specs=out_specs,
        scratch_shapes=list(scratch),
        compiler_params=pltpu.CompilerParams(vmem_limit_bytes=VMEM_BYTES),
        cost_estimate=pl.CostEstimate(flops=flops, bytes_accessed=moved, transcendentals=0),
        name=name,
    )(*args)


def shape(*dims, dtype=jnp.float32):
    return jax.ShapeDtypeStruct(dims, dtype)


def ssq_scratch(half):
    return pltpu.VMEM((8, half), jnp.float32)


def image_plan(
    inputs,
    depth_kernel,
    depth_bias,
    norm_gain,
    norm_bias,
    proj_in,
    bias_in,
    grn_gamma,
    grn_beta,
    proj_out,
    bias_out,
):
    sections = lax.axis_size("section")
    count = lax.axis_size("row")
    me = lax.axis_index("row").astype(jnp.int32)
    section = lax.axis_index("section").astype(jnp.int32).reshape(1)
    me_ref = me.reshape(1)
    part = lax.axis_index("dp").astype(jnp.int32).reshape(1)
    _, _, rows, width, channels = inputs.shape
    height = rows * count
    cells = height * width
    lanes = -(-channels // LANES) * LANES
    half = proj_in.shape[2]
    span = depth_kernel.shape[1]
    order = (0, 2, 3, 1)
    bf16 = jnp.bfloat16
    whole = shape(height, width, channels, dtype=bf16)
    piece_shape = shape(rows, width, channels, dtype=bf16)
    act_shape = shape(cells, half, dtype=bf16)
    scale_shape = shape(2, 1, half)
    matmul = 2 * cells * channels * half

    helper, source = 1, sections - 1
    pieces = []
    for by in order:
        piece = lax.dynamic_index_in_dim(inputs, me ^ by, 0, keepdims=False)[0]
        if by:
            pairs = [(source * count + (p ^ by), helper * count + p) for p in range(count)]
            piece = lax.ppermute(piece, ("section", "row"), pairs)
        pieces.append(piece)

    def other_half(x, which):
        pairs = [(2 * s + p, 2 * s + 1 - p) for s in which for p in range(2)]
        return lax.ppermute(x, ("section", "dp"), pairs)

    w_in, w_out = proj_in[0], proj_out[0]
    even = range(0, sections, 2)
    odd = range(1, sections, 2)
    other_in = other_half(w_in, even)
    other_out = other_half(w_out, even)

    held = (
        depth_kernel, depth_bias, norm_gain, norm_bias, bias_out, bias_in, grn_gamma, grn_beta
    )
    cpar, fvec = call(
        prepare_kernel,
        "prepare",
        (part, *held),
        (shape(VECTORS + 8, lanes), shape(2, 3, half)),
        specs=[SMEM] + [HBM] * len(held),
        scratch=[pltpu.VMEM(v.shape, v.dtype) for v in held]
        + [pltpu.SemaphoreType.DMA((len(held),))],
    )

    def send(x, start, end):
        return lax.ppermute(x, "section", [(start, end)])

    def conv_pieces(pieces, cpar, order, on):
        out_rows = rows + 2 * REACH
        scratch = conv_scratch(rows, out_rows, width, lanes)
        parts = []
        for piece in pieces[:-1]:
            if parts:
                piece, parts[-1] = lax.optimization_barrier((piece, parts[-1]))
            part = call(
                piece_kernel,
                "conv_piece",
                (section, piece, cpar),
                shape(out_rows, width // SUBLANES, SUBLANES, lanes),
                scratch=scratch[:3],
                on=on,
            )
            parts.append(part)
        return call(
            last_piece_kernel,
            "last_piece",
            (section, me_ref, *pieces, *parts, cpar),
            shape(2, height, width, channels, dtype=bf16),
            scratch=scratch + [conv_scratch(1, height + 2 * REACH, width, lanes)[3]],
            order=order,
            on=on,
        )

    def up_own(flat, tick):
        return call(
            up_first_kernel,
            "up_own",
            (section, flat, w_in, fvec),
            (act_shape, shape(8, half)),
            flops=matmul,
            tick=tick,
        )

    def up_other(flat, other_in, ssq, tick):
        return call(
            up_second_kernel,
            "up_other",
            (section, flat, other_in, fvec, ssq),
            (act_shape, scale_shape),
            scratch=[ssq_scratch(half)],
            flops=matmul,
            tick=tick,
        )

    def down_piece(x, acts, other_out, prev, order, tick, n):
        act_a, act_b, scale = acts
        return call(
            down_piece_kernel,
            "down_piece",
            (section, me_ref, x, act_a, act_b, w_out, other_out, scale, fvec, cpar, prev),
            piece_shape,
            flops=2 * matmul // count,
            order=order,
            tick=tick,
            n=n,
        )

    both = conv_pieces(pieces, send(cpar, 0, helper), order, helper)
    both, other_in = lax.optimization_barrier((both, other_in))
    both = send(both, helper, 0)
    act_a, ssq = up_own(both, 0)
    act_b, scale = up_other(both, other_in, ssq, 0)
    result = call(
        first_down_kernel,
        "down",
        (section, both, act_a, act_b, w_out, other_out, scale, fvec, cpar),
        whole,
        flops=2 * matmul,
    )
    x = send(result, 0, 1)
    late_in, late_out, result = lax.optimization_barrier((w_in, w_out, result))
    odd_in = other_half(late_in, odd)
    odd_out = other_half(late_out, odd)
    flat = call(
        conv_kernel,
        "conv",
        (section, x, cpar),
        whole,
        scratch=conv_scratch(height, height, width, lanes),
        tick=1,
    )
    act_a, ssq = up_own(flat, 1)
    acts = (act_a, *up_other(flat, odd_in, ssq, 1))
    kept = [down_piece(x, acts, odd_out, result, None, 1, n) for n in range(count)]
    both = conv_pieces([send(piece, 1, 2) for piece in kept], cpar, None, 2)
    result = call(
        mlp_kernel,
        "mlp",
        (section, both, w_in, other_in, w_out, other_out, fvec, cpar, *kept, result),
        whole,
        scratch=[pltpu.VMEM((cells, half), bf16)] * 2
        + [ssq_scratch(half)] * 2
        + [pltpu.VMEM((2, 1, half), jnp.float32)],
        flops=4 * matmul,
        tick=2,
    )
    x = send(result, 2, 3)
    acts = call(
        conv_up_kernel,
        "conv_up",
        (section, x, cpar, w_in, odd_in, fvec),
        (act_shape, act_shape, scale_shape),
        scratch=conv_scratch(height, height, width, lanes)
        + [pltpu.VMEM((height, width, channels), bf16)]
        + [ssq_scratch(half)] * 2,
        flops=2 * matmul,
        tick=3,
    )
    done = []
    for n in (1, 2, 3, 0):
        piece = down_piece(x, acts, odd_out, result, order, 3, n)
        if n:
            piece = lax.ppermute(piece, "row", [(p, p ^ order[n]) for p in range(count)])
        done.append(piece)
    return call(
        place_kernel,
        "place",
        (me_ref, done[3], *done[:3]),
        shape(1, count, 1, rows, width, channels, dtype=bf16),
        out_specs=HBM,
        scratch=[pltpu.SemaphoreType.DMA((count,))],
        order=order,
    )


def extended(cells, sides, width):
    for axis, dim in sides:
        count = lax.axis_size(axis)
        ends = count - 1
        head = lax.slice_in_dim(cells, 0, width, axis=dim)
        tail = lax.slice_in_dim(cells, cells.shape[dim] - width, cells.shape[dim], axis=dim)
        cells = jnp.concatenate(
            [
                lax.ppermute(tail, axis, [(i, (i + 1) % count) for i in range(ends)]),
                cells,
                lax.ppermute(head, axis, [((i + 1) % count, i) for i in range(ends)]),
            ],
            axis=dim,
        )
    return cells


def depthwise(padded, kernel, bias_term):
    channels = padded.shape[-1]
    conv_out = lax.conv_general_dilated(
        padded.astype(jnp.float32),
        kernel.astype(jnp.float32)[:, :, None, :],
        (1, 1),
        "VALID",
        dimension_numbers=("NHWC", "HWIO", "NHWC"),
        feature_group_count=channels,
        precision=lax.Precision.HIGHEST,
    )
    return conv_out + bias_term.astype(jnp.float32)


def conv_block(current, params):
    (
        depth_kernel,
        depth_bias,
        norm_gain,
        norm_bias,
        proj_in,
        bias_in,
        grn_gamma,
        grn_beta,
        proj_out,
        bias_out,
    ) = params
    num_items, num_rows, num_cols, channels = current.shape
    padded = extended(current, (("row", 1),), REACH)
    padded = jnp.pad(padded, ((0, 0), (0, 0), (REACH, REACH), (0, 0)))
    conv_out = depthwise(padded, depth_kernel, depth_bias)
    center = conv_out - jnp.mean(conv_out, axis=-1, keepdims=True)
    spread = jnp.mean(center * center, axis=-1, keepdims=True)
    normed = (
        center * lax.rsqrt(spread + EPS_NORM) * norm_gain.astype(jnp.float32)
        + norm_bias.astype(jnp.float32)
    ).astype(jnp.bfloat16)
    flat_rows = normed.reshape(num_items * num_rows * num_cols, channels)
    raised = jnp.dot(flat_rows, proj_in, preferred_element_type=jnp.float32) + bias_in.astype(
        jnp.float32
    )
    active = jax.nn.gelu(raised, approximate=False).astype(jnp.bfloat16)
    grouped = active.reshape(num_items, num_rows * num_cols, -1).astype(jnp.float32)
    local_sq = jnp.sum(grouped * grouped, axis=1)
    total_sq = lax.psum(local_sq, "row")
    magnitude = jnp.sqrt(total_sq)
    grn_ratio = magnitude / (jnp.mean(magnitude, axis=-1, keepdims=True) + EPS_GRN)
    hidden = (
        grn_gamma.astype(jnp.float32) * grouped * grn_ratio[:, None, :]
        + grn_beta.astype(jnp.float32)
        + grouped
    ).astype(jnp.bfloat16)
    update = jnp.dot(
        hidden.reshape(num_items * num_rows * num_cols, -1),
        proj_out,
        preferred_element_type=jnp.float32,
    ) + bias_out.astype(jnp.float32)
    return (
        current.astype(jnp.float32) + update.reshape(num_items, num_rows, num_cols, channels)
    ).astype(jnp.bfloat16)


def rows_plan(inputs, *weights):
    (
        depth_kernel,
        depth_bias,
        norm_gain,
        norm_bias,
        proj_in,
        bias_in,
        grn_gamma,
        grn_beta,
        proj_out,
        bias_out,
    ) = weights
    proj_in = lax.all_gather(proj_in, "dp", axis=2, tiled=True)
    proj_out = lax.all_gather(proj_out, "dp", axis=1, tiled=True)
    own_params = tuple(
        w[0]
        for w in (
            depth_kernel,
            depth_bias,
            norm_gain,
            norm_bias,
            proj_in,
            bias_in,
            grn_gamma,
            grn_beta,
            proj_out,
            bias_out,
        )
    )
    sections = lax.axis_size("section")
    section_index = lax.axis_index("section")
    num_micro = inputs.shape[0]
    num_ticks = num_micro + sections - 1
    arriving = jnp.zeros_like(inputs[0])
    saved = jnp.zeros_like(inputs)
    for tick_index in range(num_ticks):
        fresh_input = inputs[min(tick_index, num_micro - 1)]
        current = jnp.where(section_index == 0, fresh_input, arriving)
        produced = conv_block(current, own_params)
        slot_index = tick_index - section_index
        is_valid = jnp.logical_and(slot_index >= 0, slot_index < num_micro)
        safe_slot = jnp.clip(slot_index, 0, num_micro - 1)
        previous = lax.dynamic_index_in_dim(saved, safe_slot, 0, keepdims=False)
        saved = lax.dynamic_update_index_in_dim(
            saved, jnp.where(is_valid, produced, previous), safe_slot, 0
        )
        if tick_index + 1 < num_ticks:
            arriving = lax.ppermute(
                produced, "section", [(i, i + 1) for i in range(sections - 1)]
            )
    return saved[None]


def on_device(inputs, *weights):
    num_micro, images, local_rows, width, _ = inputs.shape
    one_image_each = (
        images == 1
        and lax.axis_size("row") == num_micro == 4
        and lax.axis_size("dp") == 2
        and lax.axis_size("section") == 4
        and local_rows % 4 == 0
        and width % 16 == 0
    )
    plan = image_plan if one_image_each else rows_plan
    return plan(inputs, *weights)


def solution(mesh):
    return jax.shard_map(
        on_device,
        mesh=mesh,
        in_specs=(
            P(None, "dp", "row", None, None),
            P("section", None, None, None),
            P("section", None),
            P("section", None),
            P("section", None),
            P("section", None, "dp"),
            P("section", None),
            P("section", None),
            P("section", None),
            P("section", "dp", None),
            P("section", None),
        ),
        out_specs=P("section", None, "dp", "row", None, None),
        check_vma=False,
    )
```

```python
import functools

import jax
import jax.numpy as jnp
from jax import lax
from jax.experimental import pallas as pl
from jax.experimental.pallas import tpu as pltpu
from jax.sharding import PartitionSpec as P

EPS_NORM = 1e-06
EPS_GRN = 1e-06
LANES = 128
VMEM_BYTES = 20 * 1024 * 1024
REACH = 3
CHUNK = 4
NORM_ROWS = 8
IN_ORDER = (0, 1, 2, 3)
VECTORS = 56


def fill_columns(xp, xs, x, channels):
    height, reach_cols, blocks, lanes = xs.shape
    stride = reach_cols - 2 * REACH
    width = stride * blocks
    groups = lanes // LANES
    xp[...] = jnp.zeros(xp.shape, jnp.float32)

    def rows(n, carry):
        for k in range(2):
            r = 2 * n + k
            row = x[r].astype(jnp.float32)
            for g in range(groups):
                at = slice(g * LANES, (g + 1) * LANES)
                own = row[:, g * LANES : min((g + 1) * LANES, channels)]
                xp[k * groups + g, 8 : 8 + width, 0 : own.shape[1]] = own
                for q in range(reach_cols):
                    near = pl.ds(8 - REACH + q, blocks, stride=stride)
                    xs[r, q, :, at] = xp[k * groups + g, near, :]
        return carry

    lax.fori_loop(0, height // 2, rows, 0)


def conv(xs, cpar, cq):
    rows = xs.shape[0]
    height, stride, blocks, lanes = cq.shape
    span = 2 * REACH + 1
    above = (height - rows) // 2

    def group(g, carry):
        at = pl.ds(pl.multiple_of(g * LANES, LANES), LANES)

        def column(q, carry):
            bias = jnp.broadcast_to(cpar[VECTORS : VECTORS + 1, at], (blocks, LANES))
            acc = [None if above else bias] * height
            for j in range(span):
                kern = [
                    jnp.broadcast_to(cpar[i * span + j : i * span + j + 1, at], (blocks, LANES))
                    for i in range(span)
                ]
                for r in range(rows):
                    x_row = xs[r, q + j, :, at]
                    for i in range(span):
                        h = r + above + REACH - i
                        if 0 <= h < height:
                            term = kern[i] * x_row
                            acc[h] = term if acc[h] is None else acc[h] + term
            for h in range(height):
                cq[h, q, :, at] = acc[h]
            return carry

        return lax.fori_loop(0, stride, column, carry)

    lax.fori_loop(0, lanes // LANES, group, 0)


def norm(cq, cpar, xp, flat, skip=0):
    padded, stride, blocks, lanes = cq.shape
    height = padded - 2 * skip
    gain = cpar[VECTORS + 1 : VECTORS + 2, :]
    shift = cpar[VECTORS + 2 : VECTORS + 3, :]
    channels = flat.shape[2]
    width = stride * blocks
    groups = lanes // LANES
    inside = lax.broadcasted_iota(jnp.int32, (blocks, lanes), 1) < channels

    def rows(n, carry):
        for k in range(NORM_ROWS):
            h = NORM_ROWS * n + k
            for q in range(stride):
                v = cq[h + skip, q]
                mean = jnp.sum(v, axis=-1, keepdims=True) * (1.0 / channels)
                c = jnp.where(inside, v - mean, 0.0)
                var = jnp.sum(c * c, axis=-1, keepdims=True) * (1.0 / channels)
                c = c * lax.rsqrt(var + EPS_NORM) * gain + shift
                for g in range(groups):
                    at = slice(g * LANES, (g + 1) * LANES)
                    xp[k * groups + g, pl.ds(q, blocks, stride=stride), :] = c[:, at]
            for g in range(groups):
                at = slice(g * LANES, min((g + 1) * LANES, channels))
                flat[h, :, at] = xp[k * groups + g, 0:width, 0 : at.stop - at.start].astype(
                    jnp.bfloat16
                )
        return carry

    lax.fori_loop(0, height // NORM_ROWS, rows, 0)


def conv_norm(x, cpar, flat, xp, xs, cq):
    fill_columns(xp, xs, x, x.shape[2])
    conv(xs, cpar, cq)
    norm(cq, cpar, xp, flat)


def conv_scratch(rows, out_rows, width, lanes):
    return [
        pltpu.VMEM((NORM_ROWS * lanes // LANES, width + 16, LANES), jnp.float32),
        pltpu.VMEM((rows, width // 8 + 2 * REACH, 8, lanes), jnp.float32),
        pltpu.VMEM((out_rows, width // 8, 8, lanes), jnp.float32),
    ]


def gelu(v):
    return 0.5 * v * (1.0 + lax.erf(v * (0.5**0.5)))


def up(flat, w_in, bias, act, ssq):
    height, width, channels = flat.shape
    cells = height * width
    half = w_in.shape[1]
    step = 2 * LANES

    def units(start, count):
        raised = jnp.dot(
            flat[...].reshape(cells, channels),
            w_in[:, pl.ds(start, count)],
            preferred_element_type=jnp.float32,
        )
        active = gelu(raised + bias[0:1, pl.ds(start, count)])
        act[:, pl.ds(start, count)] = active.astype(jnp.bfloat16)
        squares = (active * active).reshape(cells // 8, 8, count)
        ssq[:, pl.ds(start, count)] = jnp.sum(squares, axis=0)

    def full(n, carry):
        units(pl.multiple_of(n * step, step), step)
        return carry

    whole = half // step
    lax.fori_loop(0, whole, full, 0)
    if half % step:
        units(whole * step, half % step)


def norm_scale(ssqs, fvec, scale):
    half = fvec.shape[2]
    magnitude = [jnp.sqrt(jnp.sum(ssq[...], axis=0, keepdims=True)) for ssq in ssqs]
    mean = jnp.sum(magnitude[0] + magnitude[1], axis=1, keepdims=True) * (0.5 / half)
    for which in range(2):
        ratio = magnitude[which] / (mean + EPS_GRN)
        scale[which] = fvec[which, 1:2, :] * ratio + 1.0


def down(x_rows, first_row, acts, outs, scale, fvec, cpar):
    _, width, channels = x_rows.shape
    cells = CHUNK * width
    at = pl.ds(pl.multiple_of(first_row * width, cells), cells)
    update = cpar[VECTORS + 3 : VECTORS + 4, 0:channels]
    for which in range(2):
        a = acts[which][at, :].astype(jnp.float32)
        hidden = (a * scale[which] + fvec[which, 2:3, :]).astype(jnp.bfloat16)
        update = update + jnp.dot(hidden, outs[which][...], preferred_element_type=jnp.float32)
    return (x_rows.astype(jnp.float32) + update.reshape(CHUNK, width, channels)).astype(
        jnp.bfloat16
    )


def down_all(x, acts, outs, scale, fvec, cvec, out):
    def rows(n, carry):
        at = pl.ds(n * CHUNK, CHUNK)
        out[at] = down(x[at], n * CHUNK, acts, outs, scale, fvec, cvec)
        return carry

    lax.fori_loop(0, x.shape[0] // CHUNK, rows, 0)


def prepare_kernel(part, kernel, *refs):
    vectors, (cpar, fvec), (held, *staged), sems = refs[:7], refs[7:9], refs[9:-1], refs[-1]
    moves = [(kernel, held), *zip(vectors, staged)]
    copies = [pltpu.make_async_copy(a, b, sems.at[n]) for n, (a, b) in enumerate(moves)]
    for copy in copies:
        copy.start()
    cpar[...] = jnp.zeros(cpar.shape, jnp.float32)
    for copy in copies:
        copy.wait()
    channels = kernel.shape[3]
    span = kernel.shape[1]
    half = fvec.shape[2]
    for i in range(span):
        cpar[i * span : (i + 1) * span, 0:channels] = held[0, i].astype(jnp.float32)
    for n in range(4):
        cpar[VECTORS + n : VECTORS + n + 1, 0:channels] = staged[n][...].astype(jnp.float32)
    first = part[0] == 0
    for n in range(3):
        v = staged[4 + n][...].astype(jnp.float32)
        low, high = v[:, 0:half], v[:, half:]
        fvec[0, n : n + 1, :] = jnp.where(first, low, high)
        fvec[1, n : n + 1, :] = jnp.where(first, high, low)


def block_of(me, order, n):
    return n if order is None else me[0] ^ order[n]


def piece_kernel(section, piece, cpar, part, xp, xs, *, on):
    @pl.when(section[0] == on)
    def _():
        fill_columns(xp, xs, piece, piece.shape[2])
        conv(xs, cpar, part)


def last_piece_kernel(section, me, *refs, order, on):
    count = len(order or IN_ORDER)
    pieces, parts = refs[:count], refs[count : 2 * count - 1]
    cpar, both, xp, xs, own, cq = refs[2 * count - 1 :]
    x, flat = both.at[0], both.at[1]
    rows = pieces[0].shape[0]

    @pl.when(section[0] == on)
    def _():
        bias = cpar[VECTORS : VECTORS + 1, :].reshape(1, 1, 1, cq.shape[3])
        cq[...] = jnp.broadcast_to(bias, cq.shape)
        fill_columns(xp, xs, pieces[-1], x.shape[2])
        conv(xs, cpar, own)
        for n, (piece, part) in enumerate(zip(pieces, (*parts, own))):
            at = block_of(me, order, n) * rows
            x[pl.ds(at, rows)] = piece[...]
            cq[pl.ds(at, rows + 2 * REACH)] += part[...]
        norm(cq, cpar, xp, flat, REACH)


def conv_kernel(section, x, cpar, flat, xp, xs, cq, *, tick):
    @pl.when(section[0] == tick)
    def _():
        conv_norm(x, cpar, flat, xp, xs, cq)


def normed_part(ref):
    return ref if len(ref.shape) == 3 else ref.at[1]


def up_first_kernel(section, flat, w_in, fvec, act, ssq, *, tick):
    @pl.when(section[0] == tick)
    def _():
        up(normed_part(flat), w_in, fvec.at[0], act, ssq)


def up_second_kernel(section, flat, w_in, fvec, other, act, scale, ssq, *, tick):
    @pl.when(section[0] == tick)
    def _():
        up(normed_part(flat), w_in, fvec.at[1], act, ssq)
        norm_scale((other, ssq), fvec, scale)


def first_down_kernel(section, both, act_a, act_b, out_a, out_b, scale, fvec, cpar, out):
    @pl.when(section[0] == 0)
    def _():
        down_all(both.at[0], (act_a, act_b), (out_a, out_b), scale, fvec, cpar, out)


def down_piece_kernel(
    section, me, x, act_a, act_b, out_a, out_b, scale, fvec, cpar, prev, out, *, order, tick, n
):
    first_row = block_of(me, order, n) * CHUNK
    at = pl.ds(first_row, CHUNK)

    @pl.when(section[0] == tick)
    def _():
        out[...] = down(x[at], first_row, (act_a, act_b), (out_a, out_b), scale, fvec, cpar)

    @pl.when(section[0] != tick)
    def _():
        out[...] = prev[at]


def mlp_kernel(section, both, in_a, in_b, out_a, out_b, fvec, cpar, *refs, tick):
    *pieces, prev, out, act_a, act_b, ssq_a, ssq_b, scale = refs
    x, flat = both.at[0], both.at[1]

    @pl.when(section[0] == tick)
    def _():
        up(flat, in_a, fvec.at[0], act_a, ssq_a)
        up(flat, in_b, fvec.at[1], act_b, ssq_b)
        norm_scale((ssq_a, ssq_b), fvec, scale)
        down_all(x, (act_a, act_b), (out_a, out_b), scale, fvec, cpar, out)

    @pl.when(section[0] == tick - 1)
    def _():
        for n, piece in enumerate(pieces):
            out[n * CHUNK : (n + 1) * CHUNK] = piece[...]

    @pl.when(section[0] < tick - 1)
    def _():
        out[...] = prev[...]


def conv_up_kernel(section, x, cpar, in_a, in_b, fvec, *refs, tick):
    act_a, act_b, scale, xp, xs, cq, flat, ssq_a, ssq_b = refs

    @pl.when(section[0] == tick)
    def _():
        conv_norm(x, cpar, flat, xp, xs, cq)
        up(flat, in_a, fvec.at[0], act_a, ssq_a)
        up(flat, in_b, fvec.at[1], act_b, ssq_b)
        norm_scale((ssq_a, ssq_b), fvec, scale)


def place_kernel(me, *refs, order):
    *pieces, saved, sems = refs
    copies = [
        pltpu.make_async_copy(piece, saved.at[0, block_of(me, order, n), 0], sems.at[n])
        for n, piece in enumerate(pieces)
    ]
    for copy in copies:
        copy.start()
    for copy in copies:
        copy.wait()


SMEM = pl.BlockSpec(memory_space=pltpu.SMEM)
VMEM = pl.BlockSpec(memory_space=pltpu.VMEM)
HBM = pl.BlockSpec(memory_space=pltpu.HBM)


def call(kernel, name, args, out, specs=None, out_specs=None, scratch=(), flops=0, **static):
    if specs is None:
        specs = [SMEM if a.dtype == jnp.int32 else VMEM for a in args]
    if out_specs is None:
        out_specs = jax.tree.map(lambda _: VMEM, out)
    moved = sum(a.size * a.dtype.itemsize for a in args)
    return pl.pallas_call(
        functools.partial(kernel, **static),
        out_shape=out,
        in_specs=specs,
        out_specs=out_specs,
        scratch_shapes=list(scratch),
        compiler_params=pltpu.CompilerParams(vmem_limit_bytes=VMEM_BYTES),
        cost_estimate=pl.CostEstimate(flops=flops, bytes_accessed=moved, transcendentals=0),
        name=name,
    )(*args)


def shape(*dims, dtype=jnp.float32):
    return jax.ShapeDtypeStruct(dims, dtype)


def ssq_scratch(half):
    return pltpu.VMEM((8, half), jnp.float32)


def image_plan(
    inputs,
    depth_kernel,
    depth_bias,
    norm_gain,
    norm_bias,
    proj_in,
    bias_in,
    grn_gamma,
    grn_beta,
    proj_out,
    bias_out,
):
    sections = lax.axis_size("section")
    count = lax.axis_size("row")
    me = lax.axis_index("row").astype(jnp.int32)
    section = lax.axis_index("section").astype(jnp.int32).reshape(1)
    me_ref = me.reshape(1)
    part = lax.axis_index("dp").astype(jnp.int32).reshape(1)
    _, _, rows, width, channels = inputs.shape
    height = rows * count
    cells = height * width
    lanes = -(-channels // LANES) * LANES
    half = proj_in.shape[2]
    span = depth_kernel.shape[1]
    order = (0, 2, 3, 1)
    bf16 = jnp.bfloat16
    whole = shape(height, width, channels, dtype=bf16)
    piece_shape = shape(rows, width, channels, dtype=bf16)
    act_shape = shape(cells, half, dtype=bf16)
    scale_shape = shape(2, 1, half)
    matmul = 2 * cells * channels * half

    helper, source = 1, sections - 1
    pieces = []
    for by in order:
        piece = lax.dynamic_index_in_dim(inputs, me ^ by, 0, keepdims=False)[0]
        if by:
            pairs = [(source * count + (p ^ by), helper * count + p) for p in range(count)]
            piece = lax.ppermute(piece, ("section", "row"), pairs)
        pieces.append(piece)

    def other_half(x, which):
        pairs = [(2 * s + p, 2 * s + 1 - p) for s in which for p in range(2)]
        return lax.ppermute(x, ("section", "dp"), pairs)

    w_in, w_out = proj_in[0], proj_out[0]
    even = range(0, sections, 2)
    odd = range(1, sections, 2)
    other_in = other_half(w_in, even)
    other_out = other_half(w_out, even)

    held = (
        depth_kernel, depth_bias, norm_gain, norm_bias, bias_out, bias_in, grn_gamma, grn_beta
    )
    cpar, fvec = call(
        prepare_kernel,
        "prepare",
        (part, *held),
        (shape(VECTORS + 8, lanes), shape(2, 3, half)),
        specs=[SMEM] + [HBM] * len(held),
        scratch=[pltpu.VMEM(v.shape, v.dtype) for v in held]
        + [pltpu.SemaphoreType.DMA((len(held),))],
    )

    def send(x, start, end):
        return lax.ppermute(x, "section", [(start, end)])

    def conv_pieces(pieces, cpar, order, on):
        out_rows = rows + 2 * REACH
        scratch = conv_scratch(rows, out_rows, width, lanes)
        parts = []
        for piece in pieces[:-1]:
            if parts:
                piece, parts[-1] = lax.optimization_barrier((piece, parts[-1]))
            part = call(
                piece_kernel,
                "conv_piece",
                (section, piece, cpar),
                shape(out_rows, width // 8, 8, lanes),
                scratch=scratch[:2],
                on=on,
            )
            parts.append(part)
        return call(
            last_piece_kernel,
            "last_piece",
            (section, me_ref, *pieces, *parts, cpar),
            shape(2, height, width, channels, dtype=bf16),
            scratch=scratch + [conv_scratch(1, height + 2 * REACH, width, lanes)[2]],
            order=order,
            on=on,
        )

    def up_own(flat, tick):
        return call(
            up_first_kernel,
            "up_own",
            (section, flat, w_in, fvec),
            (act_shape, shape(8, half)),
            flops=matmul,
            tick=tick,
        )

    def up_other(flat, other_in, ssq, tick):
        return call(
            up_second_kernel,
            "up_other",
            (section, flat, other_in, fvec, ssq),
            (act_shape, scale_shape),
            scratch=[ssq_scratch(half)],
            flops=matmul,
            tick=tick,
        )

    def down_piece(x, acts, other_out, prev, order, tick, n):
        act_a, act_b, scale = acts
        return call(
            down_piece_kernel,
            "down_piece",
            (section, me_ref, x, act_a, act_b, w_out, other_out, scale, fvec, cpar, prev),
            piece_shape,
            flops=2 * matmul // count,
            order=order,
            tick=tick,
            n=n,
        )

    both = conv_pieces(pieces, send(cpar, 0, helper), order, helper)
    both, other_in = lax.optimization_barrier((both, other_in))
    both = send(both, helper, 0)
    act_a, ssq = up_own(both, 0)
    act_b, scale = up_other(both, other_in, ssq, 0)
    result = call(
        first_down_kernel,
        "down",
        (section, both, act_a, act_b, w_out, other_out, scale, fvec, cpar),
        whole,
        flops=2 * matmul,
    )
    x = send(result, 0, 1)
    late_in, late_out, result = lax.optimization_barrier((w_in, w_out, result))
    odd_in = other_half(late_in, odd)
    odd_out = other_half(late_out, odd)
    flat = call(
        conv_kernel,
        "conv",
        (section, x, cpar),
        whole,
        scratch=conv_scratch(height, height, width, lanes),
        tick=1,
    )
    act_a, ssq = up_own(flat, 1)
    acts = (act_a, *up_other(flat, odd_in, ssq, 1))
    kept = [down_piece(x, acts, odd_out, result, None, 1, n) for n in range(count)]
    both = conv_pieces([send(piece, 1, 2) for piece in kept], cpar, None, 2)
    result = call(
        mlp_kernel,
        "mlp",
        (section, both, w_in, other_in, w_out, other_out, fvec, cpar, *kept, result),
        whole,
        scratch=[pltpu.VMEM((cells, half), bf16)] * 2
        + [ssq_scratch(half)] * 2
        + [pltpu.VMEM((2, 1, half), jnp.float32)],
        flops=4 * matmul,
        tick=2,
    )
    x = send(result, 2, 3)
    acts = call(
        conv_up_kernel,
        "conv_up",
        (section, x, cpar, w_in, odd_in, fvec),
        (act_shape, act_shape, scale_shape),
        scratch=conv_scratch(height, height, width, lanes)
        + [pltpu.VMEM((height, width, channels), bf16)]
        + [ssq_scratch(half)] * 2,
        flops=2 * matmul,
        tick=3,
    )
    done = []
    for n in (1, 2, 3, 0):
        piece = down_piece(x, acts, odd_out, result, order, 3, n)
        if n:
            piece = lax.ppermute(piece, "row", [(p, p ^ order[n]) for p in range(count)])
        done.append(piece)
    return call(
        place_kernel,
        "place",
        (me_ref, done[3], *done[:3]),
        shape(1, count, 1, rows, width, channels, dtype=bf16),
        out_specs=HBM,
        scratch=[pltpu.SemaphoreType.DMA((count,))],
        order=order,
    )


def extended(cells, sides, width):
    for axis, dim in sides:
        count = lax.axis_size(axis)
        ends = count - 1
        head = lax.slice_in_dim(cells, 0, width, axis=dim)
        tail = lax.slice_in_dim(cells, cells.shape[dim] - width, cells.shape[dim], axis=dim)
        cells = jnp.concatenate(
            [
                lax.ppermute(tail, axis, [(i, (i + 1) % count) for i in range(ends)]),
                cells,
                lax.ppermute(head, axis, [((i + 1) % count, i) for i in range(ends)]),
            ],
            axis=dim,
        )
    return cells


def depthwise(padded, kernel, bias_term):
    channels = padded.shape[-1]
    conv_out = lax.conv_general_dilated(
        padded.astype(jnp.float32),
        kernel.astype(jnp.float32)[:, :, None, :],
        (1, 1),
        "VALID",
        dimension_numbers=("NHWC", "HWIO", "NHWC"),
        feature_group_count=channels,
        precision=lax.Precision.HIGHEST,
    )
    return conv_out + bias_term.astype(jnp.float32)


def conv_block(current, params):
    (
        depth_kernel,
        depth_bias,
        norm_gain,
        norm_bias,
        proj_in,
        bias_in,
        grn_gamma,
        grn_beta,
        proj_out,
        bias_out,
    ) = params
    num_items, num_rows, num_cols, channels = current.shape
    padded = extended(current, (("row", 1),), REACH)
    padded = jnp.pad(padded, ((0, 0), (0, 0), (REACH, REACH), (0, 0)))
    conv_out = depthwise(padded, depth_kernel, depth_bias)
    center = conv_out - jnp.mean(conv_out, axis=-1, keepdims=True)
    spread = jnp.mean(center * center, axis=-1, keepdims=True)
    normed = (
        center * lax.rsqrt(spread + EPS_NORM) * norm_gain.astype(jnp.float32)
        + norm_bias.astype(jnp.float32)
    ).astype(jnp.bfloat16)
    flat_rows = normed.reshape(num_items * num_rows * num_cols, channels)
    raised = jnp.dot(flat_rows, proj_in, preferred_element_type=jnp.float32) + bias_in.astype(
        jnp.float32
    )
    active = jax.nn.gelu(raised, approximate=False).astype(jnp.bfloat16)
    grouped = active.reshape(num_items, num_rows * num_cols, -1).astype(jnp.float32)
    local_sq = jnp.sum(grouped * grouped, axis=1)
    total_sq = lax.psum(local_sq, "row")
    magnitude = jnp.sqrt(total_sq)
    grn_ratio = magnitude / (jnp.mean(magnitude, axis=-1, keepdims=True) + EPS_GRN)
    hidden = (
        grn_gamma.astype(jnp.float32) * grouped * grn_ratio[:, None, :]
        + grn_beta.astype(jnp.float32)
        + grouped
    ).astype(jnp.bfloat16)
    update = jnp.dot(
        hidden.reshape(num_items * num_rows * num_cols, -1),
        proj_out,
        preferred_element_type=jnp.float32,
    ) + bias_out.astype(jnp.float32)
    return (
        current.astype(jnp.float32) + update.reshape(num_items, num_rows, num_cols, channels)
    ).astype(jnp.bfloat16)


def rows_plan(inputs, *weights):
    (
        depth_kernel,
        depth_bias,
        norm_gain,
        norm_bias,
        proj_in,
        bias_in,
        grn_gamma,
        grn_beta,
        proj_out,
        bias_out,
    ) = weights
    proj_in = lax.all_gather(proj_in, "dp", axis=2, tiled=True)
    proj_out = lax.all_gather(proj_out, "dp", axis=1, tiled=True)
    own_params = tuple(
        w[0]
        for w in (
            depth_kernel,
            depth_bias,
            norm_gain,
            norm_bias,
            proj_in,
            bias_in,
            grn_gamma,
            grn_beta,
            proj_out,
            bias_out,
        )
    )
    sections = lax.axis_size("section")
    section_index = lax.axis_index("section")
    num_micro = inputs.shape[0]
    num_ticks = num_micro + sections - 1
    arriving = jnp.zeros_like(inputs[0])
    saved = jnp.zeros_like(inputs)
    for tick_index in range(num_ticks):
        fresh_input = inputs[min(tick_index, num_micro - 1)]
        current = jnp.where(section_index == 0, fresh_input, arriving)
        produced = conv_block(current, own_params)
        slot_index = tick_index - section_index
        is_valid = jnp.logical_and(slot_index >= 0, slot_index < num_micro)
        safe_slot = jnp.clip(slot_index, 0, num_micro - 1)
        previous = lax.dynamic_index_in_dim(saved, safe_slot, 0, keepdims=False)
        saved = lax.dynamic_update_index_in_dim(
            saved, jnp.where(is_valid, produced, previous), safe_slot, 0
        )
        if tick_index + 1 < num_ticks:
            arriving = lax.ppermute(
                produced, "section", [(i, i + 1) for i in range(sections - 1)]
            )
    return saved[None]


def on_device(inputs, *weights):
    num_micro, images, local_rows, width, _ = inputs.shape
    one_image_each = (
        images == 1
        and lax.axis_size("row") == num_micro == 4
        and lax.axis_size("dp") == 2
        and lax.axis_size("section") == 4
        and local_rows % 4 == 0
        and width % 16 == 0
    )
    plan = image_plan if one_image_each else rows_plan
    return plan(inputs, *weights)


def solution(mesh):
    return jax.shard_map(
        on_device,
        mesh=mesh,
        in_specs=(
            P(None, "dp", "row", None, None),
            P("section", None, None, None),
            P("section", None),
            P("section", None),
            P("section", None),
            P("section", None, "dp"),
            P("section", None),
            P("section", None),
            P("section", None),
            P("section", "dp", None),
            P("section", None),
        ),
        out_specs=P("section", None, "dp", "row", None, None),
        check_vma=False,
    )
```

```python
import functools

import jax
import jax.numpy as jnp
from jax import lax
from jax.experimental import pallas as pl
from jax.experimental.pallas import tpu as pltpu
from jax.sharding import PartitionSpec as P

EPS_NORM = 1e-06
EPS_GRN = 1e-06
LANES = 128
VMEM_BYTES = 20 * 1024 * 1024
REACH = 3
CHUNK = 4
NORM_ROWS = 8
IN_ORDER = (0, 1, 2, 3)
VECTORS = 56


def fill_columns(xp, xs, x, channels):
    height, reach_cols, blocks, lanes = xs.shape
    stride = reach_cols - 2 * REACH
    width = stride * blocks
    groups = lanes // LANES
    xp[...] = jnp.zeros(xp.shape, jnp.float32)

    unroll = min(height, NORM_ROWS)

    def rows(n, carry):
        for k in range(unroll):
            r = unroll * n + k
            row = x[r].astype(jnp.float32)
            for g in range(groups):
                at = slice(g * LANES, (g + 1) * LANES)
                own = row[:, g * LANES : min((g + 1) * LANES, channels)]
                xp[k * groups + g, 8 : 8 + width, 0 : own.shape[1]] = own
                for q in range(reach_cols):
                    near = pl.ds(8 - REACH + q, blocks, stride=stride)
                    xs[r, q, :, at] = xp[k * groups + g, near, :]
        return carry

    lax.fori_loop(0, height // unroll, rows, 0)


def conv(xs, cpar, cq):
    rows = xs.shape[0]
    height, stride, blocks, lanes = cq.shape
    span = 2 * REACH + 1
    above = (height - rows) // 2

    def group(g, carry):
        at = pl.ds(pl.multiple_of(g * LANES, LANES), LANES)

        def column(q, carry):
            bias = jnp.broadcast_to(cpar[VECTORS : VECTORS + 1, at], (blocks, LANES))
            acc = [None if above else bias] * height
            for j in range(span):
                kern = [
                    jnp.broadcast_to(cpar[i * span + j : i * span + j + 1, at], (blocks, LANES))
                    for i in range(span)
                ]
                for r in range(rows):
                    x_row = xs[r, q + j, :, at]
                    for i in range(span):
                        h = r + above + REACH - i
                        if 0 <= h < height:
                            term = kern[i] * x_row
                            acc[h] = term if acc[h] is None else acc[h] + term
            for h in range(height):
                cq[h, q, :, at] = acc[h]
            return carry

        return lax.fori_loop(0, stride, column, carry)

    lax.fori_loop(0, lanes // LANES, group, 0)


def norm(cq, cpar, xp, flat, skip=0):
    padded, stride, blocks, lanes = cq.shape
    height = padded - 2 * skip
    gain = cpar[VECTORS + 1 : VECTORS + 2, :]
    shift = cpar[VECTORS + 2 : VECTORS + 3, :]
    channels = flat.shape[2]
    width = stride * blocks
    groups = lanes // LANES
    inside = lax.broadcasted_iota(jnp.int32, (blocks, lanes), 1) < channels

    def rows(n, carry):
        for k in range(NORM_ROWS):
            h = NORM_ROWS * n + k
            for q in range(stride):
                v = cq[h + skip, q]
                mean = jnp.sum(v, axis=-1, keepdims=True) * (1.0 / channels)
                c = jnp.where(inside, v - mean, 0.0)
                var = jnp.sum(c * c, axis=-1, keepdims=True) * (1.0 / channels)
                c = c * lax.rsqrt(var + EPS_NORM) * gain + shift
                for g in range(groups):
                    at = slice(g * LANES, (g + 1) * LANES)
                    xp[k * groups + g, pl.ds(q, blocks, stride=stride), :] = c[:, at]
            for g in range(groups):
                at = slice(g * LANES, min((g + 1) * LANES, channels))
                flat[h, :, at] = xp[k * groups + g, 0:width, 0 : at.stop - at.start].astype(
                    jnp.bfloat16
                )
        return carry

    lax.fori_loop(0, height // NORM_ROWS, rows, 0)


def conv_norm(x, cpar, flat, xp, xs, cq):
    fill_columns(xp, xs, x, x.shape[2])
    conv(xs, cpar, cq)
    norm(cq, cpar, xp, flat)


def conv_scratch(rows, out_rows, width, lanes):
    return [
        pltpu.VMEM((NORM_ROWS * lanes // LANES, width + 16, LANES), jnp.float32),
        pltpu.VMEM((rows, width // 8 + 2 * REACH, 8, lanes), jnp.float32),
        pltpu.VMEM((out_rows, width // 8, 8, lanes), jnp.float32),
    ]


def gelu(v):
    return 0.5 * v * (1.0 + lax.erf(v * (0.5**0.5)))


def up(flat, w_in, bias, act, ssq):
    height, width, channels = flat.shape
    cells = height * width
    half = w_in.shape[1]
    step = 2 * LANES

    def units(start, count):
        raised = jnp.dot(
            flat[...].reshape(cells, channels),
            w_in[:, pl.ds(start, count)],
            preferred_element_type=jnp.float32,
        )
        active = gelu(raised + bias[0:1, pl.ds(start, count)])
        act[:, pl.ds(start, count)] = active.astype(jnp.bfloat16)
        squares = (active * active).reshape(cells // 8, 8, count)
        ssq[:, pl.ds(start, count)] = jnp.sum(squares, axis=0)

    for start in range(0, half, step):
        units(start, min(step, half - start))


def norm_scale(ssqs, fvec, scale):
    half = fvec.shape[2]
    magnitude = [jnp.sqrt(jnp.sum(ssq[...], axis=0, keepdims=True)) for ssq in ssqs]
    mean = jnp.sum(magnitude[0] + magnitude[1], axis=1, keepdims=True) * (0.5 / half)
    for which in range(2):
        ratio = magnitude[which] / (mean + EPS_GRN)
        scale[which] = fvec[which, 1:2, :] * ratio + 1.0


def down(x_rows, first_row, acts, outs, scale, fvec, cpar):
    _, width, channels = x_rows.shape
    cells = CHUNK * width
    at = pl.ds(pl.multiple_of(first_row * width, cells), cells)
    update = cpar[VECTORS + 3 : VECTORS + 4, 0:channels]
    for which in range(2):
        a = acts[which][at, :].astype(jnp.float32)
        hidden = (a * scale[which] + fvec[which, 2:3, :]).astype(jnp.bfloat16)
        update = update + jnp.dot(hidden, outs[which][...], preferred_element_type=jnp.float32)
    return (x_rows.astype(jnp.float32) + update.reshape(CHUNK, width, channels)).astype(
        jnp.bfloat16
    )


def down_all(x, acts, outs, scale, fvec, cvec, out):
    def rows(n, carry):
        at = pl.ds(n * CHUNK, CHUNK)
        out[at] = down(x[at], n * CHUNK, acts, outs, scale, fvec, cvec)
        return carry

    lax.fori_loop(0, x.shape[0] // CHUNK, rows, 0)


def prepare_kernel(part, kernel, *refs):
    vectors, (cpar, fvec), (held, *staged), sems = refs[:7], refs[7:9], refs[9:-1], refs[-1]
    moves = [(kernel, held), *zip(vectors, staged)]
    copies = [pltpu.make_async_copy(a, b, sems.at[n]) for n, (a, b) in enumerate(moves)]
    for copy in copies:
        copy.start()
    cpar[...] = jnp.zeros(cpar.shape, jnp.float32)
    for copy in copies:
        copy.wait()
    channels = kernel.shape[3]
    span = kernel.shape[1]
    half = fvec.shape[2]
    for i in range(span):
        cpar[i * span : (i + 1) * span, 0:channels] = held[0, i].astype(jnp.float32)
    for n in range(4):
        cpar[VECTORS + n : VECTORS + n + 1, 0:channels] = staged[n][...].astype(jnp.float32)
    first = part[0] == 0
    for n in range(3):
        v = staged[4 + n][...].astype(jnp.float32)
        low, high = v[:, 0:half], v[:, half:]
        fvec[0, n : n + 1, :] = jnp.where(first, low, high)
        fvec[1, n : n + 1, :] = jnp.where(first, high, low)


def block_of(me, order, n):
    return n if order is None else me[0] ^ order[n]


def piece_kernel(section, piece, cpar, part, xp, xs, *, on):
    @pl.when(section[0] == on)
    def _():
        fill_columns(xp, xs, piece, piece.shape[2])
        conv(xs, cpar, part)


def last_piece_kernel(section, me, *refs, order, on):
    count = len(order or IN_ORDER)
    pieces, parts = refs[:count], refs[count : 2 * count - 1]
    cpar, both, xp, xs, own, cq = refs[2 * count - 1 :]
    x, flat = both.at[0], both.at[1]
    rows = pieces[0].shape[0]

    @pl.when(section[0] == on)
    def _():
        bias = cpar[VECTORS : VECTORS + 1, :].reshape(1, 1, 1, cq.shape[3])
        cq[...] = jnp.broadcast_to(bias, cq.shape)
        fill_columns(xp, xs, pieces[-1], x.shape[2])
        conv(xs, cpar, own)
        for n, (piece, part) in enumerate(zip(pieces, (*parts, own))):
            at = block_of(me, order, n) * rows
            x[pl.ds(at, rows)] = piece[...]
            cq[pl.ds(at, rows + 2 * REACH)] += part[...]
        norm(cq, cpar, xp, flat, REACH)


def conv_kernel(section, x, cpar, flat, xp, xs, cq, *, tick):
    @pl.when(section[0] == tick)
    def _():
        conv_norm(x, cpar, flat, xp, xs, cq)


def normed_part(ref):
    return ref if len(ref.shape) == 3 else ref.at[1]


def up_first_kernel(section, flat, w_in, fvec, act, ssq, *, tick):
    @pl.when(section[0] == tick)
    def _():
        up(normed_part(flat), w_in, fvec.at[0], act, ssq)


def up_second_kernel(section, flat, w_in, fvec, other, act, scale, ssq, *, tick):
    @pl.when(section[0] == tick)
    def _():
        up(normed_part(flat), w_in, fvec.at[1], act, ssq)
        norm_scale((other, ssq), fvec, scale)


def first_down_kernel(section, both, act_a, act_b, out_a, out_b, scale, fvec, cpar, out):
    @pl.when(section[0] == 0)
    def _():
        down_all(both.at[0], (act_a, act_b), (out_a, out_b), scale, fvec, cpar, out)


def down_piece_kernel(
    section, me, x, act_a, act_b, out_a, out_b, scale, fvec, cpar, prev, out, *, order, tick, n
):
    first_row = block_of(me, order, n) * CHUNK
    at = pl.ds(first_row, CHUNK)

    @pl.when(section[0] == tick)
    def _():
        out[...] = down(x[at], first_row, (act_a, act_b), (out_a, out_b), scale, fvec, cpar)

    @pl.when(section[0] != tick)
    def _():
        out[...] = prev[at]


def mlp_kernel(section, both, in_a, in_b, out_a, out_b, fvec, cpar, *refs, tick):
    *pieces, prev, out, act_a, act_b, ssq_a, ssq_b, scale = refs
    x, flat = both.at[0], both.at[1]

    @pl.when(section[0] == tick)
    def _():
        up(flat, in_a, fvec.at[0], act_a, ssq_a)
        up(flat, in_b, fvec.at[1], act_b, ssq_b)
        norm_scale((ssq_a, ssq_b), fvec, scale)
        down_all(x, (act_a, act_b), (out_a, out_b), scale, fvec, cpar, out)

    @pl.when(section[0] == tick - 1)
    def _():
        for n, piece in enumerate(pieces):
            out[n * CHUNK : (n + 1) * CHUNK] = piece[...]

    @pl.when(section[0] < tick - 1)
    def _():
        out[...] = prev[...]


def conv_up_kernel(section, x, cpar, in_a, in_b, fvec, *refs, tick):
    act_a, act_b, scale, xp, xs, cq, flat, ssq_a, ssq_b = refs

    @pl.when(section[0] == tick)
    def _():
        conv_norm(x, cpar, flat, xp, xs, cq)
        up(flat, in_a, fvec.at[0], act_a, ssq_a)
        up(flat, in_b, fvec.at[1], act_b, ssq_b)
        norm_scale((ssq_a, ssq_b), fvec, scale)


def place_kernel(me, *refs, order):
    *pieces, saved, sems = refs
    copies = [
        pltpu.make_async_copy(piece, saved.at[0, block_of(me, order, n), 0], sems.at[n])
        for n, piece in enumerate(pieces)
    ]
    for copy in copies:
        copy.start()
    for copy in copies:
        copy.wait()


SMEM = pl.BlockSpec(memory_space=pltpu.SMEM)
VMEM = pl.BlockSpec(memory_space=pltpu.VMEM)
HBM = pl.BlockSpec(memory_space=pltpu.HBM)


def call(kernel, name, args, out, specs=None, out_specs=None, scratch=(), flops=0, **static):
    if specs is None:
        specs = [SMEM if a.dtype == jnp.int32 else VMEM for a in args]
    if out_specs is None:
        out_specs = jax.tree.map(lambda _: VMEM, out)
    moved = sum(a.size * a.dtype.itemsize for a in args)
    return pl.pallas_call(
        functools.partial(kernel, **static),
        out_shape=out,
        in_specs=specs,
        out_specs=out_specs,
        scratch_shapes=list(scratch),
        compiler_params=pltpu.CompilerParams(vmem_limit_bytes=VMEM_BYTES),
        cost_estimate=pl.CostEstimate(flops=flops, bytes_accessed=moved, transcendentals=0),
        name=name,
    )(*args)


def shape(*dims, dtype=jnp.float32):
    return jax.ShapeDtypeStruct(dims, dtype)


def ssq_scratch(half):
    return pltpu.VMEM((8, half), jnp.float32)


def image_plan(
    inputs,
    depth_kernel,
    depth_bias,
    norm_gain,
    norm_bias,
    proj_in,
    bias_in,
    grn_gamma,
    grn_beta,
    proj_out,
    bias_out,
):
    sections = lax.axis_size("section")
    count = lax.axis_size("row")
    me = lax.axis_index("row").astype(jnp.int32)
    section = lax.axis_index("section").astype(jnp.int32).reshape(1)
    me_ref = me.reshape(1)
    part = lax.axis_index("dp").astype(jnp.int32).reshape(1)
    _, _, rows, width, channels = inputs.shape
    height = rows * count
    cells = height * width
    lanes = -(-channels // LANES) * LANES
    half = proj_in.shape[2]
    span = depth_kernel.shape[1]
    order = (0, 2, 3, 1)
    bf16 = jnp.bfloat16
    whole = shape(height, width, channels, dtype=bf16)
    piece_shape = shape(rows, width, channels, dtype=bf16)
    act_shape = shape(cells, half, dtype=bf16)
    scale_shape = shape(2, 1, half)
    matmul = 2 * cells * channels * half

    helper, source = 1, sections - 1
    pieces = []
    for by in order:
        piece = lax.dynamic_index_in_dim(inputs, me ^ by, 0, keepdims=False)[0]
        if by:
            pairs = [(source * count + (p ^ by), helper * count + p) for p in range(count)]
            piece = lax.ppermute(piece, ("section", "row"), pairs)
        pieces.append(piece)

    def other_half(x, which):
        pairs = [(2 * s + p, 2 * s + 1 - p) for s in which for p in range(2)]
        return lax.ppermute(x, ("section", "dp"), pairs)

    w_in, w_out = proj_in[0], proj_out[0]
    even = range(0, sections, 2)
    odd = range(1, sections, 2)
    other_in = other_half(w_in, even)
    other_out = other_half(w_out, even)

    held = (
        depth_kernel, depth_bias, norm_gain, norm_bias, bias_out, bias_in, grn_gamma, grn_beta
    )
    cpar, fvec = call(
        prepare_kernel,
        "prepare",
        (part, *held),
        (shape(VECTORS + 8, lanes), shape(2, 3, half)),
        specs=[SMEM] + [HBM] * len(held),
        scratch=[pltpu.VMEM(v.shape, v.dtype) for v in held]
        + [pltpu.SemaphoreType.DMA((len(held),))],
    )

    def send(x, start, end):
        return lax.ppermute(x, "section", [(start, end)])

    def conv_pieces(pieces, cpar, order, on):
        out_rows = rows + 2 * REACH
        scratch = conv_scratch(rows, out_rows, width, lanes)
        parts = []
        for piece in pieces[:-1]:
            if parts:
                piece, parts[-1] = lax.optimization_barrier((piece, parts[-1]))
            part = call(
                piece_kernel,
                "conv_piece",
                (section, piece, cpar),
                shape(out_rows, width // 8, 8, lanes),
                scratch=scratch[:2],
                on=on,
            )
            parts.append(part)
        return call(
            last_piece_kernel,
            "last_piece",
            (section, me_ref, *pieces, *parts, cpar),
            shape(2, height, width, channels, dtype=bf16),
            scratch=scratch + [conv_scratch(1, height + 2 * REACH, width, lanes)[2]],
            order=order,
            on=on,
        )

    def up_own(flat, tick):
        return call(
            up_first_kernel,
            "up_own",
            (section, flat, w_in, fvec),
            (act_shape, shape(8, half)),
            flops=matmul,
            tick=tick,
        )

    def up_other(flat, other_in, ssq, tick):
        return call(
            up_second_kernel,
            "up_other",
            (section, flat, other_in, fvec, ssq),
            (act_shape, scale_shape),
            scratch=[ssq_scratch(half)],
            flops=matmul,
            tick=tick,
        )

    def down_piece(x, acts, other_out, prev, order, tick, n):
        act_a, act_b, scale = acts
        return call(
            down_piece_kernel,
            "down_piece",
            (section, me_ref, x, act_a, act_b, w_out, other_out, scale, fvec, cpar, prev),
            piece_shape,
            flops=2 * matmul // count,
            order=order,
            tick=tick,
            n=n,
        )

    both = conv_pieces(pieces, send(cpar, 0, helper), order, helper)
    both, other_in = lax.optimization_barrier((both, other_in))
    both = send(both, helper, 0)
    act_a, ssq = up_own(both, 0)
    act_b, scale = up_other(both, other_in, ssq, 0)
    result = call(
        first_down_kernel,
        "down",
        (section, both, act_a, act_b, w_out, other_out, scale, fvec, cpar),
        whole,
        flops=2 * matmul,
    )
    x = send(result, 0, 1)
    late_in, late_out, result = lax.optimization_barrier((w_in, w_out, result))
    odd_in = other_half(late_in, odd)
    odd_out = other_half(late_out, odd)
    flat = call(
        conv_kernel,
        "conv",
        (section, x, cpar),
        whole,
        scratch=conv_scratch(height, height, width, lanes),
        tick=1,
    )
    act_a, ssq = up_own(flat, 1)
    acts = (act_a, *up_other(flat, odd_in, ssq, 1))
    kept = [down_piece(x, acts, odd_out, result, None, 1, n) for n in range(count)]
    both = conv_pieces([send(piece, 1, 2) for piece in kept], cpar, None, 2)
    result = call(
        mlp_kernel,
        "mlp",
        (section, both, w_in, other_in, w_out, other_out, fvec, cpar, *kept, result),
        whole,
        scratch=[pltpu.VMEM((cells, half), bf16)] * 2
        + [ssq_scratch(half)] * 2
        + [pltpu.VMEM((2, 1, half), jnp.float32)],
        flops=4 * matmul,
        tick=2,
    )
    x = send(result, 2, 3)
    acts = call(
        conv_up_kernel,
        "conv_up",
        (section, x, cpar, w_in, odd_in, fvec),
        (act_shape, act_shape, scale_shape),
        scratch=conv_scratch(height, height, width, lanes)
        + [pltpu.VMEM((height, width, channels), bf16)]
        + [ssq_scratch(half)] * 2,
        flops=2 * matmul,
        tick=3,
    )
    done = []
    for n in (1, 2, 3, 0):
        piece = down_piece(x, acts, odd_out, result, order, 3, n)
        if n:
            piece = lax.ppermute(piece, "row", [(p, p ^ order[n]) for p in range(count)])
        done.append(piece)
    return call(
        place_kernel,
        "place",
        (me_ref, done[3], *done[:3]),
        shape(1, count, 1, rows, width, channels, dtype=bf16),
        out_specs=HBM,
        scratch=[pltpu.SemaphoreType.DMA((count,))],
        order=order,
    )


def extended(cells, sides, width):
    for axis, dim in sides:
        count = lax.axis_size(axis)
        ends = count - 1
        head = lax.slice_in_dim(cells, 0, width, axis=dim)
        tail = lax.slice_in_dim(cells, cells.shape[dim] - width, cells.shape[dim], axis=dim)
        cells = jnp.concatenate(
            [
                lax.ppermute(tail, axis, [(i, (i + 1) % count) for i in range(ends)]),
                cells,
                lax.ppermute(head, axis, [((i + 1) % count, i) for i in range(ends)]),
            ],
            axis=dim,
        )
    return cells


def depthwise(padded, kernel, bias_term):
    channels = padded.shape[-1]
    conv_out = lax.conv_general_dilated(
        padded.astype(jnp.float32),
        kernel.astype(jnp.float32)[:, :, None, :],
        (1, 1),
        "VALID",
        dimension_numbers=("NHWC", "HWIO", "NHWC"),
        feature_group_count=channels,
        precision=lax.Precision.HIGHEST,
    )
    return conv_out + bias_term.astype(jnp.float32)


def conv_block(current, params):
    (
        depth_kernel,
        depth_bias,
        norm_gain,
        norm_bias,
        proj_in,
        bias_in,
        grn_gamma,
        grn_beta,
        proj_out,
        bias_out,
    ) = params
    num_items, num_rows, num_cols, channels = current.shape
    padded = extended(current, (("row", 1),), REACH)
    padded = jnp.pad(padded, ((0, 0), (0, 0), (REACH, REACH), (0, 0)))
    conv_out = depthwise(padded, depth_kernel, depth_bias)
    center = conv_out - jnp.mean(conv_out, axis=-1, keepdims=True)
    spread = jnp.mean(center * center, axis=-1, keepdims=True)
    normed = (
        center * lax.rsqrt(spread + EPS_NORM) * norm_gain.astype(jnp.float32)
        + norm_bias.astype(jnp.float32)
    ).astype(jnp.bfloat16)
    flat_rows = normed.reshape(num_items * num_rows * num_cols, channels)
    raised = jnp.dot(flat_rows, proj_in, preferred_element_type=jnp.float32) + bias_in.astype(
        jnp.float32
    )
    active = jax.nn.gelu(raised, approximate=False).astype(jnp.bfloat16)
    grouped = active.reshape(num_items, num_rows * num_cols, -1).astype(jnp.float32)
    local_sq = jnp.sum(grouped * grouped, axis=1)
    total_sq = lax.psum(local_sq, "row")
    magnitude = jnp.sqrt(total_sq)
    grn_ratio = magnitude / (jnp.mean(magnitude, axis=-1, keepdims=True) + EPS_GRN)
    hidden = (
        grn_gamma.astype(jnp.float32) * grouped * grn_ratio[:, None, :]
        + grn_beta.astype(jnp.float32)
        + grouped
    ).astype(jnp.bfloat16)
    update = jnp.dot(
        hidden.reshape(num_items * num_rows * num_cols, -1),
        proj_out,
        preferred_element_type=jnp.float32,
    ) + bias_out.astype(jnp.float32)
    return (
        current.astype(jnp.float32) + update.reshape(num_items, num_rows, num_cols, channels)
    ).astype(jnp.bfloat16)


def rows_plan(inputs, *weights):
    (
        depth_kernel,
        depth_bias,
        norm_gain,
        norm_bias,
        proj_in,
        bias_in,
        grn_gamma,
        grn_beta,
        proj_out,
        bias_out,
    ) = weights
    proj_in = lax.all_gather(proj_in, "dp", axis=2, tiled=True)
    proj_out = lax.all_gather(proj_out, "dp", axis=1, tiled=True)
    own_params = tuple(
        w[0]
        for w in (
            depth_kernel,
            depth_bias,
            norm_gain,
            norm_bias,
            proj_in,
            bias_in,
            grn_gamma,
            grn_beta,
            proj_out,
            bias_out,
        )
    )
    sections = lax.axis_size("section")
    section_index = lax.axis_index("section")
    num_micro = inputs.shape[0]
    num_ticks = num_micro + sections - 1
    arriving = jnp.zeros_like(inputs[0])
    saved = jnp.zeros_like(inputs)
    for tick_index in range(num_ticks):
        fresh_input = inputs[min(tick_index, num_micro - 1)]
        current = jnp.where(section_index == 0, fresh_input, arriving)
        produced = conv_block(current, own_params)
        slot_index = tick_index - section_index
        is_valid = jnp.logical_and(slot_index >= 0, slot_index < num_micro)
        safe_slot = jnp.clip(slot_index, 0, num_micro - 1)
        previous = lax.dynamic_index_in_dim(saved, safe_slot, 0, keepdims=False)
        saved = lax.dynamic_update_index_in_dim(
            saved, jnp.where(is_valid, produced, previous), safe_slot, 0
        )
        if tick_index + 1 < num_ticks:
            arriving = lax.ppermute(
                produced, "section", [(i, i + 1) for i in range(sections - 1)]
            )
    return saved[None]


def on_device(inputs, *weights):
    num_micro, images, local_rows, width, _ = inputs.shape
    one_image_each = (
        images == 1
        and lax.axis_size("row") == num_micro == 4
        and lax.axis_size("dp") == 2
        and lax.axis_size("section") == 4
        and local_rows % 4 == 0
        and width % 16 == 0
    )
    plan = image_plan if one_image_each else rows_plan
    return plan(inputs, *weights)


def solution(mesh):
    return jax.shard_map(
        on_device,
        mesh=mesh,
        in_specs=(
            P(None, "dp", "row", None, None),
            P("section", None, None, None),
            P("section", None),
            P("section", None),
            P("section", None),
            P("section", None, "dp"),
            P("section", None),
            P("section", None),
            P("section", None),
            P("section", "dp", None),
            P("section", None),
        ),
        out_specs=P("section", None, "dp", "row", None, None),
        check_vma=False,
    )
```

```python
import functools

import jax
import jax.numpy as jnp
from jax import lax
from jax.experimental import pallas as pl
from jax.experimental.pallas import tpu as pltpu
from jax.sharding import PartitionSpec as P

EPS_NORM = 1e-06
EPS_GRN = 1e-06
LANES = 128
VMEM_BYTES = 20 * 1024 * 1024
REACH = 3
CHUNK = 4
NORM_ROWS = 8
IN_ORDER = (0, 1, 2, 3)
VECTORS = 56


def fill_columns(xp, xs, x, channels):
    height, reach_cols, blocks, lanes = xs.shape
    stride = reach_cols - 2 * REACH
    width = stride * blocks
    groups = lanes // LANES
    xp[...] = jnp.zeros(xp.shape, jnp.float32)

    unroll = min(height, NORM_ROWS)

    def rows(n, carry):
        for k in range(unroll):
            r = unroll * n + k
            row = x[r].astype(jnp.float32)
            for g in range(groups):
                at = slice(g * LANES, (g + 1) * LANES)
                own = row[:, g * LANES : min((g + 1) * LANES, channels)]
                xp[k * groups + g, 8 : 8 + width, 0 : own.shape[1]] = own
                for q in range(reach_cols):
                    near = pl.ds(8 - REACH + q, blocks, stride=stride)
                    xs[r, q, :, at] = xp[k * groups + g, near, :]
        return carry

    lax.fori_loop(0, height // unroll, rows, 0)


def conv(xs, cpar, cq):
    rows = xs.shape[0]
    height, stride, blocks, lanes = cq.shape
    span = 2 * REACH + 1
    above = (height - rows) // 2

    def group(g, carry):
        at = pl.ds(pl.multiple_of(g * LANES, LANES), LANES)

        def column(q, carry):
            bias = jnp.broadcast_to(cpar[VECTORS : VECTORS + 1, at], (blocks, LANES))
            acc = [None if above else bias] * height
            for j in range(span):
                kern = [
                    jnp.broadcast_to(cpar[i * span + j : i * span + j + 1, at], (blocks, LANES))
                    for i in range(span)
                ]
                for r in range(rows):
                    x_row = xs[r, q + j, :, at]
                    for i in range(span):
                        h = r + above + REACH - i
                        if 0 <= h < height:
                            term = kern[i] * x_row
                            acc[h] = term if acc[h] is None else acc[h] + term
            for h in range(height):
                cq[h, q, :, at] = acc[h]
            return carry

        return lax.fori_loop(0, stride, column, carry)

    lax.fori_loop(0, lanes // LANES, group, 0)


def norm(cq, cpar, xp, flat, skip=0):
    padded, stride, blocks, lanes = cq.shape
    height = padded - 2 * skip
    gain = cpar[VECTORS + 1 : VECTORS + 2, :]
    shift = cpar[VECTORS + 2 : VECTORS + 3, :]
    channels = flat.shape[2]
    width = stride * blocks
    groups = lanes // LANES
    inside = lax.broadcasted_iota(jnp.int32, (blocks, lanes), 1) < channels

    def rows(n, carry):
        for k in range(NORM_ROWS):
            h = NORM_ROWS * n + k
            for q in range(stride):
                v = cq[h + skip, q]
                mean = jnp.sum(v, axis=-1, keepdims=True) * (1.0 / channels)
                c = jnp.where(inside, v - mean, 0.0)
                var = jnp.sum(c * c, axis=-1, keepdims=True) * (1.0 / channels)
                c = c * lax.rsqrt(var + EPS_NORM) * gain + shift
                for g in range(groups):
                    at = slice(g * LANES, (g + 1) * LANES)
                    xp[k * groups + g, pl.ds(q, blocks, stride=stride), :] = c[:, at]
            for g in range(groups):
                at = slice(g * LANES, min((g + 1) * LANES, channels))
                flat[h, :, at] = xp[k * groups + g, 0:width, 0 : at.stop - at.start].astype(
                    jnp.bfloat16
                )
        return carry

    lax.fori_loop(0, height // NORM_ROWS, rows, 0)


def conv_norm(x, cpar, flat, xp, xs, cq):
    fill_columns(xp, xs, x, x.shape[2])
    conv(xs, cpar, cq)
    norm(cq, cpar, xp, flat)


def conv_scratch(rows, out_rows, width, lanes):
    return [
        pltpu.VMEM((NORM_ROWS * lanes // LANES, width + 16, LANES), jnp.float32),
        pltpu.VMEM((rows, width // 8 + 2 * REACH, 8, lanes), jnp.float32),
        pltpu.VMEM((out_rows, width // 8, 8, lanes), jnp.float32),
    ]


def gelu(v):
    return 0.5 * v * (1.0 + lax.erf(v * (0.5**0.5)))


def up(flat, w_in, bias, act, ssq):
    height, width, channels = flat.shape
    cells = height * width
    half = w_in.shape[1]
    step = 2 * LANES

    def units(start, count):
        raised = jnp.dot(
            flat[...].reshape(cells, channels),
            w_in[0:channels, pl.ds(start, count)],
            preferred_element_type=jnp.float32,
        )
        active = gelu(raised + bias[0:1, pl.ds(start, count)])
        act[:, pl.ds(start, count)] = active.astype(jnp.bfloat16)
        squares = (active * active).reshape(cells // 8, 8, count)
        ssq[:, pl.ds(start, count)] = jnp.sum(squares, axis=0)

    for start in range(0, half, step):
        units(start, min(step, half - start))


def norm_scale(ssqs, fvec, scale):
    half = fvec.shape[2]
    magnitude = [jnp.sqrt(jnp.sum(ssq[...], axis=0, keepdims=True)) for ssq in ssqs]
    mean = jnp.sum(magnitude[0] + magnitude[1], axis=1, keepdims=True) * (0.5 / half)
    for which in range(2):
        ratio = magnitude[which] / (mean + EPS_GRN)
        scale[which] = fvec[which, 1:2, :] * ratio + 1.0


def down(x_rows, first_row, acts, outs, scale, fvec, cpar):
    _, width, channels = x_rows.shape
    cells = CHUNK * width
    at = pl.ds(pl.multiple_of(first_row * width, cells), cells)
    update = cpar[VECTORS + 3 : VECTORS + 4, 0:channels]
    for which in range(2):
        a = acts[which][at, :].astype(jnp.float32)
        hidden = (a * scale[which] + fvec[which, 2:3, :]).astype(jnp.bfloat16)
        update = update + jnp.dot(hidden, outs[which][...], preferred_element_type=jnp.float32)
    return (x_rows.astype(jnp.float32) + update.reshape(CHUNK, width, channels)).astype(
        jnp.bfloat16
    )


def down_all(x, acts, outs, scale, fvec, cvec, out):
    def rows(n, carry):
        at = pl.ds(n * CHUNK, CHUNK)
        out[at] = down(x[at], n * CHUNK, acts, outs, scale, fvec, cvec)
        return carry

    lax.fori_loop(0, x.shape[0] // CHUNK, rows, 0)


def prepare_kernel(part, kernel, *refs):
    vectors, (cpar, fvec), (held, *staged), sems = refs[:7], refs[7:9], refs[9:-1], refs[-1]
    moves = [(kernel, held), *zip(vectors, staged)]
    copies = [pltpu.make_async_copy(a, b, sems.at[n]) for n, (a, b) in enumerate(moves)]
    for copy in copies:
        copy.start()
    cpar[...] = jnp.zeros(cpar.shape, jnp.float32)
    for copy in copies:
        copy.wait()
    channels = kernel.shape[3]
    span = kernel.shape[1]
    half = fvec.shape[2]
    for i in range(span):
        cpar[i * span : (i + 1) * span, 0:channels] = held[0, i].astype(jnp.float32)
    for n in range(4):
        cpar[VECTORS + n : VECTORS + n + 1, 0:channels] = staged[n][...].astype(jnp.float32)
    first = part[0] == 0
    for n in range(3):
        v = staged[4 + n][...].astype(jnp.float32)
        low, high = v[:, 0:half], v[:, half:]
        fvec[0, n : n + 1, :] = jnp.where(first, low, high)
        fvec[1, n : n + 1, :] = jnp.where(first, high, low)


def block_of(me, order, n):
    return n if order is None else me[0] ^ order[n]


def piece_kernel(section, piece, cpar, part, xp, xs, *, on):
    @pl.when(section[0] == on)
    def _():
        fill_columns(xp, xs, piece, piece.shape[2])
        conv(xs, cpar, part)


def last_piece_kernel(section, me, *refs, order, on):
    count = len(order or IN_ORDER)
    pieces, parts = refs[:count], refs[count : 2 * count - 1]
    cpar, both, xp, xs, own, cq = refs[2 * count - 1 :]
    x, flat = both.at[0], both.at[1]
    rows = pieces[0].shape[0]

    @pl.when(section[0] == on)
    def _():
        bias = cpar[VECTORS : VECTORS + 1, :].reshape(1, 1, 1, cq.shape[3])
        cq[...] = jnp.broadcast_to(bias, cq.shape)
        fill_columns(xp, xs, pieces[-1], x.shape[2])
        conv(xs, cpar, own)
        for n, (piece, part) in enumerate(zip(pieces, (*parts, own))):
            at = block_of(me, order, n) * rows
            x[pl.ds(at, rows)] = piece[...]
            cq[pl.ds(at, rows + 2 * REACH)] += part[...]
        norm(cq, cpar, xp, flat, REACH)


def conv_kernel(section, x, cpar, flat, xp, xs, cq, *, tick):
    @pl.when(section[0] == tick)
    def _():
        conv_norm(x, cpar, flat, xp, xs, cq)


def normed_part(ref):
    return ref if len(ref.shape) == 3 else ref.at[1]


def unpack_kernel(packed, w_out):
    cut, channels = w_out.shape[0] // 2, w_out.shape[1]
    first = packed.shape[0] - cut
    w_out[0:cut] = packed[first:, 0:channels]
    w_out[cut:] = packed[first:, channels : 2 * channels]


def up_first_kernel(section, flat, w_in, fvec, act, ssq, *, tick):
    @pl.when(section[0] == tick)
    def _():
        up(normed_part(flat), w_in, fvec.at[0], act, ssq)


def up_second_kernel(section, flat, w_in, fvec, other, act, scale, ssq, *, tick):
    @pl.when(section[0] == tick)
    def _():
        up(normed_part(flat), w_in, fvec.at[1], act, ssq)
        norm_scale((other, ssq), fvec, scale)


def first_down_kernel(section, both, act_a, act_b, out_a, out_b, scale, fvec, cpar, out):
    @pl.when(section[0] == 0)
    def _():
        down_all(both.at[0], (act_a, act_b), (out_a, out_b), scale, fvec, cpar, out)


def down_piece_kernel(
    section, me, x, act_a, act_b, out_a, out_b, scale, fvec, cpar, prev, out, *, order, tick, n
):
    first_row = block_of(me, order, n) * CHUNK
    at = pl.ds(first_row, CHUNK)

    @pl.when(section[0] == tick)
    def _():
        out[...] = down(x[at], first_row, (act_a, act_b), (out_a, out_b), scale, fvec, cpar)

    @pl.when(section[0] != tick)
    def _():
        out[...] = prev[at]


def mlp_kernel(section, both, in_a, in_b, out_a, out_b, fvec, cpar, *refs, tick):
    *pieces, prev, out, act_a, act_b, ssq_a, ssq_b, scale = refs
    x, flat = both.at[0], both.at[1]

    @pl.when(section[0] == tick)
    def _():
        up(flat, in_a, fvec.at[0], act_a, ssq_a)
        up(flat, in_b, fvec.at[1], act_b, ssq_b)
        norm_scale((ssq_a, ssq_b), fvec, scale)
        down_all(x, (act_a, act_b), (out_a, out_b), scale, fvec, cpar, out)

    @pl.when(section[0] == tick - 1)
    def _():
        for n, piece in enumerate(pieces):
            out[n * CHUNK : (n + 1) * CHUNK] = piece[...]

    @pl.when(section[0] < tick - 1)
    def _():
        out[...] = prev[...]


def conv_up_kernel(section, x, cpar, in_a, in_b, fvec, *refs, tick):
    act_a, act_b, scale, xp, xs, cq, flat, ssq_a, ssq_b = refs

    @pl.when(section[0] == tick)
    def _():
        conv_norm(x, cpar, flat, xp, xs, cq)
        up(flat, in_a, fvec.at[0], act_a, ssq_a)
        up(flat, in_b, fvec.at[1], act_b, ssq_b)
        norm_scale((ssq_a, ssq_b), fvec, scale)


def place_kernel(me, *refs, order):
    *pieces, saved, sems = refs
    copies = [
        pltpu.make_async_copy(piece, saved.at[0, block_of(me, order, n), 0], sems.at[n])
        for n, piece in enumerate(pieces)
    ]
    for copy in copies:
        copy.start()
    for copy in copies:
        copy.wait()


SMEM = pl.BlockSpec(memory_space=pltpu.SMEM)
VMEM = pl.BlockSpec(memory_space=pltpu.VMEM)
HBM = pl.BlockSpec(memory_space=pltpu.HBM)


def call(kernel, name, args, out, specs=None, out_specs=None, scratch=(), flops=0, **static):
    if specs is None:
        specs = [SMEM if a.dtype == jnp.int32 else VMEM for a in args]
    if out_specs is None:
        out_specs = jax.tree.map(lambda _: VMEM, out)
    moved = sum(a.size * a.dtype.itemsize for a in args)
    return pl.pallas_call(
        functools.partial(kernel, **static),
        out_shape=out,
        in_specs=specs,
        out_specs=out_specs,
        scratch_shapes=list(scratch),
        compiler_params=pltpu.CompilerParams(vmem_limit_bytes=VMEM_BYTES),
        cost_estimate=pl.CostEstimate(flops=flops, bytes_accessed=moved, transcendentals=0),
        name=name,
    )(*args)


def shape(*dims, dtype=jnp.float32):
    return jax.ShapeDtypeStruct(dims, dtype)


def ssq_scratch(half):
    return pltpu.VMEM((8, half), jnp.float32)


def image_plan(
    inputs,
    depth_kernel,
    depth_bias,
    norm_gain,
    norm_bias,
    proj_in,
    bias_in,
    grn_gamma,
    grn_beta,
    proj_out,
    bias_out,
):
    sections = lax.axis_size("section")
    count = lax.axis_size("row")
    me = lax.axis_index("row").astype(jnp.int32)
    section = lax.axis_index("section").astype(jnp.int32).reshape(1)
    me_ref = me.reshape(1)
    part = lax.axis_index("dp").astype(jnp.int32).reshape(1)
    _, _, rows, width, channels = inputs.shape
    height = rows * count
    cells = height * width
    lanes = -(-channels // LANES) * LANES
    half = proj_in.shape[2]
    span = depth_kernel.shape[1]
    order = (0, 2, 3, 1)
    bf16 = jnp.bfloat16
    whole = shape(height, width, channels, dtype=bf16)
    piece_shape = shape(rows, width, channels, dtype=bf16)
    act_shape = shape(cells, half, dtype=bf16)
    scale_shape = shape(2, 1, half)
    matmul = 2 * cells * channels * half

    helper, source = 1, sections - 1
    pieces = []
    for by in order:
        piece = lax.dynamic_index_in_dim(inputs, me ^ by, 0, keepdims=False)[0]
        if by:
            pairs = [(source * count + (p ^ by), helper * count + p) for p in range(count)]
            piece = lax.ppermute(piece, ("section", "row"), pairs)
        pieces.append(piece)

    def other_half(x, which):
        pairs = [(2 * s + p, 2 * s + 1 - p) for s in which for p in range(2)]
        return lax.ppermute(x, ("section", "dp"), pairs)

    w_in, w_out = proj_in[0], proj_out[0]
    cut = half // 2
    packed = jnp.concatenate(
        [w_in, jnp.concatenate([w_out[:cut], w_out[cut:]], axis=1)], axis=0
    )
    even = range(0, sections, 2)
    odd = range(1, sections, 2)
    other = other_half(packed, even)

    held = (
        depth_kernel, depth_bias, norm_gain, norm_bias, bias_out, bias_in, grn_gamma, grn_beta
    )
    cpar, fvec = call(
        prepare_kernel,
        "prepare",
        (part, *held),
        (shape(VECTORS + 8, lanes), shape(2, 3, half)),
        specs=[SMEM] + [HBM] * len(held),
        scratch=[pltpu.VMEM(v.shape, v.dtype) for v in held]
        + [pltpu.SemaphoreType.DMA((len(held),))],
    )

    def send(x, start, end):
        return lax.ppermute(x, "section", [(start, end)])

    def conv_pieces(pieces, cpar, order, on):
        out_rows = rows + 2 * REACH
        scratch = conv_scratch(rows, out_rows, width, lanes)
        parts = []
        for piece in pieces[:-1]:
            if parts:
                piece, parts[-1] = lax.optimization_barrier((piece, parts[-1]))
            part = call(
                piece_kernel,
                "conv_piece",
                (section, piece, cpar),
                shape(out_rows, width // 8, 8, lanes),
                scratch=scratch[:2],
                on=on,
            )
            parts.append(part)
        return call(
            last_piece_kernel,
            "last_piece",
            (section, me_ref, *pieces, *parts, cpar),
            shape(2, height, width, channels, dtype=bf16),
            scratch=scratch + [conv_scratch(1, height + 2 * REACH, width, lanes)[2]],
            order=order,
            on=on,
        )

    def up_own(flat, tick):
        return call(
            up_first_kernel,
            "up_own",
            (section, flat, w_in, fvec),
            (act_shape, shape(8, half)),
            flops=matmul,
            tick=tick,
        )

    def up_other(flat, other_in, ssq, tick):
        return call(
            up_second_kernel,
            "up_other",
            (section, flat, other_in, fvec, ssq),
            (act_shape, scale_shape),
            scratch=[ssq_scratch(half)],
            flops=matmul,
            tick=tick,
        )

    def unpack(packed):
        return call(unpack_kernel, "unpack", (packed,), shape(half, channels, dtype=bf16))

    def down_piece(x, acts, other_out, prev, order, tick, n):
        act_a, act_b, scale = acts
        return call(
            down_piece_kernel,
            "down_piece",
            (section, me_ref, x, act_a, act_b, w_out, other_out, scale, fvec, cpar, prev),
            piece_shape,
            flops=2 * matmul // count,
            order=order,
            tick=tick,
            n=n,
        )

    both = conv_pieces(pieces, send(cpar, 0, helper), order, helper)
    both, other, late = lax.optimization_barrier((both, other, packed))
    odd_other = other_half(late, odd)
    both = send(both, helper, 0)
    other_out = unpack(other)
    act_a, ssq = up_own(both, 0)
    act_b, scale = up_other(both, other, ssq, 0)
    result = call(
        first_down_kernel,
        "down",
        (section, both, act_a, act_b, w_out, other_out, scale, fvec, cpar),
        whole,
        flops=2 * matmul,
    )
    x = send(result, 0, 1)
    flat = call(
        conv_kernel,
        "conv",
        (section, x, cpar),
        whole,
        scratch=conv_scratch(height, height, width, lanes),
        tick=1,
    )
    act_a, ssq = up_own(flat, 1)
    odd_other, act_a = lax.optimization_barrier((odd_other, act_a))
    odd_out = unpack(odd_other)
    acts = (act_a, *up_other(flat, odd_other, ssq, 1))
    kept = [down_piece(x, acts, odd_out, result, None, 1, n) for n in range(count)]
    both = conv_pieces([send(piece, 1, 2) for piece in kept], cpar, None, 2)
    result = call(
        mlp_kernel,
        "mlp",
        (section, both, w_in, other, w_out, other_out, fvec, cpar, *kept, result),
        whole,
        scratch=[pltpu.VMEM((cells, half), bf16)] * 2
        + [ssq_scratch(half)] * 2
        + [pltpu.VMEM((2, 1, half), jnp.float32)],
        flops=4 * matmul,
        tick=2,
    )
    x = send(result, 2, 3)
    acts = call(
        conv_up_kernel,
        "conv_up",
        (section, x, cpar, w_in, odd_other, fvec),
        (act_shape, act_shape, scale_shape),
        scratch=conv_scratch(height, height, width, lanes)
        + [pltpu.VMEM((height, width, channels), bf16)]
        + [ssq_scratch(half)] * 2,
        flops=2 * matmul,
        tick=3,
    )
    done = []
    for n in (1, 2, 3, 0):
        piece = down_piece(x, acts, odd_out, result, order, 3, n)
        if n:
            piece = lax.ppermute(piece, "row", [(p, p ^ order[n]) for p in range(count)])
        done.append(piece)
    return call(
        place_kernel,
        "place",
        (me_ref, done[3], *done[:3]),
        shape(1, count, 1, rows, width, channels, dtype=bf16),
        out_specs=HBM,
        scratch=[pltpu.SemaphoreType.DMA((count,))],
        order=order,
    )


def extended(cells, sides, width):
    for axis, dim in sides:
        count = lax.axis_size(axis)
        ends = count - 1
        head = lax.slice_in_dim(cells, 0, width, axis=dim)
        tail = lax.slice_in_dim(cells, cells.shape[dim] - width, cells.shape[dim], axis=dim)
        cells = jnp.concatenate(
            [
                lax.ppermute(tail, axis, [(i, (i + 1) % count) for i in range(ends)]),
                cells,
                lax.ppermute(head, axis, [((i + 1) % count, i) for i in range(ends)]),
            ],
            axis=dim,
        )
    return cells


def depthwise(padded, kernel, bias_term):
    channels = padded.shape[-1]
    conv_out = lax.conv_general_dilated(
        padded.astype(jnp.float32),
        kernel.astype(jnp.float32)[:, :, None, :],
        (1, 1),
        "VALID",
        dimension_numbers=("NHWC", "HWIO", "NHWC"),
        feature_group_count=channels,
        precision=lax.Precision.HIGHEST,
    )
    return conv_out + bias_term.astype(jnp.float32)


def conv_block(current, params):
    (
        depth_kernel,
        depth_bias,
        norm_gain,
        norm_bias,
        proj_in,
        bias_in,
        grn_gamma,
        grn_beta,
        proj_out,
        bias_out,
    ) = params
    num_items, num_rows, num_cols, channels = current.shape
    padded = extended(current, (("row", 1),), REACH)
    padded = jnp.pad(padded, ((0, 0), (0, 0), (REACH, REACH), (0, 0)))
    conv_out = depthwise(padded, depth_kernel, depth_bias)
    center = conv_out - jnp.mean(conv_out, axis=-1, keepdims=True)
    spread = jnp.mean(center * center, axis=-1, keepdims=True)
    normed = (
        center * lax.rsqrt(spread + EPS_NORM) * norm_gain.astype(jnp.float32)
        + norm_bias.astype(jnp.float32)
    ).astype(jnp.bfloat16)
    flat_rows = normed.reshape(num_items * num_rows * num_cols, channels)
    raised = jnp.dot(flat_rows, proj_in, preferred_element_type=jnp.float32) + bias_in.astype(
        jnp.float32
    )
    active = jax.nn.gelu(raised, approximate=False).astype(jnp.bfloat16)
    grouped = active.reshape(num_items, num_rows * num_cols, -1).astype(jnp.float32)
    local_sq = jnp.sum(grouped * grouped, axis=1)
    total_sq = lax.psum(local_sq, "row")
    magnitude = jnp.sqrt(total_sq)
    grn_ratio = magnitude / (jnp.mean(magnitude, axis=-1, keepdims=True) + EPS_GRN)
    hidden = (
        grn_gamma.astype(jnp.float32) * grouped * grn_ratio[:, None, :]
        + grn_beta.astype(jnp.float32)
        + grouped
    ).astype(jnp.bfloat16)
    update = jnp.dot(
        hidden.reshape(num_items * num_rows * num_cols, -1),
        proj_out,
        preferred_element_type=jnp.float32,
    ) + bias_out.astype(jnp.float32)
    return (
        current.astype(jnp.float32) + update.reshape(num_items, num_rows, num_cols, channels)
    ).astype(jnp.bfloat16)


def rows_plan(inputs, *weights):
    (
        depth_kernel,
        depth_bias,
        norm_gain,
        norm_bias,
        proj_in,
        bias_in,
        grn_gamma,
        grn_beta,
        proj_out,
        bias_out,
    ) = weights
    proj_in = lax.all_gather(proj_in, "dp", axis=2, tiled=True)
    proj_out = lax.all_gather(proj_out, "dp", axis=1, tiled=True)
    own_params = tuple(
        w[0]
        for w in (
            depth_kernel,
            depth_bias,
            norm_gain,
            norm_bias,
            proj_in,
            bias_in,
            grn_gamma,
            grn_beta,
            proj_out,
            bias_out,
        )
    )
    sections = lax.axis_size("section")
    section_index = lax.axis_index("section")
    num_micro = inputs.shape[0]
    num_ticks = num_micro + sections - 1
    arriving = jnp.zeros_like(inputs[0])
    saved = jnp.zeros_like(inputs)
    for tick_index in range(num_ticks):
        fresh_input = inputs[min(tick_index, num_micro - 1)]
        current = jnp.where(section_index == 0, fresh_input, arriving)
        produced = conv_block(current, own_params)
        slot_index = tick_index - section_index
        is_valid = jnp.logical_and(slot_index >= 0, slot_index < num_micro)
        safe_slot = jnp.clip(slot_index, 0, num_micro - 1)
        previous = lax.dynamic_index_in_dim(saved, safe_slot, 0, keepdims=False)
        saved = lax.dynamic_update_index_in_dim(
            saved, jnp.where(is_valid, produced, previous), safe_slot, 0
        )
        if tick_index + 1 < num_ticks:
            arriving = lax.ppermute(
                produced, "section", [(i, i + 1) for i in range(sections - 1)]
            )
    return saved[None]


def on_device(inputs, *weights):
    num_micro, images, local_rows, width, channels = inputs.shape
    one_image_each = (
        images == 1
        and lax.axis_size("row") == num_micro == 4
        and lax.axis_size("dp") == 2
        and lax.axis_size("section") == 4
        and local_rows % 4 == 0
        and width % 16 == 0
        and weights[4].shape[2] == 2 * channels
    )
    plan = image_plan if one_image_each else rows_plan
    return plan(inputs, *weights)


def solution(mesh):
    return jax.shard_map(
        on_device,
        mesh=mesh,
        in_specs=(
            P(None, "dp", "row", None, None),
            P("section", None, None, None),
            P("section", None),
            P("section", None),
            P("section", None),
            P("section", None, "dp"),
            P("section", None),
            P("section", None),
            P("section", None),
            P("section", "dp", None),
            P("section", None),
        ),
        out_specs=P("section", None, "dp", "row", None, None),
        check_vma=False,
    )
```

```python
import functools

import jax
import jax.numpy as jnp
from jax import lax
from jax.experimental import pallas as pl
from jax.experimental.pallas import tpu as pltpu
from jax.sharding import PartitionSpec as P

EPS_NORM = 1e-06
EPS_GRN = 1e-06
LANES = 128
VMEM_BYTES = 20 * 1024 * 1024
REACH = 3
CHUNK = 4
NORM_ROWS = 8
IN_ORDER = (0, 1, 2, 3)
VECTORS = 56


def fill_columns(xp, xs, x, channels):
    height, reach_cols, blocks, lanes = xs.shape
    stride = reach_cols - 2 * REACH
    width = stride * blocks
    groups = lanes // LANES
    xp[...] = jnp.zeros(xp.shape, jnp.float32)

    unroll = min(height, NORM_ROWS)

    def rows(n, carry):
        for k in range(unroll):
            r = unroll * n + k
            row = x[r].astype(jnp.float32)
            for g in range(groups):
                at = slice(g * LANES, (g + 1) * LANES)
                own = row[:, g * LANES : min((g + 1) * LANES, channels)]
                xp[k * groups + g, 8 : 8 + width, 0 : own.shape[1]] = own
                for q in range(reach_cols):
                    near = pl.ds(8 - REACH + q, blocks, stride=stride)
                    xs[r, q, :, at] = xp[k * groups + g, near, :]
        return carry

    lax.fori_loop(0, height // unroll, rows, 0)


def conv(xs, cpar, cq):
    rows = xs.shape[0]
    height, stride, blocks, lanes = cq.shape
    span = 2 * REACH + 1
    above = (height - rows) // 2

    def group(g, carry):
        at = pl.ds(pl.multiple_of(g * LANES, LANES), LANES)

        def column(q, carry):
            bias = jnp.broadcast_to(cpar[VECTORS : VECTORS + 1, at], (blocks, LANES))
            acc = [None if above else bias] * height
            for j in range(span):
                kern = [
                    jnp.broadcast_to(cpar[i * span + j : i * span + j + 1, at], (blocks, LANES))
                    for i in range(span)
                ]
                for r in range(rows):
                    x_row = xs[r, q + j, :, at]
                    for i in range(span):
                        h = r + above + REACH - i
                        if 0 <= h < height:
                            term = kern[i] * x_row
                            acc[h] = term if acc[h] is None else acc[h] + term
            for h in range(height):
                cq[h, q, :, at] = acc[h]
            return carry

        return lax.fori_loop(0, stride, column, carry)

    lax.fori_loop(0, lanes // LANES, group, 0)


def norm(cq, cpar, xp, flat, skip=0):
    padded, stride, blocks, lanes = cq.shape
    height = padded - 2 * skip
    gain = cpar[VECTORS + 1 : VECTORS + 2, :]
    shift = cpar[VECTORS + 2 : VECTORS + 3, :]
    channels = flat.shape[2]
    width = stride * blocks
    groups = lanes // LANES
    inside = lax.broadcasted_iota(jnp.int32, (blocks, lanes), 1) < channels

    def rows(n, carry):
        for k in range(NORM_ROWS):
            h = NORM_ROWS * n + k
            for q in range(stride):
                v = cq[h + skip, q]
                mean = jnp.sum(v, axis=-1, keepdims=True) * (1.0 / channels)
                c = jnp.where(inside, v - mean, 0.0)
                var = jnp.sum(c * c, axis=-1, keepdims=True) * (1.0 / channels)
                c = c * lax.rsqrt(var + EPS_NORM) * gain + shift
                for g in range(groups):
                    at = slice(g * LANES, (g + 1) * LANES)
                    xp[k * groups + g, pl.ds(q, blocks, stride=stride), :] = c[:, at]
            for g in range(groups):
                at = slice(g * LANES, min((g + 1) * LANES, channels))
                flat[h, :, at] = xp[k * groups + g, 0:width, 0 : at.stop - at.start].astype(
                    jnp.bfloat16
                )
        return carry

    lax.fori_loop(0, height // NORM_ROWS, rows, 0)


def conv_norm(x, cpar, flat, xp, xs, cq):
    fill_columns(xp, xs, x, x.shape[2])
    conv(xs, cpar, cq)
    norm(cq, cpar, xp, flat)


def conv_scratch(rows, out_rows, width, lanes):
    return [
        pltpu.VMEM((NORM_ROWS * lanes // LANES, width + 16, LANES), jnp.float32),
        pltpu.VMEM((rows, width // 8 + 2 * REACH, 8, lanes), jnp.float32),
        pltpu.VMEM((out_rows, width // 8, 8, lanes), jnp.float32),
    ]


def gelu(v):
    return 0.5 * v * (1.0 + lax.erf(v * (0.5**0.5)))


def up(flat, w_in, bias, act, ssq):
    height, width, channels = flat.shape
    cells = height * width
    half = w_in.shape[1]
    step = 2 * LANES

    def units(start, count):
        raised = jnp.dot(
            flat[...].reshape(cells, channels),
            w_in[0:channels, pl.ds(start, count)],
            preferred_element_type=jnp.float32,
        )
        active = gelu(raised + bias[0:1, pl.ds(start, count)])
        act[:, pl.ds(start, count)] = active.astype(jnp.bfloat16)
        squares = (active * active).reshape(cells // 8, 8, count)
        ssq[:, pl.ds(start, count)] = jnp.sum(squares, axis=0)

    for start in range(0, half, step):
        units(start, min(step, half - start))


def norm_scale(ssqs, fvec, scale):
    half = fvec.shape[2]
    magnitude = [jnp.sqrt(jnp.sum(ssq[...], axis=0, keepdims=True)) for ssq in ssqs]
    mean = jnp.sum(magnitude[0] + magnitude[1], axis=1, keepdims=True) * (0.5 / half)
    for which in range(2):
        ratio = magnitude[which] / (mean + EPS_GRN)
        scale[which] = fvec[which, 1:2, :] * ratio + 1.0


def down(x_rows, first_row, acts, outs, scale, fvec, cpar):
    _, width, channels = x_rows.shape
    cells = CHUNK * width
    at = pl.ds(pl.multiple_of(first_row * width, cells), cells)
    update = cpar[VECTORS + 3 : VECTORS + 4, 0:channels]
    for which in range(2):
        a = acts[which][at, :].astype(jnp.float32)
        hidden = (a * scale[which] + fvec[which, 2:3, :]).astype(jnp.bfloat16)
        update = update + jnp.dot(hidden, outs[which][...], preferred_element_type=jnp.float32)
    return (x_rows.astype(jnp.float32) + update.reshape(CHUNK, width, channels)).astype(
        jnp.bfloat16
    )


def down_all(x, acts, outs, scale, fvec, cvec, out):
    def rows(n, carry):
        at = pl.ds(n * CHUNK, CHUNK)
        out[at] = down(x[at], n * CHUNK, acts, outs, scale, fvec, cvec)
        return carry

    lax.fori_loop(0, x.shape[0] // CHUNK, rows, 0)


def prepare_kernel(part, kernel, *refs):
    vectors, (cpar, fvec), (held, *staged), sems = refs[:7], refs[7:9], refs[9:-1], refs[-1]
    moves = [(kernel, held), *zip(vectors, staged)]
    copies = [pltpu.make_async_copy(a, b, sems.at[n]) for n, (a, b) in enumerate(moves)]
    for copy in copies:
        copy.start()
    cpar[...] = jnp.zeros(cpar.shape, jnp.float32)
    for copy in copies:
        copy.wait()
    channels = kernel.shape[3]
    span = kernel.shape[1]
    half = fvec.shape[2]
    for i in range(span):
        cpar[i * span : (i + 1) * span, 0:channels] = held[0, i].astype(jnp.float32)
    for n in range(4):
        cpar[VECTORS + n : VECTORS + n + 1, 0:channels] = staged[n][...].astype(jnp.float32)
    first = part[0] == 0
    for n in range(3):
        v = staged[4 + n][...].astype(jnp.float32)
        low, high = v[:, 0:half], v[:, half:]
        fvec[0, n : n + 1, :] = jnp.where(first, low, high)
        fvec[1, n : n + 1, :] = jnp.where(first, high, low)


def block_of(me, order, n):
    return n if order is None else me[0] ^ order[n]


def piece_kernel(section, piece, cpar, part, xp, xs, *, on):
    @pl.when(section[0] == on)
    def _():
        fill_columns(xp, xs, piece, piece.shape[2])
        conv(xs, cpar, part)


def last_piece_kernel(section, me, *refs, order, on):
    count = len(order or IN_ORDER)
    pieces, parts = refs[:count], refs[count : 2 * count - 1]
    cpar, both, xp, xs, own, cq = refs[2 * count - 1 :]
    x, flat = both.at[0], both.at[1]
    rows = pieces[0].shape[0]

    @pl.when(section[0] == on)
    def _():
        bias = cpar[VECTORS : VECTORS + 1, :].reshape(1, 1, 1, cq.shape[3])
        cq[...] = jnp.broadcast_to(bias, cq.shape)
        fill_columns(xp, xs, pieces[-1], x.shape[2])
        conv(xs, cpar, own)
        for n, (piece, part) in enumerate(zip(pieces, (*parts, own))):
            at = block_of(me, order, n) * rows
            x[pl.ds(at, rows)] = piece[...]
            cq[pl.ds(at, rows + 2 * REACH)] += part[...]
        norm(cq, cpar, xp, flat, REACH)


def conv_kernel(section, x, cpar, flat, xp, xs, cq, *, tick):
    @pl.when(section[0] == tick)
    def _():
        conv_norm(x, cpar, flat, xp, xs, cq)


def normed_part(ref):
    return ref if len(ref.shape) == 3 else ref.at[1]


def unpack_kernel(packed, w_out):
    cut, channels = w_out.shape[0] // 2, w_out.shape[1]
    first = packed.shape[0] - cut
    w_out[0:cut] = packed[first:, 0:channels]
    w_out[cut:] = packed[first:, channels : 2 * channels]


def up_first_kernel(section, flat, w_in, fvec, act, ssq, *, tick):
    @pl.when(section[0] == tick)
    def _():
        up(normed_part(flat), w_in, fvec.at[0], act, ssq)


def up_second_kernel(section, flat, w_in, fvec, other, act, scale, ssq, *, tick):
    @pl.when(section[0] == tick)
    def _():
        up(normed_part(flat), w_in, fvec.at[1], act, ssq)
        norm_scale((other, ssq), fvec, scale)


def first_down_kernel(section, both, act_a, act_b, out_a, out_b, scale, fvec, cpar, out):
    @pl.when(section[0] == 0)
    def _():
        down_all(both.at[0], (act_a, act_b), (out_a, out_b), scale, fvec, cpar, out)


def down_piece_kernel(
    section, me, x, act_a, act_b, out_a, out_b, scale, fvec, cpar, prev, out, *, order, tick, n
):
    first_row = block_of(me, order, n) * CHUNK
    at = pl.ds(first_row, CHUNK)

    @pl.when(section[0] == tick)
    def _():
        out[...] = down(x[at], first_row, (act_a, act_b), (out_a, out_b), scale, fvec, cpar)

    @pl.when(section[0] != tick)
    def _():
        out[...] = prev[at]


def mlp_kernel(section, both, in_a, in_b, out_a, out_b, fvec, cpar, *refs, tick):
    *pieces, prev, out, act_a, act_b, ssq_a, ssq_b, scale = refs
    x, flat = both.at[0], both.at[1]

    @pl.when(section[0] == tick)
    def _():
        up(flat, in_a, fvec.at[0], act_a, ssq_a)
        up(flat, in_b, fvec.at[1], act_b, ssq_b)
        norm_scale((ssq_a, ssq_b), fvec, scale)
        down_all(x, (act_a, act_b), (out_a, out_b), scale, fvec, cpar, out)

    @pl.when(section[0] == tick - 1)
    def _():
        for n, piece in enumerate(pieces):
            out[n * CHUNK : (n + 1) * CHUNK] = piece[...]

    @pl.when(section[0] < tick - 1)
    def _():
        out[...] = prev[...]


def conv_up_kernel(section, x, cpar, in_a, in_b, fvec, *refs, tick):
    act_a, act_b, scale, xp, xs, cq, flat, ssq_a, ssq_b = refs

    @pl.when(section[0] == tick)
    def _():
        conv_norm(x, cpar, flat, xp, xs, cq)
        up(flat, in_a, fvec.at[0], act_a, ssq_a)
        up(flat, in_b, fvec.at[1], act_b, ssq_b)
        norm_scale((ssq_a, ssq_b), fvec, scale)


def place_kernel(me, *refs, order):
    *pieces, saved, sems = refs
    copies = [
        pltpu.make_async_copy(piece, saved.at[0, block_of(me, order, n), 0], sems.at[n])
        for n, piece in enumerate(pieces)
    ]
    for copy in copies:
        copy.start()
    for copy in copies:
        copy.wait()


SMEM = pl.BlockSpec(memory_space=pltpu.SMEM)
VMEM = pl.BlockSpec(memory_space=pltpu.VMEM)
HBM = pl.BlockSpec(memory_space=pltpu.HBM)


def call(kernel, name, args, out, specs=None, out_specs=None, scratch=(), flops=0, **static):
    if specs is None:
        specs = [SMEM if a.dtype == jnp.int32 else VMEM for a in args]
    if out_specs is None:
        out_specs = jax.tree.map(lambda _: VMEM, out)
    moved = sum(a.size * a.dtype.itemsize for a in args)
    return pl.pallas_call(
        functools.partial(kernel, **static),
        out_shape=out,
        in_specs=specs,
        out_specs=out_specs,
        scratch_shapes=list(scratch),
        compiler_params=pltpu.CompilerParams(vmem_limit_bytes=VMEM_BYTES),
        cost_estimate=pl.CostEstimate(flops=flops, bytes_accessed=moved, transcendentals=0),
        name=name,
    )(*args)


def shape(*dims, dtype=jnp.float32):
    return jax.ShapeDtypeStruct(dims, dtype)


def ssq_scratch(half):
    return pltpu.VMEM((8, half), jnp.float32)


def image_plan(
    inputs,
    depth_kernel,
    depth_bias,
    norm_gain,
    norm_bias,
    proj_in,
    bias_in,
    grn_gamma,
    grn_beta,
    proj_out,
    bias_out,
):
    sections = lax.axis_size("section")
    count = lax.axis_size("row")
    me = lax.axis_index("row").astype(jnp.int32)
    section = lax.axis_index("section").astype(jnp.int32).reshape(1)
    me_ref = me.reshape(1)
    part = lax.axis_index("dp").astype(jnp.int32).reshape(1)
    _, _, rows, width, channels = inputs.shape
    height = rows * count
    cells = height * width
    lanes = -(-channels // LANES) * LANES
    half = proj_in.shape[2]
    span = depth_kernel.shape[1]
    order = (0, 2, 3, 1)
    bf16 = jnp.bfloat16
    whole = shape(height, width, channels, dtype=bf16)
    piece_shape = shape(rows, width, channels, dtype=bf16)
    act_shape = shape(cells, half, dtype=bf16)
    scale_shape = shape(2, 1, half)
    matmul = 2 * cells * channels * half

    helper, source = 1, sections - 1
    pieces = []
    for by in order:
        piece = lax.dynamic_index_in_dim(inputs, me ^ by, 0, keepdims=False)[0]
        if by:
            pairs = [(source * count + (p ^ by), helper * count + p) for p in range(count)]
            piece = lax.ppermute(piece, ("section", "row"), pairs)
        pieces.append(piece)

    def other_half(x, which):
        pairs = [(2 * s + p, 2 * s + 1 - p) for s in which for p in range(2)]
        return lax.ppermute(x, ("section", "dp"), pairs)

    w_in, w_out = proj_in[0], proj_out[0]
    cut = half // 2
    even = range(0, sections, 2)
    odd = range(1, sections, 2)
    other_in = other_half(w_in, even)
    other_out = other_half(w_out, even)

    held = (
        depth_kernel, depth_bias, norm_gain, norm_bias, bias_out, bias_in, grn_gamma, grn_beta
    )
    cpar, fvec = call(
        prepare_kernel,
        "prepare",
        (part, *held),
        (shape(VECTORS + 8, lanes), shape(2, 3, half)),
        specs=[SMEM] + [HBM] * len(held),
        scratch=[pltpu.VMEM(v.shape, v.dtype) for v in held]
        + [pltpu.SemaphoreType.DMA((len(held),))],
    )

    def send(x, start, end):
        return lax.ppermute(x, "section", [(start, end)])

    def conv_pieces(pieces, cpar, order, on):
        out_rows = rows + 2 * REACH
        scratch = conv_scratch(rows, out_rows, width, lanes)
        parts = []
        for piece in pieces[:-1]:
            if parts:
                piece, parts[-1] = lax.optimization_barrier((piece, parts[-1]))
            part = call(
                piece_kernel,
                "conv_piece",
                (section, piece, cpar),
                shape(out_rows, width // 8, 8, lanes),
                scratch=scratch[:2],
                on=on,
            )
            parts.append(part)
        return call(
            last_piece_kernel,
            "last_piece",
            (section, me_ref, *pieces, *parts, cpar),
            shape(2, height, width, channels, dtype=bf16),
            scratch=scratch + [conv_scratch(1, height + 2 * REACH, width, lanes)[2]],
            order=order,
            on=on,
        )

    def up_own(flat, tick):
        return call(
            up_first_kernel,
            "up_own",
            (section, flat, w_in, fvec),
            (act_shape, shape(8, half)),
            flops=matmul,
            tick=tick,
        )

    def up_other(flat, other_in, ssq, tick):
        return call(
            up_second_kernel,
            "up_other",
            (section, flat, other_in, fvec, ssq),
            (act_shape, scale_shape),
            scratch=[ssq_scratch(half)],
            flops=matmul,
            tick=tick,
        )

    def unpack(packed):
        return call(unpack_kernel, "unpack", (packed,), shape(half, channels, dtype=bf16))

    def down_piece(x, acts, other_out, prev, order, tick, n):
        act_a, act_b, scale = acts
        return call(
            down_piece_kernel,
            "down_piece",
            (section, me_ref, x, act_a, act_b, w_out, other_out, scale, fvec, cpar, prev),
            piece_shape,
            flops=2 * matmul // count,
            order=order,
            tick=tick,
            n=n,
        )

    both = conv_pieces(pieces, send(cpar, 0, helper), order, helper)
    both, other_in, late_in, late_out = lax.optimization_barrier((both, other_in, w_in, w_out))
    late = jnp.concatenate(
        [late_in, jnp.concatenate([late_out[:cut], late_out[cut:]], axis=1)], axis=0
    )
    odd_other = other_half(late, odd)
    both = send(both, helper, 0)
    act_a, ssq = up_own(both, 0)
    act_b, scale = up_other(both, other_in, ssq, 0)
    result = call(
        first_down_kernel,
        "down",
        (section, both, act_a, act_b, w_out, other_out, scale, fvec, cpar),
        whole,
        flops=2 * matmul,
    )
    x = send(result, 0, 1)
    flat = call(
        conv_kernel,
        "conv",
        (section, x, cpar),
        whole,
        scratch=conv_scratch(height, height, width, lanes),
        tick=1,
    )
    act_a, ssq = up_own(flat, 1)
    odd_other, act_a = lax.optimization_barrier((odd_other, act_a))
    odd_out = unpack(odd_other)
    acts = (act_a, *up_other(flat, odd_other, ssq, 1))
    kept = [down_piece(x, acts, odd_out, result, None, 1, n) for n in range(count)]
    both = conv_pieces([send(piece, 1, 2) for piece in kept], cpar, None, 2)
    result = call(
        mlp_kernel,
        "mlp",
        (section, both, w_in, other_in, w_out, other_out, fvec, cpar, *kept, result),
        whole,
        scratch=[pltpu.VMEM((cells, half), bf16)] * 2
        + [ssq_scratch(half)] * 2
        + [pltpu.VMEM((2, 1, half), jnp.float32)],
        flops=4 * matmul,
        tick=2,
    )
    x = send(result, 2, 3)
    acts = call(
        conv_up_kernel,
        "conv_up",
        (section, x, cpar, w_in, odd_other, fvec),
        (act_shape, act_shape, scale_shape),
        scratch=conv_scratch(height, height, width, lanes)
        + [pltpu.VMEM((height, width, channels), bf16)]
        + [ssq_scratch(half)] * 2,
        flops=2 * matmul,
        tick=3,
    )
    done = []
    for n in (1, 2, 3, 0):
        piece = down_piece(x, acts, odd_out, result, order, 3, n)
        if n:
            piece = lax.ppermute(piece, "row", [(p, p ^ order[n]) for p in range(count)])
        done.append(piece)
    return call(
        place_kernel,
        "place",
        (me_ref, done[3], *done[:3]),
        shape(1, count, 1, rows, width, channels, dtype=bf16),
        out_specs=HBM,
        scratch=[pltpu.SemaphoreType.DMA((count,))],
        order=order,
    )


def extended(cells, sides, width):
    for axis, dim in sides:
        count = lax.axis_size(axis)
        ends = count - 1
        head = lax.slice_in_dim(cells, 0, width, axis=dim)
        tail = lax.slice_in_dim(cells, cells.shape[dim] - width, cells.shape[dim], axis=dim)
        cells = jnp.concatenate(
            [
                lax.ppermute(tail, axis, [(i, (i + 1) % count) for i in range(ends)]),
                cells,
                lax.ppermute(head, axis, [((i + 1) % count, i) for i in range(ends)]),
            ],
            axis=dim,
        )
    return cells


def depthwise(padded, kernel, bias_term):
    channels = padded.shape[-1]
    conv_out = lax.conv_general_dilated(
        padded.astype(jnp.float32),
        kernel.astype(jnp.float32)[:, :, None, :],
        (1, 1),
        "VALID",
        dimension_numbers=("NHWC", "HWIO", "NHWC"),
        feature_group_count=channels,
        precision=lax.Precision.HIGHEST,
    )
    return conv_out + bias_term.astype(jnp.float32)


def conv_block(current, params):
    (
        depth_kernel,
        depth_bias,
        norm_gain,
        norm_bias,
        proj_in,
        bias_in,
        grn_gamma,
        grn_beta,
        proj_out,
        bias_out,
    ) = params
    num_items, num_rows, num_cols, channels = current.shape
    padded = extended(current, (("row", 1),), REACH)
    padded = jnp.pad(padded, ((0, 0), (0, 0), (REACH, REACH), (0, 0)))
    conv_out = depthwise(padded, depth_kernel, depth_bias)
    center = conv_out - jnp.mean(conv_out, axis=-1, keepdims=True)
    spread = jnp.mean(center * center, axis=-1, keepdims=True)
    normed = (
        center * lax.rsqrt(spread + EPS_NORM) * norm_gain.astype(jnp.float32)
        + norm_bias.astype(jnp.float32)
    ).astype(jnp.bfloat16)
    flat_rows = normed.reshape(num_items * num_rows * num_cols, channels)
    raised = jnp.dot(flat_rows, proj_in, preferred_element_type=jnp.float32) + bias_in.astype(
        jnp.float32
    )
    active = jax.nn.gelu(raised, approximate=False).astype(jnp.bfloat16)
    grouped = active.reshape(num_items, num_rows * num_cols, -1).astype(jnp.float32)
    local_sq = jnp.sum(grouped * grouped, axis=1)
    total_sq = lax.psum(local_sq, "row")
    magnitude = jnp.sqrt(total_sq)
    grn_ratio = magnitude / (jnp.mean(magnitude, axis=-1, keepdims=True) + EPS_GRN)
    hidden = (
        grn_gamma.astype(jnp.float32) * grouped * grn_ratio[:, None, :]
        + grn_beta.astype(jnp.float32)
        + grouped
    ).astype(jnp.bfloat16)
    update = jnp.dot(
        hidden.reshape(num_items * num_rows * num_cols, -1),
        proj_out,
        preferred_element_type=jnp.float32,
    ) + bias_out.astype(jnp.float32)
    return (
        current.astype(jnp.float32) + update.reshape(num_items, num_rows, num_cols, channels)
    ).astype(jnp.bfloat16)


def rows_plan(inputs, *weights):
    (
        depth_kernel,
        depth_bias,
        norm_gain,
        norm_bias,
        proj_in,
        bias_in,
        grn_gamma,
        grn_beta,
        proj_out,
        bias_out,
    ) = weights
    proj_in = lax.all_gather(proj_in, "dp", axis=2, tiled=True)
    proj_out = lax.all_gather(proj_out, "dp", axis=1, tiled=True)
    own_params = tuple(
        w[0]
        for w in (
            depth_kernel,
            depth_bias,
            norm_gain,
            norm_bias,
            proj_in,
            bias_in,
            grn_gamma,
            grn_beta,
            proj_out,
            bias_out,
        )
    )
    sections = lax.axis_size("section")
    section_index = lax.axis_index("section")
    num_micro = inputs.shape[0]
    num_ticks = num_micro + sections - 1
    arriving = jnp.zeros_like(inputs[0])
    saved = jnp.zeros_like(inputs)
    for tick_index in range(num_ticks):
        fresh_input = inputs[min(tick_index, num_micro - 1)]
        current = jnp.where(section_index == 0, fresh_input, arriving)
        produced = conv_block(current, own_params)
        slot_index = tick_index - section_index
        is_valid = jnp.logical_and(slot_index >= 0, slot_index < num_micro)
        safe_slot = jnp.clip(slot_index, 0, num_micro - 1)
        previous = lax.dynamic_index_in_dim(saved, safe_slot, 0, keepdims=False)
        saved = lax.dynamic_update_index_in_dim(
            saved, jnp.where(is_valid, produced, previous), safe_slot, 0
        )
        if tick_index + 1 < num_ticks:
            arriving = lax.ppermute(
                produced, "section", [(i, i + 1) for i in range(sections - 1)]
            )
    return saved[None]


def on_device(inputs, *weights):
    num_micro, images, local_rows, width, channels = inputs.shape
    one_image_each = (
        images == 1
        and lax.axis_size("row") == num_micro == 4
        and lax.axis_size("dp") == 2
        and lax.axis_size("section") == 4
        and local_rows % 4 == 0
        and width % 16 == 0
        and weights[4].shape[2] == 2 * channels
    )
    plan = image_plan if one_image_each else rows_plan
    return plan(inputs, *weights)


def solution(mesh):
    return jax.shard_map(
        on_device,
        mesh=mesh,
        in_specs=(
            P(None, "dp", "row", None, None),
            P("section", None, None, None),
            P("section", None),
            P("section", None),
            P("section", None),
            P("section", None, "dp"),
            P("section", None),
            P("section", None),
            P("section", None),
            P("section", "dp", None),
            P("section", None),
        ),
        out_specs=P("section", None, "dp", "row", None, None),
        check_vma=False,
    )
```

```python
import functools

import jax
import jax.numpy as jnp
from jax import lax
from jax.experimental import pallas as pl
from jax.experimental.pallas import tpu as pltpu
from jax.sharding import PartitionSpec as P

EPS_NORM = 1e-06
EPS_GRN = 1e-06
LANES = 128
VMEM_BYTES = 20 * 1024 * 1024
REACH = 3
CHUNK = 4
NORM_ROWS = 8
IN_ORDER = (0, 1, 2, 3)
VECTORS = 56


def fill_columns(xp, xs, x, channels):
    height, reach_cols, blocks, lanes = xs.shape
    stride = reach_cols - 2 * REACH
    width = stride * blocks
    groups = lanes // LANES
    xp[...] = jnp.zeros(xp.shape, jnp.float32)

    unroll = min(height, NORM_ROWS)

    def rows(n, carry):
        for k in range(unroll):
            r = unroll * n + k
            row = x[r].astype(jnp.float32)
            for g in range(groups):
                at = slice(g * LANES, (g + 1) * LANES)
                own = row[:, g * LANES : min((g + 1) * LANES, channels)]
                xp[k * groups + g, 8 : 8 + width, 0 : own.shape[1]] = own
                for q in range(reach_cols):
                    near = pl.ds(8 - REACH + q, blocks, stride=stride)
                    xs[r, q, :, at] = xp[k * groups + g, near, :]
        return carry

    lax.fori_loop(0, height // unroll, rows, 0)


def conv(xs, cpar, cq):
    rows = xs.shape[0]
    height, stride, blocks, lanes = cq.shape
    span = 2 * REACH + 1
    above = (height - rows) // 2

    def group(g, carry):
        at = pl.ds(pl.multiple_of(g * LANES, LANES), LANES)

        def column(q, carry):
            bias = jnp.broadcast_to(cpar[VECTORS : VECTORS + 1, at], (blocks, LANES))
            acc = [None if above else bias] * height
            for j in range(span):
                kern = [
                    jnp.broadcast_to(cpar[i * span + j : i * span + j + 1, at], (blocks, LANES))
                    for i in range(span)
                ]
                for r in range(rows):
                    x_row = xs[r, q + j, :, at]
                    for i in range(span):
                        h = r + above + REACH - i
                        if 0 <= h < height:
                            term = kern[i] * x_row
                            acc[h] = term if acc[h] is None else acc[h] + term
            for h in range(height):
                cq[h, q, :, at] = acc[h]
            return carry

        return lax.fori_loop(0, stride, column, carry)

    lax.fori_loop(0, lanes // LANES, group, 0)


def norm(cq, cpar, xp, flat, skip=0):
    padded, stride, blocks, lanes = cq.shape
    height = padded - 2 * skip
    gain = cpar[VECTORS + 1 : VECTORS + 2, :]
    shift = cpar[VECTORS + 2 : VECTORS + 3, :]
    channels = flat.shape[2]
    width = stride * blocks
    groups = lanes // LANES
    inside = lax.broadcasted_iota(jnp.int32, (blocks, lanes), 1) < channels

    def rows(n, carry):
        for k in range(NORM_ROWS):
            h = NORM_ROWS * n + k
            for q in range(stride):
                v = cq[h + skip, q]
                mean = jnp.sum(v, axis=-1, keepdims=True) * (1.0 / channels)
                c = jnp.where(inside, v - mean, 0.0)
                var = jnp.sum(c * c, axis=-1, keepdims=True) * (1.0 / channels)
                c = c * lax.rsqrt(var + EPS_NORM) * gain + shift
                for g in range(groups):
                    at = slice(g * LANES, (g + 1) * LANES)
                    xp[k * groups + g, pl.ds(q, blocks, stride=stride), :] = c[:, at]
            for g in range(groups):
                at = slice(g * LANES, min((g + 1) * LANES, channels))
                flat[h, :, at] = xp[k * groups + g, 0:width, 0 : at.stop - at.start].astype(
                    jnp.bfloat16
                )
        return carry

    lax.fori_loop(0, height // NORM_ROWS, rows, 0)


def conv_norm(x, cpar, flat, xp, xs, cq):
    fill_columns(xp, xs, x, x.shape[2])
    conv(xs, cpar, cq)
    norm(cq, cpar, xp, flat)


def conv_scratch(rows, out_rows, width, lanes):
    return [
        pltpu.VMEM((NORM_ROWS * lanes // LANES, width + 16, LANES), jnp.float32),
        pltpu.VMEM((rows, width // 8 + 2 * REACH, 8, lanes), jnp.float32),
        pltpu.VMEM((out_rows, width // 8, 8, lanes), jnp.float32),
    ]


def gelu(v):
    return 0.5 * v * (1.0 + lax.erf(v * (0.5**0.5)))


def up(flat, w_in, bias, act, ssq):
    height, width, channels = flat.shape
    cells = height * width
    half = w_in.shape[1]
    step = 2 * LANES

    def units(start, count):
        raised = jnp.dot(
            flat[...].reshape(cells, channels),
            w_in[0:channels, pl.ds(start, count)],
            preferred_element_type=jnp.float32,
        )
        active = gelu(raised + bias[0:1, pl.ds(start, count)])
        act[:, pl.ds(start, count)] = active.astype(jnp.bfloat16)
        squares = (active * active).reshape(cells // 8, 8, count)
        ssq[:, pl.ds(start, count)] = jnp.sum(squares, axis=0)

    for start in range(0, half, step):
        units(start, min(step, half - start))


def norm_scale(ssqs, fvec, scale):
    half = fvec.shape[2]
    magnitude = [jnp.sqrt(jnp.sum(ssq[...], axis=0, keepdims=True)) for ssq in ssqs]
    mean = jnp.sum(magnitude[0] + magnitude[1], axis=1, keepdims=True) * (0.5 / half)
    for which in range(2):
        ratio = magnitude[which] / (mean + EPS_GRN)
        scale[which] = fvec[which, 1:2, :] * ratio + 1.0


def down(x_rows, first_row, acts, outs, scale, fvec, cpar):
    _, width, channels = x_rows.shape
    cells = CHUNK * width
    at = pl.ds(pl.multiple_of(first_row * width, cells), cells)
    update = cpar[VECTORS + 3 : VECTORS + 4, 0:channels]
    for which in range(2):
        a = acts[which][at, :].astype(jnp.float32)
        hidden = (a * scale[which] + fvec[which, 2:3, :]).astype(jnp.bfloat16)
        update = update + jnp.dot(hidden, outs[which][...], preferred_element_type=jnp.float32)
    return (x_rows.astype(jnp.float32) + update.reshape(CHUNK, width, channels)).astype(
        jnp.bfloat16
    )


def down_all(x, acts, outs, scale, fvec, cvec, out):
    def rows(n, carry):
        at = pl.ds(n * CHUNK, CHUNK)
        out[at] = down(x[at], n * CHUNK, acts, outs, scale, fvec, cvec)
        return carry

    lax.fori_loop(0, x.shape[0] // CHUNK, rows, 0)


def prepare_kernel(part, kernel, *refs):
    vectors, (cpar, fvec), (held, *staged), sems = refs[:7], refs[7:9], refs[9:-1], refs[-1]
    moves = [(kernel, held), *zip(vectors, staged)]
    copies = [pltpu.make_async_copy(a, b, sems.at[n]) for n, (a, b) in enumerate(moves)]
    for copy in copies:
        copy.start()
    cpar[...] = jnp.zeros(cpar.shape, jnp.float32)
    for copy in copies:
        copy.wait()
    channels = kernel.shape[3]
    span = kernel.shape[1]
    half = fvec.shape[2]
    for i in range(span):
        cpar[i * span : (i + 1) * span, 0:channels] = held[0, i].astype(jnp.float32)
    for n in range(4):
        cpar[VECTORS + n : VECTORS + n + 1, 0:channels] = staged[n][...].astype(jnp.float32)
    first = part[0] == 0
    for n in range(3):
        v = staged[4 + n][...].astype(jnp.float32)
        low, high = v[:, 0:half], v[:, half:]
        fvec[0, n : n + 1, :] = jnp.where(first, low, high)
        fvec[1, n : n + 1, :] = jnp.where(first, high, low)


def block_of(me, order, n):
    return n if order is None else me[0] ^ order[n]


def piece_kernel(section, piece, cpar, part, xp, xs, *, on):
    @pl.when(section[0] == on)
    def _():
        fill_columns(xp, xs, piece, piece.shape[2])
        conv(xs, cpar, part)


def last_piece_kernel(section, me, *refs, order, on):
    count = len(order or IN_ORDER)
    pieces, parts = refs[:count], refs[count : 2 * count - 1]
    cpar, both, xp, xs, own, cq = refs[2 * count - 1 :]
    x, flat = both.at[0], both.at[1]
    rows = pieces[0].shape[0]

    @pl.when(section[0] == on)
    def _():
        bias = cpar[VECTORS : VECTORS + 1, :].reshape(1, 1, 1, cq.shape[3])
        cq[...] = jnp.broadcast_to(bias, cq.shape)
        fill_columns(xp, xs, pieces[-1], x.shape[2])
        conv(xs, cpar, own)
        for n, (piece, part) in enumerate(zip(pieces, (*parts, own))):
            at = block_of(me, order, n) * rows
            x[pl.ds(at, rows)] = piece[...]
            cq[pl.ds(at, rows + 2 * REACH)] += part[...]
        norm(cq, cpar, xp, flat, REACH)


def conv_kernel(section, x, cpar, flat, xp, xs, cq, *, tick):
    @pl.when(section[0] == tick)
    def _():
        conv_norm(x, cpar, flat, xp, xs, cq)


def normed_part(ref):
    return ref if len(ref.shape) == 3 else ref.at[1]


def unpack_kernel(packed, w_out):
    cut, channels = w_out.shape[0] // 2, w_out.shape[1]
    first = packed.shape[0] - cut
    w_out[0:cut] = packed[first:, 0:channels]
    w_out[cut:] = packed[first:, channels : 2 * channels]


def up_first_kernel(section, flat, w_in, fvec, act, ssq, *, tick):
    @pl.when(section[0] == tick)
    def _():
        up(normed_part(flat), w_in, fvec.at[0], act, ssq)


def up_second_kernel(section, flat, w_in, fvec, other, act, scale, ssq, *, tick):
    @pl.when(section[0] == tick)
    def _():
        up(normed_part(flat), w_in, fvec.at[1], act, ssq)
        norm_scale((other, ssq), fvec, scale)


def first_down_kernel(section, both, act_a, act_b, out_a, out_b, scale, fvec, cpar, out):
    @pl.when(section[0] == 0)
    def _():
        down_all(both.at[0], (act_a, act_b), (out_a, out_b), scale, fvec, cpar, out)


def down_piece_kernel(
    section, me, x, act_a, act_b, out_a, out_b, scale, fvec, cpar, prev, out, *, order, tick, n
):
    first_row = block_of(me, order, n) * CHUNK
    at = pl.ds(first_row, CHUNK)

    @pl.when(section[0] == tick)
    def _():
        out[...] = down(x[at], first_row, (act_a, act_b), (out_a, out_b), scale, fvec, cpar)

    @pl.when(section[0] != tick)
    def _():
        out[...] = prev[at]


def mlp_kernel(section, both, in_a, in_b, out_a, out_b, fvec, cpar, *refs, tick):
    *pieces, prev, out, act_a, act_b, ssq_a, ssq_b, scale = refs
    x, flat = both.at[0], both.at[1]

    @pl.when(section[0] == tick)
    def _():
        up(flat, in_a, fvec.at[0], act_a, ssq_a)
        up(flat, in_b, fvec.at[1], act_b, ssq_b)
        norm_scale((ssq_a, ssq_b), fvec, scale)
        down_all(x, (act_a, act_b), (out_a, out_b), scale, fvec, cpar, out)

    @pl.when(section[0] == tick - 1)
    def _():
        for n, piece in enumerate(pieces):
            out[n * CHUNK : (n + 1) * CHUNK] = piece[...]

    @pl.when(section[0] < tick - 1)
    def _():
        out[...] = prev[...]


def conv_up_kernel(section, x, cpar, in_a, in_b, fvec, *refs, tick):
    act_a, act_b, scale, xp, xs, cq, flat, ssq_a, ssq_b = refs

    @pl.when(section[0] == tick)
    def _():
        conv_norm(x, cpar, flat, xp, xs, cq)
        up(flat, in_a, fvec.at[0], act_a, ssq_a)
        up(flat, in_b, fvec.at[1], act_b, ssq_b)
        norm_scale((ssq_a, ssq_b), fvec, scale)


def place_kernel(me, *refs, order):
    *pieces, saved, sems = refs
    copies = [
        pltpu.make_async_copy(piece, saved.at[0, block_of(me, order, n), 0], sems.at[n])
        for n, piece in enumerate(pieces)
    ]
    for copy in copies:
        copy.start()
    for copy in copies:
        copy.wait()


SMEM = pl.BlockSpec(memory_space=pltpu.SMEM)
VMEM = pl.BlockSpec(memory_space=pltpu.VMEM)
HBM = pl.BlockSpec(memory_space=pltpu.HBM)


def call(kernel, name, args, out, specs=None, out_specs=None, scratch=(), flops=0, **static):
    if specs is None:
        specs = [SMEM if a.dtype == jnp.int32 else VMEM for a in args]
    if out_specs is None:
        out_specs = jax.tree.map(lambda _: VMEM, out)
    moved = sum(a.size * a.dtype.itemsize for a in args)
    return pl.pallas_call(
        functools.partial(kernel, **static),
        out_shape=out,
        in_specs=specs,
        out_specs=out_specs,
        scratch_shapes=list(scratch),
        compiler_params=pltpu.CompilerParams(vmem_limit_bytes=VMEM_BYTES),
        cost_estimate=pl.CostEstimate(flops=flops, bytes_accessed=moved, transcendentals=0),
        name=name,
    )(*args)


def shape(*dims, dtype=jnp.float32):
    return jax.ShapeDtypeStruct(dims, dtype)


def ssq_scratch(half):
    return pltpu.VMEM((8, half), jnp.float32)


def image_plan(
    inputs,
    depth_kernel,
    depth_bias,
    norm_gain,
    norm_bias,
    proj_in,
    bias_in,
    grn_gamma,
    grn_beta,
    proj_out,
    bias_out,
):
    sections = lax.axis_size("section")
    count = lax.axis_size("row")
    me = lax.axis_index("row").astype(jnp.int32)
    section = lax.axis_index("section").astype(jnp.int32).reshape(1)
    me_ref = me.reshape(1)
    part = lax.axis_index("dp").astype(jnp.int32).reshape(1)
    _, _, rows, width, channels = inputs.shape
    height = rows * count
    cells = height * width
    lanes = -(-channels // LANES) * LANES
    half = proj_in.shape[2]
    span = depth_kernel.shape[1]
    order = (0, 2, 1, 3)
    bf16 = jnp.bfloat16
    whole = shape(height, width, channels, dtype=bf16)
    piece_shape = shape(rows, width, channels, dtype=bf16)
    act_shape = shape(cells, half, dtype=bf16)
    scale_shape = shape(2, 1, half)
    matmul = 2 * cells * channels * half

    helper, source = 1, sections - 1
    pieces = []
    for by in order:
        piece = lax.dynamic_index_in_dim(inputs, me ^ by, 0, keepdims=False)[0]
        if by:
            pairs = [(source * count + (p ^ by), helper * count + p) for p in range(count)]
            piece = lax.ppermute(piece, ("section", "row"), pairs)
        pieces.append(piece)

    def other_half(x, which):
        pairs = [(2 * s + p, 2 * s + 1 - p) for s in which for p in range(2)]
        return lax.ppermute(x, ("section", "dp"), pairs)

    w_in, w_out = proj_in[0], proj_out[0]
    cut = half // 2
    even = range(0, sections, 2)
    odd = range(1, sections, 2)
    other_in = other_half(w_in, even)
    other_out = other_half(w_out, even)

    held = (
        depth_kernel, depth_bias, norm_gain, norm_bias, bias_out, bias_in, grn_gamma, grn_beta
    )
    cpar, fvec = call(
        prepare_kernel,
        "prepare",
        (part, *held),
        (shape(VECTORS + 8, lanes), shape(2, 3, half)),
        specs=[SMEM] + [HBM] * len(held),
        scratch=[pltpu.VMEM(v.shape, v.dtype) for v in held]
        + [pltpu.SemaphoreType.DMA((len(held),))],
    )

    def send(x, start, end):
        return lax.ppermute(x, "section", [(start, end)])

    def conv_pieces(pieces, cpar, order, on):
        out_rows = rows + 2 * REACH
        scratch = conv_scratch(rows, out_rows, width, lanes)
        parts = []
        for piece in pieces[:-1]:
            if parts:
                piece, parts[-1] = lax.optimization_barrier((piece, parts[-1]))
            part = call(
                piece_kernel,
                "conv_piece",
                (section, piece, cpar),
                shape(out_rows, width // 8, 8, lanes),
                scratch=scratch[:2],
                on=on,
            )
            parts.append(part)
        return call(
            last_piece_kernel,
            "last_piece",
            (section, me_ref, *pieces, *parts, cpar),
            shape(2, height, width, channels, dtype=bf16),
            scratch=scratch + [conv_scratch(1, height + 2 * REACH, width, lanes)[2]],
            order=order,
            on=on,
        )

    def up_own(flat, tick):
        return call(
            up_first_kernel,
            "up_own",
            (section, flat, w_in, fvec),
            (act_shape, shape(8, half)),
            flops=matmul,
            tick=tick,
        )

    def up_other(flat, other_in, ssq, tick):
        return call(
            up_second_kernel,
            "up_other",
            (section, flat, other_in, fvec, ssq),
            (act_shape, scale_shape),
            scratch=[ssq_scratch(half)],
            flops=matmul,
            tick=tick,
        )

    def unpack(packed):
        return call(unpack_kernel, "unpack", (packed,), shape(half, channels, dtype=bf16))

    def down_piece(x, acts, other_out, prev, order, tick, n):
        act_a, act_b, scale = acts
        return call(
            down_piece_kernel,
            "down_piece",
            (section, me_ref, x, act_a, act_b, w_out, other_out, scale, fvec, cpar, prev),
            piece_shape,
            flops=2 * matmul // count,
            order=order,
            tick=tick,
            n=n,
        )

    both = conv_pieces(pieces, send(cpar, 0, helper), order, helper)
    both, other_in, late_in, late_out = lax.optimization_barrier((both, other_in, w_in, w_out))
    late = jnp.concatenate(
        [late_in, jnp.concatenate([late_out[:cut], late_out[cut:]], axis=1)], axis=0
    )
    odd_other = other_half(late, odd)
    both = send(both, helper, 0)
    act_a, ssq = up_own(both, 0)
    act_b, scale = up_other(both, other_in, ssq, 0)
    result = call(
        first_down_kernel,
        "down",
        (section, both, act_a, act_b, w_out, other_out, scale, fvec, cpar),
        whole,
        flops=2 * matmul,
    )
    x = send(result, 0, 1)
    flat = call(
        conv_kernel,
        "conv",
        (section, x, cpar),
        whole,
        scratch=conv_scratch(height, height, width, lanes),
        tick=1,
    )
    act_a, ssq = up_own(flat, 1)
    odd_other, act_a = lax.optimization_barrier((odd_other, act_a))
    odd_out = unpack(odd_other)
    acts = (act_a, *up_other(flat, odd_other, ssq, 1))
    kept = [down_piece(x, acts, odd_out, result, None, 1, n) for n in range(count)]
    both = conv_pieces([send(piece, 1, 2) for piece in kept], cpar, None, 2)
    result = call(
        mlp_kernel,
        "mlp",
        (section, both, w_in, other_in, w_out, other_out, fvec, cpar, *kept, result),
        whole,
        scratch=[pltpu.VMEM((cells, half), bf16)] * 2
        + [ssq_scratch(half)] * 2
        + [pltpu.VMEM((2, 1, half), jnp.float32)],
        flops=4 * matmul,
        tick=2,
    )
    x = send(result, 2, 3)
    acts = call(
        conv_up_kernel,
        "conv_up",
        (section, x, cpar, w_in, odd_other, fvec),
        (act_shape, act_shape, scale_shape),
        scratch=conv_scratch(height, height, width, lanes)
        + [pltpu.VMEM((height, width, channels), bf16)]
        + [ssq_scratch(half)] * 2,
        flops=2 * matmul,
        tick=3,
    )
    done = []
    for n in (1, 2, 3, 0):
        piece = down_piece(x, acts, odd_out, result, order, 3, n)
        if n:
            piece = lax.ppermute(piece, "row", [(p, p ^ order[n]) for p in range(count)])
        done.append(piece)
    return call(
        place_kernel,
        "place",
        (me_ref, done[3], *done[:3]),
        shape(1, count, 1, rows, width, channels, dtype=bf16),
        out_specs=HBM,
        scratch=[pltpu.SemaphoreType.DMA((count,))],
        order=order,
    )


def extended(cells, sides, width):
    for axis, dim in sides:
        count = lax.axis_size(axis)
        ends = count - 1
        head = lax.slice_in_dim(cells, 0, width, axis=dim)
        tail = lax.slice_in_dim(cells, cells.shape[dim] - width, cells.shape[dim], axis=dim)
        cells = jnp.concatenate(
            [
                lax.ppermute(tail, axis, [(i, (i + 1) % count) for i in range(ends)]),
                cells,
                lax.ppermute(head, axis, [((i + 1) % count, i) for i in range(ends)]),
            ],
            axis=dim,
        )
    return cells


def depthwise(padded, kernel, bias_term):
    channels = padded.shape[-1]
    conv_out = lax.conv_general_dilated(
        padded.astype(jnp.float32),
        kernel.astype(jnp.float32)[:, :, None, :],
        (1, 1),
        "VALID",
        dimension_numbers=("NHWC", "HWIO", "NHWC"),
        feature_group_count=channels,
        precision=lax.Precision.HIGHEST,
    )
    return conv_out + bias_term.astype(jnp.float32)


def conv_block(current, params):
    (
        depth_kernel,
        depth_bias,
        norm_gain,
        norm_bias,
        proj_in,
        bias_in,
        grn_gamma,
        grn_beta,
        proj_out,
        bias_out,
    ) = params
    num_items, num_rows, num_cols, channels = current.shape
    padded = extended(current, (("row", 1),), REACH)
    padded = jnp.pad(padded, ((0, 0), (0, 0), (REACH, REACH), (0, 0)))
    conv_out = depthwise(padded, depth_kernel, depth_bias)
    center = conv_out - jnp.mean(conv_out, axis=-1, keepdims=True)
    spread = jnp.mean(center * center, axis=-1, keepdims=True)
    normed = (
        center * lax.rsqrt(spread + EPS_NORM) * norm_gain.astype(jnp.float32)
        + norm_bias.astype(jnp.float32)
    ).astype(jnp.bfloat16)
    flat_rows = normed.reshape(num_items * num_rows * num_cols, channels)
    raised = jnp.dot(flat_rows, proj_in, preferred_element_type=jnp.float32) + bias_in.astype(
        jnp.float32
    )
    active = jax.nn.gelu(raised, approximate=False).astype(jnp.bfloat16)
    grouped = active.reshape(num_items, num_rows * num_cols, -1).astype(jnp.float32)
    local_sq = jnp.sum(grouped * grouped, axis=1)
    total_sq = lax.psum(local_sq, "row")
    magnitude = jnp.sqrt(total_sq)
    grn_ratio = magnitude / (jnp.mean(magnitude, axis=-1, keepdims=True) + EPS_GRN)
    hidden = (
        grn_gamma.astype(jnp.float32) * grouped * grn_ratio[:, None, :]
        + grn_beta.astype(jnp.float32)
        + grouped
    ).astype(jnp.bfloat16)
    update = jnp.dot(
        hidden.reshape(num_items * num_rows * num_cols, -1),
        proj_out,
        preferred_element_type=jnp.float32,
    ) + bias_out.astype(jnp.float32)
    return (
        current.astype(jnp.float32) + update.reshape(num_items, num_rows, num_cols, channels)
    ).astype(jnp.bfloat16)


def rows_plan(inputs, *weights):
    (
        depth_kernel,
        depth_bias,
        norm_gain,
        norm_bias,
        proj_in,
        bias_in,
        grn_gamma,
        grn_beta,
        proj_out,
        bias_out,
    ) = weights
    proj_in = lax.all_gather(proj_in, "dp", axis=2, tiled=True)
    proj_out = lax.all_gather(proj_out, "dp", axis=1, tiled=True)
    own_params = tuple(
        w[0]
        for w in (
            depth_kernel,
            depth_bias,
            norm_gain,
            norm_bias,
            proj_in,
            bias_in,
            grn_gamma,
            grn_beta,
            proj_out,
            bias_out,
        )
    )
    sections = lax.axis_size("section")
    section_index = lax.axis_index("section")
    num_micro = inputs.shape[0]
    num_ticks = num_micro + sections - 1
    arriving = jnp.zeros_like(inputs[0])
    saved = jnp.zeros_like(inputs)
    for tick_index in range(num_ticks):
        fresh_input = inputs[min(tick_index, num_micro - 1)]
        current = jnp.where(section_index == 0, fresh_input, arriving)
        produced = conv_block(current, own_params)
        slot_index = tick_index - section_index
        is_valid = jnp.logical_and(slot_index >= 0, slot_index < num_micro)
        safe_slot = jnp.clip(slot_index, 0, num_micro - 1)
        previous = lax.dynamic_index_in_dim(saved, safe_slot, 0, keepdims=False)
        saved = lax.dynamic_update_index_in_dim(
            saved, jnp.where(is_valid, produced, previous), safe_slot, 0
        )
        if tick_index + 1 < num_ticks:
            arriving = lax.ppermute(
                produced, "section", [(i, i + 1) for i in range(sections - 1)]
            )
    return saved[None]


def on_device(inputs, *weights):
    num_micro, images, local_rows, width, channels = inputs.shape
    one_image_each = (
        images == 1
        and lax.axis_size("row") == num_micro == 4
        and lax.axis_size("dp") == 2
        and lax.axis_size("section") == 4
        and local_rows % 4 == 0
        and width % 16 == 0
        and weights[4].shape[2] == 2 * channels
    )
    plan = image_plan if one_image_each else rows_plan
    return plan(inputs, *weights)


def solution(mesh):
    return jax.shard_map(
        on_device,
        mesh=mesh,
        in_specs=(
            P(None, "dp", "row", None, None),
            P("section", None, None, None),
            P("section", None),
            P("section", None),
            P("section", None),
            P("section", None, "dp"),
            P("section", None),
            P("section", None),
            P("section", None),
            P("section", "dp", None),
            P("section", None),
        ),
        out_specs=P("section", None, "dp", "row", None, None),
        check_vma=False,
    )
```

```python
import functools

import jax
import jax.numpy as jnp
from jax import lax
from jax.experimental import pallas as pl
from jax.experimental.pallas import tpu as pltpu
from jax.sharding import PartitionSpec as P

EPS_NORM = 1e-06
EPS_GRN = 1e-06
LANES = 128
VMEM_BYTES = 20 * 1024 * 1024
REACH = 3
CHUNK = 4
NORM_ROWS = 16
IN_ORDER = (0, 1, 2, 3)
VECTORS = 56


def fill_columns(xp, xs, x, channels):
    height, reach_cols, blocks, lanes = xs.shape
    stride = reach_cols - 2 * REACH
    width = stride * blocks
    groups = lanes // LANES
    xp[...] = jnp.zeros(xp.shape, jnp.float32)

    unroll = min(height, NORM_ROWS)

    def rows(n, carry):
        for k in range(unroll):
            r = unroll * n + k
            row = x[r].astype(jnp.float32)
            for g in range(groups):
                at = slice(g * LANES, (g + 1) * LANES)
                own = row[:, g * LANES : min((g + 1) * LANES, channels)]
                xp[k * groups + g, 8 : 8 + width, 0 : own.shape[1]] = own
                for q in range(reach_cols):
                    near = pl.ds(8 - REACH + q, blocks, stride=stride)
                    xs[r, q, :, at] = xp[k * groups + g, near, :]
        return carry

    lax.fori_loop(0, height // unroll, rows, 0)


def conv(xs, cpar, cq):
    rows = xs.shape[0]
    height, stride, blocks, lanes = cq.shape
    span = 2 * REACH + 1
    above = (height - rows) // 2

    def group(g, carry):
        at = pl.ds(pl.multiple_of(g * LANES, LANES), LANES)

        def column(q, carry):
            bias = jnp.broadcast_to(cpar[VECTORS : VECTORS + 1, at], (blocks, LANES))
            acc = [None if above else bias] * height
            for j in range(span):
                kern = [
                    jnp.broadcast_to(cpar[i * span + j : i * span + j + 1, at], (blocks, LANES))
                    for i in range(span)
                ]
                for r in range(rows):
                    x_row = xs[r, q + j, :, at]
                    for i in range(span):
                        h = r + above + REACH - i
                        if 0 <= h < height:
                            term = kern[i] * x_row
                            acc[h] = term if acc[h] is None else acc[h] + term
            for h in range(height):
                cq[h, q, :, at] = acc[h]
            return carry

        return lax.fori_loop(0, stride, column, carry, unroll=2)

    lax.fori_loop(0, lanes // LANES, group, 0)


def norm(cq, cpar, xp, flat, skip=0):
    padded, stride, blocks, lanes = cq.shape
    height = padded - 2 * skip
    gain = cpar[VECTORS + 1 : VECTORS + 2, :]
    shift = cpar[VECTORS + 2 : VECTORS + 3, :]
    channels = flat.shape[2]
    width = stride * blocks
    groups = lanes // LANES
    inside = lax.broadcasted_iota(jnp.int32, (blocks, lanes), 1) < channels

    def rows(n, carry):
        for k in range(NORM_ROWS):
            h = NORM_ROWS * n + k
            for q in range(stride):
                v = cq[h + skip, q]
                mean = jnp.sum(v, axis=-1, keepdims=True) * (1.0 / channels)
                c = jnp.where(inside, v - mean, 0.0)
                var = jnp.sum(c * c, axis=-1, keepdims=True) * (1.0 / channels)
                c = c * lax.rsqrt(var + EPS_NORM) * gain + shift
                for g in range(groups):
                    at = slice(g * LANES, (g + 1) * LANES)
                    xp[k * groups + g, pl.ds(q, blocks, stride=stride), :] = c[:, at]
            for g in range(groups):
                at = slice(g * LANES, min((g + 1) * LANES, channels))
                flat[h, :, at] = xp[k * groups + g, 0:width, 0 : at.stop - at.start].astype(
                    jnp.bfloat16
                )
        return carry

    lax.fori_loop(0, height // NORM_ROWS, rows, 0)


def conv_norm(x, cpar, flat, xp, xs, cq):
    fill_columns(xp, xs, x, x.shape[2])
    conv(xs, cpar, cq)
    norm(cq, cpar, xp, flat)


def conv_scratch(rows, out_rows, width, lanes):
    return [
        pltpu.VMEM((NORM_ROWS * lanes // LANES, width + 16, LANES), jnp.float32),
        pltpu.VMEM((rows, width // 8 + 2 * REACH, 8, lanes), jnp.float32),
        pltpu.VMEM((out_rows, width // 8, 8, lanes), jnp.float32),
    ]


def gelu(v):
    return 0.5 * v * (1.0 + lax.erf(v * (0.5**0.5)))


def up(flat, w_in, bias, act, ssq):
    height, width, channels = flat.shape
    cells = height * width
    half = w_in.shape[1]
    step = 2 * LANES

    def units(start, count):
        raised = jnp.dot(
            flat[...].reshape(cells, channels),
            w_in[0:channels, pl.ds(start, count)],
            preferred_element_type=jnp.float32,
        )
        active = gelu(raised + bias[0:1, pl.ds(start, count)])
        act[:, pl.ds(start, count)] = active.astype(jnp.bfloat16)
        squares = (active * active).reshape(cells // 8, 8, count)
        ssq[:, pl.ds(start, count)] = jnp.sum(squares, axis=0)

    for start in range(0, half, step):
        units(start, min(step, half - start))


def norm_scale(ssqs, fvec, scale):
    half = fvec.shape[2]
    magnitude = [jnp.sqrt(jnp.sum(ssq[...], axis=0, keepdims=True)) for ssq in ssqs]
    mean = jnp.sum(magnitude[0] + magnitude[1], axis=1, keepdims=True) * (0.5 / half)
    for which in range(2):
        ratio = magnitude[which] / (mean + EPS_GRN)
        scale[which] = fvec[which, 1:2, :] * ratio + 1.0


def down(x_rows, first_row, acts, outs, scale, fvec, cpar):
    _, width, channels = x_rows.shape
    cells = CHUNK * width
    at = pl.ds(pl.multiple_of(first_row * width, cells), cells)
    update = cpar[VECTORS + 3 : VECTORS + 4, 0:channels]
    for which in range(2):
        a = acts[which][at, :].astype(jnp.float32)
        hidden = (a * scale[which] + fvec[which, 2:3, :]).astype(jnp.bfloat16)
        update = update + jnp.dot(hidden, outs[which][...], preferred_element_type=jnp.float32)
    return (x_rows.astype(jnp.float32) + update.reshape(CHUNK, width, channels)).astype(
        jnp.bfloat16
    )


def down_all(x, acts, outs, scale, fvec, cvec, out):
    def rows(n, carry):
        at = pl.ds(n * CHUNK, CHUNK)
        out[at] = down(x[at], n * CHUNK, acts, outs, scale, fvec, cvec)
        return carry

    lax.fori_loop(0, x.shape[0] // CHUNK, rows, 0)


def prepare_kernel(part, kernel, *refs):
    vectors, (cpar, fvec), (held, *staged), sems = refs[:7], refs[7:9], refs[9:-1], refs[-1]
    moves = [(kernel, held), *zip(vectors, staged)]
    copies = [pltpu.make_async_copy(a, b, sems.at[n]) for n, (a, b) in enumerate(moves)]
    for copy in copies:
        copy.start()
    cpar[...] = jnp.zeros(cpar.shape, jnp.float32)
    for copy in copies:
        copy.wait()
    channels = kernel.shape[3]
    span = kernel.shape[1]
    half = fvec.shape[2]
    for i in range(span):
        cpar[i * span : (i + 1) * span, 0:channels] = held[0, i].astype(jnp.float32)
    for n in range(4):
        cpar[VECTORS + n : VECTORS + n + 1, 0:channels] = staged[n][...].astype(jnp.float32)
    first = part[0] == 0
    for n in range(3):
        v = staged[4 + n][...].astype(jnp.float32)
        low, high = v[:, 0:half], v[:, half:]
        fvec[0, n : n + 1, :] = jnp.where(first, low, high)
        fvec[1, n : n + 1, :] = jnp.where(first, high, low)


def block_of(me, order, n):
    return n if order is None else me[0] ^ order[n]


def piece_kernel(section, piece, cpar, part, xp, xs, *, on):
    @pl.when(section[0] == on)
    def _():
        fill_columns(xp, xs, piece, piece.shape[2])
        conv(xs, cpar, part)


def last_piece_kernel(section, me, *refs, order, on):
    count = len(order or IN_ORDER)
    pieces, parts = refs[:count], refs[count : 2 * count - 1]
    cpar, both, xp, xs, own, cq = refs[2 * count - 1 :]
    x, flat = both.at[0], both.at[1]
    rows = pieces[0].shape[0]

    @pl.when(section[0] == on)
    def _():
        bias = cpar[VECTORS : VECTORS + 1, :].reshape(1, 1, 1, cq.shape[3])
        cq[...] = jnp.broadcast_to(bias, cq.shape)
        fill_columns(xp, xs, pieces[-1], x.shape[2])
        conv(xs, cpar, own)
        for n, (piece, part) in enumerate(zip(pieces, (*parts, own))):
            at = block_of(me, order, n) * rows
            x[pl.ds(at, rows)] = piece[...]
            cq[pl.ds(at, rows + 2 * REACH)] += part[...]
        norm(cq, cpar, xp, flat, REACH)


def conv_kernel(section, x, cpar, flat, xp, xs, cq, *, tick):
    @pl.when(section[0] == tick)
    def _():
        conv_norm(x, cpar, flat, xp, xs, cq)


def normed_part(ref):
    return ref if len(ref.shape) == 3 else ref.at[1]


def unpack_kernel(packed, w_out):
    cut, channels = w_out.shape[0] // 2, w_out.shape[1]
    first = packed.shape[0] - cut
    w_out[0:cut] = packed[first:, 0:channels]
    w_out[cut:] = packed[first:, channels : 2 * channels]


def up_first_kernel(section, flat, w_in, fvec, act, ssq, *, tick):
    @pl.when(section[0] == tick)
    def _():
        up(normed_part(flat), w_in, fvec.at[0], act, ssq)


def up_second_kernel(section, flat, w_in, fvec, other, act, scale, ssq, *, tick):
    @pl.when(section[0] == tick)
    def _():
        up(normed_part(flat), w_in, fvec.at[1], act, ssq)
        norm_scale((other, ssq), fvec, scale)


def first_down_kernel(section, both, act_a, act_b, out_a, out_b, scale, fvec, cpar, out):
    @pl.when(section[0] == 0)
    def _():
        down_all(both.at[0], (act_a, act_b), (out_a, out_b), scale, fvec, cpar, out)


def down_piece_kernel(
    section, me, x, act_a, act_b, out_a, out_b, scale, fvec, cpar, prev, out, *, order, tick, n
):
    first_row = block_of(me, order, n) * CHUNK
    at = pl.ds(first_row, CHUNK)

    @pl.when(section[0] == tick)
    def _():
        out[...] = down(x[at], first_row, (act_a, act_b), (out_a, out_b), scale, fvec, cpar)

    @pl.when(section[0] != tick)
    def _():
        out[...] = prev[at]


def mlp_kernel(section, both, in_a, in_b, out_a, out_b, fvec, cpar, *refs, tick):
    *pieces, prev, out, act_a, act_b, ssq_a, ssq_b, scale = refs
    x, flat = both.at[0], both.at[1]

    @pl.when(section[0] == tick)
    def _():
        up(flat, in_a, fvec.at[0], act_a, ssq_a)
        up(flat, in_b, fvec.at[1], act_b, ssq_b)
        norm_scale((ssq_a, ssq_b), fvec, scale)
        down_all(x, (act_a, act_b), (out_a, out_b), scale, fvec, cpar, out)

    @pl.when(section[0] == tick - 1)
    def _():
        for n, piece in enumerate(pieces):
            out[n * CHUNK : (n + 1) * CHUNK] = piece[...]

    @pl.when(section[0] < tick - 1)
    def _():
        out[...] = prev[...]


def conv_up_kernel(section, x, cpar, in_a, in_b, fvec, *refs, tick):
    act_a, act_b, scale, xp, xs, cq, flat, ssq_a, ssq_b = refs

    @pl.when(section[0] == tick)
    def _():
        conv_norm(x, cpar, flat, xp, xs, cq)
        up(flat, in_a, fvec.at[0], act_a, ssq_a)
        up(flat, in_b, fvec.at[1], act_b, ssq_b)
        norm_scale((ssq_a, ssq_b), fvec, scale)


def place_kernel(me, *refs, order):
    *pieces, saved, sems = refs
    copies = [
        pltpu.make_async_copy(piece, saved.at[0, block_of(me, order, n), 0], sems.at[n])
        for n, piece in enumerate(pieces)
    ]
    for copy in copies:
        copy.start()
    for copy in copies:
        copy.wait()


SMEM = pl.BlockSpec(memory_space=pltpu.SMEM)
VMEM = pl.BlockSpec(memory_space=pltpu.VMEM)
HBM = pl.BlockSpec(memory_space=pltpu.HBM)


def call(kernel, name, args, out, specs=None, out_specs=None, scratch=(), flops=0, **static):
    if specs is None:
        specs = [SMEM if a.dtype == jnp.int32 else VMEM for a in args]
    if out_specs is None:
        out_specs = jax.tree.map(lambda _: VMEM, out)
    moved = sum(a.size * a.dtype.itemsize for a in args)
    return pl.pallas_call(
        functools.partial(kernel, **static),
        out_shape=out,
        in_specs=specs,
        out_specs=out_specs,
        scratch_shapes=list(scratch),
        compiler_params=pltpu.CompilerParams(vmem_limit_bytes=VMEM_BYTES),
        cost_estimate=pl.CostEstimate(flops=flops, bytes_accessed=moved, transcendentals=0),
        name=name,
    )(*args)


def shape(*dims, dtype=jnp.float32):
    return jax.ShapeDtypeStruct(dims, dtype)


def ssq_scratch(half):
    return pltpu.VMEM((8, half), jnp.float32)


def image_plan(
    inputs,
    depth_kernel,
    depth_bias,
    norm_gain,
    norm_bias,
    proj_in,
    bias_in,
    grn_gamma,
    grn_beta,
    proj_out,
    bias_out,
):
    sections = lax.axis_size("section")
    count = lax.axis_size("row")
    me = lax.axis_index("row").astype(jnp.int32)
    section = lax.axis_index("section").astype(jnp.int32).reshape(1)
    me_ref = me.reshape(1)
    part = lax.axis_index("dp").astype(jnp.int32).reshape(1)
    _, _, rows, width, channels = inputs.shape
    height = rows * count
    cells = height * width
    lanes = -(-channels // LANES) * LANES
    half = proj_in.shape[2]
    span = depth_kernel.shape[1]
    order = (0, 2, 3, 1)
    bf16 = jnp.bfloat16
    whole = shape(height, width, channels, dtype=bf16)
    piece_shape = shape(rows, width, channels, dtype=bf16)
    act_shape = shape(cells, half, dtype=bf16)
    scale_shape = shape(2, 1, half)
    matmul = 2 * cells * channels * half

    helper, source = 1, sections - 1
    pieces = []
    for by in order:
        piece = lax.dynamic_index_in_dim(inputs, me ^ by, 0, keepdims=False)[0]
        if by:
            pairs = [(source * count + (p ^ by), helper * count + p) for p in range(count)]
            piece = lax.ppermute(piece, ("section", "row"), pairs)
        pieces.append(piece)

    def other_half(x, which):
        pairs = [(2 * s + p, 2 * s + 1 - p) for s in which for p in range(2)]
        return lax.ppermute(x, ("section", "dp"), pairs)

    w_in, w_out = proj_in[0], proj_out[0]
    cut = half // 2
    even = range(0, sections, 2)
    odd = range(1, sections, 2)
    other_in = other_half(w_in, even)
    other_out = other_half(w_out, even)

    held = (
        depth_kernel, depth_bias, norm_gain, norm_bias, bias_out, bias_in, grn_gamma, grn_beta
    )
    cpar, fvec = call(
        prepare_kernel,
        "prepare",
        (part, *held),
        (shape(VECTORS + 8, lanes), shape(2, 3, half)),
        specs=[SMEM] + [HBM] * len(held),
        scratch=[pltpu.VMEM(v.shape, v.dtype) for v in held]
        + [pltpu.SemaphoreType.DMA((len(held),))],
    )

    def send(x, start, end):
        return lax.ppermute(x, "section", [(start, end)])

    def conv_pieces(pieces, cpar, order, on):
        out_rows = rows + 2 * REACH
        scratch = conv_scratch(rows, out_rows, width, lanes)
        parts = []
        for piece in pieces[:-1]:
            if parts:
                piece, parts[-1] = lax.optimization_barrier((piece, parts[-1]))
            part = call(
                piece_kernel,
                "conv_piece",
                (section, piece, cpar),
                shape(out_rows, width // 8, 8, lanes),
                scratch=scratch[:2],
                on=on,
            )
            parts.append(part)
        return call(
            last_piece_kernel,
            "last_piece",
            (section, me_ref, *pieces, *parts, cpar),
            shape(2, height, width, channels, dtype=bf16),
            scratch=scratch + [conv_scratch(1, height + 2 * REACH, width, lanes)[2]],
            order=order,
            on=on,
        )

    def up_own(flat, tick):
        return call(
            up_first_kernel,
            "up_own",
            (section, flat, w_in, fvec),
            (act_shape, shape(8, half)),
            flops=matmul,
            tick=tick,
        )

    def up_other(flat, other_in, ssq, tick):
        return call(
            up_second_kernel,
            "up_other",
            (section, flat, other_in, fvec, ssq),
            (act_shape, scale_shape),
            scratch=[ssq_scratch(half)],
            flops=matmul,
            tick=tick,
        )

    def unpack(packed):
        return call(unpack_kernel, "unpack", (packed,), shape(half, channels, dtype=bf16))

    def down_piece(x, acts, other_out, prev, order, tick, n):
        act_a, act_b, scale = acts
        return call(
            down_piece_kernel,
            "down_piece",
            (section, me_ref, x, act_a, act_b, w_out, other_out, scale, fvec, cpar, prev),
            piece_shape,
            flops=2 * matmul // count,
            order=order,
            tick=tick,
            n=n,
        )

    both = conv_pieces(pieces, send(cpar, 0, helper), order, helper)
    both, other_in, late_in, late_out = lax.optimization_barrier((both, other_in, w_in, w_out))
    late = jnp.concatenate(
        [late_in, jnp.concatenate([late_out[:cut], late_out[cut:]], axis=1)], axis=0
    )
    odd_other = other_half(late, odd)
    both = send(both, helper, 0)
    act_a, ssq = up_own(both, 0)
    act_b, scale = up_other(both, other_in, ssq, 0)
    result = call(
        first_down_kernel,
        "down",
        (section, both, act_a, act_b, w_out, other_out, scale, fvec, cpar),
        whole,
        flops=2 * matmul,
    )
    x = send(result, 0, 1)
    flat = call(
        conv_kernel,
        "conv",
        (section, x, cpar),
        whole,
        scratch=conv_scratch(height, height, width, lanes),
        tick=1,
    )
    act_a, ssq = up_own(flat, 1)
    odd_other, act_a = lax.optimization_barrier((odd_other, act_a))
    odd_out = unpack(odd_other)
    acts = (act_a, *up_other(flat, odd_other, ssq, 1))
    kept = [down_piece(x, acts, odd_out, result, None, 1, n) for n in range(count)]
    both = conv_pieces([send(piece, 1, 2) for piece in kept], cpar, None, 2)
    result = call(
        mlp_kernel,
        "mlp",
        (section, both, w_in, other_in, w_out, other_out, fvec, cpar, *kept, result),
        whole,
        scratch=[pltpu.VMEM((cells, half), bf16)] * 2
        + [ssq_scratch(half)] * 2
        + [pltpu.VMEM((2, 1, half), jnp.float32)],
        flops=4 * matmul,
        tick=2,
    )
    x = send(result, 2, 3)
    acts = call(
        conv_up_kernel,
        "conv_up",
        (section, x, cpar, w_in, odd_other, fvec),
        (act_shape, act_shape, scale_shape),
        scratch=conv_scratch(height, height, width, lanes)
        + [pltpu.VMEM((height, width, channels), bf16)]
        + [ssq_scratch(half)] * 2,
        flops=2 * matmul,
        tick=3,
    )
    done = []
    for n in (1, 2, 3, 0):
        piece = down_piece(x, acts, odd_out, result, order, 3, n)
        if n:
            piece = lax.ppermute(piece, "row", [(p, p ^ order[n]) for p in range(count)])
        done.append(piece)
    return call(
        place_kernel,
        "place",
        (me_ref, done[3], *done[:3]),
        shape(1, count, 1, rows, width, channels, dtype=bf16),
        out_specs=HBM,
        scratch=[pltpu.SemaphoreType.DMA((count,))],
        order=order,
    )


def extended(cells, sides, width):
    for axis, dim in sides:
        count = lax.axis_size(axis)
        ends = count - 1
        head = lax.slice_in_dim(cells, 0, width, axis=dim)
        tail = lax.slice_in_dim(cells, cells.shape[dim] - width, cells.shape[dim], axis=dim)
        cells = jnp.concatenate(
            [
                lax.ppermute(tail, axis, [(i, (i + 1) % count) for i in range(ends)]),
                cells,
                lax.ppermute(head, axis, [((i + 1) % count, i) for i in range(ends)]),
            ],
            axis=dim,
        )
    return cells


def depthwise(padded, kernel, bias_term):
    channels = padded.shape[-1]
    conv_out = lax.conv_general_dilated(
        padded.astype(jnp.float32),
        kernel.astype(jnp.float32)[:, :, None, :],
        (1, 1),
        "VALID",
        dimension_numbers=("NHWC", "HWIO", "NHWC"),
        feature_group_count=channels,
        precision=lax.Precision.HIGHEST,
    )
    return conv_out + bias_term.astype(jnp.float32)


def conv_block(current, params):
    (
        depth_kernel,
        depth_bias,
        norm_gain,
        norm_bias,
        proj_in,
        bias_in,
        grn_gamma,
        grn_beta,
        proj_out,
        bias_out,
    ) = params
    num_items, num_rows, num_cols, channels = current.shape
    padded = extended(current, (("row", 1),), REACH)
    padded = jnp.pad(padded, ((0, 0), (0, 0), (REACH, REACH), (0, 0)))
    conv_out = depthwise(padded, depth_kernel, depth_bias)
    center = conv_out - jnp.mean(conv_out, axis=-1, keepdims=True)
    spread = jnp.mean(center * center, axis=-1, keepdims=True)
    normed = (
        center * lax.rsqrt(spread + EPS_NORM) * norm_gain.astype(jnp.float32)
        + norm_bias.astype(jnp.float32)
    ).astype(jnp.bfloat16)
    flat_rows = normed.reshape(num_items * num_rows * num_cols, channels)
    raised = jnp.dot(flat_rows, proj_in, preferred_element_type=jnp.float32) + bias_in.astype(
        jnp.float32
    )
    active = jax.nn.gelu(raised, approximate=False).astype(jnp.bfloat16)
    grouped = active.reshape(num_items, num_rows * num_cols, -1).astype(jnp.float32)
    local_sq = jnp.sum(grouped * grouped, axis=1)
    total_sq = lax.psum(local_sq, "row")
    magnitude = jnp.sqrt(total_sq)
    grn_ratio = magnitude / (jnp.mean(magnitude, axis=-1, keepdims=True) + EPS_GRN)
    hidden = (
        grn_gamma.astype(jnp.float32) * grouped * grn_ratio[:, None, :]
        + grn_beta.astype(jnp.float32)
        + grouped
    ).astype(jnp.bfloat16)
    update = jnp.dot(
        hidden.reshape(num_items * num_rows * num_cols, -1),
        proj_out,
        preferred_element_type=jnp.float32,
    ) + bias_out.astype(jnp.float32)
    return (
        current.astype(jnp.float32) + update.reshape(num_items, num_rows, num_cols, channels)
    ).astype(jnp.bfloat16)


def rows_plan(inputs, *weights):
    (
        depth_kernel,
        depth_bias,
        norm_gain,
        norm_bias,
        proj_in,
        bias_in,
        grn_gamma,
        grn_beta,
        proj_out,
        bias_out,
    ) = weights
    proj_in = lax.all_gather(proj_in, "dp", axis=2, tiled=True)
    proj_out = lax.all_gather(proj_out, "dp", axis=1, tiled=True)
    own_params = tuple(
        w[0]
        for w in (
            depth_kernel,
            depth_bias,
            norm_gain,
            norm_bias,
            proj_in,
            bias_in,
            grn_gamma,
            grn_beta,
            proj_out,
            bias_out,
        )
    )
    sections = lax.axis_size("section")
    section_index = lax.axis_index("section")
    num_micro = inputs.shape[0]
    num_ticks = num_micro + sections - 1
    arriving = jnp.zeros_like(inputs[0])
    saved = jnp.zeros_like(inputs)
    for tick_index in range(num_ticks):
        fresh_input = inputs[min(tick_index, num_micro - 1)]
        current = jnp.where(section_index == 0, fresh_input, arriving)
        produced = conv_block(current, own_params)
        slot_index = tick_index - section_index
        is_valid = jnp.logical_and(slot_index >= 0, slot_index < num_micro)
        safe_slot = jnp.clip(slot_index, 0, num_micro - 1)
        previous = lax.dynamic_index_in_dim(saved, safe_slot, 0, keepdims=False)
        saved = lax.dynamic_update_index_in_dim(
            saved, jnp.where(is_valid, produced, previous), safe_slot, 0
        )
        if tick_index + 1 < num_ticks:
            arriving = lax.ppermute(
                produced, "section", [(i, i + 1) for i in range(sections - 1)]
            )
    return saved[None]


def on_device(inputs, *weights):
    num_micro, images, local_rows, width, channels = inputs.shape
    one_image_each = (
        images == 1
        and lax.axis_size("row") == num_micro == 4
        and lax.axis_size("dp") == 2
        and lax.axis_size("section") == 4
        and local_rows % 4 == 0
        and width % 16 == 0
        and weights[4].shape[2] == 2 * channels
    )
    plan = image_plan if one_image_each else rows_plan
    return plan(inputs, *weights)


def solution(mesh):
    return jax.shard_map(
        on_device,
        mesh=mesh,
        in_specs=(
            P(None, "dp", "row", None, None),
            P("section", None, None, None),
            P("section", None),
            P("section", None),
            P("section", None),
            P("section", None, "dp"),
            P("section", None),
            P("section", None),
            P("section", None),
            P("section", "dp", None),
            P("section", None),
        ),
        out_specs=P("section", None, "dp", "row", None, None),
        check_vma=False,
    )
```

```python
import functools

import jax
import jax.numpy as jnp
from jax import lax
from jax.experimental import pallas as pl
from jax.experimental.pallas import tpu as pltpu
from jax.sharding import PartitionSpec as P

EPS_NORM = 1e-06
EPS_GRN = 1e-06
LANES = 128
VMEM_BYTES = 20 * 1024 * 1024
REACH = 3
CHUNK = 4
NORM_ROWS = 16
IN_ORDER = (0, 1, 2, 3)
VECTORS = 56


def fill_columns(xp, xs, x, channels):
    height, reach_cols, blocks, lanes = xs.shape
    stride = reach_cols - 2 * REACH
    width = stride * blocks
    groups = lanes // LANES
    unroll = min(height, NORM_ROWS)
    border = jnp.zeros((unroll * groups, 8, LANES), jnp.float32)
    xp[0 : unroll * groups, 0:8, :] = border
    xp[0 : unroll * groups, 8 + width : 16 + width, :] = border
    if lanes > channels:
        for k in range(unroll):
            last = k * groups + groups - 1
            xp[last, 8 : 8 + width, :] = jnp.zeros((width, LANES), jnp.float32)

    def rows(n, carry):
        for k in range(unroll):
            r = unroll * n + k
            row = x[r].astype(jnp.float32)
            for g in range(groups):
                at = slice(g * LANES, (g + 1) * LANES)
                own = row[:, g * LANES : min((g + 1) * LANES, channels)]
                xp[k * groups + g, 8 : 8 + width, 0 : own.shape[1]] = own
                for q in range(reach_cols):
                    near = pl.ds(8 - REACH + q, blocks, stride=stride)
                    xs[r, q, :, at] = xp[k * groups + g, near, :]
        return carry

    lax.fori_loop(0, height // unroll, rows, 0)


def conv(xs, cpar, cq):
    rows = xs.shape[0]
    height, stride, blocks, lanes = cq.shape
    span = 2 * REACH + 1
    above = (height - rows) // 2

    def group(g, carry):
        at = pl.ds(pl.multiple_of(g * LANES, LANES), LANES)

        def column(q, carry):
            bias = jnp.broadcast_to(cpar[VECTORS : VECTORS + 1, at], (blocks, LANES))
            acc = [None if above else bias] * height
            for j in range(span):
                kern = [
                    jnp.broadcast_to(cpar[i * span + j : i * span + j + 1, at], (blocks, LANES))
                    for i in range(span)
                ]
                for r in range(rows):
                    x_row = xs[r, q + j, :, at]
                    for i in range(span):
                        h = r + above + REACH - i
                        if 0 <= h < height:
                            term = kern[i] * x_row
                            acc[h] = term if acc[h] is None else acc[h] + term
            for h in range(height):
                cq[h, q, :, at] = acc[h]
            return carry

        return lax.fori_loop(0, stride, column, carry, unroll=2)

    lax.fori_loop(0, lanes // LANES, group, 0)


def norm(cq, cpar, xp, flat, skip=0):
    padded, stride, blocks, lanes = cq.shape
    height = padded - 2 * skip
    gain = cpar[VECTORS + 1 : VECTORS + 2, :]
    shift = cpar[VECTORS + 2 : VECTORS + 3, :]
    channels = flat.shape[2]
    width = stride * blocks
    groups = lanes // LANES
    inside = lax.broadcasted_iota(jnp.int32, (blocks, lanes), 1) < channels

    def rows(n, carry):
        for k in range(NORM_ROWS):
            h = NORM_ROWS * n + k
            for q in range(stride):
                v = cq[h + skip, q]
                mean = jnp.sum(v, axis=-1, keepdims=True) * (1.0 / channels)
                c = jnp.where(inside, v - mean, 0.0)
                var = jnp.sum(c * c, axis=-1, keepdims=True) * (1.0 / channels)
                c = c * lax.rsqrt(var + EPS_NORM) * gain + shift
                for g in range(groups):
                    at = slice(g * LANES, (g + 1) * LANES)
                    xp[k * groups + g, pl.ds(q, blocks, stride=stride), :] = c[:, at]
            for g in range(groups):
                at = slice(g * LANES, min((g + 1) * LANES, channels))
                flat[h, :, at] = xp[k * groups + g, 0:width, 0 : at.stop - at.start].astype(
                    jnp.bfloat16
                )
        return carry

    lax.fori_loop(0, height // NORM_ROWS, rows, 0)


def conv_norm(x, cpar, flat, xp, xs, cq):
    fill_columns(xp, xs, x, x.shape[2])
    conv(xs, cpar, cq)
    norm(cq, cpar, xp, flat)


def conv_scratch(rows, out_rows, width, lanes):
    return [
        pltpu.VMEM((NORM_ROWS * lanes // LANES, width + 16, LANES), jnp.float32),
        pltpu.VMEM((rows, width // 8 + 2 * REACH, 8, lanes), jnp.float32),
        pltpu.VMEM((out_rows, width // 8, 8, lanes), jnp.float32),
    ]


def gelu(v):
    return 0.5 * v * (1.0 + lax.erf(v * (0.5**0.5)))


def up(flat, w_in, bias, act, ssq):
    height, width, channels = flat.shape
    cells = height * width
    half = w_in.shape[1]
    step = 2 * LANES

    def units(start, count):
        raised = jnp.dot(
            flat[...].reshape(cells, channels),
            w_in[0:channels, pl.ds(start, count)],
            preferred_element_type=jnp.float32,
        )
        active = gelu(raised + bias[0:1, pl.ds(start, count)])
        act[:, pl.ds(start, count)] = active.astype(jnp.bfloat16)
        squares = (active * active).reshape(cells // 8, 8, count)
        ssq[:, pl.ds(start, count)] = jnp.sum(squares, axis=0)

    for start in range(0, half, step):
        units(start, min(step, half - start))


def norm_scale(ssqs, fvec, scale):
    half = fvec.shape[2]
    magnitude = [jnp.sqrt(jnp.sum(ssq[...], axis=0, keepdims=True)) for ssq in ssqs]
    mean = jnp.sum(magnitude[0] + magnitude[1], axis=1, keepdims=True) * (0.5 / half)
    for which in range(2):
        ratio = magnitude[which] / (mean + EPS_GRN)
        scale[which] = fvec[which, 1:2, :] * ratio + 1.0


def down(x_rows, first_row, acts, outs, scale, fvec, cpar):
    _, width, channels = x_rows.shape
    cells = CHUNK * width
    at = pl.ds(pl.multiple_of(first_row * width, cells), cells)
    update = cpar[VECTORS + 3 : VECTORS + 4, 0:channels]
    for which in range(2):
        a = acts[which][at, :].astype(jnp.float32)
        hidden = (a * scale[which] + fvec[which, 2:3, :]).astype(jnp.bfloat16)
        update = update + jnp.dot(hidden, outs[which][...], preferred_element_type=jnp.float32)
    return (x_rows.astype(jnp.float32) + update.reshape(CHUNK, width, channels)).astype(
        jnp.bfloat16
    )


def down_all(x, acts, outs, scale, fvec, cvec, out):
    def rows(n, carry):
        at = pl.ds(n * CHUNK, CHUNK)
        out[at] = down(x[at], n * CHUNK, acts, outs, scale, fvec, cvec)
        return carry

    lax.fori_loop(0, x.shape[0] // CHUNK, rows, 0)


def prepare_kernel(part, kernel, *refs):
    vectors, (cpar, fvec), (held, *staged), sems = refs[:7], refs[7:9], refs[9:-1], refs[-1]
    moves = [(kernel, held), *zip(vectors, staged)]
    copies = [pltpu.make_async_copy(a, b, sems.at[n]) for n, (a, b) in enumerate(moves)]
    for copy in copies:
        copy.start()
    cpar[...] = jnp.zeros(cpar.shape, jnp.float32)
    for copy in copies:
        copy.wait()
    channels = kernel.shape[3]
    span = kernel.shape[1]
    half = fvec.shape[2]
    for i in range(span):
        cpar[i * span : (i + 1) * span, 0:channels] = held[0, i].astype(jnp.float32)
    for n in range(4):
        cpar[VECTORS + n : VECTORS + n + 1, 0:channels] = staged[n][...].astype(jnp.float32)
    first = part[0] == 0
    for n in range(3):
        v = staged[4 + n][...].astype(jnp.float32)
        low, high = v[:, 0:half], v[:, half:]
        fvec[0, n : n + 1, :] = jnp.where(first, low, high)
        fvec[1, n : n + 1, :] = jnp.where(first, high, low)


def block_of(me, order, n):
    return n if order is None else me[0] ^ order[n]


def piece_kernel(section, piece, cpar, part, xp, xs, *, on):
    @pl.when(section[0] == on)
    def _():
        fill_columns(xp, xs, piece, piece.shape[2])
        conv(xs, cpar, part)


def last_piece_kernel(section, me, *refs, order, on):
    count = len(order or IN_ORDER)
    pieces, parts = refs[:count], refs[count : 2 * count - 1]
    cpar, both, xp, xs, own, cq = refs[2 * count - 1 :]
    x, flat = both.at[0], both.at[1]
    rows = pieces[0].shape[0]

    @pl.when(section[0] == on)
    def _():
        bias = cpar[VECTORS : VECTORS + 1, :].reshape(1, 1, 1, cq.shape[3])
        cq[...] = jnp.broadcast_to(bias, cq.shape)
        fill_columns(xp, xs, pieces[-1], x.shape[2])
        conv(xs, cpar, own)
        for n, (piece, part) in enumerate(zip(pieces, (*parts, own))):
            at = block_of(me, order, n) * rows
            x[pl.ds(at, rows)] = piece[...]
            cq[pl.ds(at, rows + 2 * REACH)] += part[...]
        norm(cq, cpar, xp, flat, REACH)


def conv_kernel(section, x, cpar, flat, xp, xs, cq, *, tick):
    @pl.when(section[0] == tick)
    def _():
        conv_norm(x, cpar, flat, xp, xs, cq)


def normed_part(ref):
    return ref if len(ref.shape) == 3 else ref.at[1]


def unpack_kernel(packed, w_out):
    cut, channels = w_out.shape[0] // 2, w_out.shape[1]
    first = packed.shape[0] - cut
    w_out[0:cut] = packed[first:, 0:channels]
    w_out[cut:] = packed[first:, channels : 2 * channels]


def up_first_kernel(section, flat, w_in, fvec, act, ssq, *, tick):
    @pl.when(section[0] == tick)
    def _():
        up(normed_part(flat), w_in, fvec.at[0], act, ssq)


def up_second_kernel(section, flat, w_in, fvec, other, act, scale, ssq, *, tick):
    @pl.when(section[0] == tick)
    def _():
        up(normed_part(flat), w_in, fvec.at[1], act, ssq)
        norm_scale((other, ssq), fvec, scale)


def first_down_kernel(section, both, act_a, act_b, out_a, out_b, scale, fvec, cpar, out):
    @pl.when(section[0] == 0)
    def _():
        down_all(both.at[0], (act_a, act_b), (out_a, out_b), scale, fvec, cpar, out)


def down_piece_kernel(
    section, me, x, act_a, act_b, out_a, out_b, scale, fvec, cpar, prev, out, *, order, tick, n
):
    first_row = block_of(me, order, n) * CHUNK
    at = pl.ds(first_row, CHUNK)

    @pl.when(section[0] == tick)
    def _():
        out[...] = down(x[at], first_row, (act_a, act_b), (out_a, out_b), scale, fvec, cpar)

    @pl.when(section[0] != tick)
    def _():
        out[...] = prev[at]


def mlp_kernel(section, both, in_a, in_b, out_a, out_b, fvec, cpar, *refs, tick):
    *pieces, prev, out, act_a, act_b, ssq_a, ssq_b, scale = refs
    x, flat = both.at[0], both.at[1]

    @pl.when(section[0] == tick)
    def _():
        up(flat, in_a, fvec.at[0], act_a, ssq_a)
        up(flat, in_b, fvec.at[1], act_b, ssq_b)
        norm_scale((ssq_a, ssq_b), fvec, scale)
        down_all(x, (act_a, act_b), (out_a, out_b), scale, fvec, cpar, out)

    @pl.when(section[0] == tick - 1)
    def _():
        for n, piece in enumerate(pieces):
            out[n * CHUNK : (n + 1) * CHUNK] = piece[...]

    @pl.when(section[0] < tick - 1)
    def _():
        out[...] = prev[...]


def conv_up_kernel(section, x, cpar, in_a, in_b, fvec, *refs, tick):
    act_a, act_b, scale, xp, xs, cq, flat, ssq_a, ssq_b = refs

    @pl.when(section[0] == tick)
    def _():
        conv_norm(x, cpar, flat, xp, xs, cq)
        up(flat, in_a, fvec.at[0], act_a, ssq_a)
        up(flat, in_b, fvec.at[1], act_b, ssq_b)
        norm_scale((ssq_a, ssq_b), fvec, scale)


def place_kernel(me, *refs, order):
    *pieces, saved, sems = refs
    copies = [
        pltpu.make_async_copy(piece, saved.at[0, block_of(me, order, n), 0], sems.at[n])
        for n, piece in enumerate(pieces)
    ]
    for copy in copies:
        copy.start()
    for copy in copies:
        copy.wait()


SMEM = pl.BlockSpec(memory_space=pltpu.SMEM)
VMEM = pl.BlockSpec(memory_space=pltpu.VMEM)
HBM = pl.BlockSpec(memory_space=pltpu.HBM)


def call(kernel, name, args, out, specs=None, out_specs=None, scratch=(), flops=0, **static):
    if specs is None:
        specs = [SMEM if a.dtype == jnp.int32 else VMEM for a in args]
    if out_specs is None:
        out_specs = jax.tree.map(lambda _: VMEM, out)
    moved = sum(a.size * a.dtype.itemsize for a in args)
    return pl.pallas_call(
        functools.partial(kernel, **static),
        out_shape=out,
        in_specs=specs,
        out_specs=out_specs,
        scratch_shapes=list(scratch),
        compiler_params=pltpu.CompilerParams(vmem_limit_bytes=VMEM_BYTES),
        cost_estimate=pl.CostEstimate(flops=flops, bytes_accessed=moved, transcendentals=0),
        name=name,
    )(*args)


def shape(*dims, dtype=jnp.float32):
    return jax.ShapeDtypeStruct(dims, dtype)


def ssq_scratch(half):
    return pltpu.VMEM((8, half), jnp.float32)


def image_plan(
    inputs,
    depth_kernel,
    depth_bias,
    norm_gain,
    norm_bias,
    proj_in,
    bias_in,
    grn_gamma,
    grn_beta,
    proj_out,
    bias_out,
):
    sections = lax.axis_size("section")
    count = lax.axis_size("row")
    me = lax.axis_index("row").astype(jnp.int32)
    section = lax.axis_index("section").astype(jnp.int32).reshape(1)
    me_ref = me.reshape(1)
    part = lax.axis_index("dp").astype(jnp.int32).reshape(1)
    _, _, rows, width, channels = inputs.shape
    height = rows * count
    cells = height * width
    lanes = -(-channels // LANES) * LANES
    half = proj_in.shape[2]
    span = depth_kernel.shape[1]
    order = (0, 2, 3, 1)
    bf16 = jnp.bfloat16
    whole = shape(height, width, channels, dtype=bf16)
    piece_shape = shape(rows, width, channels, dtype=bf16)
    act_shape = shape(cells, half, dtype=bf16)
    scale_shape = shape(2, 1, half)
    matmul = 2 * cells * channels * half

    helper, source = 1, sections - 1
    pieces = []
    for by in order:
        piece = lax.dynamic_index_in_dim(inputs, me ^ by, 0, keepdims=False)[0]
        if by:
            pairs = [(source * count + (p ^ by), helper * count + p) for p in range(count)]
            piece = lax.ppermute(piece, ("section", "row"), pairs)
        pieces.append(piece)

    def other_half(x, which):
        pairs = [(2 * s + p, 2 * s + 1 - p) for s in which for p in range(2)]
        return lax.ppermute(x, ("section", "dp"), pairs)

    w_in, w_out = proj_in[0], proj_out[0]
    cut = half // 2
    even = range(0, sections, 2)
    odd = range(1, sections, 2)
    other_in = other_half(w_in, even)
    other_out = other_half(w_out, even)

    held = (
        depth_kernel, depth_bias, norm_gain, norm_bias, bias_out, bias_in, grn_gamma, grn_beta
    )
    cpar, fvec = call(
        prepare_kernel,
        "prepare",
        (part, *held),
        (shape(VECTORS + 8, lanes), shape(2, 3, half)),
        specs=[SMEM] + [HBM] * len(held),
        scratch=[pltpu.VMEM(v.shape, v.dtype) for v in held]
        + [pltpu.SemaphoreType.DMA((len(held),))],
    )

    def send(x, start, end):
        return lax.ppermute(x, "section", [(start, end)])

    def conv_pieces(pieces, cpar, order, on):
        out_rows = rows + 2 * REACH
        scratch = conv_scratch(rows, out_rows, width, lanes)
        parts = []
        for piece in pieces[:-1]:
            if parts:
                piece, parts[-1] = lax.optimization_barrier((piece, parts[-1]))
            part = call(
                piece_kernel,
                "conv_piece",
                (section, piece, cpar),
                shape(out_rows, width // 8, 8, lanes),
                scratch=scratch[:2],
                on=on,
            )
            parts.append(part)
        return call(
            last_piece_kernel,
            "last_piece",
            (section, me_ref, *pieces, *parts, cpar),
            shape(2, height, width, channels, dtype=bf16),
            scratch=scratch + [conv_scratch(1, height + 2 * REACH, width, lanes)[2]],
            order=order,
            on=on,
        )

    def up_own(flat, tick):
        return call(
            up_first_kernel,
            "up_own",
            (section, flat, w_in, fvec),
            (act_shape, shape(8, half)),
            flops=matmul,
            tick=tick,
        )

    def up_other(flat, other_in, ssq, tick):
        return call(
            up_second_kernel,
            "up_other",
            (section, flat, other_in, fvec, ssq),
            (act_shape, scale_shape),
            scratch=[ssq_scratch(half)],
            flops=matmul,
            tick=tick,
        )

    def unpack(packed):
        return call(unpack_kernel, "unpack", (packed,), shape(half, channels, dtype=bf16))

    def down_piece(x, acts, other_out, prev, order, tick, n):
        act_a, act_b, scale = acts
        return call(
            down_piece_kernel,
            "down_piece",
            (section, me_ref, x, act_a, act_b, w_out, other_out, scale, fvec, cpar, prev),
            piece_shape,
            flops=2 * matmul // count,
            order=order,
            tick=tick,
            n=n,
        )

    both = conv_pieces(pieces, send(cpar, 0, helper), order, helper)
    both, other_in, late_in, late_out = lax.optimization_barrier((both, other_in, w_in, w_out))
    late = jnp.concatenate(
        [late_in, jnp.concatenate([late_out[:cut], late_out[cut:]], axis=1)], axis=0
    )
    odd_other = other_half(late, odd)
    both = send(both, helper, 0)
    act_a, ssq = up_own(both, 0)
    act_b, scale = up_other(both, other_in, ssq, 0)
    result = call(
        first_down_kernel,
        "down",
        (section, both, act_a, act_b, w_out, other_out, scale, fvec, cpar),
        whole,
        flops=2 * matmul,
    )
    x = send(result, 0, 1)
    flat = call(
        conv_kernel,
        "conv",
        (section, x, cpar),
        whole,
        scratch=conv_scratch(height, height, width, lanes),
        tick=1,
    )
    act_a, ssq = up_own(flat, 1)
    odd_other, act_a = lax.optimization_barrier((odd_other, act_a))
    odd_out = unpack(odd_other)
    acts = (act_a, *up_other(flat, odd_other, ssq, 1))
    kept = [down_piece(x, acts, odd_out, result, None, 1, n) for n in range(count)]
    both = conv_pieces([send(piece, 1, 2) for piece in kept], cpar, None, 2)
    result = call(
        mlp_kernel,
        "mlp",
        (section, both, w_in, other_in, w_out, other_out, fvec, cpar, *kept, result),
        whole,
        scratch=[pltpu.VMEM((cells, half), bf16)] * 2
        + [ssq_scratch(half)] * 2
        + [pltpu.VMEM((2, 1, half), jnp.float32)],
        flops=4 * matmul,
        tick=2,
    )
    x = send(result, 2, 3)
    acts = call(
        conv_up_kernel,
        "conv_up",
        (section, x, cpar, w_in, odd_other, fvec),
        (act_shape, act_shape, scale_shape),
        scratch=conv_scratch(height, height, width, lanes)
        + [pltpu.VMEM((height, width, channels), bf16)]
        + [ssq_scratch(half)] * 2,
        flops=2 * matmul,
        tick=3,
    )
    done = []
    for n in (1, 2, 3, 0):
        piece = down_piece(x, acts, odd_out, result, order, 3, n)
        if n:
            piece = lax.ppermute(piece, "row", [(p, p ^ order[n]) for p in range(count)])
        done.append(piece)
    return call(
        place_kernel,
        "place",
        (me_ref, done[3], *done[:3]),
        shape(1, count, 1, rows, width, channels, dtype=bf16),
        out_specs=HBM,
        scratch=[pltpu.SemaphoreType.DMA((count,))],
        order=order,
    )


def extended(cells, sides, width):
    for axis, dim in sides:
        count = lax.axis_size(axis)
        ends = count - 1
        head = lax.slice_in_dim(cells, 0, width, axis=dim)
        tail = lax.slice_in_dim(cells, cells.shape[dim] - width, cells.shape[dim], axis=dim)
        cells = jnp.concatenate(
            [
                lax.ppermute(tail, axis, [(i, (i + 1) % count) for i in range(ends)]),
                cells,
                lax.ppermute(head, axis, [((i + 1) % count, i) for i in range(ends)]),
            ],
            axis=dim,
        )
    return cells


def depthwise(padded, kernel, bias_term):
    channels = padded.shape[-1]
    conv_out = lax.conv_general_dilated(
        padded.astype(jnp.float32),
        kernel.astype(jnp.float32)[:, :, None, :],
        (1, 1),
        "VALID",
        dimension_numbers=("NHWC", "HWIO", "NHWC"),
        feature_group_count=channels,
        precision=lax.Precision.HIGHEST,
    )
    return conv_out + bias_term.astype(jnp.float32)


def conv_block(current, params):
    (
        depth_kernel,
        depth_bias,
        norm_gain,
        norm_bias,
        proj_in,
        bias_in,
        grn_gamma,
        grn_beta,
        proj_out,
        bias_out,
    ) = params
    num_items, num_rows, num_cols, channels = current.shape
    padded = extended(current, (("row", 1),), REACH)
    padded = jnp.pad(padded, ((0, 0), (0, 0), (REACH, REACH), (0, 0)))
    conv_out = depthwise(padded, depth_kernel, depth_bias)
    center = conv_out - jnp.mean(conv_out, axis=-1, keepdims=True)
    spread = jnp.mean(center * center, axis=-1, keepdims=True)
    normed = (
        center * lax.rsqrt(spread + EPS_NORM) * norm_gain.astype(jnp.float32)
        + norm_bias.astype(jnp.float32)
    ).astype(jnp.bfloat16)
    flat_rows = normed.reshape(num_items * num_rows * num_cols, channels)
    raised = jnp.dot(flat_rows, proj_in, preferred_element_type=jnp.float32) + bias_in.astype(
        jnp.float32
    )
    active = jax.nn.gelu(raised, approximate=False).astype(jnp.bfloat16)
    grouped = active.reshape(num_items, num_rows * num_cols, -1).astype(jnp.float32)
    local_sq = jnp.sum(grouped * grouped, axis=1)
    total_sq = lax.psum(local_sq, "row")
    magnitude = jnp.sqrt(total_sq)
    grn_ratio = magnitude / (jnp.mean(magnitude, axis=-1, keepdims=True) + EPS_GRN)
    hidden = (
        grn_gamma.astype(jnp.float32) * grouped * grn_ratio[:, None, :]
        + grn_beta.astype(jnp.float32)
        + grouped
    ).astype(jnp.bfloat16)
    update = jnp.dot(
        hidden.reshape(num_items * num_rows * num_cols, -1),
        proj_out,
        preferred_element_type=jnp.float32,
    ) + bias_out.astype(jnp.float32)
    return (
        current.astype(jnp.float32) + update.reshape(num_items, num_rows, num_cols, channels)
    ).astype(jnp.bfloat16)


def rows_plan(inputs, *weights):
    (
        depth_kernel,
        depth_bias,
        norm_gain,
        norm_bias,
        proj_in,
        bias_in,
        grn_gamma,
        grn_beta,
        proj_out,
        bias_out,
    ) = weights
    proj_in = lax.all_gather(proj_in, "dp", axis=2, tiled=True)
    proj_out = lax.all_gather(proj_out, "dp", axis=1, tiled=True)
    own_params = tuple(
        w[0]
        for w in (
            depth_kernel,
            depth_bias,
            norm_gain,
            norm_bias,
            proj_in,
            bias_in,
            grn_gamma,
            grn_beta,
            proj_out,
            bias_out,
        )
    )
    sections = lax.axis_size("section")
    section_index = lax.axis_index("section")
    num_micro = inputs.shape[0]
    num_ticks = num_micro + sections - 1
    arriving = jnp.zeros_like(inputs[0])
    saved = jnp.zeros_like(inputs)
    for tick_index in range(num_ticks):
        fresh_input = inputs[min(tick_index, num_micro - 1)]
        current = jnp.where(section_index == 0, fresh_input, arriving)
        produced = conv_block(current, own_params)
        slot_index = tick_index - section_index
        is_valid = jnp.logical_and(slot_index >= 0, slot_index < num_micro)
        safe_slot = jnp.clip(slot_index, 0, num_micro - 1)
        previous = lax.dynamic_index_in_dim(saved, safe_slot, 0, keepdims=False)
        saved = lax.dynamic_update_index_in_dim(
            saved, jnp.where(is_valid, produced, previous), safe_slot, 0
        )
        if tick_index + 1 < num_ticks:
            arriving = lax.ppermute(
                produced, "section", [(i, i + 1) for i in range(sections - 1)]
            )
    return saved[None]


def on_device(inputs, *weights):
    num_micro, images, local_rows, width, channels = inputs.shape
    one_image_each = (
        images == 1
        and lax.axis_size("row") == num_micro == 4
        and lax.axis_size("dp") == 2
        and lax.axis_size("section") == 4
        and local_rows % 4 == 0
        and width % 16 == 0
        and weights[4].shape[2] == 2 * channels
    )
    plan = image_plan if one_image_each else rows_plan
    return plan(inputs, *weights)


def solution(mesh):
    return jax.shard_map(
        on_device,
        mesh=mesh,
        in_specs=(
            P(None, "dp", "row", None, None),
            P("section", None, None, None),
            P("section", None),
            P("section", None),
            P("section", None),
            P("section", None, "dp"),
            P("section", None),
            P("section", None),
            P("section", None),
            P("section", "dp", None),
            P("section", None),
        ),
        out_specs=P("section", None, "dp", "row", None, None),
        check_vma=False,
    )
```

```python
import functools

import jax
import jax.numpy as jnp
from jax import lax
from jax.experimental import pallas as pl
from jax.experimental.pallas import tpu as pltpu
from jax.sharding import PartitionSpec as P

EPS_NORM = 1e-06
EPS_GRN = 1e-06
LANES = 128
VMEM_BYTES = 20 * 1024 * 1024
REACH = 3
CHUNK = 4
NORM_ROWS = 16
IN_ORDER = (0, 1, 2, 3)
VECTORS = 56


def fill_columns(xp, xs, x, channels):
    height, reach_cols, blocks, lanes = xs.shape
    stride = reach_cols - 2 * REACH
    width = stride * blocks
    groups = lanes // LANES
    unroll = min(height, NORM_ROWS)
    border = jnp.zeros((unroll * groups, 8, LANES), jnp.float32)
    xp[0 : unroll * groups, 0:8, :] = border
    xp[0 : unroll * groups, 8 + width : 16 + width, :] = border
    if lanes > channels:
        for k in range(unroll):
            last = k * groups + groups - 1
            xp[last, 8 : 8 + width, :] = jnp.zeros((width, LANES), jnp.float32)

    def rows(n, carry):
        for k in range(unroll):
            r = unroll * n + k
            row = x[r].astype(jnp.float32)
            for g in range(groups):
                at = slice(g * LANES, (g + 1) * LANES)
                own = row[:, g * LANES : min((g + 1) * LANES, channels)]
                xp[k * groups + g, 8 : 8 + width, 0 : own.shape[1]] = own
                for q in range(reach_cols):
                    near = pl.ds(8 - REACH + q, blocks, stride=stride)
                    xs[r, q, :, at] = xp[k * groups + g, near, :]
        return carry

    lax.fori_loop(0, height // unroll, rows, 0)


def conv(xs, cpar, cq):
    rows = xs.shape[0]
    height, stride, blocks, lanes = cq.shape
    span = 2 * REACH + 1
    above = (height - rows) // 2

    def group(g, carry):
        at = pl.ds(pl.multiple_of(g * LANES, LANES), LANES)

        def column(q, carry):
            bias = jnp.broadcast_to(cpar[VECTORS : VECTORS + 1, at], (blocks, LANES))
            acc = [None if above else bias] * height
            for j in range(span):
                kern = [
                    jnp.broadcast_to(cpar[i * span + j : i * span + j + 1, at], (blocks, LANES))
                    for i in range(span)
                ]
                for r in range(rows):
                    x_row = xs[r, q + j, :, at]
                    for i in range(span):
                        h = r + above + REACH - i
                        if 0 <= h < height:
                            term = kern[i] * x_row
                            acc[h] = term if acc[h] is None else acc[h] + term
            for h in range(height):
                cq[h, q, :, at] = acc[h]
            return carry

        return lax.fori_loop(0, stride, column, carry, unroll=2)

    lax.fori_loop(0, lanes // LANES, group, 0)


def norm(cq, cpar, xp, flat, skip=0):
    padded, stride, blocks, lanes = cq.shape
    height = padded - 2 * skip
    gain = cpar[VECTORS + 1 : VECTORS + 2, :]
    shift = cpar[VECTORS + 2 : VECTORS + 3, :]
    channels = flat.shape[2]
    width = stride * blocks
    groups = lanes // LANES
    inside = lax.broadcasted_iota(jnp.int32, (blocks, lanes), 1) < channels

    def rows(n, carry):
        for k in range(NORM_ROWS):
            h = NORM_ROWS * n + k
            for q in range(stride):
                v = cq[h + skip, q]
                mean = jnp.sum(v, axis=-1, keepdims=True) * (1.0 / channels)
                c = jnp.where(inside, v - mean, 0.0)
                var = jnp.sum(c * c, axis=-1, keepdims=True) * (1.0 / channels)
                c = c * lax.rsqrt(var + EPS_NORM) * gain + shift
                for g in range(groups):
                    at = slice(g * LANES, (g + 1) * LANES)
                    xp[k * groups + g, pl.ds(q, blocks, stride=stride), :] = c[:, at]
            for g in range(groups):
                at = slice(g * LANES, min((g + 1) * LANES, channels))
                flat[h, :, at] = xp[k * groups + g, 0:width, 0 : at.stop - at.start].astype(
                    jnp.bfloat16
                )
        return carry

    lax.fori_loop(0, height // NORM_ROWS, rows, 0)


def conv_norm(x, cpar, flat, xp, xs, cq):
    fill_columns(xp, xs, x, x.shape[2])
    conv(xs, cpar, cq)
    norm(cq, cpar, xp, flat)


def conv_scratch(rows, out_rows, width, lanes):
    return [
        pltpu.VMEM((NORM_ROWS * lanes // LANES, width + 16, LANES), jnp.float32),
        pltpu.VMEM((rows, width // 8 + 2 * REACH, 8, lanes), jnp.float32),
        pltpu.VMEM((out_rows, width // 8, 8, lanes), jnp.float32),
    ]


def gelu(v):
    return 0.5 * v * (1.0 + lax.erf(v * (0.5**0.5)))


def up(flat, w_in, bias, act, ssq):
    height, width, channels = flat.shape
    cells = height * width
    half = w_in.shape[1]
    step = 2 * LANES

    def units(start, count):
        raised = jnp.dot(
            flat[...].reshape(cells, channels),
            w_in[0:channels, pl.ds(start, count)],
            preferred_element_type=jnp.float32,
        )
        active = gelu(raised + bias[0:1, pl.ds(start, count)])
        act[:, pl.ds(start, count)] = active.astype(jnp.bfloat16)
        squares = (active * active).reshape(cells // 8, 8, count)
        ssq[:, pl.ds(start, count)] = jnp.sum(squares, axis=0)

    for start in range(0, half, step):
        units(start, min(step, half - start))


def norm_scale(ssqs, fvec, scale):
    half = fvec.shape[2]
    magnitude = [jnp.sqrt(jnp.sum(ssq[...], axis=0, keepdims=True)) for ssq in ssqs]
    mean = jnp.sum(magnitude[0] + magnitude[1], axis=1, keepdims=True) * (0.5 / half)
    for which in range(2):
        ratio = magnitude[which] / (mean + EPS_GRN)
        scale[which] = fvec[which, 1:2, :] * ratio + 1.0


def down(x_rows, first_row, acts, outs, scale, fvec, cpar):
    _, width, channels = x_rows.shape
    cells = CHUNK * width
    at = pl.ds(pl.multiple_of(first_row * width, cells), cells)
    update = cpar[VECTORS + 3 : VECTORS + 4, 0:channels]
    for which in range(2):
        a = acts[which][at, :].astype(jnp.float32)
        hidden = (a * scale[which] + fvec[which, 2:3, :]).astype(jnp.bfloat16)
        update = update + jnp.dot(hidden, outs[which][...], preferred_element_type=jnp.float32)
    return (x_rows.astype(jnp.float32) + update.reshape(CHUNK, width, channels)).astype(
        jnp.bfloat16
    )


def down_all(x, acts, outs, scale, fvec, cvec, out):
    def rows(n, carry):
        at = pl.ds(n * CHUNK, CHUNK)
        out[at] = down(x[at], n * CHUNK, acts, outs, scale, fvec, cvec)
        return carry

    lax.fori_loop(0, x.shape[0] // CHUNK, rows, 0)


def prepare_kernel(part, kernel, *refs):
    vectors, (cpar, fvec) = refs[:7], refs[7:]
    cpar[...] = jnp.zeros(cpar.shape, jnp.float32)
    channels = kernel.shape[3]
    span = kernel.shape[1]
    half = fvec.shape[2]
    for i in range(span):
        cpar[i * span : (i + 1) * span, 0:channels] = kernel[0, i].astype(jnp.float32)
    for n in range(4):
        cpar[VECTORS + n : VECTORS + n + 1, 0:channels] = vectors[n][...].astype(jnp.float32)
    first = part[0] == 0
    for n in range(3):
        v = vectors[4 + n][...].astype(jnp.float32)
        low, high = v[:, 0:half], v[:, half:]
        fvec[0, n : n + 1, :] = jnp.where(first, low, high)
        fvec[1, n : n + 1, :] = jnp.where(first, high, low)


def block_of(me, order, n):
    return n if order is None else me[0] ^ order[n]


def piece_kernel(section, piece, cpar, part, xp, xs, *, on):
    @pl.when(section[0] == on)
    def _():
        fill_columns(xp, xs, piece, piece.shape[2])
        conv(xs, cpar, part)


def last_piece_kernel(section, me, *refs, order, on):
    count = len(order or IN_ORDER)
    pieces, parts = refs[:count], refs[count : 2 * count - 1]
    cpar, both, xp, xs, own, cq = refs[2 * count - 1 :]
    x, flat = both.at[0], both.at[1]
    rows = pieces[0].shape[0]

    @pl.when(section[0] == on)
    def _():
        bias = cpar[VECTORS : VECTORS + 1, :].reshape(1, 1, 1, cq.shape[3])
        cq[...] = jnp.broadcast_to(bias, cq.shape)
        fill_columns(xp, xs, pieces[-1], x.shape[2])
        conv(xs, cpar, own)
        for n, (piece, part) in enumerate(zip(pieces, (*parts, own))):
            at = block_of(me, order, n) * rows
            x[pl.ds(at, rows)] = piece[...]
            cq[pl.ds(at, rows + 2 * REACH)] += part[...]
        norm(cq, cpar, xp, flat, REACH)


def conv_kernel(section, x, cpar, flat, xp, xs, cq, *, tick):
    @pl.when(section[0] == tick)
    def _():
        conv_norm(x, cpar, flat, xp, xs, cq)


def normed_part(ref):
    return ref if len(ref.shape) == 3 else ref.at[1]


def unpack_kernel(packed, w_out):
    cut, channels = w_out.shape[0] // 2, w_out.shape[1]
    first = packed.shape[0] - cut
    w_out[0:cut] = packed[first:, 0:channels]
    w_out[cut:] = packed[first:, channels : 2 * channels]


def up_first_kernel(section, flat, w_in, fvec, act, ssq, *, tick):
    @pl.when(section[0] == tick)
    def _():
        up(normed_part(flat), w_in, fvec.at[0], act, ssq)


def up_second_kernel(section, flat, w_in, fvec, other, act, scale, ssq, *, tick):
    @pl.when(section[0] == tick)
    def _():
        up(normed_part(flat), w_in, fvec.at[1], act, ssq)
        norm_scale((other, ssq), fvec, scale)


def first_down_kernel(section, both, act_a, act_b, out_a, out_b, scale, fvec, cpar, out):
    @pl.when(section[0] == 0)
    def _():
        down_all(both.at[0], (act_a, act_b), (out_a, out_b), scale, fvec, cpar, out)


def down_piece_kernel(
    section, me, x, act_a, act_b, out_a, out_b, scale, fvec, cpar, prev, out, *, order, tick, n
):
    first_row = block_of(me, order, n) * CHUNK
    at = pl.ds(first_row, CHUNK)

    @pl.when(section[0] == tick)
    def _():
        out[...] = down(x[at], first_row, (act_a, act_b), (out_a, out_b), scale, fvec, cpar)

    @pl.when(section[0] != tick)
    def _():
        out[...] = prev[at]


def mlp_kernel(section, both, in_a, in_b, out_a, out_b, fvec, cpar, *refs, tick):
    *pieces, prev, out, act_a, act_b, ssq_a, ssq_b, scale = refs
    x, flat = both.at[0], both.at[1]

    @pl.when(section[0] == tick)
    def _():
        up(flat, in_a, fvec.at[0], act_a, ssq_a)
        up(flat, in_b, fvec.at[1], act_b, ssq_b)
        norm_scale((ssq_a, ssq_b), fvec, scale)
        down_all(x, (act_a, act_b), (out_a, out_b), scale, fvec, cpar, out)

    @pl.when(section[0] == tick - 1)
    def _():
        for n, piece in enumerate(pieces):
            out[n * CHUNK : (n + 1) * CHUNK] = piece[...]

    @pl.when(section[0] < tick - 1)
    def _():
        out[...] = prev[...]


def conv_up_kernel(section, x, cpar, in_a, in_b, fvec, *refs, tick):
    act_a, act_b, scale, xp, xs, cq, flat, ssq_a, ssq_b = refs

    @pl.when(section[0] == tick)
    def _():
        conv_norm(x, cpar, flat, xp, xs, cq)
        up(flat, in_a, fvec.at[0], act_a, ssq_a)
        up(flat, in_b, fvec.at[1], act_b, ssq_b)
        norm_scale((ssq_a, ssq_b), fvec, scale)


def place_kernel(me, *refs, order):
    *pieces, saved, sems = refs
    copies = [
        pltpu.make_async_copy(piece, saved.at[0, block_of(me, order, n), 0], sems.at[n])
        for n, piece in enumerate(pieces)
    ]
    for copy in copies:
        copy.start()
    for copy in copies:
        copy.wait()


SMEM = pl.BlockSpec(memory_space=pltpu.SMEM)
VMEM = pl.BlockSpec(memory_space=pltpu.VMEM)
HBM = pl.BlockSpec(memory_space=pltpu.HBM)


def call(kernel, name, args, out, specs=None, out_specs=None, scratch=(), flops=0, **static):
    if specs is None:
        specs = [SMEM if a.dtype == jnp.int32 else VMEM for a in args]
    if out_specs is None:
        out_specs = jax.tree.map(lambda _: VMEM, out)
    moved = sum(a.size * a.dtype.itemsize for a in args)
    return pl.pallas_call(
        functools.partial(kernel, **static),
        out_shape=out,
        in_specs=specs,
        out_specs=out_specs,
        scratch_shapes=list(scratch),
        compiler_params=pltpu.CompilerParams(vmem_limit_bytes=VMEM_BYTES),
        cost_estimate=pl.CostEstimate(flops=flops, bytes_accessed=moved, transcendentals=0),
        name=name,
    )(*args)


def shape(*dims, dtype=jnp.float32):
    return jax.ShapeDtypeStruct(dims, dtype)


def ssq_scratch(half):
    return pltpu.VMEM((8, half), jnp.float32)


def image_plan(
    inputs,
    depth_kernel,
    depth_bias,
    norm_gain,
    norm_bias,
    proj_in,
    bias_in,
    grn_gamma,
    grn_beta,
    proj_out,
    bias_out,
):
    sections = lax.axis_size("section")
    count = lax.axis_size("row")
    me = lax.axis_index("row").astype(jnp.int32)
    section = lax.axis_index("section").astype(jnp.int32).reshape(1)
    me_ref = me.reshape(1)
    part = lax.axis_index("dp").astype(jnp.int32).reshape(1)
    _, _, rows, width, channels = inputs.shape
    height = rows * count
    cells = height * width
    lanes = -(-channels // LANES) * LANES
    half = proj_in.shape[2]
    span = depth_kernel.shape[1]
    order = (0, 2, 3, 1)
    bf16 = jnp.bfloat16
    whole = shape(height, width, channels, dtype=bf16)
    piece_shape = shape(rows, width, channels, dtype=bf16)
    act_shape = shape(cells, half, dtype=bf16)
    scale_shape = shape(2, 1, half)
    matmul = 2 * cells * channels * half

    helper, source = 1, sections - 1
    pieces = []
    for by in order:
        piece = lax.dynamic_index_in_dim(inputs, me ^ by, 0, keepdims=False)[0]
        if by:
            pairs = [(source * count + (p ^ by), helper * count + p) for p in range(count)]
            piece = lax.ppermute(piece, ("section", "row"), pairs)
        pieces.append(piece)

    def other_half(x, which):
        pairs = [(2 * s + p, 2 * s + 1 - p) for s in which for p in range(2)]
        return lax.ppermute(x, ("section", "dp"), pairs)

    w_in, w_out = proj_in[0], proj_out[0]
    cut = half // 2
    even = range(0, sections, 2)
    odd = range(1, sections, 2)
    other_in = other_half(w_in, even)
    other_out = other_half(w_out, even)

    held = (
        depth_kernel, depth_bias, norm_gain, norm_bias, bias_out, bias_in, grn_gamma, grn_beta
    )
    cpar, fvec = call(
        prepare_kernel,
        "prepare",
        (part, *held),
        (shape(VECTORS + 8, lanes), shape(2, 3, half)),
    )

    def send(x, start, end):
        return lax.ppermute(x, "section", [(start, end)])

    def conv_pieces(pieces, cpar, order, on):
        out_rows = rows + 2 * REACH
        scratch = conv_scratch(rows, out_rows, width, lanes)
        parts = []
        for piece in pieces[:-1]:
            if parts:
                piece, parts[-1] = lax.optimization_barrier((piece, parts[-1]))
            part = call(
                piece_kernel,
                "conv_piece",
                (section, piece, cpar),
                shape(out_rows, width // 8, 8, lanes),
                scratch=scratch[:2],
                on=on,
            )
            parts.append(part)
        return call(
            last_piece_kernel,
            "last_piece",
            (section, me_ref, *pieces, *parts, cpar),
            shape(2, height, width, channels, dtype=bf16),
            scratch=scratch + [conv_scratch(1, height + 2 * REACH, width, lanes)[2]],
            order=order,
            on=on,
        )

    def up_own(flat, tick):
        return call(
            up_first_kernel,
            "up_own",
            (section, flat, w_in, fvec),
            (act_shape, shape(8, half)),
            flops=matmul,
            tick=tick,
        )

    def up_other(flat, other_in, ssq, tick):
        return call(
            up_second_kernel,
            "up_other",
            (section, flat, other_in, fvec, ssq),
            (act_shape, scale_shape),
            scratch=[ssq_scratch(half)],
            flops=matmul,
            tick=tick,
        )

    def unpack(packed):
        return call(unpack_kernel, "unpack", (packed,), shape(half, channels, dtype=bf16))

    def down_piece(x, acts, other_out, prev, order, tick, n):
        act_a, act_b, scale = acts
        return call(
            down_piece_kernel,
            "down_piece",
            (section, me_ref, x, act_a, act_b, w_out, other_out, scale, fvec, cpar, prev),
            piece_shape,
            flops=2 * matmul // count,
            order=order,
            tick=tick,
            n=n,
        )

    both = conv_pieces(pieces, send(cpar, 0, helper), order, helper)
    both, other_in, late_in, late_out = lax.optimization_barrier((both, other_in, w_in, w_out))
    late = jnp.concatenate(
        [late_in, jnp.concatenate([late_out[:cut], late_out[cut:]], axis=1)], axis=0
    )
    odd_other = other_half(late, odd)
    both = send(both, helper, 0)
    act_a, ssq = up_own(both, 0)
    act_b, scale = up_other(both, other_in, ssq, 0)
    result = call(
        first_down_kernel,
        "down",
        (section, both, act_a, act_b, w_out, other_out, scale, fvec, cpar),
        whole,
        flops=2 * matmul,
    )
    x = send(result, 0, 1)
    flat = call(
        conv_kernel,
        "conv",
        (section, x, cpar),
        whole,
        scratch=conv_scratch(height, height, width, lanes),
        tick=1,
    )
    act_a, ssq = up_own(flat, 1)
    odd_other, act_a = lax.optimization_barrier((odd_other, act_a))
    odd_out = unpack(odd_other)
    acts = (act_a, *up_other(flat, odd_other, ssq, 1))
    kept = [down_piece(x, acts, odd_out, result, None, 1, n) for n in range(count)]
    both = conv_pieces([send(piece, 1, 2) for piece in kept], cpar, None, 2)
    result = call(
        mlp_kernel,
        "mlp",
        (section, both, w_in, other_in, w_out, other_out, fvec, cpar, *kept, result),
        whole,
        scratch=[pltpu.VMEM((cells, half), bf16)] * 2
        + [ssq_scratch(half)] * 2
        + [pltpu.VMEM((2, 1, half), jnp.float32)],
        flops=4 * matmul,
        tick=2,
    )
    x = send(result, 2, 3)
    acts = call(
        conv_up_kernel,
        "conv_up",
        (section, x, cpar, w_in, odd_other, fvec),
        (act_shape, act_shape, scale_shape),
        scratch=conv_scratch(height, height, width, lanes)
        + [pltpu.VMEM((height, width, channels), bf16)]
        + [ssq_scratch(half)] * 2,
        flops=2 * matmul,
        tick=3,
    )
    done = []
    for n in (1, 2, 3, 0):
        piece = down_piece(x, acts, odd_out, result, order, 3, n)
        if n:
            piece = lax.ppermute(piece, "row", [(p, p ^ order[n]) for p in range(count)])
        done.append(piece)
    return call(
        place_kernel,
        "place",
        (me_ref, done[3], *done[:3]),
        shape(1, count, 1, rows, width, channels, dtype=bf16),
        out_specs=HBM,
        scratch=[pltpu.SemaphoreType.DMA((count,))],
        order=order,
    )


def extended(cells, sides, width):
    for axis, dim in sides:
        count = lax.axis_size(axis)
        ends = count - 1
        head = lax.slice_in_dim(cells, 0, width, axis=dim)
        tail = lax.slice_in_dim(cells, cells.shape[dim] - width, cells.shape[dim], axis=dim)
        cells = jnp.concatenate(
            [
                lax.ppermute(tail, axis, [(i, (i + 1) % count) for i in range(ends)]),
                cells,
                lax.ppermute(head, axis, [((i + 1) % count, i) for i in range(ends)]),
            ],
            axis=dim,
        )
    return cells


def depthwise(padded, kernel, bias_term):
    channels = padded.shape[-1]
    conv_out = lax.conv_general_dilated(
        padded.astype(jnp.float32),
        kernel.astype(jnp.float32)[:, :, None, :],
        (1, 1),
        "VALID",
        dimension_numbers=("NHWC", "HWIO", "NHWC"),
        feature_group_count=channels,
        precision=lax.Precision.HIGHEST,
    )
    return conv_out + bias_term.astype(jnp.float32)


def conv_block(current, params):
    (
        depth_kernel,
        depth_bias,
        norm_gain,
        norm_bias,
        proj_in,
        bias_in,
        grn_gamma,
        grn_beta,
        proj_out,
        bias_out,
    ) = params
    num_items, num_rows, num_cols, channels = current.shape
    padded = extended(current, (("row", 1),), REACH)
    padded = jnp.pad(padded, ((0, 0), (0, 0), (REACH, REACH), (0, 0)))
    conv_out = depthwise(padded, depth_kernel, depth_bias)
    center = conv_out - jnp.mean(conv_out, axis=-1, keepdims=True)
    spread = jnp.mean(center * center, axis=-1, keepdims=True)
    normed = (
        center * lax.rsqrt(spread + EPS_NORM) * norm_gain.astype(jnp.float32)
        + norm_bias.astype(jnp.float32)
    ).astype(jnp.bfloat16)
    flat_rows = normed.reshape(num_items * num_rows * num_cols, channels)
    raised = jnp.dot(flat_rows, proj_in, preferred_element_type=jnp.float32) + bias_in.astype(
        jnp.float32
    )
    active = jax.nn.gelu(raised, approximate=False).astype(jnp.bfloat16)
    grouped = active.reshape(num_items, num_rows * num_cols, -1).astype(jnp.float32)
    local_sq = jnp.sum(grouped * grouped, axis=1)
    total_sq = lax.psum(local_sq, "row")
    magnitude = jnp.sqrt(total_sq)
    grn_ratio = magnitude / (jnp.mean(magnitude, axis=-1, keepdims=True) + EPS_GRN)
    hidden = (
        grn_gamma.astype(jnp.float32) * grouped * grn_ratio[:, None, :]
        + grn_beta.astype(jnp.float32)
        + grouped
    ).astype(jnp.bfloat16)
    update = jnp.dot(
        hidden.reshape(num_items * num_rows * num_cols, -1),
        proj_out,
        preferred_element_type=jnp.float32,
    ) + bias_out.astype(jnp.float32)
    return (
        current.astype(jnp.float32) + update.reshape(num_items, num_rows, num_cols, channels)
    ).astype(jnp.bfloat16)


def rows_plan(inputs, *weights):
    (
        depth_kernel,
        depth_bias,
        norm_gain,
        norm_bias,
        proj_in,
        bias_in,
        grn_gamma,
        grn_beta,
        proj_out,
        bias_out,
    ) = weights
    proj_in = lax.all_gather(proj_in, "dp", axis=2, tiled=True)
    proj_out = lax.all_gather(proj_out, "dp", axis=1, tiled=True)
    own_params = tuple(
        w[0]
        for w in (
            depth_kernel,
            depth_bias,
            norm_gain,
            norm_bias,
            proj_in,
            bias_in,
            grn_gamma,
            grn_beta,
            proj_out,
            bias_out,
        )
    )
    sections = lax.axis_size("section")
    section_index = lax.axis_index("section")
    num_micro = inputs.shape[0]
    num_ticks = num_micro + sections - 1
    arriving = jnp.zeros_like(inputs[0])
    saved = jnp.zeros_like(inputs)
    for tick_index in range(num_ticks):
        fresh_input = inputs[min(tick_index, num_micro - 1)]
        current = jnp.where(section_index == 0, fresh_input, arriving)
        produced = conv_block(current, own_params)
        slot_index = tick_index - section_index
        is_valid = jnp.logical_and(slot_index >= 0, slot_index < num_micro)
        safe_slot = jnp.clip(slot_index, 0, num_micro - 1)
        previous = lax.dynamic_index_in_dim(saved, safe_slot, 0, keepdims=False)
        saved = lax.dynamic_update_index_in_dim(
            saved, jnp.where(is_valid, produced, previous), safe_slot, 0
        )
        if tick_index + 1 < num_ticks:
            arriving = lax.ppermute(
                produced, "section", [(i, i + 1) for i in range(sections - 1)]
            )
    return saved[None]


def on_device(inputs, *weights):
    num_micro, images, local_rows, width, channels = inputs.shape
    one_image_each = (
        images == 1
        and lax.axis_size("row") == num_micro == 4
        and lax.axis_size("dp") == 2
        and lax.axis_size("section") == 4
        and local_rows % 4 == 0
        and width % 16 == 0
        and weights[4].shape[2] == 2 * channels
    )
    plan = image_plan if one_image_each else rows_plan
    return plan(inputs, *weights)


def solution(mesh):
    return jax.shard_map(
        on_device,
        mesh=mesh,
        in_specs=(
            P(None, "dp", "row", None, None),
            P("section", None, None, None),
            P("section", None),
            P("section", None),
            P("section", None),
            P("section", None, "dp"),
            P("section", None),
            P("section", None),
            P("section", None),
            P("section", "dp", None),
            P("section", None),
        ),
        out_specs=P("section", None, "dp", "row", None, None),
        check_vma=False,
    )
```
